32 devices in a mesh: gx: 4 (over z), gy: 8 (over y, x, core).
Axes of the slice: x: 2, y: 2, z: 4, core: 2. Of those that a mesh axis runs over, the one named last changes fastest.
Arguments:
- right_side: float32 [2, 512, 1024], P(None, 'gx', 'gy'), may hold values from -6 to 6
- shift_coef: float32 [512, 1024], P('gx', 'gy'), may hold values from 0.0001 to 0.001
- viscosity: float32 [512, 1024], P('gx', 'gy'), may hold values from 1 to 10
- wet_tiles: int32 [4, 8], P('gx', 'gy'), may hold values from 0 to 1, as said below
Outputs:
- velocity: float32 [2, 512, 1024], P(None, 'gx', 'gy')
The draws below stay inside these ranges and needn't reach their ends.
Inputs may be any that keep to these rules, and one draw needn't show every extreme that they name: `wet_tiles`: 1 marks a wet tile of 128 x 128 cells, 0 a dry one.
All inputs are finite; a program needn't handle non-finite values.
Results may differ from the reference program's by a relative error of at most 0.00002.
Values sent between devices are 32-bit elements; how exact they have to be, the bound alone decides.
No kernel may reach another device: no remote copies, remote signals or barrier semaphores. Data moves between devices by JAX's collectives and lax.ppermute only.
A program may use at most 64 MiB of HBM per device.

```python
import math
import jax
import jax.numpy as jnp
from jax import lax

TILE = 128
LOCAL = 4
COARSE = 4
COARSE_SWEEPS = 8
NX = 512
NY = 1024


def draw_wet_tiles(key, part):
    tile_rows = NX // TILE
    tile_cols = NY // TILE
    position = lax.broadcasted_iota(jnp.int32, (tile_rows, tile_cols), 0)
    threshold = 40 + 55 * position // max(tile_rows - 1, 1)
    rolled = jax.random.randint(key, (tile_rows, tile_cols), 0, 100)
    return (rolled < threshold).astype(jnp.int32)


def levels(stream_key, dims, pieces, low, top_value):
    def one(dim, parts):
        draws = jax.random.uniform(jax.random.fold_in(jax.random.fold_in(stream_key, 6), dim), (parts,), jnp.float32, low / len(pieces), top_value / len(pieces))
        return jnp.repeat(jnp.exp(draws), dims[dim] // parts).reshape((-1,) + (1,) * (len(dims) - dim - 1))

    factor_of = one(*pieces[0])
    for cut in pieces[1:]:
        factor_of = factor_of * one(*cut)
    return factor_of


def bell_draw(stream_key, extent, scale, most, shards=(), kind=jnp.bfloat16):
    values = scale * jax.random.normal(stream_key, extent, jnp.float32)
    if shards:
        values = values * levels(stream_key, extent, shards, -0.22, 0.18)
    return jnp.clip(values, -most, most).astype(kind)


def setup_inputs(seed: int = 0) -> dict:
    splits = jax.random.split(jax.random.key(seed), 5)
    right_side = bell_draw(splits[0], (2, NX, NY), 1.0, 6.0, ((1, 4), (2, 8)), jnp.float32)
    shift_coef = jnp.clip(jnp.exp(math.log(0.001) - 2.3025852 * jax.random.uniform(splits[1], (NX, NY), jnp.float32) ** levels(splits[1], (NX, NY), ((0, 4), (1, 8)), -0.2, 0.2)), 0.0001, 0.001)
    viscosity = jnp.clip(jnp.exp(math.log(10.0) - 2.3025851 * jax.random.uniform(splits[2], (NX, NY), jnp.float32) ** levels(splits[2], (NX, NY), ((0, 4), (1, 8)), -0.2, 0.2)), 1.0, 10.0)
    wet_tiles = draw_wet_tiles(jax.random.fold_in(splits[4], 71), 0)
    return {"right_side": right_side, "shift_coef": shift_coef, "viscosity": viscosity, "wet_tiles": wet_tiles}


OMEGA = 0.8


def pad_last(field):
    return jnp.pad(field, [(0, 0)] * (field.ndim - 2) + [(1, 1), (1, 1)])


def face_coefs(padded):
    inner = padded[1:-1, 1:-1]
    return jnp.stack([jnp.minimum(inner, padded[:-2, 1:-1]), jnp.minimum(inner, padded[2:, 1:-1]),
                      jnp.minimum(inner, padded[1:-1, :-2]), jnp.minimum(inner, padded[1:-1, 2:])])


def apply_padded(padded, conduct, reaction, spacing):
    inner = padded[:, 1:-1, 1:-1]
    outflow = conduct[0] * (inner - padded[:, :-2, 1:-1]) + conduct[1] * (inner - padded[:, 2:, 1:-1])
    outflow = outflow + conduct[2] * (inner - padded[:, 1:-1, :-2]) + conduct[3] * (inner - padded[:, 1:-1, 2:])
    return reaction * inner + spacing * outflow


def shrink(field):
    size_x, size_y = field.shape[-2:]
    blocks = field.reshape(field.shape[:-2] + (size_x // 2, 2, size_y // 2, 2))
    return jnp.mean(blocks, axis=(-3, -1))


def widen(field):
    return jnp.repeat(jnp.repeat(field, 2, axis=-2), 2, axis=-1)


def level_solve(grid_level, source, reaction, viscous):
    conduct = face_coefs(pad_last(viscous))
    spacing = 0.25 ** grid_level
    diagonal = reaction + spacing * jnp.sum(conduct, axis=0)
    if grid_level == LOCAL + COARSE:
        iterate = jnp.zeros_like(source)
        for sweep_index in range(COARSE_SWEEPS):
            iterate = iterate + OMEGA * (source - apply_padded(pad_last(iterate), conduct, reaction, spacing)) / diagonal
        return iterate
    iterate = OMEGA * source / diagonal
    residual = source - apply_padded(pad_last(iterate), conduct, reaction, spacing)
    correction = level_solve(grid_level + 1, shrink(residual), shrink(reaction), shrink(viscous))
    iterate = iterate + widen(correction)
    return iterate + OMEGA * (source - apply_padded(pad_last(iterate), conduct, reaction, spacing)) / diagonal


def reference(right_side, shift_coef, viscosity, wet_tiles):
    wetness = jnp.repeat(jnp.repeat(wet_tiles, TILE, axis=0), TILE, axis=1).astype(jnp.float32)
    return level_solve(0, right_side * wetness, shift_coef, viscosity * wetness)
```

```python
import functools

import jax
import jax.numpy as jnp
from jax import lax
from jax.experimental import pallas as pl
from jax.experimental.pallas import tpu as pltpu
from jax.sharding import PartitionSpec as P

LOCAL = 4
COARSE = 4
COARSE_SWEEPS = 8
OMEGA = 0.8
KEEP = 1.0 - OMEGA

LANES = 128
SUB = 8
HALO = 24
WIDE = 32
GUARD = 8
ROWS = [(LANES + 2 * HALO) >> level for level in range(LOCAL)]
TILES = [-(-rows // SUB) for rows in ROWS]
HELD = [GUARD + SUB * tiles + 16 for tiles in TILES]
RIM = [HALO >> level for level in range(LOCAL)]
F32 = jnp.float32
VMEM_LIMIT = 48 * 1024 * 1024

X0, X1, EAST, WEST, SOUTH, WEIGHT, S0, S1 = range(8)


def iota(dim, shape=(SUB, LANES)):
    return lax.broadcasted_iota(jnp.int32, shape, dim)


def lane_take(tile, index):
    return jnp.take_along_axis(tile, index, axis=1)


def lane_roll(tile, shift):
    return pltpu.roll(tile, shift % LANES, 1)


def eastern(columns, lane):
    rolled = [lane_roll(c, -1) for c in columns]
    if len(columns) == 1:
        return rolled
    return [jnp.where(lane == LANES - 1, rolled[1 - i], rolled[i]) for i in range(2)]


def western(columns, lane):
    rolled = [lane_roll(c, 1) for c in columns]
    if len(columns) == 1:
        return rolled
    return [jnp.where(lane == 0, rolled[1 - i], rolled[i]) for i in range(2)]


def bands_kernel(wet, right_side, shift_coef, viscosity, first, second):
    odd = lax.axis_index("gx") % 2
    wetness = wet[0, 0].astype(F32)
    bottom = LANES - HALO
    starts = (bottom - bottom * odd, bottom * odd)
    for start, out in zip(starts, (first, second)):
        rows = pl.ds(pl.multiple_of(start, SUB), HALO)
        out[0:HALO, :] = right_side[0, rows, :] * wetness
        out[HALO : 2 * HALO, :] = right_side[1, rows, :] * wetness
        out[2 * HALO : 3 * HALO, :] = shift_coef[rows, :]
        out[3 * HALO : 4 * HALO, :] = viscosity[rows, :] * wetness


def strips_kernel(
    size_x, wet, right_side, shift_coef, viscosity, got_first, got_second, held, first, second
):
    index_x = lax.axis_index("gx")
    odd_x = index_x % 2 == 1
    odd_y = lax.axis_index("gy") % 2 == 1
    wetness = wet[0, 0].astype(F32)
    above = (index_x > 0).astype(F32)
    below = (index_x < size_x - 1).astype(F32)
    top = GUARD + HALO
    low = top + LANES
    held[:, 0:GUARD, :] = jnp.zeros((4, GUARD, LANES), F32)
    held[:, low + HALO :, :] = jnp.zeros((4, HELD[0] - low - HALO, LANES), F32)
    for field in range(4):
        rows = slice(field * HALO, (field + 1) * HALO)
        one, two = got_first[rows, :], got_second[rows, :]
        before = jnp.where(odd_x, one, two)
        after = jnp.where(odd_x, two, one)
        if field == 3:
            before, after = before * above, after * below
        own = (
            right_side[field] * wetness
            if field < 2
            else (shift_coef[...] if field == 2 else viscosity[...] * wetness)
        )
        held[field, GUARD:top, :] = before
        held[field, top:low, :] = own
        held[field, low : low + HALO, :] = after
    lane = iota(1)
    for tile in range(TILES[0]):
        row = GUARD + SUB * tile
        left = right = None
        for field in range(4):
            value = held[field, row : row + SUB, :]
            to_left = lane_roll(value, WIDE * field)
            to_right = lane_roll(value, WIDE * field - (LANES - WIDE))
            if field == 0:
                left, right = to_left, to_right
            else:
                left = jnp.where(lane < WIDE * field, left, to_left)
                right = jnp.where(lane < WIDE * field, right, to_right)
        first[SUB * tile : SUB * tile + SUB, :] = jnp.where(odd_y, left, right)
        second[SUB * tile : SUB * tile + SUB, :] = jnp.where(odd_y, right, left)


def relax_level(level, count, source, reaction, viscous, put):
    lane = iota(1)
    for tile in range(TILES[level]):
        row = GUARD + SUB * tile
        here = [viscous(c, row) for c in range(count)]
        east = [jnp.minimum(a, b) for a, b in zip(here, eastern(here, lane))]
        west = western(east, lane)
        for c in range(count):
            north = jnp.minimum(here[c], viscous(c, row - 1))
            south = jnp.minimum(here[c], viscous(c, row + 1))
            diagonal = reaction(c, row) + (east[c] + west[c] + (north + south))
            weight = OMEGA / diagonal
            put(c, row, east[c], west[c], south, weight)
            put(c, row, None, source(0, c, row) * weight, source(1, c, row) * weight, None)


def down_kernel(
    size_y,
    devices,
    held,
    got_first,
    got_second,
    chunks,
    state0,
    state1,
    state2,
    state3,
    beside,
    beside_coefs,
    left_over,
    coef1,
    coef2,
    coef3,
):
    index_y = lax.axis_index("gy")
    odd_y = index_y % 2 == 1
    left_ok = (index_y > 0).astype(F32)
    right_ok = (index_y < size_y - 1).astype(F32)
    lane = iota(1)
    sub = iota(0)
    states = [state0, state1, state2, state3]
    coefs = [None, coef1, coef2, coef3]

    beside[:, 0:GUARD, :] = jnp.zeros((4, GUARD, LANES), F32)
    beside[:, GUARD + ROWS[0] :, :] = jnp.zeros((4, HELD[0] - GUARD - ROWS[0], LANES), F32)
    for tile in range(TILES[0]):
        rows = slice(SUB * tile, SUB * tile + SUB)
        one, two = got_first[rows, :], got_second[rows, :]
        after = jnp.where(odd_y, two, one)
        before = jnp.where(odd_y, one, two)
        for field in range(4):
            value_after = lane_roll(after, -WIDE * field)
            value_before = lane_roll(before, LANES - WIDE - WIDE * field)
            if field == 3:
                value_after, value_before = value_after * right_ok, value_before * left_ok
            blank = jnp.full((SUB, LANES), 1.0 if field == 2 else 0.0, F32)
            value = jnp.where(
                lane < HALO, value_after, jnp.where(lane >= LANES - HALO, value_before, blank)
            )
            beside[field, GUARD + SUB * tile : GUARD + SUB * tile + SUB, :] = value

    for level in range(LOCAL):
        end = GUARD + SUB * TILES[level]
        states[level][:, 0:GUARD, :] = jnp.zeros((8, GUARD, LANES), F32)
        states[level][:, end:, :] = jnp.zeros((8, HELD[level] - end, LANES), F32)
        if level == 0:
            beside_coefs[:, 0:GUARD, :] = jnp.zeros((3, GUARD, LANES), F32)
            beside_coefs[:, end:, :] = jnp.zeros((3, HELD[0] - end, LANES), F32)
        else:
            for slot, fill in ((0, 1.0), (1, 0.0)):
                coefs[level][slot, 0:GUARD, :] = jnp.full((GUARD, LANES), fill, F32)
                coefs[level][slot, end:, :] = jnp.full((HELD[level] - end, LANES), fill, F32)
    left_over[:, 0:GUARD, :] = jnp.zeros((4, GUARD, LANES), F32)
    left_over[:, GUARD + ROWS[0] :, :] = jnp.zeros((4, HELD[0] - GUARD - ROWS[0], LANES), F32)

    def tile_of(ref, slot, row):
        return ref[slot, row : row + SUB, :]

    for level in range(LOCAL):
        state, coef = states[level], coefs[level]
        count = 2 if level == 0 else 1
        if level == 0:

            def source(comp, c, row):
                return tile_of(held if c == 0 else beside, comp, row)

            def reaction(c, row):
                return tile_of(held if c == 0 else beside, 2, row)

            def viscous(c, row):
                return tile_of(held if c == 0 else beside, 3, row)

            def iterate(comp, c, row):
                return tile_of(state0, 2 * comp + c, row)

            def face(kind, c, row):
                return tile_of(state0, 4 + kind, row) if c == 0 else tile_of(beside_coefs, kind, row)

            def put(c, row, east, a, b, weight):
                rows = slice(row, row + SUB)
                if east is None:
                    state0[c, rows, :] = a
                    state0[2 + c, rows, :] = b
                elif c == 0:
                    state0[4, rows, :] = east
                    state0[5, rows, :] = a
                    state0[6, rows, :] = b
                    state0[7, rows, :] = weight
                else:
                    beside_coefs[0, rows, :] = east
                    beside_coefs[1, rows, :] = a
                    beside_coefs[2, rows, :] = b

        else:

            def source(comp, c, row):
                return tile_of(state, S0 + comp, row)

            def reaction(c, row):
                return tile_of(coef, 0, row)

            def viscous(c, row):
                return tile_of(coef, 1, row)

            def iterate(comp, c, row):
                return tile_of(state, X0 + comp, row)

            def face(kind, c, row):
                return tile_of(state, EAST + kind, row)

            def put(c, row, east, a, b, weight):
                rows = slice(row, row + SUB)
                if east is None:
                    state[X0, rows, :] = a
                    state[X1, rows, :] = b
                else:
                    state[EAST, rows, :] = east
                    state[WEST, rows, :] = a
                    state[SOUTH, rows, :] = b
                    state[WEIGHT, rows, :] = weight

        relax_level(level, count, source, reaction, viscous, put)
        for tile in range(TILES[level]):
            row = GUARD + SUB * tile
            for comp in range(2):
                here = [iterate(comp, c, row) for c in range(count)]
                east, west = eastern(here, lane), western(here, lane)
                for c in range(count):
                    total = face(0, c, row) * east[c] + face(1, c, row) * west[c]
                    total = total + (
                        face(2, c, row) * iterate(comp, c, row + 1)
                        + face(2, c, row - 1) * iterate(comp, c, row - 1)
                    )
                    left_over[2 * comp + c, row : row + SUB, :] = (
                        KEEP * source(comp, c, row) + total
                    )

        def pairs(ref, slot, start):
            value = ref[slot, pl.ds(start, SUB, stride=2), :]
            value = value + ref[slot, pl.ds(start + 1, SUB, stride=2), :]
            return value + lane_roll(value, -1)

        def coef_ref(kind, c):
            if level == 0:
                return (held if c == 0 else beside), 2 + kind
            return coef, kind

        if level < LOCAL - 1:
            spread = (2 * lane) & (LANES - 1)

            def narrowed(refs, start):
                values = [lane_take(pairs(ref, slot, start), spread) for ref, slot in refs]
                if len(values) == 1:
                    return values[0]
                return jnp.where(lane < LANES // 2, values[0], values[1])

            for tile in range(TILES[level + 1]):
                start = GUARD + 2 * SUB * tile
                rows = slice(GUARD + SUB * tile, GUARD + SUB * tile + SUB)
                for comp in range(2):
                    refs = [(left_over, 2 * comp + c) for c in range(count)]
                    states[level + 1][S0 + comp, rows, :] = 0.25 * narrowed(refs, start)
                for kind, scale in ((0, 0.25), (1, 0.0625)):
                    refs = [coef_ref(kind, c) for c in range(count)]
                    coefs[level + 1][kind, rows, :] = scale * narrowed(refs, start)
        else:
            start = GUARD + RIM[level]
            spread = 2 * (lane & (SUB - 1))
            own = [
                0.25 * lane_take(pairs(left_over, 0, start), spread),
                0.25 * lane_take(pairs(left_over, 2, start), spread),
                0.25 * lane_take(pairs(coef, 0, start), spread),
                0.0625 * lane_take(pairs(coef, 1, start), spread),
            ]
            chosen = ((lane >> 3) & (SUB - 1)) == sub
            lower = lane < LANES // 2

            def packed(a, b):
                value = jnp.where(chosen, jnp.where(lower, a, b), 0.0)
                return jnp.sum(value, axis=0, keepdims=True)

            tile = jnp.where(sub % 2 == 0, packed(own[0], own[1]), packed(own[2], own[3]))
            for block in range(2 * devices // SUB):
                chunks[SUB * block : SUB * block + SUB, :] = tile


def coarse_solve(fields, rows_total, cols_total):
    shape = fields[0].shape
    width = shape[1]
    row, lane = iota(0, shape), iota(1, shape)

    def shifted(value, amount, axis):
        return pltpu.roll(value, amount % shape[axis], axis)

    def folded(value, step, scale):
        other = jnp.where(
            (row & step) != 0, shifted(value, step, 0), shifted(value, -step, 0)
        )
        value = value + other
        other = jnp.where(
            (lane & step) != 0, shifted(value, step, 1), shifted(value, -step, 1)
        )
        return scale * (value + other)

    sources = fields[:2]
    reaction = jnp.where(lane < cols_total, fields[2], 1.0)
    viscous = fields[3]
    stored = []
    for level in range(COARSE + 1):
        step = 1 << level
        east = jnp.minimum(viscous, shifted(viscous, -step, 1))
        east = jnp.where(lane < cols_total - step, east, 0.0)
        south = jnp.minimum(viscous, shifted(viscous, -step, 0))
        south = jnp.where(row < rows_total - step, south, 0.0)
        west, north = shifted(east, step, 1), shifted(south, step, 0)
        diagonal = reaction + ((east + west) + (north + south))
        weight = OMEGA / diagonal

        def around(value, east=east, west=west, north=north, south=south, step=step):
            total = east * shifted(value, -step, 1) + west * shifted(value, step, 1)
            return total + (south * shifted(value, -step, 0) + north * shifted(value, step, 0))

        iterates = [weight * s for s in sources]
        if level == COARSE:
            for _ in range(COARSE_SWEEPS - 1):
                iterates = [
                    KEEP * x + weight * (s + around(x)) for x, s in zip(iterates, sources)
                ]
            break
        stored.append((sources, iterates, weight, around))
        sources = [
            folded(KEEP * s + around(x), step, 0.25) for x, s in zip(iterates, sources)
        ]
        reaction = folded(reaction, step, 0.25)
        viscous = folded(viscous, step, 0.0625)
    for sources, before, weight, around in reversed(stored):
        iterates = [x + c for x, c in zip(before, iterates)]
        iterates = [KEEP * x + weight * (s + around(x)) for x, s in zip(iterates, sources)]
    return iterates


def up_kernel(
    size_x,
    size_y,
    gathered,
    held,
    state0,
    state1,
    state2,
    state3,
    out,
    grid,
    whole,
    window,
    wide0,
    wide1,
    wide2,
    wide3,
    corr1,
    corr2,
    corr3,
):
    index_x, index_y = lax.axis_index("gx"), lax.axis_index("gy")
    cells = LANES >> LOCAL
    rows_total, cols_total = cells * size_x, cells * size_y
    width = max(LANES, cols_total)
    columns = width // LANES
    per_column = LANES // cells

    lane = iota(1)
    tall = iota(1, (2 * size_x, LANES))
    for column in range(columns):
        targets = [[jnp.zeros((2 * size_x, LANES), F32)] * cells for _ in range(2)]
        for place in range(min(per_column, size_y - column * per_column)):
            j = column * per_column + place
            chunk = jnp.concatenate(
                [gathered[pl.ds(2 * j + h, size_x, stride=2 * size_y), :] for h in range(2)], 0
            )
            mine = (tall // cells) == place
            turns = {}
            for half in range(2):
                for r in range(cells):
                    shift = (cells * (place - r) - half * LANES // 2) % LANES
                    if shift not in turns:
                        turns[shift] = lane_roll(chunk, shift)
                    targets[half][r] = jnp.where(mine, turns[shift], targets[half][r])
        lanes = slice(LANES * column, LANES * column + LANES)
        for half in range(2):
            for r in range(cells):
                for h in range(2):
                    grid[2 * h + half, column, pl.ds(r, size_x, stride=cells), :] = targets[half][r][
                        h * size_x : (h + 1) * size_x
                    ]
    fields = [
        jnp.concatenate([grid[f, c] for c in range(columns)], 1) if columns > 1 else grid[f, 0]
        for f in range(4)
    ]
    corrections = coarse_solve(fields, rows_total, cols_total)

    narrow = (((((lane + 32) & (LANES - 1)) - 32) >> 1)) & (LANES - 1)
    for comp in range(2):
        turned = pltpu.roll(corrections[comp], (width - cells * index_y) % width, 1)
        if columns == 1:
            whole[comp, GUARD : GUARD + rows_total, :] = turned
        else:
            tall_lane = iota(1, (rows_total, LANES))
            whole[comp, GUARD : GUARD + rows_total, :] = jnp.where(
                tall_lane < LANES // 2, turned[:, :LANES], turned[:, width - LANES :]
            )
        whole[comp, 0:GUARD, :] = jnp.zeros((GUARD, LANES), F32)
        whole[comp, GUARD + rows_total :, :] = jnp.zeros((2 * SUB, LANES), F32)
        start = pl.multiple_of(cells * index_x, SUB)
        window[comp] = whole[comp, pl.ds(start, 4 * SUB), :]
        for tile in range(2):
            value = lane_take(window[comp, 7 + SUB * tile : 15 + SUB * tile, :], narrow)
            begin = GUARD + RIM[3] - 2 + 2 * SUB * tile
            wide3[comp, pl.ds(begin, SUB, stride=2), :] = value
            wide3[comp, pl.ds(begin + 1, SUB, stride=2), :] = value

    states = [state0, state1, state2, state3]
    wides = [wide0, wide1, wide2, wide3]
    corrs = [None, corr1, corr2, corr3]
    for level in (3, 2, 1):
        state, wide, corr = states[level], wides[level], corrs[level]
        first = (GUARD + RIM[level] - 1) // SUB * SUB
        last = GUARD + RIM[level] + (LANES >> level)
        for row in range(first, last + 1, SUB):
            rows = slice(row, row + SUB)
            for comp in range(2):

                def total(at, comp=comp):
                    return state[X0 + comp, at : at + SUB, :] + wide[comp, at : at + SUB, :]

                here = total(row)
                around = state[EAST, rows, :] * lane_roll(here, -1)
                around = around + state[WEST, rows, :] * lane_roll(here, 1)
                around = around + (
                    state[SOUTH, rows, :] * total(row + 1)
                    + state[SOUTH, row - 1 : row - 1 + SUB, :] * total(row - 1)
                )
                corr[comp, rows, :] = KEEP * here + state[WEIGHT, rows, :] * (
                    state[S0 + comp, rows, :] + around
                )
        fine = level - 1
        begin = GUARD + RIM[level] - 1
        target = GUARD + RIM[fine] - 2
        for tile in range(-(-((LANES >> level) + 2) // SUB)):
            at = begin + SUB * tile
            to = target + 2 * SUB * tile
            for comp in range(2):
                value = corr[comp, at : at + SUB, :]
                if fine > 0:
                    copies = [(comp, lane_take(value, narrow))]
                else:
                    half = lane >> 1
                    copies = [
                        (2 * comp, lane_take(value, half)),
                        (2 * comp + 1, lane_take(value, half + LANES // 2)),
                    ]
                for slot, copy in copies:
                    wides[fine][slot, pl.ds(to, SUB, stride=2), :] = copy
                    wides[fine][slot, pl.ds(to + 1, SUB, stride=2), :] = copy

    for tile in range(LANES // SUB):
        row = GUARD + HALO + SUB * tile
        rows = slice(row, row + SUB)
        for comp in range(2):

            def total(c, at, comp=comp):
                slot = 2 * comp + c
                return state0[slot, at : at + SUB, :] + wide0[slot, at : at + SUB, :]

            here, other = total(0, row), total(1, row)
            east = jnp.where(lane == LANES - 1, lane_roll(other, -1), lane_roll(here, -1))
            west = jnp.where(lane == 0, lane_roll(other, 1), lane_roll(here, 1))
            around = state0[4, rows, :] * east + state0[5, rows, :] * west
            around = around + (
                state0[6, rows, :] * total(0, row + 1)
                + state0[6, row - 1 : row - 1 + SUB, :] * total(0, row - 1)
            )
            out[comp, SUB * tile : SUB * tile + SUB, :] = KEEP * here + state0[7, rows, :] * (
                held[comp, rows, :] + around
            )


def params():
    return pltpu.CompilerParams(vmem_limit_bytes=VMEM_LIMIT)


VMEM_SPEC = pl.BlockSpec(memory_space=pltpu.VMEM)
SMEM_SPEC = pl.BlockSpec(memory_space=pltpu.SMEM)


def swap_routes(size_x, size_y):
    def index(i, j):
        return i * size_y + j

    routes = []
    for axis in range(2):
        size = (size_x, size_y)[axis]
        for offset in range(2):
            route = []
            for i in range(size_x):
                for j in range(size_y):
                    here = (i, j)[axis]
                    other = here + 1 if here % 2 == offset else here - 1
                    if 0 <= other < size:
                        peer = (other, j) if axis == 0 else (i, other)
                    else:
                        peer = (i, j ^ 1) if axis == 0 else (i ^ 1, j)
                    route.append((index(i, j), index(*peer)))
            routes.append(route)
    return routes


def per_device(size_x, size_y, right_side, shift_coef, viscosity, wet_tiles):
    axes = ("gx", "gy")
    devices = size_x * size_y
    routes = swap_routes(size_x, size_y)
    band = jax.ShapeDtypeStruct((4 * HALO, LANES), F32)
    first, second = pl.pallas_call(
        bands_kernel,
        out_shape=(band, band),
        in_specs=[SMEM_SPEC, VMEM_SPEC, VMEM_SPEC, VMEM_SPEC],
        out_specs=(VMEM_SPEC, VMEM_SPEC),
        compiler_params=params(),
        name="bands",
    )(wet_tiles, right_side, shift_coef, viscosity)
    first = lax.ppermute(first, axes, routes[0])
    second = lax.ppermute(second, axes, routes[1])
    strip = jax.ShapeDtypeStruct((ROWS[0], LANES), F32)
    held, first, second = pl.pallas_call(
        functools.partial(strips_kernel, size_x),
        out_shape=(pltpu.VMEM((4, HELD[0], LANES), F32), strip, strip),
        in_specs=[SMEM_SPEC] + [VMEM_SPEC] * 5,
        out_specs=(VMEM_SPEC,) * 3,
        compiler_params=params(),
        name="strips",
    )(wet_tiles, right_side, shift_coef, viscosity, first, second)
    first = lax.ppermute(first, axes, routes[2])
    second = lax.ppermute(second, axes, routes[3])
    chunks, *states = pl.pallas_call(
        functools.partial(down_kernel, size_y, devices),
        out_shape=(jax.ShapeDtypeStruct((2 * devices, LANES), F32),)
        + tuple(pltpu.VMEM((8, HELD[level], LANES), F32) for level in range(LOCAL)),
        in_specs=[VMEM_SPEC] * 3,
        out_specs=(VMEM_SPEC,) * (1 + LOCAL),
        scratch_shapes=[
            pltpu.VMEM((4, HELD[0], LANES), F32),
            pltpu.VMEM((3, HELD[0], LANES), F32),
            pltpu.VMEM((4, HELD[0], LANES), F32),
        ]
        + [pltpu.VMEM((2, HELD[level], LANES), F32) for level in range(1, LOCAL)],
        compiler_params=params(),
        name="down",
    )(held, first, second)
    gathered = lax.all_to_all(chunks, axes, 0, 0, tiled=True)
    rows_total = (LANES >> LOCAL) * size_x
    columns = max(LANES, (LANES >> LOCAL) * size_y) // LANES
    return pl.pallas_call(
        functools.partial(up_kernel, size_x, size_y),
        out_shape=jax.ShapeDtypeStruct((2, LANES, LANES), F32),
        in_specs=[VMEM_SPEC] * (2 + LOCAL),
        out_specs=VMEM_SPEC,
        scratch_shapes=[
            pltpu.VMEM((4, columns, rows_total, LANES), F32),
            pltpu.VMEM((2, GUARD + rows_total + 2 * SUB, LANES), F32),
            pltpu.VMEM((2, 4 * SUB, LANES), F32),
            pltpu.VMEM((4, HELD[0], LANES), F32),
        ]
        + [pltpu.VMEM((2, HELD[level], LANES), F32) for level in range(1, LOCAL)]
        + [pltpu.VMEM((2, HELD[level], LANES), F32) for level in range(1, LOCAL)],
        compiler_params=params(),
        name="up",
    )(gathered, held, *states)


def solution(mesh):
    sizes = dict(mesh.shape)
    placed = (P(None, "gx", "gy"), P("gx", "gy"), P("gx", "gy"), P("gx", "gy"))
    return jax.shard_map(
        functools.partial(per_device, sizes["gx"], sizes["gy"]),
        mesh=mesh,
        in_specs=placed,
        out_specs=P(None, "gx", "gy"),
        check_vma=False,
    )
```

```python
import functools

import jax
import jax.numpy as jnp
from jax import lax
from jax.experimental import pallas as pl
from jax.experimental.pallas import tpu as pltpu
from jax.sharding import PartitionSpec as P

LOCAL = 4
COARSE = 4
COARSE_SWEEPS = 8
OMEGA = 0.8
KEEP = 1.0 - OMEGA

LANES = 128
SUB = 8
HALO = 24
WIDE = 32
GUARD = 8
ROWS = [(LANES + 2 * HALO) >> level for level in range(LOCAL)]
TILES = [-(-rows // SUB) for rows in ROWS]
HELD = [GUARD + SUB * tiles + 16 for tiles in TILES]
RIM = [HALO >> level for level in range(LOCAL)]
F32 = jnp.float32
VMEM_LIMIT = 48 * 1024 * 1024

X0, X1, EAST, WEST, SOUTH, WEIGHT, S0, S1 = range(8)


def iota(dim, shape=(SUB, LANES)):
    return lax.broadcasted_iota(jnp.int32, shape, dim)


def lane_take(tile, index):
    return jnp.take_along_axis(tile, index, axis=1)


def lane_roll(tile, shift):
    return pltpu.roll(tile, shift % LANES, 1)


def eastern(columns, lane):
    rolled = [lane_roll(c, -1) for c in columns]
    if len(columns) == 1:
        return rolled
    return [jnp.where(lane == LANES - 1, rolled[1 - i], rolled[i]) for i in range(2)]


def western(columns, lane):
    rolled = [lane_roll(c, 1) for c in columns]
    if len(columns) == 1:
        return rolled
    return [jnp.where(lane == 0, rolled[1 - i], rolled[i]) for i in range(2)]


def bands_kernel(wet, right_side, shift_coef, viscosity, held, first, second, sems):
    odd = lax.axis_index("gx") % 2
    wetness = wet[0, 0].astype(F32)
    top = GUARD + HALO
    own = pl.ds(top, LANES)
    sources = (right_side.at[0], right_side.at[1], shift_coef, viscosity)
    copies = [
        pltpu.make_async_copy(sources[field], held.at[field, own, :], sems.at[field])
        for field in range(4)
    ]
    for copy in copies:
        copy.start()
    bottom = LANES - HALO
    starts = (top + bottom - bottom * odd, top + bottom * odd)
    for field in range(4):
        copies[field].wait()
        for start, out in zip(starts, (first, second)):
            value = held[field, pl.ds(pl.multiple_of(start, SUB), HALO), :]
            out[field * HALO : (field + 1) * HALO, :] = value if field == 2 else value * wetness


def strips_kernel(
    size_x, wet, before_held, got_first, got_second, held, first, second
):
    index_x = lax.axis_index("gx")
    odd_x = index_x % 2 == 1
    odd_y = lax.axis_index("gy") % 2 == 1
    wetness = wet[0, 0].astype(F32)
    above = (index_x > 0).astype(F32)
    below = (index_x < size_x - 1).astype(F32)
    top = GUARD + HALO
    low = top + LANES
    held[:, 0:GUARD, :] = jnp.zeros((4, GUARD, LANES), F32)
    held[:, low + HALO :, :] = jnp.zeros((4, HELD[0] - low - HALO, LANES), F32)
    for field in range(4):
        rows = slice(field * HALO, (field + 1) * HALO)
        one, two = got_first[rows, :], got_second[rows, :]
        before = jnp.where(odd_x, one, two)
        after = jnp.where(odd_x, two, one)
        if field == 3:
            before, after = before * above, after * below
        held[field, GUARD:top, :] = before
        if field != 2:
            held[field, top:low, :] = before_held[field, top:low, :] * wetness
        held[field, low : low + HALO, :] = after
    lane = iota(1)
    for tile in range(TILES[0]):
        row = GUARD + SUB * tile
        left = right = None
        for field in range(4):
            value = held[field, row : row + SUB, :]
            to_left = lane_roll(value, WIDE * field)
            to_right = lane_roll(value, WIDE * field - (LANES - WIDE))
            if field == 0:
                left, right = to_left, to_right
            else:
                left = jnp.where(lane < WIDE * field, left, to_left)
                right = jnp.where(lane < WIDE * field, right, to_right)
        first[SUB * tile : SUB * tile + SUB, :] = jnp.where(odd_y, left, right)
        second[SUB * tile : SUB * tile + SUB, :] = jnp.where(odd_y, right, left)


def relax_level(level, count, source, reaction, viscous, put):
    lane = iota(1)
    for tile in range(TILES[level]):
        row = GUARD + SUB * tile
        here = [viscous(c, row) for c in range(count)]
        east = [jnp.minimum(a, b) for a, b in zip(here, eastern(here, lane))]
        west = western(east, lane)
        for c in range(count):
            north = jnp.minimum(here[c], viscous(c, row - 1))
            south = jnp.minimum(here[c], viscous(c, row + 1))
            diagonal = reaction(c, row) + (east[c] + west[c] + (north + south))
            weight = OMEGA / diagonal
            put(c, row, east[c], west[c], south, weight)
            put(c, row, None, source(0, c, row) * weight, source(1, c, row) * weight, None)


def down_kernel(
    size_y,
    devices,
    held,
    got_first,
    got_second,
    chunks,
    state0,
    state1,
    state2,
    state3,
    beside,
    beside_coefs,
    left_over,
    coef1,
    coef2,
    coef3,
):
    index_y = lax.axis_index("gy")
    odd_y = index_y % 2 == 1
    left_ok = (index_y > 0).astype(F32)
    right_ok = (index_y < size_y - 1).astype(F32)
    lane = iota(1)
    sub = iota(0)
    states = [state0, state1, state2, state3]
    coefs = [None, coef1, coef2, coef3]

    beside[:, 0:GUARD, :] = jnp.zeros((4, GUARD, LANES), F32)
    beside[:, GUARD + ROWS[0] :, :] = jnp.zeros((4, HELD[0] - GUARD - ROWS[0], LANES), F32)
    for tile in range(TILES[0]):
        rows = slice(SUB * tile, SUB * tile + SUB)
        one, two = got_first[rows, :], got_second[rows, :]
        after = jnp.where(odd_y, two, one)
        before = jnp.where(odd_y, one, two)
        for field in range(4):
            value_after = lane_roll(after, -WIDE * field)
            value_before = lane_roll(before, LANES - WIDE - WIDE * field)
            if field == 3:
                value_after, value_before = value_after * right_ok, value_before * left_ok
            blank = jnp.full((SUB, LANES), 1.0 if field == 2 else 0.0, F32)
            value = jnp.where(
                lane < HALO, value_after, jnp.where(lane >= LANES - HALO, value_before, blank)
            )
            beside[field, GUARD + SUB * tile : GUARD + SUB * tile + SUB, :] = value

    for level in range(LOCAL):
        end = GUARD + SUB * TILES[level]
        states[level][:, 0:GUARD, :] = jnp.zeros((8, GUARD, LANES), F32)
        states[level][:, end:, :] = jnp.zeros((8, HELD[level] - end, LANES), F32)
        if level == 0:
            beside_coefs[:, 0:GUARD, :] = jnp.zeros((3, GUARD, LANES), F32)
            beside_coefs[:, end:, :] = jnp.zeros((3, HELD[0] - end, LANES), F32)
        else:
            for slot, fill in ((0, 1.0), (1, 0.0)):
                coefs[level][slot, 0:GUARD, :] = jnp.full((GUARD, LANES), fill, F32)
                coefs[level][slot, end:, :] = jnp.full((HELD[level] - end, LANES), fill, F32)
    left_over[:, 0:GUARD, :] = jnp.zeros((4, GUARD, LANES), F32)
    left_over[:, GUARD + ROWS[0] :, :] = jnp.zeros((4, HELD[0] - GUARD - ROWS[0], LANES), F32)

    def tile_of(ref, slot, row):
        return ref[slot, row : row + SUB, :]

    for level in range(LOCAL):
        state, coef = states[level], coefs[level]
        count = 2 if level == 0 else 1
        if level == 0:

            def source(comp, c, row):
                return tile_of(held if c == 0 else beside, comp, row)

            def reaction(c, row):
                return tile_of(held if c == 0 else beside, 2, row)

            def viscous(c, row):
                return tile_of(held if c == 0 else beside, 3, row)

            def iterate(comp, c, row):
                return tile_of(state0, 2 * comp + c, row)

            def face(kind, c, row):
                return tile_of(state0, 4 + kind, row) if c == 0 else tile_of(beside_coefs, kind, row)

            def put(c, row, east, a, b, weight):
                rows = slice(row, row + SUB)
                if east is None:
                    state0[c, rows, :] = a
                    state0[2 + c, rows, :] = b
                elif c == 0:
                    state0[4, rows, :] = east
                    state0[5, rows, :] = a
                    state0[6, rows, :] = b
                    state0[7, rows, :] = weight
                else:
                    beside_coefs[0, rows, :] = east
                    beside_coefs[1, rows, :] = a
                    beside_coefs[2, rows, :] = b

        else:

            def source(comp, c, row):
                return tile_of(state, S0 + comp, row)

            def reaction(c, row):
                return tile_of(coef, 0, row)

            def viscous(c, row):
                return tile_of(coef, 1, row)

            def iterate(comp, c, row):
                return tile_of(state, X0 + comp, row)

            def face(kind, c, row):
                return tile_of(state, EAST + kind, row)

            def put(c, row, east, a, b, weight):
                rows = slice(row, row + SUB)
                if east is None:
                    state[X0, rows, :] = a
                    state[X1, rows, :] = b
                else:
                    state[EAST, rows, :] = east
                    state[WEST, rows, :] = a
                    state[SOUTH, rows, :] = b
                    state[WEIGHT, rows, :] = weight

        relax_level(level, count, source, reaction, viscous, put)
        for tile in range(TILES[level]):
            row = GUARD + SUB * tile
            for comp in range(2):
                here = [iterate(comp, c, row) for c in range(count)]
                east, west = eastern(here, lane), western(here, lane)
                for c in range(count):
                    total = face(0, c, row) * east[c] + face(1, c, row) * west[c]
                    total = total + (
                        face(2, c, row) * iterate(comp, c, row + 1)
                        + face(2, c, row - 1) * iterate(comp, c, row - 1)
                    )
                    left_over[2 * comp + c, row : row + SUB, :] = (
                        KEEP * source(comp, c, row) + total
                    )

        def pairs(ref, slot, start):
            value = ref[slot, pl.ds(start, SUB, stride=2), :]
            value = value + ref[slot, pl.ds(start + 1, SUB, stride=2), :]
            return value + lane_roll(value, -1)

        def coef_ref(kind, c):
            if level == 0:
                return (held if c == 0 else beside), 2 + kind
            return coef, kind

        if level < LOCAL - 1:
            spread = (2 * lane) & (LANES - 1)

            def narrowed(refs, start):
                values = [lane_take(pairs(ref, slot, start), spread) for ref, slot in refs]
                if len(values) == 1:
                    return values[0]
                return jnp.where(lane < LANES // 2, values[0], values[1])

            for tile in range(TILES[level + 1]):
                start = GUARD + 2 * SUB * tile
                rows = slice(GUARD + SUB * tile, GUARD + SUB * tile + SUB)
                for comp in range(2):
                    refs = [(left_over, 2 * comp + c) for c in range(count)]
                    states[level + 1][S0 + comp, rows, :] = 0.25 * narrowed(refs, start)
                for kind, scale in ((0, 0.25), (1, 0.0625)):
                    refs = [coef_ref(kind, c) for c in range(count)]
                    coefs[level + 1][kind, rows, :] = scale * narrowed(refs, start)
        else:
            start = GUARD + RIM[level]
            spread = 2 * (lane & (SUB - 1))
            own = [
                0.25 * lane_take(pairs(left_over, 0, start), spread),
                0.25 * lane_take(pairs(left_over, 2, start), spread),
                0.25 * lane_take(pairs(coef, 0, start), spread),
                0.0625 * lane_take(pairs(coef, 1, start), spread),
            ]
            chosen = ((lane >> 3) & (SUB - 1)) == sub
            lower = lane < LANES // 2

            def packed(a, b):
                value = jnp.where(chosen, jnp.where(lower, a, b), 0.0)
                return jnp.sum(value, axis=0, keepdims=True)

            tile = jnp.where(sub % 2 == 0, packed(own[0], own[1]), packed(own[2], own[3]))
            for block in range(2 * devices // SUB):
                chunks[SUB * block : SUB * block + SUB, :] = tile


def coarse_solve(fields, rows_total, cols_total):
    shape = fields[0].shape
    width = shape[1]
    row, lane = iota(0, shape), iota(1, shape)

    def shifted(value, amount, axis):
        return pltpu.roll(value, amount % shape[axis], axis)

    def folded(value, step, scale):
        other = jnp.where(
            (row & step) != 0, shifted(value, step, 0), shifted(value, -step, 0)
        )
        value = value + other
        other = jnp.where(
            (lane & step) != 0, shifted(value, step, 1), shifted(value, -step, 1)
        )
        return scale * (value + other)

    sources = fields[:2]
    reaction = jnp.where(lane < cols_total, fields[2], 1.0)
    viscous = fields[3]
    stored = []
    for level in range(COARSE + 1):
        step = 1 << level
        east = jnp.minimum(viscous, shifted(viscous, -step, 1))
        east = jnp.where(lane < cols_total - step, east, 0.0)
        south = jnp.minimum(viscous, shifted(viscous, -step, 0))
        south = jnp.where(row < rows_total - step, south, 0.0)
        west, north = shifted(east, step, 1), shifted(south, step, 0)
        diagonal = reaction + ((east + west) + (north + south))
        weight = OMEGA / diagonal

        def around(value, east=east, west=west, north=north, south=south, step=step):
            total = east * shifted(value, -step, 1) + west * shifted(value, step, 1)
            return total + (south * shifted(value, -step, 0) + north * shifted(value, step, 0))

        iterates = [weight * s for s in sources]
        if level == COARSE:
            for _ in range(COARSE_SWEEPS - 1):
                iterates = [
                    KEEP * x + weight * (s + around(x)) for x, s in zip(iterates, sources)
                ]
            break
        stored.append((sources, iterates, weight, around))
        sources = [
            folded(KEEP * s + around(x), step, 0.25) for x, s in zip(iterates, sources)
        ]
        reaction = folded(reaction, step, 0.25)
        viscous = folded(viscous, step, 0.0625)
    for sources, before, weight, around in reversed(stored):
        iterates = [x + c for x, c in zip(before, iterates)]
        iterates = [KEEP * x + weight * (s + around(x)) for x, s in zip(iterates, sources)]
    return iterates


def up_kernel(
    size_x,
    size_y,
    gathered,
    held,
    state0,
    state1,
    state2,
    state3,
    out,
    grid,
    whole,
    window,
    wide0,
    wide1,
    wide2,
    wide3,
    corr1,
    corr2,
    corr3,
):
    index_x, index_y = lax.axis_index("gx"), lax.axis_index("gy")
    cells = LANES >> LOCAL
    rows_total, cols_total = cells * size_x, cells * size_y
    width = max(LANES, cols_total)
    columns = width // LANES
    per_column = LANES // cells

    lane = iota(1)
    tall = iota(1, (2 * size_x, LANES))
    for column in range(columns):
        targets = [[jnp.zeros((2 * size_x, LANES), F32)] * cells for _ in range(2)]
        for place in range(min(per_column, size_y - column * per_column)):
            j = column * per_column + place
            chunk = jnp.concatenate(
                [gathered[pl.ds(2 * j + h, size_x, stride=2 * size_y), :] for h in range(2)], 0
            )
            mine = (tall // cells) == place
            turns = {}
            for half in range(2):
                for r in range(cells):
                    shift = (cells * (place - r) - half * LANES // 2) % LANES
                    if shift not in turns:
                        turns[shift] = lane_roll(chunk, shift)
                    targets[half][r] = jnp.where(mine, turns[shift], targets[half][r])
        lanes = slice(LANES * column, LANES * column + LANES)
        for half in range(2):
            for r in range(cells):
                for h in range(2):
                    grid[2 * h + half, column, pl.ds(r, size_x, stride=cells), :] = targets[half][r][
                        h * size_x : (h + 1) * size_x
                    ]
    fields = [
        jnp.concatenate([grid[f, c] for c in range(columns)], 1) if columns > 1 else grid[f, 0]
        for f in range(4)
    ]
    corrections = coarse_solve(fields, rows_total, cols_total)

    narrow = (((((lane + 32) & (LANES - 1)) - 32) >> 1)) & (LANES - 1)
    for comp in range(2):
        turned = pltpu.roll(corrections[comp], (width - cells * index_y) % width, 1)
        if columns == 1:
            whole[comp, GUARD : GUARD + rows_total, :] = turned
        else:
            tall_lane = iota(1, (rows_total, LANES))
            whole[comp, GUARD : GUARD + rows_total, :] = jnp.where(
                tall_lane < LANES // 2, turned[:, :LANES], turned[:, width - LANES :]
            )
        whole[comp, 0:GUARD, :] = jnp.zeros((GUARD, LANES), F32)
        whole[comp, GUARD + rows_total :, :] = jnp.zeros((2 * SUB, LANES), F32)
        start = pl.multiple_of(cells * index_x, SUB)
        window[comp] = whole[comp, pl.ds(start, 4 * SUB), :]
        for tile in range(2):
            value = lane_take(window[comp, 7 + SUB * tile : 15 + SUB * tile, :], narrow)
            begin = GUARD + RIM[3] - 2 + 2 * SUB * tile
            wide3[comp, pl.ds(begin, SUB, stride=2), :] = value
            wide3[comp, pl.ds(begin + 1, SUB, stride=2), :] = value

    states = [state0, state1, state2, state3]
    wides = [wide0, wide1, wide2, wide3]
    corrs = [None, corr1, corr2, corr3]
    for level in (3, 2, 1):
        state, wide, corr = states[level], wides[level], corrs[level]
        first = (GUARD + RIM[level] - 1) // SUB * SUB
        last = GUARD + RIM[level] + (LANES >> level)
        for row in range(first, last + 1, SUB):
            rows = slice(row, row + SUB)
            for comp in range(2):

                def total(at, comp=comp):
                    return state[X0 + comp, at : at + SUB, :] + wide[comp, at : at + SUB, :]

                here = total(row)
                around = state[EAST, rows, :] * lane_roll(here, -1)
                around = around + state[WEST, rows, :] * lane_roll(here, 1)
                around = around + (
                    state[SOUTH, rows, :] * total(row + 1)
                    + state[SOUTH, row - 1 : row - 1 + SUB, :] * total(row - 1)
                )
                corr[comp, rows, :] = KEEP * here + state[WEIGHT, rows, :] * (
                    state[S0 + comp, rows, :] + around
                )
        fine = level - 1
        begin = GUARD + RIM[level] - 1
        target = GUARD + RIM[fine] - 2
        for tile in range(-(-((LANES >> level) + 2) // SUB)):
            at = begin + SUB * tile
            to = target + 2 * SUB * tile
            for comp in range(2):
                value = corr[comp, at : at + SUB, :]
                if fine > 0:
                    copies = [(comp, lane_take(value, narrow))]
                else:
                    half = lane >> 1
                    copies = [
                        (2 * comp, lane_take(value, half)),
                        (2 * comp + 1, lane_take(value, half + LANES // 2)),
                    ]
                for slot, copy in copies:
                    wides[fine][slot, pl.ds(to, SUB, stride=2), :] = copy
                    wides[fine][slot, pl.ds(to + 1, SUB, stride=2), :] = copy

    for tile in range(LANES // SUB):
        row = GUARD + HALO + SUB * tile
        rows = slice(row, row + SUB)
        for comp in range(2):

            def total(c, at, comp=comp):
                slot = 2 * comp + c
                return state0[slot, at : at + SUB, :] + wide0[slot, at : at + SUB, :]

            here, other = total(0, row), total(1, row)
            east = jnp.where(lane == LANES - 1, lane_roll(other, -1), lane_roll(here, -1))
            west = jnp.where(lane == 0, lane_roll(other, 1), lane_roll(here, 1))
            around = state0[4, rows, :] * east + state0[5, rows, :] * west
            around = around + (
                state0[6, rows, :] * total(0, row + 1)
                + state0[6, row - 1 : row - 1 + SUB, :] * total(0, row - 1)
            )
            out[comp, SUB * tile : SUB * tile + SUB, :] = KEEP * here + state0[7, rows, :] * (
                held[comp, rows, :] + around
            )


def params():
    return pltpu.CompilerParams(vmem_limit_bytes=VMEM_LIMIT)


VMEM_SPEC = pl.BlockSpec(memory_space=pltpu.VMEM)
SMEM_SPEC = pl.BlockSpec(memory_space=pltpu.SMEM)


def swap_routes(size_x, size_y):
    def index(i, j):
        return i * size_y + j

    routes = []
    for axis in range(2):
        size = (size_x, size_y)[axis]
        for offset in range(2):
            route = []
            for i in range(size_x):
                for j in range(size_y):
                    here = (i, j)[axis]
                    other = here + 1 if here % 2 == offset else here - 1
                    if 0 <= other < size:
                        peer = (other, j) if axis == 0 else (i, other)
                    else:
                        peer = (i, j ^ 1) if axis == 0 else (i ^ 1, j)
                    route.append((index(i, j), index(*peer)))
            routes.append(route)
    return routes


def per_device(size_x, size_y, right_side, shift_coef, viscosity, wet_tiles):
    axes = ("gx", "gy")
    devices = size_x * size_y
    routes = swap_routes(size_x, size_y)
    band = jax.ShapeDtypeStruct((4 * HALO, LANES), F32)
    held, first, second = pl.pallas_call(
        bands_kernel,
        out_shape=(pltpu.VMEM((4, HELD[0], LANES), F32), band, band),
        in_specs=[SMEM_SPEC] + [pl.BlockSpec(memory_space=pltpu.HBM)] * 3,
        out_specs=(VMEM_SPEC,) * 3,
        scratch_shapes=[pltpu.SemaphoreType.DMA((4,))],
        compiler_params=params(),
        name="bands",
    )(wet_tiles, *[pltpu.with_memory_space_constraint(a, pltpu.HBM) for a in (right_side, shift_coef, viscosity)])
    second = lax.ppermute(second, axes, routes[1])
    first = lax.ppermute(first, axes, routes[0])
    strip = jax.ShapeDtypeStruct((ROWS[0], LANES), F32)
    held, first, second = pl.pallas_call(
        functools.partial(strips_kernel, size_x),
        out_shape=(pltpu.VMEM((4, HELD[0], LANES), F32), strip, strip),
        in_specs=[SMEM_SPEC] + [VMEM_SPEC] * 3,
        out_specs=(VMEM_SPEC,) * 3,
        input_output_aliases={1: 0},
        compiler_params=params(),
        name="strips",
    )(wet_tiles, held, first, second)
    second = lax.ppermute(second, axes, routes[3])
    first = lax.ppermute(first, axes, routes[2])
    chunks, *states = pl.pallas_call(
        functools.partial(down_kernel, size_y, devices),
        out_shape=(jax.ShapeDtypeStruct((2 * devices, LANES), F32),)
        + tuple(pltpu.VMEM((8, HELD[level], LANES), F32) for level in range(LOCAL)),
        in_specs=[VMEM_SPEC] * 3,
        out_specs=(VMEM_SPEC,) * (1 + LOCAL),
        scratch_shapes=[
            pltpu.VMEM((4, HELD[0], LANES), F32),
            pltpu.VMEM((3, HELD[0], LANES), F32),
            pltpu.VMEM((4, HELD[0], LANES), F32),
        ]
        + [pltpu.VMEM((2, HELD[level], LANES), F32) for level in range(1, LOCAL)],
        compiler_params=params(),
        name="down",
    )(held, first, second)
    gathered = lax.all_to_all(chunks, axes, 0, 0, tiled=True)
    rows_total = (LANES >> LOCAL) * size_x
    columns = max(LANES, (LANES >> LOCAL) * size_y) // LANES
    return pl.pallas_call(
        functools.partial(up_kernel, size_x, size_y),
        out_shape=jax.ShapeDtypeStruct((2, LANES, LANES), F32),
        in_specs=[VMEM_SPEC] * (2 + LOCAL),
        out_specs=VMEM_SPEC,
        scratch_shapes=[
            pltpu.VMEM((4, columns, rows_total, LANES), F32),
            pltpu.VMEM((2, GUARD + rows_total + 2 * SUB, LANES), F32),
            pltpu.VMEM((2, 4 * SUB, LANES), F32),
            pltpu.VMEM((4, HELD[0], LANES), F32),
        ]
        + [pltpu.VMEM((2, HELD[level], LANES), F32) for level in range(1, LOCAL)]
        + [pltpu.VMEM((2, HELD[level], LANES), F32) for level in range(1, LOCAL)],
        compiler_params=params(),
        name="up",
    )(gathered, held, *states)


def solution(mesh):
    sizes = dict(mesh.shape)
    placed = (P(None, "gx", "gy"), P("gx", "gy"), P("gx", "gy"), P("gx", "gy"))
    return jax.shard_map(
        functools.partial(per_device, sizes["gx"], sizes["gy"]),
        mesh=mesh,
        in_specs=placed,
        out_specs=P(None, "gx", "gy"),
        check_vma=False,
    )
```

```python
import functools

import jax
import jax.numpy as jnp
from jax import lax
from jax.experimental import pallas as pl
from jax.experimental.pallas import tpu as pltpu
from jax.sharding import PartitionSpec as P

LOCAL = 4
COARSE = 4
COARSE_SWEEPS = 8
OMEGA = 0.8
KEEP = 1.0 - OMEGA

LANES = 128
HALF = LANES // 2
SUB = 8
HALO = 16
GUARD = 8
CELLS = LANES >> LOCAL
ROWS = [(LANES + 2 * HALO) >> level for level in range(LOCAL)]
TILES = [-(-rows // SUB) for rows in ROWS]
HELD = [GUARD + SUB * tiles + 16 for tiles in TILES]
RIM = [HALO >> level for level in range(LOCAL)]
TOP = GUARD + HALO
LOW = TOP + LANES
HALF_TILES = TILES[0] // 2
MESSAGE = ROWS[0] // 2
CHUNK = 4
F32 = jnp.float32
VMEM_LIMIT = 48 * 1024 * 1024

EVEN, ODD, LEFT_ODD, RIGHT_EVEN = range(4)
SWEPT, CENTRE, SIDE, ACROSS = 0, 4, 6, 8
STATE = 10
ITERATE, WEIGHT = 10, 14


def iota(dim, shape=(SUB, LANES)):
    return lax.broadcasted_iota(jnp.int32, shape, dim)


def lane_take(tile, index):
    return jnp.take_along_axis(tile, index, axis=1)


def lane_roll(tile, shift):
    return pltpu.roll(tile, shift % LANES, 1)


def tile_at(ref, slot, row):
    return ref[slot, row : row + SUB, :]


def bands_kernel(wet, right_side, shift_coef, viscosity, held, first, second, sems):
    odd = lax.axis_index("gx") % 2
    wetness = wet[0, 0].astype(F32)
    own = pl.ds(TOP, LANES)
    sources = (right_side.at[0], right_side.at[1], shift_coef, viscosity)
    copies = [
        pltpu.make_async_copy(sources[field], held.at[field, own, :], sems.at[field])
        for field in range(4)
    ]
    for copy in copies:
        copy.start()
    bottom = LANES - HALO
    starts = (TOP + bottom - bottom * odd, TOP + bottom * odd)
    for field in range(4):
        copies[field].wait()
        for start, out in zip(starts, (first, second)):
            value = held[field, pl.ds(pl.multiple_of(start, SUB), HALO), :]
            out[field * HALO : (field + 1) * HALO, :] = value if field == 2 else value * wetness


def strips_kernel(size_x, wet, before_held, got_first, got_second, held, first, second):
    index_x = lax.axis_index("gx")
    odd_x = index_x % 2 == 1
    odd_y = lax.axis_index("gy") % 2 == 1
    wetness = wet[0, 0].astype(F32)
    above = (index_x > 0).astype(F32)
    below = (index_x < size_x - 1).astype(F32)
    for field in range(4):
        rows = slice(field * HALO, (field + 1) * HALO)
        one, two = got_first[rows, :], got_second[rows, :]
        before = jnp.where(odd_x, one, two)
        after = jnp.where(odd_x, two, one)
        if field == 3:
            before, after = before * above, after * below
        held[field, GUARD:TOP, :] = before
        if field != 2:
            held[field, TOP:LOW, :] = before_held[field, TOP:LOW, :] * wetness
        held[field, LOW : LOW + HALO, :] = after
    lane = iota(1)
    for tile in range(HALF_TILES):
        left = right = None
        for half in range(2):
            row = GUARD + SUB * (tile + half * HALF_TILES)
            for field in range(4):
                value = held[field, row : row + SUB, :]
                place = HALF * half + HALO * field
                other = HALF * (1 - half) + HALO * field
                to_left = lane_roll(value, place)
                to_right = lane_roll(value, other - (LANES - HALO))
                if left is None:
                    left, right = to_left, to_right
                else:
                    left = jnp.where(lane >= place, to_left, left)
                    right = jnp.where((lane >= other) & (lane < other + HALO), to_right, right)
        rows = slice(SUB * tile, SUB * tile + SUB)
        first[rows, :] = jnp.where(odd_y, left, right)
        second[rows, :] = jnp.where(odd_y, right, left)


def down_kernel(size_y, devices, held, got_first, got_second, chunks, *refs):
    states, refs = refs[:LOCAL], refs[LOCAL:]
    fields, refs = refs[:LOCAL], refs[LOCAL:]
    iterates, refs = refs[:LOCAL], refs[LOCAL:]
    faces, refs = refs[:LOCAL], refs[LOCAL:]
    sums, ring = refs[:LOCAL], refs[LOCAL]
    index_y = lax.axis_index("gy")
    odd_y = index_y % 2 == 1
    lane, sub = iota(1), iota(0)
    side_ok = jnp.where(
        lane < 96, (index_y < size_y - 1).astype(F32), (index_y > 0).astype(F32)
    )
    odd_row = (sub & 1) == 1
    inner = lane < HALF

    spread = 2 * lane
    for tile in range(HALF_TILES):
        rows = slice(SUB * tile, SUB * tile + SUB)
        one, two = got_first[rows, :], got_second[rows, :]
        after = jnp.where(odd_y, two, one)
        before = jnp.where(odd_y, one, two)
        for half in range(2):
            row = GUARD + SUB * (tile + half * HALF_TILES)
            rims = jnp.where(inner, after, before) if half == 0 else jnp.where(inner, before, after)
            base = jnp.where((lane < 96) == (half == 0), 0, HALF) + 2 * (lane & 7)
            for field in range(4):
                own = held[field, row : row + SUB, :]
                for parity in range(2):
                    mine = lane_take(own, (spread + parity) & (LANES - 1))
                    rim = lane_take(rims, base + (HALO * field + parity))
                    if field == 3:
                        rim = rim * side_ok
                    fields[0][2 * field + parity, row : row + SUB, :] = jnp.where(inner, mine, rim)

    def source_slot(level, comp, kind):
        return 2 * comp + kind if level == 0 else 4 * comp + kind

    def iterate_slot(level, comp, kind):
        return 2 * comp + kind if level == 0 else 4 * comp + kind

    for level in range(LOCAL):
        field, iterate, face, state, summed = (
            fields[level],
            iterates[level],
            faces[level],
            states[level],
            sums[level],
        )
        reaction_at, viscous_at = (4, 6) if level == 0 else (8, 10)
        for tile in range(TILES[level]):
            row = GUARD + SUB * tile
            rows = slice(row, row + SUB)
            here = [tile_at(field, viscous_at + p, row) for p in range(2)]
            if level == 0:
                left_odd, right_even = lane_roll(here[1], 1), lane_roll(here[0], -1)
            else:
                left_odd = tile_at(field, viscous_at + LEFT_ODD, row)
                right_even = tile_at(field, viscous_at + RIGHT_EVEN, row)
            middle = jnp.minimum(here[0], here[1])
            outer = [jnp.minimum(here[0], left_odd), jnp.minimum(here[1], right_even)]
            face[0, rows, :] = middle
            weights = []
            for p in range(2):
                north = jnp.minimum(here[p], tile_at(field, viscous_at + p, row - 1))
                south = jnp.minimum(here[p], tile_at(field, viscous_at + p, row + 1))
                diagonal = tile_at(field, reaction_at + p, row) + (
                    (middle + outer[p]) + (north + south)
                )
                weights.append(OMEGA / diagonal)
                face[1 + p, rows, :] = outer[p]
                face[3 + p, rows, :] = south
                face[5 + p, rows, :] = weights[p]
            if level > 0:
                weights += [lane_roll(weights[1], 1), lane_roll(weights[0], -1)]
            for comp in range(2):
                for kind, weight in enumerate(weights):
                    iterate[iterate_slot(level, comp, kind), rows, :] = weight * tile_at(
                        field, source_slot(level, comp, kind), row
                    )
        for tile in range(TILES[level]):
            row = GUARD + SUB * tile
            rows = slice(row, row + SUB)
            middle = face[0, rows, :]
            outer = [face[1 + p, rows, :] for p in range(2)]
            south = [face[3 + p, rows, :] for p in range(2)]
            north = [tile_at(face, 3 + p, row - 1) for p in range(2)]
            weights = [face[5 + p, rows, :] for p in range(2)]
            for comp in range(2):
                here = [tile_at(iterate, iterate_slot(level, comp, p), row) for p in range(2)]
                if level == 0:
                    beyond = [lane_roll(here[1], 1), lane_roll(here[0], -1)]
                else:
                    beyond = [
                        tile_at(iterate, iterate_slot(level, comp, kind), row)
                        for kind in (LEFT_ODD, RIGHT_EVEN)
                    ]
                total = None
                for p in range(2):
                    slot = iterate_slot(level, comp, p)
                    around = middle * here[1 - p] + outer[p] * beyond[p]
                    around = around + (
                        south[p] * tile_at(iterate, slot, row + 1)
                        + north[p] * tile_at(iterate, slot, row - 1)
                    )
                    left = KEEP * tile_at(field, source_slot(level, comp, p), row) + around
                    state[SWEPT + 2 * comp + p, rows, :] = here[p] + weights[p] * left
                    if level == LOCAL - 1:
                        ring[2 * comp + p, rows, :] = left
                        state[ITERATE + 2 * comp + p, rows, :] = here[p]
                    total = left if total is None else total + left
                summed[comp, rows, :] = total
            for p in range(2):
                within = jnp.where(odd_row, north[p], south[p])
                across = jnp.where(odd_row, south[p], north[p])
                state[CENTRE + p, rows, :] = KEEP + weights[p] * (middle + within)
                state[SIDE + p, rows, :] = weights[p] * outer[p]
                state[ACROSS + p, rows, :] = weights[p] * across
                if level == LOCAL - 1:
                    state[WEIGHT + p, rows, :] = weights[p]

        def pairs(ref, slot, start):
            return (
                ref[slot, pl.ds(start, SUB, stride=2), :]
                + ref[slot, pl.ds(start + 1, SUB, stride=2), :]
            )

        def coefficient(at, start):
            return pairs(field, at, start) + pairs(field, at + 1, start)

        if level < LOCAL - 1:
            coarse = fields[level + 1]
            takes = [(spread + offset) & (LANES - 1) for offset in (0, 1, -1, 2)]
            for tile in range(TILES[level + 1]):
                start = GUARD + 2 * SUB * tile
                rows = slice(GUARD + SUB * tile, GUARD + SUB * tile + SUB)
                viscous = 0.0625 * coefficient(viscous_at, start)
                reaction = 0.25 * coefficient(reaction_at, start)
                for kind in range(4):
                    coarse[10 + kind, rows, :] = lane_take(viscous, takes[kind])
                for kind in range(2):
                    coarse[8 + kind, rows, :] = lane_take(reaction, takes[kind])
                for comp in range(2):
                    source = 0.25 * pairs(summed, comp, start)
                    for kind in range(4):
                        coarse[4 * comp + kind, rows, :] = lane_take(source, takes[kind])
            continue

        start = GUARD + RIM[level]
        column = lane & (SUB - 1)
        own = [
            lane_take(0.25 * pairs(summed, 0, start), column),
            lane_take(0.25 * pairs(summed, 1, start), column),
            lane_take(0.25 * coefficient(reaction_at, start), column),
            lane_take(0.0625 * coefficient(viscous_at, start), column),
        ]
        chosen = ((lane >> 3) & (SUB - 1)) == sub
        edge = (lane >> 4) & 3
        place = lane & 15

        def packed(value):
            return jnp.sum(value, axis=0, keepdims=True)

        def joined(a, b):
            return packed(jnp.where(chosen, jnp.where(inner, a, b), 0.0))

        rims = jnp.zeros((SUB, LANES), F32)
        for part in range(2):
            for p in range(2):
                index = jnp.where(edge < 2, column, 0 if p == 0 else SUB - 1)
                along = (edge == part) & ((place >> 3) == p) & (sub == (0 if part == 0 else SUB - 1))
                up = (edge == 2 + p) & (place == sub + SUB * part)
                row = start + SUB * part
                value = jnp.where(
                    inner,
                    lane_take(tile_at(ring, p, row), index),
                    lane_take(tile_at(ring, 2 + p, row), index),
                )
                rims = jnp.where(along | up, value, rims)
        kind = sub % CHUNK
        tile = jnp.where(
            kind == 0,
            joined(own[0], own[1]),
            jnp.where(kind == 1, joined(own[2], own[3]), jnp.where(kind == 2, packed(rims), 0.0)),
        )
        for block in range(CHUNK * devices // SUB):
            chunks[SUB * block : SUB * block + SUB, :] = tile


def coarse_solve(fields, rows_total, cols_total):
    shape = fields[0].shape
    width = shape[1]
    row, lane = iota(0, shape), iota(1, shape)

    def along(value, amount):
        return pltpu.roll(value, amount % width, 1)

    def down(value, amount):
        return pltpu.roll(value, amount % shape[0], 0)

    sources = fields[:2]
    reaction = jnp.where(lane < cols_total, fields[2], 1.0)
    viscous = fields[3]
    stored = []
    for level in range(COARSE):
        step = 1 << level
        odd_lane, odd_row = (lane & step) != 0, (row & step) != 0

        def paired(value):
            return (
                jnp.where(odd_lane, along(value, step), value),
                jnp.where(odd_lane, value, along(value, -step)),
            )

        def outside(value):
            return (
                jnp.where(odd_lane, along(value, 2 * step), along(value, step)),
                jnp.where(odd_lane, along(value, -step), along(value, -2 * step)),
            )

        here, reactions = paired(viscous), paired(reaction)
        beyond = outside(viscous)
        beyond = (
            jnp.where(lane < 2 * step, 0.0, beyond[0]),
            jnp.where(lane < cols_total - 2 * step, beyond[1], 0.0),
        )
        middle = jnp.minimum(here[0], here[1])
        outer = [jnp.minimum(a, b) for a, b in zip(here, beyond)]
        north, south, weights = [], [], []
        for p in range(2):
            above = jnp.where(row < step, 0.0, down(here[p], step))
            below = jnp.where(row < rows_total - step, down(here[p], -step), 0.0)
            north.append(jnp.minimum(here[p], above))
            south.append(jnp.minimum(here[p], below))
            diagonal = reactions[p] + ((middle + outer[p]) + (north[p] + south[p]))
            weights.append(OMEGA / diagonal)
        weights_beyond = (along(weights[1], 2 * step), along(weights[0], -2 * step))
        swept, remaining = [], []
        for source in sources:
            values, values_beyond = paired(source), outside(source)
            x = [w * s for w, s in zip(weights, values)]
            x_beyond = [w * s for w, s in zip(weights_beyond, values_beyond)]
            total = None
            for p in range(2):
                around = middle * x[1 - p] + outer[p] * x_beyond[p]
                around = around + (south[p] * down(x[p], -step) + north[p] * down(x[p], step))
                left = KEEP * values[p] + around
                swept.append(x[p] + weights[p] * left)
                total = left if total is None else total + left
            remaining.append(total)
        centre, side, across = [], [], []
        for p in range(2):
            within = jnp.where(odd_row, north[p], south[p])
            out = jnp.where(odd_row, south[p], north[p])
            centre.append(KEEP + weights[p] * (middle + within))
            side.append(weights[p] * outer[p])
            across.append(weights[p] * out)
        stored.append((step, odd_lane, odd_row, swept, centre, side, across))

        def folded(value, scale):
            return scale * (value + jnp.where(odd_row, down(value, step), down(value, -step)))

        sources = [folded(total, 0.25) for total in remaining]
        reaction = folded(reactions[0] + reactions[1], 0.25)
        viscous = folded(here[0] + here[1], 0.0625)

    block = 1 << COARSE
    rows_left, cols_left = rows_total // block, cols_total // block
    cells = [(i, j) for i in range(rows_left) for j in range(cols_left)]

    def spread_cells(value):
        found = {}
        for i, j in cells:
            column, place = divmod(block * j, LANES)
            tile = value[block * i : block * i + SUB, LANES * column : LANES * column + LANES]
            found[i, j] = lane_take(tile, jnp.full((SUB, LANES), place, jnp.int32))
        return found

    source_cells = [spread_cells(s) for s in sources]
    reaction_cells, viscous_cells = spread_cells(reaction), spread_cells(viscous)
    pulls, weight_cells = {}, {}
    for i, j in cells:
        near = [c for c in ((i - 1, j), (i + 1, j), (i, j - 1), (i, j + 1)) if c in viscous_cells]
        links = [(c, jnp.minimum(viscous_cells[i, j], viscous_cells[c])) for c in near]
        diagonal = reaction_cells[i, j] + sum(c for _, c in links)
        weight_cells[i, j] = OMEGA / diagonal
        pulls[i, j] = [(c, weight_cells[i, j] * link) for c, link in links]
    solved = []
    for comp in range(2):
        pushed = {c: weight_cells[c] * source_cells[comp][c] for c in cells}
        values = pushed
        for _ in range(COARSE_SWEEPS - 1):
            values = {
                c: (KEEP * values[c] + pushed[c])
                + sum(pull * values[other] for other, pull in pulls[c])
                for c in cells
            }
        solved.append(values)

    def laid(values, di, dj):
        tiles = []
        nothing = jnp.zeros((SUB, LANES), F32)
        for tile in range(shape[0] // SUB):
            i = SUB * tile // block
            if di:
                i += 1 if (SUB * tile // (block // 2)) % 2 else -1
            columns = []
            for column in range(width // LANES):
                place = iota(1) // block + column * (LANES // block)
                value = nothing
                for j in range(cols_left):
                    if (i, j) in values and column * LANES <= (j - dj) * block < (column + 1) * LANES:
                        value = jnp.where(place == j - dj, values[i, j], value)
                columns.append(value)
            tiles.append(columns[0] if len(columns) == 1 else jnp.concatenate(columns, 1))
        return jnp.concatenate(tiles, 0)

    corrections = None
    for step, odd_lane, odd_row, swept, centre, side, across in reversed(stored):
        found = []
        for comp in range(2):
            if corrections is None:
                here = laid(solved[comp], 0, 0)
                beyond = [laid(solved[comp], 0, -1), laid(solved[comp], 0, 1)]
                out = laid(solved[comp], 1, 0)
            else:
                here = corrections[comp]
                beyond = [along(here, 2 * step), along(here, -2 * step)]
                out = jnp.where(odd_row, down(here, -step), down(here, step))
            parts = [
                (swept[2 * comp + p] + centre[p] * here) + (side[p] * beyond[p] + across[p] * out)
                for p in range(2)
            ]
            found.append(jnp.where(odd_lane, parts[1], parts[0]))
        corrections = found
    return corrections


def up_kernel(size_x, size_y, gathered, state0, state1, state2, state3, out, *refs):
    grid, whole, swept3, corr1, corr2, corr3, merged0, merged1, merged2 = refs
    index_x, index_y = lax.axis_index("gx"), lax.axis_index("gy")
    rows_total, cols_total = CELLS * size_x, CELLS * size_y
    width = max(LANES, cols_total)
    columns = width // LANES
    per_column = LANES // CELLS
    lane, sub = iota(1), iota(0)

    tall = iota(1, (2 * size_x, LANES))
    for column in range(columns):
        targets = [[jnp.zeros((2 * size_x, LANES), F32)] * CELLS for _ in range(2)]
        for place in range(min(per_column, size_y - column * per_column)):
            j = column * per_column + place
            chunk = jnp.concatenate(
                [
                    gathered[pl.ds(CHUNK * j + h, size_x, stride=CHUNK * size_y), :]
                    for h in range(2)
                ],
                0,
            )
            mine = (tall // CELLS) == place
            turns = {}
            for half in range(2):
                for r in range(CELLS):
                    shift = (CELLS * (place - r) - half * HALF) % LANES
                    if shift not in turns:
                        turns[shift] = lane_roll(chunk, shift)
                    targets[half][r] = jnp.where(mine, turns[shift], targets[half][r])
        for half in range(2):
            for r in range(CELLS):
                for h in range(2):
                    grid[2 * h + half, column, pl.ds(r, size_x, stride=CELLS), :] = targets[half][r][
                        h * size_x : (h + 1) * size_x
                    ]
    fields = [
        jnp.concatenate([grid[f, c] for c in range(columns)], 1) if columns > 1 else grid[f, 0]
        for f in range(4)
    ]

    def ring_row(dx, dy):
        i = jnp.clip(index_x + dx, 0, size_x - 1)
        j = jnp.clip(index_y + dy, 0, size_y - 1)
        return jnp.broadcast_to(
            gathered[pl.ds(CHUNK * (i * size_y + j) + 2, 1), :], (SUB, LANES)
        )

    beside = {
        (dx, dy): ring_row(dx, dy) for dx in (-1, 0, 1) for dy in (-1, 0, 1) if dx or dy
    }
    start = GUARD + RIM[3]
    for comp in range(2):
        base = comp * HALF
        for p in range(2):
            slot = 2 * comp + p
            end = 7 if p else 0
            corner_lane = LANES - 1 if p else SUB
            dy = -1 if p else 1
            for tile in range(2):
                at = start + SUB * tile
                index = base + (48 if p else 32) + SUB * tile + sub
                ringed = lane_take(beside[0, dy], index)
                swept = jnp.where(
                    lane == corner_lane,
                    tile_at(state3, ITERATE + slot, at) + tile_at(state3, WEIGHT + p, at) * ringed,
                    tile_at(state3, SWEPT + slot, at),
                )
                swept3[slot, at : at + SUB, :] = swept
            for dx, at, edge in ((-1, start - 1, 16), (1, start + 2 * SUB, 0)):
                index = base + edge + 8 * p
                ringed = jnp.where(
                    lane == corner_lane,
                    lane_take(beside[dx, dy], jnp.full((SUB, LANES), index + end, jnp.int32)),
                    lane_take(beside[dx, 0], index + (lane & 7)),
                )
                rows = slice(at, at + 1)
                swept3[slot, rows, :] = (
                    state3[ITERATE + slot, rows, :] + state3[WEIGHT + p, rows, :] * ringed[0:1]
                )

    corrections = coarse_solve(fields, rows_total, cols_total)

    for comp in range(2):
        for kind in range(3):
            shift = (width - CELLS * index_y + (0, -1, 1)[kind] + width) % width
            turned = pltpu.roll(corrections[comp], shift, 1)
            if columns > 1:
                tall_lane = iota(1, (rows_total, LANES))
                turned = jnp.where(
                    tall_lane < HALF, turned[:, :LANES], turned[:, width - LANES :]
                )
            slot = 3 * comp + kind
            whole[slot, 2 * GUARD : 2 * GUARD + rows_total, :] = turned
            whole[slot, 0 : 2 * GUARD, :] = jnp.zeros((2 * GUARD, LANES), F32)
            whole[slot, 2 * GUARD + rows_total :, :] = jnp.zeros((3 * SUB, LANES), F32)

    def swept_rows(ref, level, coarse_row, parity, here, beyond, across, comp):
        at = pl.ds(GUARD + RIM[level] + 2 * coarse_row + parity, SUB, stride=2)
        state = (state0, state1, state2, state3)[level]
        return [
            (ref[SWEPT + 2 * comp + p, at, :] + state[CENTRE + p, at, :] * here)
            + (state[SIDE + p, at, :] * beyond[p] + state[ACROSS + p, at, :] * across)
            for p in range(2)
        ]

    base = pl.multiple_of(CELLS * index_x, SUB)
    for comp in range(2):
        window = [whole[3 * comp + kind, pl.ds(base, 6 * SUB), :] for kind in range(3)]
        for tile in range(2):
            first = SUB * tile - 1
            at = 2 * GUARD + first
            here, right, left = [w[at : at + SUB] for w in window]
            for parity in range(2):
                shifted = at + (1 if parity else -1)
                across = window[0][shifted : shifted + SUB]
                found = swept_rows(swept3, 3, first, parity, here, (left, right), across, comp)
                rows = pl.ds(GUARD + RIM[3] + 2 * first + parity, SUB, stride=2)
                for p in range(2):
                    corr3[2 * comp + p, rows, :] = found[p]

    corrs = [None, corr1, corr2, corr3]
    merged = [merged0, merged1, merged2]
    near = ((((lane + 32) & (LANES - 1)) - 32) >> 1) & (LANES - 1)
    odd_lane = (lane & 1) == 1
    for level in (2, 1, 0):
        coarse = level + 1
        corr, state, whole_rows = corrs[coarse], (state0, state1, state2)[level], merged[level]
        count = (LANES >> coarse) + 2
        origin = GUARD + RIM[coarse]
        sides = {}
        for tile in range(-(-count // SUB)):
            at = origin - 1 + SUB * tile
            for comp in range(2):
                even, odd = tile_at(corr, 2 * comp, at), tile_at(corr, 2 * comp + 1, at)
                even_here, odd_here = lane_take(even, near), lane_take(odd, near)
                even_next = lane_take(even, (near + 1) & (LANES - 1))
                odd_last = lane_take(odd, (near - 1) & (LANES - 1))
                here = jnp.where(odd_lane, odd_here, even_here)
                whole_rows[3 * comp, at : at + SUB, :] = here
                whole_rows[3 * comp + 1, at : at + SUB, :] = jnp.where(
                    odd_lane, even_next, odd_here
                )
                whole_rows[3 * comp + 2, at : at + SUB, :] = jnp.where(
                    odd_lane, even_here, odd_last
                )
        if level > 0:
            first, tiles = -1, -(-count // SUB)
        else:
            first, tiles = 0, (count - 2) // SUB
        for tile in range(tiles):
            coarse_row = first + SUB * tile
            at = origin + coarse_row
            for comp in range(2):
                here, right, left = [tile_at(whole_rows, 3 * comp + k, at) for k in range(3)]
                for parity in range(2):
                    across = tile_at(whole_rows, 3 * comp, at + (1 if parity else -1))
                    found = swept_rows(
                        state, level, coarse_row, parity, here, (left, right), across, comp
                    )
                    if level > 0:
                        rows = pl.ds(GUARD + RIM[level] + 2 * coarse_row + parity, SUB, stride=2)
                        for p in range(2):
                            corrs[level][2 * comp + p, rows, :] = found[p]
                    else:
                        rows = pl.ds(2 * coarse_row + parity, SUB, stride=2)
                        out[comp, rows, :] = jnp.where(
                            odd_lane,
                            lane_take(found[1], lane >> 1),
                            lane_take(found[0], lane >> 1),
                        )


def params():
    return pltpu.CompilerParams(vmem_limit_bytes=VMEM_LIMIT)


VMEM_SPEC = pl.BlockSpec(memory_space=pltpu.VMEM)
SMEM_SPEC = pl.BlockSpec(memory_space=pltpu.SMEM)
HBM_SPEC = pl.BlockSpec(memory_space=pltpu.HBM)


def swap_routes(size_x, size_y):
    def index(i, j):
        return i * size_y + j

    routes = []
    for axis in range(2):
        size = (size_x, size_y)[axis]
        for offset in range(2):
            route = []
            for i in range(size_x):
                for j in range(size_y):
                    here = (i, j)[axis]
                    other = here + 1 if here % 2 == offset else here - 1
                    if 0 <= other < size:
                        peer = (other, j) if axis == 0 else (i, other)
                    else:
                        peer = (i, j ^ 1) if axis == 0 else (i ^ 1, j)
                    route.append((index(i, j), index(*peer)))
            routes.append(route)
    return routes


def per_device(size_x, size_y, right_side, shift_coef, viscosity, wet_tiles):
    axes = ("gx", "gy")
    devices = size_x * size_y
    routes = swap_routes(size_x, size_y)
    band = jax.ShapeDtypeStruct((4 * HALO, LANES), F32)
    held_shape = pltpu.VMEM((4, HELD[0], LANES), F32)
    held, first, second = pl.pallas_call(
        bands_kernel,
        out_shape=(held_shape, band, band),
        in_specs=[SMEM_SPEC] + [HBM_SPEC] * 3,
        out_specs=(VMEM_SPEC,) * 3,
        scratch_shapes=[pltpu.SemaphoreType.DMA((4,))],
        compiler_params=params(),
        name="bands",
    )(
        wet_tiles,
        *[
            pltpu.with_memory_space_constraint(array, pltpu.HBM)
            for array in (right_side, shift_coef, viscosity)
        ],
    )
    second = lax.ppermute(second, axes, routes[1])
    first = lax.ppermute(first, axes, routes[0])
    strip = jax.ShapeDtypeStruct((MESSAGE, LANES), F32)
    held, first, second = pl.pallas_call(
        functools.partial(strips_kernel, size_x),
        out_shape=(held_shape, strip, strip),
        in_specs=[SMEM_SPEC] + [VMEM_SPEC] * 3,
        out_specs=(VMEM_SPEC,) * 3,
        input_output_aliases={1: 0},
        compiler_params=params(),
        name="strips",
    )(wet_tiles, held, first, second)
    second = lax.ppermute(second, axes, routes[3])
    first = lax.ppermute(first, axes, routes[2])

    def buffers(counts):
        return [pltpu.VMEM((n, HELD[level], LANES), F32) for level, n in enumerate(counts)]

    chunks, *states = pl.pallas_call(
        functools.partial(down_kernel, size_y, devices),
        out_shape=(jax.ShapeDtypeStruct((CHUNK * devices, LANES), F32),)
        + tuple(buffers([STATE, STATE, STATE, STATE + 6])),
        in_specs=[VMEM_SPEC] * 3,
        out_specs=(VMEM_SPEC,) * (1 + LOCAL),
        scratch_shapes=buffers([8, 14, 14, 14])
        + buffers([4, 8, 8, 8])
        + buffers([7] * 4)
        + buffers([2] * 4)
        + [pltpu.VMEM((4, HELD[3], LANES), F32)],
        compiler_params=params(),
        name="down",
    )(held, first, second)
    gathered = lax.all_to_all(chunks, axes, 0, 0, tiled=True)
    rows_total = CELLS * size_x
    columns = max(LANES, CELLS * size_y) // LANES
    return pl.pallas_call(
        functools.partial(up_kernel, size_x, size_y),
        out_shape=jax.ShapeDtypeStruct((2, LANES, LANES), F32),
        in_specs=[VMEM_SPEC] * (1 + LOCAL),
        out_specs=VMEM_SPEC,
        scratch_shapes=[
            pltpu.VMEM((4, columns, rows_total, LANES), F32),
            pltpu.VMEM((6, rows_total + 5 * SUB, LANES), F32),
            pltpu.VMEM((4, HELD[3], LANES), F32),
        ]
        + [pltpu.VMEM((4, HELD[level], LANES), F32) for level in (1, 2, 3)]
        + [pltpu.VMEM((6, HELD[level + 1], LANES), F32) for level in (0, 1, 2)],
        compiler_params=params(),
        name="up",
    )(gathered, *states)


def solution(mesh):
    sizes = dict(mesh.shape)
    placed = (P(None, "gx", "gy"), P("gx", "gy"), P("gx", "gy"), P("gx", "gy"))
    return jax.shard_map(
        functools.partial(per_device, sizes["gx"], sizes["gy"]),
        mesh=mesh,
        in_specs=placed,
        out_specs=P(None, "gx", "gy"),
        check_vma=False,
    )
```

```python
import functools

import jax
import jax.numpy as jnp
from jax import lax
from jax.experimental import pallas as pl
from jax.experimental.pallas import tpu as pltpu
from jax.sharding import PartitionSpec as P

LOCAL = 4
COARSE = 4
COARSE_SWEEPS = 8
OMEGA = 0.8
KEEP = 1.0 - OMEGA

LANES = 128
HALF = LANES // 2
SUB = 8
HALO = 16
GUARD = 8
CELLS = LANES >> LOCAL
ROWS = [(LANES + 2 * HALO) >> level for level in range(LOCAL)]
TILES = [-(-rows // SUB) for rows in ROWS]
HELD = [GUARD + SUB * tiles + 16 for tiles in TILES]
RIM = [HALO >> level for level in range(LOCAL)]
TOP = GUARD + HALO
LOW = TOP + LANES
HALF_TILES = TILES[0] // 2
MESSAGE = ROWS[0] // 2
CHUNK = 4
F32 = jnp.float32
VMEM_LIMIT = 48 * 1024 * 1024

EVEN, ODD, LEFT_ODD, RIGHT_EVEN = range(4)
SWEPT, CENTRE, SIDE, ACROSS = 0, 4, 6, 8
STATE = 10
ITERATE, WEIGHT = 10, 14


def iota(dim, shape=(SUB, LANES)):
    return lax.broadcasted_iota(jnp.int32, shape, dim)


def lane_take(tile, index):
    return jnp.take_along_axis(tile, index, axis=1)


def lane_roll(tile, shift):
    return pltpu.roll(tile, shift % LANES, 1)


def tile_at(ref, slot, row):
    return ref[slot, row : row + SUB, :]


def bands_kernel(wet, right_side, shift_coef, viscosity, held, first, second, sems):
    odd = lax.axis_index("gx") % 2
    wetness = wet[0, 0].astype(F32)
    own = pl.ds(TOP, LANES)
    sources = (right_side.at[0], right_side.at[1], shift_coef, viscosity)
    copies = [
        pltpu.make_async_copy(sources[field], held.at[field, own, :], sems.at[field])
        for field in range(4)
    ]
    for copy in copies:
        copy.start()
    bottom = LANES - HALO
    starts = (TOP + bottom - bottom * odd, TOP + bottom * odd)
    for field in range(4):
        copies[field].wait()
        for start, out in zip(starts, (first, second)):
            value = held[field, pl.ds(pl.multiple_of(start, SUB), HALO), :]
            out[field * HALO : (field + 1) * HALO, :] = value if field == 2 else value * wetness


def strips_kernel(size_x, wet, before_held, got_first, got_second, held, first, second):
    index_x = lax.axis_index("gx")
    odd_x = index_x % 2 == 1
    odd_y = lax.axis_index("gy") % 2 == 1
    wetness = wet[0, 0].astype(F32)
    above = (index_x > 0).astype(F32)
    below = (index_x < size_x - 1).astype(F32)
    for field in range(4):
        rows = slice(field * HALO, (field + 1) * HALO)
        one, two = got_first[rows, :], got_second[rows, :]
        before = jnp.where(odd_x, one, two)
        after = jnp.where(odd_x, two, one)
        if field == 3:
            before, after = before * above, after * below
        held[field, GUARD:TOP, :] = before
        if field != 2:
            held[field, TOP:LOW, :] = before_held[field, TOP:LOW, :] * wetness
        held[field, LOW : LOW + HALO, :] = after
    lane = iota(1)
    for tile in range(HALF_TILES):
        left = right = None
        for half in range(2):
            row = GUARD + SUB * (tile + half * HALF_TILES)
            for field in range(4):
                value = held[field, row : row + SUB, :]
                place = HALF * half + HALO * field
                other = HALF * (1 - half) + HALO * field
                to_left = lane_roll(value, place)
                to_right = lane_roll(value, other - (LANES - HALO))
                if left is None:
                    left, right = to_left, to_right
                else:
                    left = jnp.where(lane >= place, to_left, left)
                    right = jnp.where((lane >= other) & (lane < other + HALO), to_right, right)
        rows = slice(SUB * tile, SUB * tile + SUB)
        first[rows, :] = jnp.where(odd_y, left, right)
        second[rows, :] = jnp.where(odd_y, right, left)


def down_kernel(size_y, devices, got_second, got_first, held, chunks, *refs):
    states, refs = refs[:LOCAL], refs[LOCAL:]
    fields, refs = refs[:LOCAL], refs[LOCAL:]
    iterates, refs = refs[:LOCAL], refs[LOCAL:]
    faces, refs = refs[:LOCAL], refs[LOCAL:]
    sums, ring = refs[:LOCAL], refs[LOCAL]
    index_y = lax.axis_index("gy")
    odd_y = index_y % 2 == 1
    lane, sub = iota(1), iota(0)
    side_ok = jnp.where(
        lane < 96, (index_y < size_y - 1).astype(F32), (index_y > 0).astype(F32)
    )
    odd_row = (sub & 1) == 1
    inner = lane < HALF

    spread = 2 * lane
    for tile in range(HALF_TILES):
        rows = slice(SUB * tile, SUB * tile + SUB)
        one, two = got_first[rows, :], got_second[rows, :]
        after = jnp.where(odd_y, two, one)
        before = jnp.where(odd_y, one, two)
        for half in range(2):
            row = GUARD + SUB * (tile + half * HALF_TILES)
            rims = jnp.where(inner, after, before) if half == 0 else jnp.where(inner, before, after)
            base = jnp.where((lane < 96) == (half == 0), 0, HALF) + 2 * (lane & 7)
            for field in range(4):
                own = held[field, row : row + SUB, :]
                for parity in range(2):
                    mine = lane_take(own, (spread + parity) & (LANES - 1))
                    rim = lane_take(rims, base + (HALO * field + parity))
                    if field == 3:
                        rim = rim * side_ok
                    fields[0][2 * field + parity, row : row + SUB, :] = jnp.where(inner, mine, rim)

    def source_slot(level, comp, kind):
        return 2 * comp + kind if level == 0 else 4 * comp + kind

    def iterate_slot(level, comp, kind):
        return 2 * comp + kind if level == 0 else 4 * comp + kind

    for level in range(LOCAL):
        field, iterate, face, state, summed = (
            fields[level],
            iterates[level],
            faces[level],
            states[level],
            sums[level],
        )
        reaction_at, viscous_at = (4, 6) if level == 0 else (8, 10)
        for tile in range(TILES[level]):
            row = GUARD + SUB * tile
            rows = slice(row, row + SUB)
            here = [tile_at(field, viscous_at + p, row) for p in range(2)]
            if level == 0:
                left_odd, right_even = lane_roll(here[1], 1), lane_roll(here[0], -1)
            else:
                left_odd = tile_at(field, viscous_at + LEFT_ODD, row)
                right_even = tile_at(field, viscous_at + RIGHT_EVEN, row)
            middle = jnp.minimum(here[0], here[1])
            outer = [jnp.minimum(here[0], left_odd), jnp.minimum(here[1], right_even)]
            face[0, rows, :] = middle
            weights = []
            for p in range(2):
                north = jnp.minimum(here[p], tile_at(field, viscous_at + p, row - 1))
                south = jnp.minimum(here[p], tile_at(field, viscous_at + p, row + 1))
                diagonal = tile_at(field, reaction_at + p, row) + (
                    (middle + outer[p]) + (north + south)
                )
                weights.append(OMEGA / diagonal)
                face[1 + p, rows, :] = outer[p]
                face[3 + p, rows, :] = south
                face[5 + p, rows, :] = weights[p]
            if level > 0:
                weights += [lane_roll(weights[1], 1), lane_roll(weights[0], -1)]
            for comp in range(2):
                for kind, weight in enumerate(weights):
                    iterate[iterate_slot(level, comp, kind), rows, :] = weight * tile_at(
                        field, source_slot(level, comp, kind), row
                    )
        for tile in range(TILES[level]):
            row = GUARD + SUB * tile
            rows = slice(row, row + SUB)
            middle = face[0, rows, :]
            outer = [face[1 + p, rows, :] for p in range(2)]
            south = [face[3 + p, rows, :] for p in range(2)]
            north = [tile_at(face, 3 + p, row - 1) for p in range(2)]
            weights = [face[5 + p, rows, :] for p in range(2)]
            for comp in range(2):
                here = [tile_at(iterate, iterate_slot(level, comp, p), row) for p in range(2)]
                if level == 0:
                    beyond = [lane_roll(here[1], 1), lane_roll(here[0], -1)]
                else:
                    beyond = [
                        tile_at(iterate, iterate_slot(level, comp, kind), row)
                        for kind in (LEFT_ODD, RIGHT_EVEN)
                    ]
                total = None
                for p in range(2):
                    slot = iterate_slot(level, comp, p)
                    around = middle * here[1 - p] + outer[p] * beyond[p]
                    around = around + (
                        south[p] * tile_at(iterate, slot, row + 1)
                        + north[p] * tile_at(iterate, slot, row - 1)
                    )
                    left = KEEP * tile_at(field, source_slot(level, comp, p), row) + around
                    state[SWEPT + 2 * comp + p, rows, :] = here[p] + weights[p] * left
                    if level == LOCAL - 1:
                        ring[2 * comp + p, rows, :] = left
                        state[ITERATE + 2 * comp + p, rows, :] = here[p]
                    total = left if total is None else total + left
                summed[comp, rows, :] = total
            for p in range(2):
                within = jnp.where(odd_row, north[p], south[p])
                across = jnp.where(odd_row, south[p], north[p])
                state[CENTRE + p, rows, :] = KEEP + weights[p] * (middle + within)
                state[SIDE + p, rows, :] = weights[p] * outer[p]
                state[ACROSS + p, rows, :] = weights[p] * across
                if level == LOCAL - 1:
                    state[WEIGHT + p, rows, :] = weights[p]

        def pairs(ref, slot, start):
            return (
                ref[slot, pl.ds(start, SUB, stride=2), :]
                + ref[slot, pl.ds(start + 1, SUB, stride=2), :]
            )

        def coefficient(at, start):
            return pairs(field, at, start) + pairs(field, at + 1, start)

        if level < LOCAL - 1:
            coarse = fields[level + 1]
            takes = [(spread + offset) & (LANES - 1) for offset in (0, 1, -1, 2)]
            for tile in range(TILES[level + 1]):
                start = GUARD + 2 * SUB * tile
                rows = slice(GUARD + SUB * tile, GUARD + SUB * tile + SUB)
                viscous = 0.0625 * coefficient(viscous_at, start)
                reaction = 0.25 * coefficient(reaction_at, start)
                for kind in range(4):
                    coarse[10 + kind, rows, :] = lane_take(viscous, takes[kind])
                for kind in range(2):
                    coarse[8 + kind, rows, :] = lane_take(reaction, takes[kind])
                for comp in range(2):
                    source = 0.25 * pairs(summed, comp, start)
                    for kind in range(4):
                        coarse[4 * comp + kind, rows, :] = lane_take(source, takes[kind])
            continue

        start = GUARD + RIM[level]
        column = lane & (SUB - 1)
        own = [
            lane_take(0.25 * pairs(summed, 0, start), column),
            lane_take(0.25 * pairs(summed, 1, start), column),
            lane_take(0.25 * coefficient(reaction_at, start), column),
            lane_take(0.0625 * coefficient(viscous_at, start), column),
        ]
        chosen = ((lane >> 3) & (SUB - 1)) == sub
        edge = (lane >> 4) & 3
        place = lane & 15

        def packed(value):
            return jnp.sum(value, axis=0, keepdims=True)

        def joined(a, b):
            return packed(jnp.where(chosen, jnp.where(inner, a, b), 0.0))

        rims = jnp.zeros((SUB, LANES), F32)
        for part in range(2):
            for p in range(2):
                index = jnp.where(edge < 2, column, 0 if p == 0 else SUB - 1)
                along = (edge == part) & ((place >> 3) == p) & (sub == (0 if part == 0 else SUB - 1))
                up = (edge == 2 + p) & (place == sub + SUB * part)
                row = start + SUB * part
                value = jnp.where(
                    inner,
                    lane_take(tile_at(ring, p, row), index),
                    lane_take(tile_at(ring, 2 + p, row), index),
                )
                rims = jnp.where(along | up, value, rims)
        kind = sub % CHUNK
        tile = jnp.where(
            kind == 0,
            joined(own[0], own[1]),
            jnp.where(kind == 1, joined(own[2], own[3]), jnp.where(kind == 2, packed(rims), 0.0)),
        )
        for block in range(CHUNK * devices // SUB):
            chunks[SUB * block : SUB * block + SUB, :] = tile


def coarse_solve(fields, rows_total, cols_total):
    shape = fields[0].shape
    width = shape[1]
    row, lane = iota(0, shape), iota(1, shape)

    def along(value, amount):
        return pltpu.roll(value, amount % width, 1)

    def down(value, amount):
        return pltpu.roll(value, amount % shape[0], 0)

    sources = fields[:2]
    reaction = jnp.where(lane < cols_total, fields[2], 1.0)
    viscous = fields[3]
    stored = []
    for level in range(COARSE):
        step = 1 << level
        odd_lane, odd_row = (lane & step) != 0, (row & step) != 0

        def paired(value):
            return (
                jnp.where(odd_lane, along(value, step), value),
                jnp.where(odd_lane, value, along(value, -step)),
            )

        def outside(value):
            return (
                jnp.where(odd_lane, along(value, 2 * step), along(value, step)),
                jnp.where(odd_lane, along(value, -step), along(value, -2 * step)),
            )

        here, reactions = paired(viscous), paired(reaction)
        beyond = outside(viscous)
        beyond = (
            jnp.where(lane < 2 * step, 0.0, beyond[0]),
            jnp.where(lane < cols_total - 2 * step, beyond[1], 0.0),
        )
        middle = jnp.minimum(here[0], here[1])
        outer = [jnp.minimum(a, b) for a, b in zip(here, beyond)]
        north, south, weights = [], [], []
        for p in range(2):
            above = jnp.where(row < step, 0.0, down(here[p], step))
            below = jnp.where(row < rows_total - step, down(here[p], -step), 0.0)
            north.append(jnp.minimum(here[p], above))
            south.append(jnp.minimum(here[p], below))
            diagonal = reactions[p] + ((middle + outer[p]) + (north[p] + south[p]))
            weights.append(OMEGA / diagonal)
        weights_beyond = (along(weights[1], 2 * step), along(weights[0], -2 * step))
        swept, remaining = [], []
        for source in sources:
            values, values_beyond = paired(source), outside(source)
            x = [w * s for w, s in zip(weights, values)]
            x_beyond = [w * s for w, s in zip(weights_beyond, values_beyond)]
            total = None
            for p in range(2):
                around = middle * x[1 - p] + outer[p] * x_beyond[p]
                around = around + (south[p] * down(x[p], -step) + north[p] * down(x[p], step))
                left = KEEP * values[p] + around
                swept.append(x[p] + weights[p] * left)
                total = left if total is None else total + left
            remaining.append(total)
        centre, side, across = [], [], []
        for p in range(2):
            within = jnp.where(odd_row, north[p], south[p])
            out = jnp.where(odd_row, south[p], north[p])
            centre.append(KEEP + weights[p] * (middle + within))
            side.append(weights[p] * outer[p])
            across.append(weights[p] * out)
        stored.append((step, odd_lane, odd_row, swept, centre, side, across))

        def folded(value, scale):
            return scale * (value + jnp.where(odd_row, down(value, step), down(value, -step)))

        sources = [folded(total, 0.25) for total in remaining]
        reaction = folded(reactions[0] + reactions[1], 0.25)
        viscous = folded(here[0] + here[1], 0.0625)

    block = 1 << COARSE
    rows_left, cols_left = rows_total // block, cols_total // block
    cells = [(i, j) for i in range(rows_left) for j in range(cols_left)]

    def spread_cells(value):
        found = {}
        for i, j in cells:
            column, place = divmod(block * j, LANES)
            tile = value[block * i : block * i + SUB, LANES * column : LANES * column + LANES]
            found[i, j] = lane_take(tile, jnp.full((SUB, LANES), place, jnp.int32))
        return found

    source_cells = [spread_cells(s) for s in sources]
    reaction_cells, viscous_cells = spread_cells(reaction), spread_cells(viscous)
    pulls, weight_cells = {}, {}
    for i, j in cells:
        near = [c for c in ((i - 1, j), (i + 1, j), (i, j - 1), (i, j + 1)) if c in viscous_cells]
        links = [(c, jnp.minimum(viscous_cells[i, j], viscous_cells[c])) for c in near]
        diagonal = reaction_cells[i, j] + sum(c for _, c in links)
        weight_cells[i, j] = OMEGA / diagonal
        pulls[i, j] = [(c, weight_cells[i, j] * link) for c, link in links]
    solved = []
    for comp in range(2):
        pushed = {c: weight_cells[c] * source_cells[comp][c] for c in cells}
        values = pushed
        for _ in range(COARSE_SWEEPS - 1):
            values = {
                c: (KEEP * values[c] + pushed[c])
                + sum(pull * values[other] for other, pull in pulls[c])
                for c in cells
            }
        solved.append(values)

    def laid(values, di, dj):
        tiles = []
        nothing = jnp.zeros((SUB, LANES), F32)
        for tile in range(shape[0] // SUB):
            i = SUB * tile // block
            if di:
                i += 1 if (SUB * tile // (block // 2)) % 2 else -1
            columns = []
            for column in range(width // LANES):
                place = iota(1) // block + column * (LANES // block)
                value = nothing
                for j in range(cols_left):
                    if (i, j) in values and column * LANES <= (j - dj) * block < (column + 1) * LANES:
                        value = jnp.where(place == j - dj, values[i, j], value)
                columns.append(value)
            tiles.append(columns[0] if len(columns) == 1 else jnp.concatenate(columns, 1))
        return jnp.concatenate(tiles, 0)

    corrections = None
    for step, odd_lane, odd_row, swept, centre, side, across in reversed(stored):
        found = []
        for comp in range(2):
            if corrections is None:
                here = laid(solved[comp], 0, 0)
                beyond = [laid(solved[comp], 0, -1), laid(solved[comp], 0, 1)]
                out = laid(solved[comp], 1, 0)
            else:
                here = corrections[comp]
                beyond = [along(here, 2 * step), along(here, -2 * step)]
                out = jnp.where(odd_row, down(here, -step), down(here, step))
            parts = [
                (swept[2 * comp + p] + centre[p] * here) + (side[p] * beyond[p] + across[p] * out)
                for p in range(2)
            ]
            found.append(jnp.where(odd_lane, parts[1], parts[0]))
        corrections = found
    return corrections


def up_kernel(size_x, size_y, gathered, state0, state1, state2, state3, out, *refs):
    grid, whole, swept3, corr1, corr2, corr3, merged0, merged1, merged2 = refs
    index_x, index_y = lax.axis_index("gx"), lax.axis_index("gy")
    rows_total, cols_total = CELLS * size_x, CELLS * size_y
    width = max(LANES, cols_total)
    columns = width // LANES
    per_column = LANES // CELLS
    lane, sub = iota(1), iota(0)

    tall = iota(1, (2 * size_x, LANES))
    for column in range(columns):
        targets = [[jnp.zeros((2 * size_x, LANES), F32)] * CELLS for _ in range(2)]
        for place in range(min(per_column, size_y - column * per_column)):
            j = column * per_column + place
            chunk = jnp.concatenate(
                [
                    gathered[pl.ds(CHUNK * j + h, size_x, stride=CHUNK * size_y), :]
                    for h in range(2)
                ],
                0,
            )
            mine = (tall // CELLS) == place
            turns = {}
            for half in range(2):
                for r in range(CELLS):
                    shift = (CELLS * (place - r) - half * HALF) % LANES
                    if shift not in turns:
                        turns[shift] = lane_roll(chunk, shift)
                    targets[half][r] = jnp.where(mine, turns[shift], targets[half][r])
        for half in range(2):
            for r in range(CELLS):
                for h in range(2):
                    grid[2 * h + half, column, pl.ds(r, size_x, stride=CELLS), :] = targets[half][r][
                        h * size_x : (h + 1) * size_x
                    ]
    fields = [
        jnp.concatenate([grid[f, c] for c in range(columns)], 1) if columns > 1 else grid[f, 0]
        for f in range(4)
    ]

    def ring_row(dx, dy):
        i = jnp.clip(index_x + dx, 0, size_x - 1)
        j = jnp.clip(index_y + dy, 0, size_y - 1)
        return jnp.broadcast_to(
            gathered[pl.ds(CHUNK * (i * size_y + j) + 2, 1), :], (SUB, LANES)
        )

    beside = {
        (dx, dy): ring_row(dx, dy) for dx in (-1, 0, 1) for dy in (-1, 0, 1) if dx or dy
    }
    start = GUARD + RIM[3]
    for comp in range(2):
        base = comp * HALF
        for p in range(2):
            slot = 2 * comp + p
            end = 7 if p else 0
            corner_lane = LANES - 1 if p else SUB
            dy = -1 if p else 1
            for tile in range(2):
                at = start + SUB * tile
                index = base + (48 if p else 32) + SUB * tile + sub
                ringed = lane_take(beside[0, dy], index)
                swept = jnp.where(
                    lane == corner_lane,
                    tile_at(state3, ITERATE + slot, at) + tile_at(state3, WEIGHT + p, at) * ringed,
                    tile_at(state3, SWEPT + slot, at),
                )
                swept3[slot, at : at + SUB, :] = swept
            for dx, at, edge in ((-1, start - 1, 16), (1, start + 2 * SUB, 0)):
                index = base + edge + 8 * p
                ringed = jnp.where(
                    lane == corner_lane,
                    lane_take(beside[dx, dy], jnp.full((SUB, LANES), index + end, jnp.int32)),
                    lane_take(beside[dx, 0], index + (lane & 7)),
                )
                rows = slice(at, at + 1)
                swept3[slot, rows, :] = (
                    state3[ITERATE + slot, rows, :] + state3[WEIGHT + p, rows, :] * ringed[0:1]
                )

    corrections = coarse_solve(fields, rows_total, cols_total)

    for comp in range(2):
        for kind in range(3):
            shift = (width - CELLS * index_y + (0, -1, 1)[kind] + width) % width
            turned = pltpu.roll(corrections[comp], shift, 1)
            if columns > 1:
                tall_lane = iota(1, (rows_total, LANES))
                turned = jnp.where(
                    tall_lane < HALF, turned[:, :LANES], turned[:, width - LANES :]
                )
            slot = 3 * comp + kind
            whole[slot, 2 * GUARD : 2 * GUARD + rows_total, :] = turned
            whole[slot, 0 : 2 * GUARD, :] = jnp.zeros((2 * GUARD, LANES), F32)
            whole[slot, 2 * GUARD + rows_total :, :] = jnp.zeros((3 * SUB, LANES), F32)

    def swept_rows(ref, level, coarse_row, parity, here, beyond, across, comp):
        at = pl.ds(GUARD + RIM[level] + 2 * coarse_row + parity, SUB, stride=2)
        state = (state0, state1, state2, state3)[level]
        return [
            (ref[SWEPT + 2 * comp + p, at, :] + state[CENTRE + p, at, :] * here)
            + (state[SIDE + p, at, :] * beyond[p] + state[ACROSS + p, at, :] * across)
            for p in range(2)
        ]

    base = pl.multiple_of(CELLS * index_x, SUB)
    for comp in range(2):
        window = [whole[3 * comp + kind, pl.ds(base, 6 * SUB), :] for kind in range(3)]
        for tile in range(2):
            first = SUB * tile - 1
            at = 2 * GUARD + first
            here, right, left = [w[at : at + SUB] for w in window]
            for parity in range(2):
                shifted = at + (1 if parity else -1)
                across = window[0][shifted : shifted + SUB]
                found = swept_rows(swept3, 3, first, parity, here, (left, right), across, comp)
                rows = pl.ds(GUARD + RIM[3] + 2 * first + parity, SUB, stride=2)
                for p in range(2):
                    corr3[2 * comp + p, rows, :] = found[p]

    corrs = [None, corr1, corr2, corr3]
    merged = [merged0, merged1, merged2]
    near = ((((lane + 32) & (LANES - 1)) - 32) >> 1) & (LANES - 1)
    odd_lane = (lane & 1) == 1
    for level in (2, 1, 0):
        coarse = level + 1
        corr, state, whole_rows = corrs[coarse], (state0, state1, state2)[level], merged[level]
        count = (LANES >> coarse) + 2
        origin = GUARD + RIM[coarse]
        sides = {}
        for tile in range(-(-count // SUB)):
            at = origin - 1 + SUB * tile
            for comp in range(2):
                even, odd = tile_at(corr, 2 * comp, at), tile_at(corr, 2 * comp + 1, at)
                even_here, odd_here = lane_take(even, near), lane_take(odd, near)
                even_next = lane_take(even, (near + 1) & (LANES - 1))
                odd_last = lane_take(odd, (near - 1) & (LANES - 1))
                here = jnp.where(odd_lane, odd_here, even_here)
                whole_rows[3 * comp, at : at + SUB, :] = here
                whole_rows[3 * comp + 1, at : at + SUB, :] = jnp.where(
                    odd_lane, even_next, odd_here
                )
                whole_rows[3 * comp + 2, at : at + SUB, :] = jnp.where(
                    odd_lane, even_here, odd_last
                )
        if level > 0:
            first, tiles = -1, -(-count // SUB)
        else:
            first, tiles = 0, (count - 2) // SUB
        for tile in range(tiles):
            coarse_row = first + SUB * tile
            at = origin + coarse_row
            for comp in range(2):
                here, right, left = [tile_at(whole_rows, 3 * comp + k, at) for k in range(3)]
                for parity in range(2):
                    across = tile_at(whole_rows, 3 * comp, at + (1 if parity else -1))
                    found = swept_rows(
                        state, level, coarse_row, parity, here, (left, right), across, comp
                    )
                    if level > 0:
                        rows = pl.ds(GUARD + RIM[level] + 2 * coarse_row + parity, SUB, stride=2)
                        for p in range(2):
                            corrs[level][2 * comp + p, rows, :] = found[p]
                    else:
                        rows = pl.ds(2 * coarse_row + parity, SUB, stride=2)
                        out[comp, rows, :] = jnp.where(
                            odd_lane,
                            lane_take(found[1], lane >> 1),
                            lane_take(found[0], lane >> 1),
                        )


def params():
    return pltpu.CompilerParams(vmem_limit_bytes=VMEM_LIMIT)


VMEM_SPEC = pl.BlockSpec(memory_space=pltpu.VMEM)
SMEM_SPEC = pl.BlockSpec(memory_space=pltpu.SMEM)
HBM_SPEC = pl.BlockSpec(memory_space=pltpu.HBM)


def swap_routes(size_x, size_y):
    def index(i, j):
        return i * size_y + j

    routes = []
    for axis in range(2):
        size = (size_x, size_y)[axis]
        for offset in range(2):
            route = []
            for i in range(size_x):
                for j in range(size_y):
                    here = (i, j)[axis]
                    other = here + 1 if here % 2 == offset else here - 1
                    if 0 <= other < size:
                        peer = (other, j) if axis == 0 else (i, other)
                    else:
                        peer = (i, j ^ 1) if axis == 0 else (i ^ 1, j)
                    route.append((index(i, j), index(*peer)))
            routes.append(route)
    return routes


def per_device(size_x, size_y, right_side, shift_coef, viscosity, wet_tiles):
    axes = ("gx", "gy")
    devices = size_x * size_y
    routes = swap_routes(size_x, size_y)
    band = jax.ShapeDtypeStruct((4 * HALO, LANES), F32)
    held_shape = pltpu.VMEM((4, HELD[0], LANES), F32)
    held, first, second = pl.pallas_call(
        bands_kernel,
        out_shape=(held_shape, band, band),
        in_specs=[SMEM_SPEC] + [HBM_SPEC] * 3,
        out_specs=(VMEM_SPEC,) * 3,
        scratch_shapes=[pltpu.SemaphoreType.DMA((4,))],
        compiler_params=params(),
        name="bands",
    )(
        wet_tiles,
        *[
            pltpu.with_memory_space_constraint(array, pltpu.HBM)
            for array in (right_side, shift_coef, viscosity)
        ],
    )
    second = lax.ppermute(second, axes, routes[1])
    first = lax.ppermute(first, axes, routes[0])
    strip = jax.ShapeDtypeStruct((MESSAGE, LANES), F32)
    held, first, second = pl.pallas_call(
        functools.partial(strips_kernel, size_x),
        out_shape=(held_shape, strip, strip),
        in_specs=[SMEM_SPEC] + [VMEM_SPEC] * 3,
        out_specs=(VMEM_SPEC,) * 3,
        input_output_aliases={1: 0},
        compiler_params=params(),
        name="strips",
    )(wet_tiles, held, first, second)
    second = lax.ppermute(second, axes, routes[3])
    first = lax.ppermute(first, axes, routes[2])

    def buffers(counts):
        return [pltpu.VMEM((n, HELD[level], LANES), F32) for level, n in enumerate(counts)]

    chunks, *states = pl.pallas_call(
        functools.partial(down_kernel, size_y, devices),
        out_shape=(jax.ShapeDtypeStruct((CHUNK * devices, LANES), F32),)
        + tuple(buffers([STATE, STATE, STATE, STATE + 6])),
        in_specs=[VMEM_SPEC] * 3,
        out_specs=(VMEM_SPEC,) * (1 + LOCAL),
        scratch_shapes=buffers([8, 14, 14, 14])
        + buffers([4, 8, 8, 8])
        + buffers([7] * 4)
        + buffers([2] * 4)
        + [pltpu.VMEM((4, HELD[3], LANES), F32)],
        compiler_params=params(),
        name="down",
    )(second, first, held)
    gathered = lax.all_to_all(chunks, axes, 0, 0, tiled=True)
    rows_total = CELLS * size_x
    columns = max(LANES, CELLS * size_y) // LANES
    return pl.pallas_call(
        functools.partial(up_kernel, size_x, size_y),
        out_shape=jax.ShapeDtypeStruct((2, LANES, LANES), F32),
        in_specs=[VMEM_SPEC] * (1 + LOCAL),
        out_specs=VMEM_SPEC,
        scratch_shapes=[
            pltpu.VMEM((4, columns, rows_total, LANES), F32),
            pltpu.VMEM((6, rows_total + 5 * SUB, LANES), F32),
            pltpu.VMEM((4, HELD[3], LANES), F32),
        ]
        + [pltpu.VMEM((4, HELD[level], LANES), F32) for level in (1, 2, 3)]
        + [pltpu.VMEM((6, HELD[level + 1], LANES), F32) for level in (0, 1, 2)],
        compiler_params=params(),
        name="up",
    )(gathered, *states)


def solution(mesh):
    sizes = dict(mesh.shape)
    placed = (P(None, "gx", "gy"), P("gx", "gy"), P("gx", "gy"), P("gx", "gy"))
    return jax.shard_map(
        functools.partial(per_device, sizes["gx"], sizes["gy"]),
        mesh=mesh,
        in_specs=placed,
        out_specs=P(None, "gx", "gy"),
        check_vma=False,
    )
```

```python
import functools

import jax
import jax.numpy as jnp
from jax import lax
from jax.experimental import pallas as pl
from jax.experimental.pallas import tpu as pltpu
from jax.sharding import PartitionSpec as P

LOCAL = 4
COARSE = 4
COARSE_SWEEPS = 8
OMEGA = 0.8
KEEP = 1.0 - OMEGA

LANES = 128
HALF = LANES // 2
SUB = 8
HALO = 16
GUARD = 8
CELLS = LANES >> LOCAL
ROWS = [(LANES + 2 * HALO) >> level for level in range(LOCAL)]
TILES = [-(-rows // SUB) for rows in ROWS]
HELD = [GUARD + SUB * tiles + 16 for tiles in TILES]
RIM = [HALO >> level for level in range(LOCAL)]
TOP = GUARD + HALO
LOW = TOP + LANES
HALF_TILES = TILES[0] // 2
MESSAGE = ROWS[0] // 2
CHUNK = 4
F32 = jnp.float32
VMEM_LIMIT = 48 * 1024 * 1024

SWEPT, CENTRE, SIDE, ACROSS = 0, 4, 6, 8
STATE = 10
ITERATE, WEIGHT = 10, 14


def iota(dim, shape=(SUB, LANES)):
    return lax.broadcasted_iota(jnp.int32, shape, dim)


def lane_take(tile, index):
    return jnp.take_along_axis(tile, index, axis=1)


def lane_roll(tile, shift):
    return pltpu.roll(tile, shift % LANES, 1)


def tile_at(ref, slot, row):
    return ref[slot, row : row + SUB, :]


def bands_kernel(wet, right_side, shift_coef, viscosity, held, first, second, sems):
    odd = lax.axis_index("gx") % 2
    wetness = wet[0, 0].astype(F32)
    own = pl.ds(TOP, LANES)
    sources = (right_side.at[0], right_side.at[1], shift_coef, viscosity)
    copies = [
        pltpu.make_async_copy(sources[field], held.at[field, own, :], sems.at[field])
        for field in range(4)
    ]
    for copy in copies:
        copy.start()
    bottom = LANES - HALO
    starts = (TOP + bottom - bottom * odd, TOP + bottom * odd)
    for field in range(4):
        copies[field].wait()
        for start, out in zip(starts, (first, second)):
            value = held[field, pl.ds(pl.multiple_of(start, SUB), HALO), :]
            out[field * HALO : (field + 1) * HALO, :] = value if field == 2 else value * wetness


def rim_place(half, lane):
    to_left = ((lane >> 3) & 1) == half
    q = jnp.where(to_left, lane, (lane - (56 + 8 * half)) & (LANES - 1)) >> 4
    cell = 2 * (lane & 7) + (q & 1) + jnp.where(to_left, 0, LANES - HALO)
    return to_left, q >> 1, cell


def strips_kernel(size_x, wet, held, got_first, got_second, first, second):
    index_x = lax.axis_index("gx")
    odd_x = index_x % 2 == 1
    odd_y = lax.axis_index("gy") % 2 == 1
    wetness = wet[0, 0].astype(F32)
    above = (index_x > 0).astype(F32)
    below = (index_x < size_x - 1).astype(F32)
    lane = iota(1)
    rim_tiles = HALO // SUB

    def piece(field, tile):
        if rim_tiles <= tile < TILES[0] - rim_tiles:
            row = GUARD + SUB * tile
            return held[field, row : row + SUB, :]
        top = tile < rim_tiles
        row = field * HALO + SUB * (tile if top else tile - (TILES[0] - rim_tiles))
        one, two = got_first[row : row + SUB, :], got_second[row : row + SUB, :]
        return jnp.where(odd_x, one, two) if top else jnp.where(odd_x, two, one)

    places = [rim_place(half, lane) for half in range(2)]
    for tile in range(HALF_TILES):
        found = []
        for half in range(2):
            to_left, owner, cell = places[half]
            at = tile + half * HALF_TILES
            value = None
            for field in range(4):
                part = lane_take(piece(field, at), cell)
                value = part if value is None else jnp.where(owner == field, part, value)
            if rim_tiles <= at < TILES[0] - rim_tiles:
                value = value * jnp.where(owner == 2, 1.0, wetness)
            else:
                value = value * jnp.where(owner == 3, above if at < rim_tiles else below, 1.0)
            found.append(value)
        left = jnp.where(places[0][0], found[0], found[1])
        right = jnp.where(places[0][0], found[1], found[0])
        rows = slice(SUB * tile, SUB * tile + SUB)
        first[rows, :] = jnp.where(odd_y, left, right)
        second[rows, :] = jnp.where(odd_y, right, left)


def halves_kernel(size_x, wet, held, got_first, got_second, fields):
    index_x = lax.axis_index("gx")
    odd_x = index_x % 2 == 1
    wetness = wet[0, 0].astype(F32)
    above = (index_x > 0).astype(F32)
    below = (index_x < size_x - 1).astype(F32)
    lane = iota(1)
    rim_tiles = HALO // SUB
    for tile in range(TILES[0]):
        row = GUARD + SUB * tile
        for field in range(4):
            if rim_tiles <= tile < TILES[0] - rim_tiles:
                value = held[field, row : row + SUB, :]
                if field != 2:
                    value = value * wetness
            else:
                top = tile < rim_tiles
                at = field * HALO + SUB * (tile if top else tile - (TILES[0] - rim_tiles))
                one, two = got_first[at : at + SUB, :], got_second[at : at + SUB, :]
                value = jnp.where(odd_x, one, two) if top else jnp.where(odd_x, two, one)
                if field == 3:
                    value = value * (above if top else below)
            for parity in range(2):
                fields[2 * field + parity, row : row + SUB, :] = lane_take(
                    value, (2 * lane + parity) & (LANES - 1)
                )


def down_kernel(size_y, devices, got_second, got_first, held, chunks, *refs):
    states, refs = refs[:LOCAL], refs[LOCAL:]
    viscous, refs = refs[:LOCAL], refs[LOCAL:]
    iterates, refs = refs[:LOCAL], refs[LOCAL:]
    sums, ring = refs[:LOCAL], refs[LOCAL]
    index_y = lax.axis_index("gy")
    odd_y = index_y % 2 == 1
    lane, sub = iota(1), iota(0)
    side_ok = jnp.where(
        lane < 96, (index_y < size_y - 1).astype(F32), (index_y > 0).astype(F32)
    )
    odd_row = (sub & 1) == 1
    inner = lane < HALF
    even_block = ((lane >> 3) & 1) == 0

    def finest(tile):
        half, at = divmod(tile, HALF_TILES)
        one, two = (r[SUB * at : SUB * at + SUB, :] for r in (got_first, got_second))
        after, before = jnp.where(odd_y, two, one), jnp.where(odd_y, one, two)
        rims = jnp.where(even_block, after, before) if half == 0 else jnp.where(
            even_block, before, after
        )
        row = GUARD + SUB * tile
        values = []
        for slot in range(8):
            rim = lane_roll(rims, HALF - 16 * slot - 8 * half)
            if slot >= 4:
                rim = jnp.where(side_ok > 0, rim, 1.0 if slot < 6 else 0.0)
            values.append(jnp.where(inner, held[slot, row : row + SUB, :], rim))
        return [values[0:2], values[2:4]], values[4:6], values[6:8]

    def paired(ref, slot, start):
        return (
            ref[slot, pl.ds(start, SUB, stride=2), :] + ref[slot, pl.ds(start + 1, SUB, stride=2), :]
        )

    takes = [(2 * lane + offset) & (LANES - 1) for offset in (0, 1, -1, 2)]

    def coarser(level):
        def load(tile):
            start = GUARD + 2 * SUB * tile
            ref = sums[level - 1]
            reaction = 0.25 * paired(ref, 2, start)
            viscosity = 0.0625 * paired(ref, 3, start)
            sources = [0.25 * paired(ref, comp, start) for comp in range(2)]
            return (
                [[lane_take(s, t) for t in takes] for s in sources],
                [lane_take(reaction, t) for t in takes[:2]],
                [lane_take(viscosity, t) for t in takes],
            )

        return load

    def faces(level, row, fields):
        sources, reaction, here = fields
        if level == 0:
            left_odd, right_even = lane_roll(here[1], 1), lane_roll(here[0], -1)
        else:
            left_odd, right_even = here[2:]
        middle = jnp.minimum(here[0], here[1])
        outer = [jnp.minimum(here[0], left_odd), jnp.minimum(here[1], right_even)]
        north, south, weights = [], [], []
        for p in range(2):
            north.append(jnp.minimum(here[p], tile_at(viscous[level], p, row - 1)))
            south.append(jnp.minimum(here[p], tile_at(viscous[level], p, row + 1)))
            weights.append(OMEGA / (reaction[p] + ((middle + outer[p]) + (north[p] + south[p]))))
        if level > 0:
            weights += [lane_roll(weights[1], 1), lane_roll(weights[0], -1)]
        swept = [[w * s for w, s in zip(weights, source)] for source in sources]
        for comp in range(2):
            for p in range(2):
                iterates[level][2 * comp + p, row : row + SUB, :] = swept[comp][p]
        return sources, middle, outer, north, south, weights, swept

    def residual(level, row, values):
        sources, middle, outer, north, south, weights, swept = values
        state, iterate = states[level], iterates[level]
        rows = slice(row, row + SUB)
        kept = level > 0 or TOP <= row < LOW
        for comp in range(2):
            here = swept[comp][:2]
            if level == 0:
                beyond = [lane_roll(here[1], 1), lane_roll(here[0], -1)]
            else:
                beyond = swept[comp][2:]
            total = None
            for p in range(2):
                slot = 2 * comp + p
                around = middle * here[1 - p] + outer[p] * beyond[p]
                around = around + (
                    south[p] * tile_at(iterate, slot, row + 1)
                    + north[p] * tile_at(iterate, slot, row - 1)
                )
                left = KEEP * sources[comp][p] + around
                if kept:
                    state[SWEPT + slot, rows, :] = here[p] + weights[p] * left
                if level == LOCAL - 1:
                    ring[slot, rows, :] = left
                    state[ITERATE + slot, rows, :] = here[p]
                total = left if total is None else total + left
            sums[level][comp, rows, :] = total
        if kept:
            for p in range(2):
                within = jnp.where(odd_row, north[p], south[p])
                across = jnp.where(odd_row, south[p], north[p])
                state[CENTRE + p, rows, :] = KEEP + weights[p] * (middle + within)
                state[SIDE + p, rows, :] = weights[p] * outer[p]
                state[ACROSS + p, rows, :] = weights[p] * across
                if level == LOCAL - 1:
                    state[WEIGHT + p, rows, :] = weights[p]

    for level in range(LOCAL):
        load = finest if level == 0 else coarser(level)
        loaded, swept = {}, {}
        for turn in range(TILES[level] + 2):
            if turn < TILES[level]:
                row = GUARD + SUB * turn
                loaded[turn] = load(turn)
                _, reaction, here = loaded[turn]
                for p in range(2):
                    viscous[level][p, row : row + SUB, :] = here[p]
                sums[level][2, row : row + SUB, :] = reaction[0] + reaction[1]
                sums[level][3, row : row + SUB, :] = here[0] + here[1]
            if 0 <= turn - 1 < TILES[level]:
                row = GUARD + SUB * (turn - 1)
                swept[turn - 1] = faces(level, row, loaded.pop(turn - 1))
            if turn >= 2:
                residual(level, GUARD + SUB * (turn - 2), swept.pop(turn - 2))

    start = GUARD + RIM[LOCAL - 1]
    column = lane & (SUB - 1)
    own = [
        lane_take(scale * paired(sums[LOCAL - 1], slot, start), column)
        for slot, scale in enumerate((0.25, 0.25, 0.25, 0.0625))
    ]
    chosen = ((lane >> 3) & (SUB - 1)) == sub
    edge = (lane >> 4) & 3
    place = lane & 15

    def packed(value):
        return jnp.sum(value, axis=0, keepdims=True)

    def joined(a, b):
        return packed(jnp.where(chosen, jnp.where(inner, a, b), 0.0))

    rims = jnp.zeros((SUB, LANES), F32)
    for p in range(2):
        index = jnp.where(edge < 2, column, 0 if p == 0 else SUB - 1)
        for part in range(2):
            along = (edge == part) & ((place >> 3) == p) & (sub == (0 if part == 0 else SUB - 1))
            up = (edge == 2 + p) & (place == sub + SUB * part)
            row = start + SUB * part
            value = jnp.where(
                inner,
                lane_take(tile_at(ring, p, row), index),
                lane_take(tile_at(ring, 2 + p, row), index),
            )
            rims = jnp.where(along | up, value, rims)
    kind = sub % CHUNK
    tile = jnp.where(
        kind == 0,
        joined(own[0], own[1]),
        jnp.where(kind == 1, joined(own[2], own[3]), jnp.where(kind == 2, packed(rims), 0.0)),
    )
    for block in range(CHUNK * devices // SUB):
        chunks[SUB * block : SUB * block + SUB, :] = tile


def coarse_solve(fields, rows_total, cols_total):
    shape = fields[0].shape
    width = shape[1]
    row, lane = iota(0, shape), iota(1, shape)

    def along(value, amount):
        return pltpu.roll(value, amount % width, 1)

    def down(value, amount):
        return pltpu.roll(value, amount % shape[0], 0)

    sources = fields[:2]
    reaction = jnp.where(lane < cols_total, fields[2], 1.0)
    viscous = fields[3]
    stored = []
    for level in range(COARSE):
        step = 1 << level
        odd_lane, odd_row = (lane & step) != 0, (row & step) != 0

        def paired(value):
            return (
                jnp.where(odd_lane, along(value, step), value),
                jnp.where(odd_lane, value, along(value, -step)),
            )

        def outside(value):
            return (
                jnp.where(odd_lane, along(value, 2 * step), along(value, step)),
                jnp.where(odd_lane, along(value, -step), along(value, -2 * step)),
            )

        here, reactions = paired(viscous), paired(reaction)
        beyond = outside(viscous)
        beyond = (
            jnp.where(lane < 2 * step, 0.0, beyond[0]),
            jnp.where(lane < cols_total - 2 * step, beyond[1], 0.0),
        )
        middle = jnp.minimum(here[0], here[1])
        outer = [jnp.minimum(a, b) for a, b in zip(here, beyond)]
        north, south, weights = [], [], []
        for p in range(2):
            above = jnp.where(row < step, 0.0, down(here[p], step))
            below = jnp.where(row < rows_total - step, down(here[p], -step), 0.0)
            north.append(jnp.minimum(here[p], above))
            south.append(jnp.minimum(here[p], below))
            diagonal = reactions[p] + ((middle + outer[p]) + (north[p] + south[p]))
            weights.append(OMEGA / diagonal)
        weights_beyond = (along(weights[1], 2 * step), along(weights[0], -2 * step))
        swept, remaining = [], []
        for source in sources:
            values, values_beyond = paired(source), outside(source)
            x = [w * s for w, s in zip(weights, values)]
            x_beyond = [w * s for w, s in zip(weights_beyond, values_beyond)]
            total = None
            for p in range(2):
                around = middle * x[1 - p] + outer[p] * x_beyond[p]
                around = around + (south[p] * down(x[p], -step) + north[p] * down(x[p], step))
                left = KEEP * values[p] + around
                swept.append(x[p] + weights[p] * left)
                total = left if total is None else total + left
            remaining.append(total)
        centre, side, across = [], [], []
        for p in range(2):
            within = jnp.where(odd_row, north[p], south[p])
            out = jnp.where(odd_row, south[p], north[p])
            centre.append(KEEP + weights[p] * (middle + within))
            side.append(weights[p] * outer[p])
            across.append(weights[p] * out)
        stored.append((step, odd_lane, odd_row, swept, centre, side, across))

        def folded(value, scale):
            return scale * (value + jnp.where(odd_row, down(value, step), down(value, -step)))

        sources = [folded(total, 0.25) for total in remaining]
        reaction = folded(reactions[0] + reactions[1], 0.25)
        viscous = folded(here[0] + here[1], 0.0625)

    block = 1 << COARSE
    rows_left, cols_left = rows_total // block, cols_total // block
    cells = [(i, j) for i in range(rows_left) for j in range(cols_left)]

    def spread_cells(value):
        found = {}
        for i, j in cells:
            column, place = divmod(block * j, LANES)
            tile = value[block * i : block * i + SUB, LANES * column : LANES * column + LANES]
            found[i, j] = lane_take(tile, jnp.full((SUB, LANES), place, jnp.int32))
        return found

    source_cells = [spread_cells(s) for s in sources]
    reaction_cells, viscous_cells = spread_cells(reaction), spread_cells(viscous)
    pulls, weight_cells = {}, {}
    for i, j in cells:
        near = [c for c in ((i - 1, j), (i + 1, j), (i, j - 1), (i, j + 1)) if c in viscous_cells]
        links = [(c, jnp.minimum(viscous_cells[i, j], viscous_cells[c])) for c in near]
        diagonal = reaction_cells[i, j] + sum(c for _, c in links)
        weight_cells[i, j] = OMEGA / diagonal
        pulls[i, j] = [(c, weight_cells[i, j] * link) for c, link in links]
    solved = []
    for comp in range(2):
        pushed = {c: weight_cells[c] * source_cells[comp][c] for c in cells}
        values = pushed
        for _ in range(COARSE_SWEEPS - 1):
            values = {
                c: (KEEP * values[c] + pushed[c])
                + sum(pull * values[other] for other, pull in pulls[c])
                for c in cells
            }
        solved.append(values)

    def laid(values, di, dj):
        tiles = []
        nothing = jnp.zeros((SUB, LANES), F32)
        for tile in range(shape[0] // SUB):
            i = SUB * tile // block
            if di:
                i += 1 if (SUB * tile // (block // 2)) % 2 else -1
            columns = []
            for column in range(width // LANES):
                place = iota(1) // block + column * (LANES // block)
                value = nothing
                for j in range(cols_left):
                    if (i, j) in values and column * LANES <= (j - dj) * block < (column + 1) * LANES:
                        value = jnp.where(place == j - dj, values[i, j], value)
                columns.append(value)
            tiles.append(columns[0] if len(columns) == 1 else jnp.concatenate(columns, 1))
        return jnp.concatenate(tiles, 0)

    corrections = None
    for step, odd_lane, odd_row, swept, centre, side, across in reversed(stored):
        found = []
        for comp in range(2):
            if corrections is None:
                here = laid(solved[comp], 0, 0)
                beyond = [laid(solved[comp], 0, -1), laid(solved[comp], 0, 1)]
                out = laid(solved[comp], 1, 0)
            else:
                here = corrections[comp]
                beyond = [along(here, 2 * step), along(here, -2 * step)]
                out = jnp.where(odd_row, down(here, -step), down(here, step))
            parts = [
                (swept[2 * comp + p] + centre[p] * here) + (side[p] * beyond[p] + across[p] * out)
                for p in range(2)
            ]
            found.append(jnp.where(odd_lane, parts[1], parts[0]))
        corrections = found
    return corrections


def up_kernel(size_x, size_y, gathered, state0, state1, state2, state3, out, *refs):
    grid, whole, swept3, corr1, corr2, corr3, merged0, merged1, merged2 = refs
    index_x, index_y = lax.axis_index("gx"), lax.axis_index("gy")
    rows_total, cols_total = CELLS * size_x, CELLS * size_y
    width = max(LANES, cols_total)
    columns = width // LANES
    per_column = LANES // CELLS
    lane, sub = iota(1), iota(0)

    tall = iota(1, (2 * size_x, LANES))
    for column in range(columns):
        targets = [[jnp.zeros((2 * size_x, LANES), F32)] * CELLS for _ in range(2)]
        for place in range(min(per_column, size_y - column * per_column)):
            j = column * per_column + place
            chunk = jnp.concatenate(
                [
                    gathered[pl.ds(CHUNK * j + h, size_x, stride=CHUNK * size_y), :]
                    for h in range(2)
                ],
                0,
            )
            mine = (tall // CELLS) == place
            turns = {}
            for half in range(2):
                for r in range(CELLS):
                    shift = (CELLS * (place - r) - half * HALF) % LANES
                    if shift not in turns:
                        turns[shift] = lane_roll(chunk, shift)
                    targets[half][r] = jnp.where(mine, turns[shift], targets[half][r])
        for half in range(2):
            for r in range(CELLS):
                for h in range(2):
                    grid[2 * h + half, column, pl.ds(r, size_x, stride=CELLS), :] = targets[half][r][
                        h * size_x : (h + 1) * size_x
                    ]
    fields = [
        jnp.concatenate([grid[f, c] for c in range(columns)], 1) if columns > 1 else grid[f, 0]
        for f in range(4)
    ]

    def ring_row(dx, dy):
        i = jnp.clip(index_x + dx, 0, size_x - 1)
        j = jnp.clip(index_y + dy, 0, size_y - 1)
        return jnp.broadcast_to(
            gathered[pl.ds(CHUNK * (i * size_y + j) + 2, 1), :], (SUB, LANES)
        )

    beside = {
        (dx, dy): ring_row(dx, dy) for dx in (-1, 0, 1) for dy in (-1, 0, 1) if dx or dy
    }
    start = GUARD + RIM[3]
    for comp in range(2):
        base = comp * HALF
        for p in range(2):
            slot = 2 * comp + p
            end = 7 if p else 0
            corner_lane = LANES - 1 if p else SUB
            dy = -1 if p else 1
            for tile in range(2):
                at = start + SUB * tile
                index = base + (48 if p else 32) + SUB * tile + sub
                ringed = lane_take(beside[0, dy], index)
                swept = jnp.where(
                    lane == corner_lane,
                    tile_at(state3, ITERATE + slot, at) + tile_at(state3, WEIGHT + p, at) * ringed,
                    tile_at(state3, SWEPT + slot, at),
                )
                swept3[slot, at : at + SUB, :] = swept
            for dx, at, edge in ((-1, start - 1, 16), (1, start + 2 * SUB, 0)):
                index = base + edge + 8 * p
                ringed = jnp.where(
                    lane == corner_lane,
                    lane_take(beside[dx, dy], jnp.full((SUB, LANES), index + end, jnp.int32)),
                    lane_take(beside[dx, 0], index + (lane & 7)),
                )
                rows = slice(at, at + 1)
                swept3[slot, rows, :] = (
                    state3[ITERATE + slot, rows, :] + state3[WEIGHT + p, rows, :] * ringed[0:1]
                )

    corrections = coarse_solve(fields, rows_total, cols_total)

    for comp in range(2):
        for kind in range(3):
            shift = (width - CELLS * index_y + (0, -1, 1)[kind] + width) % width
            turned = pltpu.roll(corrections[comp], shift, 1)
            if columns > 1:
                tall_lane = iota(1, (rows_total, LANES))
                turned = jnp.where(
                    tall_lane < HALF, turned[:, :LANES], turned[:, width - LANES :]
                )
            slot = 3 * comp + kind
            whole[slot, 2 * GUARD : 2 * GUARD + rows_total, :] = turned
            whole[slot, 0 : 2 * GUARD, :] = jnp.zeros((2 * GUARD, LANES), F32)
            whole[slot, 2 * GUARD + rows_total :, :] = jnp.zeros((3 * SUB, LANES), F32)

    def swept_rows(ref, level, coarse_row, parity, here, beyond, across, comp):
        at = pl.ds(GUARD + RIM[level] + 2 * coarse_row + parity, SUB, stride=2)
        state = (state0, state1, state2, state3)[level]
        return [
            (ref[SWEPT + 2 * comp + p, at, :] + state[CENTRE + p, at, :] * here)
            + (state[SIDE + p, at, :] * beyond[p] + state[ACROSS + p, at, :] * across)
            for p in range(2)
        ]

    base = pl.multiple_of(CELLS * index_x, SUB)
    for comp in range(2):
        window = [whole[3 * comp + kind, pl.ds(base, 6 * SUB), :] for kind in range(3)]
        for tile in range(2):
            first = SUB * tile - 1
            at = 2 * GUARD + first
            here, right, left = [w[at : at + SUB] for w in window]
            for parity in range(2):
                shifted = at + (1 if parity else -1)
                across = window[0][shifted : shifted + SUB]
                found = swept_rows(swept3, 3, first, parity, here, (left, right), across, comp)
                rows = pl.ds(GUARD + RIM[3] + 2 * first + parity, SUB, stride=2)
                for p in range(2):
                    corr3[2 * comp + p, rows, :] = found[p]

    corrs = [None, corr1, corr2, corr3]
    merged = [merged0, merged1, merged2]
    near = ((((lane + 32) & (LANES - 1)) - 32) >> 1) & (LANES - 1)
    odd_lane = (lane & 1) == 1
    for level in (2, 1, 0):
        coarse = level + 1
        corr, state, whole_rows = corrs[coarse], (state0, state1, state2)[level], merged[level]
        count = (LANES >> coarse) + 2
        origin = GUARD + RIM[coarse]
        sides = {}
        for tile in range(-(-count // SUB)):
            at = origin - 1 + SUB * tile
            for comp in range(2):
                even, odd = tile_at(corr, 2 * comp, at), tile_at(corr, 2 * comp + 1, at)
                even_here, odd_here = lane_take(even, near), lane_take(odd, near)
                even_next = lane_take(even, (near + 1) & (LANES - 1))
                odd_last = lane_take(odd, (near - 1) & (LANES - 1))
                here = jnp.where(odd_lane, odd_here, even_here)
                whole_rows[3 * comp, at : at + SUB, :] = here
                whole_rows[3 * comp + 1, at : at + SUB, :] = jnp.where(
                    odd_lane, even_next, odd_here
                )
                whole_rows[3 * comp + 2, at : at + SUB, :] = jnp.where(
                    odd_lane, even_here, odd_last
                )
        if level > 0:
            first, tiles = -1, -(-count // SUB)
        else:
            first, tiles = 0, (count - 2) // SUB
        for tile in range(tiles):
            coarse_row = first + SUB * tile
            at = origin + coarse_row
            for comp in range(2):
                here, right, left = [tile_at(whole_rows, 3 * comp + k, at) for k in range(3)]
                for parity in range(2):
                    across = tile_at(whole_rows, 3 * comp, at + (1 if parity else -1))
                    found = swept_rows(
                        state, level, coarse_row, parity, here, (left, right), across, comp
                    )
                    if level > 0:
                        rows = pl.ds(GUARD + RIM[level] + 2 * coarse_row + parity, SUB, stride=2)
                        for p in range(2):
                            corrs[level][2 * comp + p, rows, :] = found[p]
                    else:
                        rows = pl.ds(2 * coarse_row + parity, SUB, stride=2)
                        out[comp, rows, :] = jnp.where(
                            odd_lane,
                            lane_take(found[1], lane >> 1),
                            lane_take(found[0], lane >> 1),
                        )


def params():
    return pltpu.CompilerParams(vmem_limit_bytes=VMEM_LIMIT)


VMEM_SPEC = pl.BlockSpec(memory_space=pltpu.VMEM)
SMEM_SPEC = pl.BlockSpec(memory_space=pltpu.SMEM)
HBM_SPEC = pl.BlockSpec(memory_space=pltpu.HBM)


def swap_routes(size_x, size_y):
    def index(i, j):
        return i * size_y + j

    routes = []
    for axis in range(2):
        size = (size_x, size_y)[axis]
        for offset in range(2):
            route = []
            for i in range(size_x):
                for j in range(size_y):
                    here = (i, j)[axis]
                    other = here + 1 if here % 2 == offset else here - 1
                    if 0 <= other < size:
                        peer = (other, j) if axis == 0 else (i, other)
                    else:
                        peer = (i, j ^ 1) if axis == 0 else (i ^ 1, j)
                    route.append((index(i, j), index(*peer)))
            routes.append(route)
    return routes


def per_device(size_x, size_y, right_side, shift_coef, viscosity, wet_tiles):
    axes = ("gx", "gy")
    devices = size_x * size_y
    routes = swap_routes(size_x, size_y)
    band = jax.ShapeDtypeStruct((4 * HALO, LANES), F32)
    held_shape = pltpu.VMEM((4, HELD[0], LANES), F32)
    held, first, second = pl.pallas_call(
        bands_kernel,
        out_shape=(held_shape, band, band),
        in_specs=[SMEM_SPEC] + [HBM_SPEC] * 3,
        out_specs=(VMEM_SPEC,) * 3,
        scratch_shapes=[pltpu.SemaphoreType.DMA((4,))],
        compiler_params=params(),
        name="bands",
    )(
        wet_tiles,
        *[
            pltpu.with_memory_space_constraint(array, pltpu.HBM)
            for array in (right_side, shift_coef, viscosity)
        ],
    )
    second = lax.ppermute(second, axes, routes[1])
    first = lax.ppermute(first, axes, routes[0])
    strip = jax.ShapeDtypeStruct((MESSAGE, LANES), F32)
    got = (first, second)
    first, second = pl.pallas_call(
        functools.partial(strips_kernel, size_x),
        out_shape=(strip, strip),
        in_specs=[SMEM_SPEC] + [VMEM_SPEC] * 3,
        out_specs=(VMEM_SPEC,) * 2,
        compiler_params=params(),
        name="strips",
    )(wet_tiles, held, *got)
    fields = pl.pallas_call(
        functools.partial(halves_kernel, size_x),
        out_shape=pltpu.VMEM((8, HELD[0], LANES), F32),
        in_specs=[SMEM_SPEC] + [VMEM_SPEC] * 3,
        out_specs=VMEM_SPEC,
        cost_estimate=pl.CostEstimate(flops=1 << 20, bytes_accessed=1 << 21, transcendentals=0),
        compiler_params=params(),
        name="halves",
    )(wet_tiles, held, *got)
    second = lax.ppermute(second, axes, routes[3])
    first = lax.ppermute(first, axes, routes[2])

    def buffers(counts):
        return [pltpu.VMEM((n, HELD[level], LANES), F32) for level, n in enumerate(counts)]

    chunks, *states = pl.pallas_call(
        functools.partial(down_kernel, size_y, devices),
        out_shape=(jax.ShapeDtypeStruct((CHUNK * devices, LANES), F32),)
        + tuple(buffers([STATE, STATE, STATE, STATE + 6])),
        in_specs=[VMEM_SPEC] * 3,
        out_specs=(VMEM_SPEC,) * (1 + LOCAL),
        scratch_shapes=buffers([2] * 4)
        + buffers([4] * 4)
        + buffers([4] * 4)
        + [pltpu.VMEM((4, HELD[3], LANES), F32)],
        compiler_params=params(),
        name="down",
    )(second, first, fields)
    gathered = lax.all_to_all(chunks, axes, 0, 0, tiled=True)
    rows_total = CELLS * size_x
    columns = max(LANES, CELLS * size_y) // LANES
    return pl.pallas_call(
        functools.partial(up_kernel, size_x, size_y),
        out_shape=jax.ShapeDtypeStruct((2, LANES, LANES), F32),
        in_specs=[VMEM_SPEC] * (1 + LOCAL),
        out_specs=VMEM_SPEC,
        scratch_shapes=[
            pltpu.VMEM((4, columns, rows_total, LANES), F32),
            pltpu.VMEM((6, rows_total + 5 * SUB, LANES), F32),
            pltpu.VMEM((4, HELD[3], LANES), F32),
        ]
        + [pltpu.VMEM((4, HELD[level], LANES), F32) for level in (1, 2, 3)]
        + [pltpu.VMEM((6, HELD[level + 1], LANES), F32) for level in (0, 1, 2)],
        compiler_params=params(),
        name="up",
    )(gathered, *states)


def solution(mesh):
    sizes = dict(mesh.shape)
    placed = (P(None, "gx", "gy"), P("gx", "gy"), P("gx", "gy"), P("gx", "gy"))
    return jax.shard_map(
        functools.partial(per_device, sizes["gx"], sizes["gy"]),
        mesh=mesh,
        in_specs=placed,
        out_specs=P(None, "gx", "gy"),
        check_vma=False,
    )
```

```python
import functools

import jax
import jax.numpy as jnp
from jax import lax
from jax.experimental import pallas as pl
from jax.experimental.pallas import tpu as pltpu
from jax.sharding import PartitionSpec as P

LOCAL = 4
COARSE = 4
COARSE_SWEEPS = 8
OMEGA = 0.8
KEEP = 1.0 - OMEGA

LANES = 128
HALF = LANES // 2
SUB = 8
HALO = 16
GUARD = 8
CELLS = LANES >> LOCAL
ROWS = [(LANES + 2 * HALO) >> level for level in range(LOCAL)]
TILES = [-(-rows // SUB) for rows in ROWS]
HELD = [GUARD + SUB * tiles + 16 for tiles in TILES]
RIM = [HALO >> level for level in range(LOCAL)]
TOP = GUARD + HALO
LOW = TOP + LANES
HALF_TILES = TILES[0] // 2
MESSAGE = ROWS[0] // 2
CHUNK = 4
F32 = jnp.float32
VMEM_LIMIT = 48 * 1024 * 1024

SWEPT, CENTRE, SIDE, ACROSS = 0, 4, 6, 8
STATE = 10
ITERATE, WEIGHT = 10, 14


def iota(dim, shape=(SUB, LANES)):
    return lax.broadcasted_iota(jnp.int32, shape, dim)


def lane_take(tile, index):
    return jnp.take_along_axis(tile, index, axis=1)


def lane_roll(tile, shift):
    return pltpu.roll(tile, shift % LANES, 1)


def tile_at(ref, slot, row):
    return ref[slot, row : row + SUB, :]


def bands_kernel(wet, right_side, shift_coef, viscosity, held, first, second, sems):
    odd = lax.axis_index("gx") % 2
    wetness = wet[0, 0].astype(F32)
    own = pl.ds(TOP, LANES)
    sources = (right_side.at[0], right_side.at[1], shift_coef, viscosity)
    copies = [
        pltpu.make_async_copy(sources[field], held.at[field, own, :], sems.at[field])
        for field in range(4)
    ]
    for copy in copies:
        copy.start()
    bottom = LANES - HALO
    starts = (TOP + bottom - bottom * odd, TOP + bottom * odd)
    for field in range(4):
        copies[field].wait()
        for start, out in zip(starts, (first, second)):
            value = held[field, pl.ds(pl.multiple_of(start, SUB), HALO), :]
            out[field * HALO : (field + 1) * HALO, :] = value if field == 2 else value * wetness


def rim_place(half, lane):
    to_left = ((lane >> 3) & 1) == half
    q = jnp.where(to_left, lane, (lane - (56 + 8 * half)) & (LANES - 1)) >> 4
    cell = 2 * (lane & 7) + (q & 1) + jnp.where(to_left, 0, LANES - HALO)
    return to_left, q >> 1, cell


def strips_kernel(size_x, wet, held, got_first, got_second, first, second):
    index_x = lax.axis_index("gx")
    odd_x = index_x % 2 == 1
    odd_y = lax.axis_index("gy") % 2 == 1
    wetness = wet[0, 0].astype(F32)
    above = (index_x > 0).astype(F32)
    below = (index_x < size_x - 1).astype(F32)
    lane = iota(1)
    rim_tiles = HALO // SUB

    def piece(field, tile):
        if rim_tiles <= tile < TILES[0] - rim_tiles:
            row = GUARD + SUB * tile
            return held[field, row : row + SUB, :]
        top = tile < rim_tiles
        row = field * HALO + SUB * (tile if top else tile - (TILES[0] - rim_tiles))
        one, two = got_first[row : row + SUB, :], got_second[row : row + SUB, :]
        return jnp.where(odd_x, one, two) if top else jnp.where(odd_x, two, one)

    places = [rim_place(half, lane) for half in range(2)]
    for tile in range(HALF_TILES):
        found = []
        for half in range(2):
            to_left, owner, cell = places[half]
            at = tile + half * HALF_TILES
            value = None
            for field in range(4):
                part = lane_take(piece(field, at), cell)
                value = part if value is None else jnp.where(owner == field, part, value)
            if rim_tiles <= at < TILES[0] - rim_tiles:
                value = value * jnp.where(owner == 2, 1.0, wetness)
            else:
                value = value * jnp.where(owner == 3, above if at < rim_tiles else below, 1.0)
            found.append(value)
        left = jnp.where(places[0][0], found[0], found[1])
        right = jnp.where(places[0][0], found[1], found[0])
        rows = slice(SUB * tile, SUB * tile + SUB)
        first[rows, :] = jnp.where(odd_y, left, right)
        second[rows, :] = jnp.where(odd_y, right, left)


def halves_kernel(size_x, wet, held, got_first, got_second, fields):
    index_x = lax.axis_index("gx")
    odd_x = index_x % 2 == 1
    wetness = wet[0, 0].astype(F32)
    above = (index_x > 0).astype(F32)
    below = (index_x < size_x - 1).astype(F32)
    lane = iota(1)
    rim_tiles = HALO // SUB
    for tile in range(TILES[0]):
        row = GUARD + SUB * tile
        for field in range(4):
            if rim_tiles <= tile < TILES[0] - rim_tiles:
                value = held[field, row : row + SUB, :]
                if field != 2:
                    value = value * wetness
            else:
                top = tile < rim_tiles
                at = field * HALO + SUB * (tile if top else tile - (TILES[0] - rim_tiles))
                one, two = got_first[at : at + SUB, :], got_second[at : at + SUB, :]
                value = jnp.where(odd_x, one, two) if top else jnp.where(odd_x, two, one)
                if field == 3:
                    value = value * (above if top else below)
            for parity in range(2):
                fields[2 * field + parity, row : row + SUB, :] = lane_take(
                    value, (2 * lane + parity) & (LANES - 1)
                )


def down_kernel(size_y, devices, got_second, got_first, held, chunks, *refs):
    states, refs = refs[:LOCAL], refs[LOCAL:]
    viscous, refs = refs[:LOCAL], refs[LOCAL:]
    reactions, refs = refs[:LOCAL], refs[LOCAL:]
    sources, refs = refs[:LOCAL], refs[LOCAL:]
    weights, refs = refs[:LOCAL], refs[LOCAL:]
    iterates, refs = refs[:LOCAL], refs[LOCAL:]
    sums, (outers, ring) = refs[:LOCAL], refs[LOCAL:]
    index_y = lax.axis_index("gy")
    odd_y = index_y % 2 == 1
    lane, sub = iota(1), iota(0)
    side_ok = jnp.where(
        lane < 96, (index_y < size_y - 1).astype(F32), (index_y > 0).astype(F32)
    )
    odd_row = (sub & 1) == 1
    inner = lane < HALF
    even_block = ((lane >> 3) & 1) == 0

    def tiles(level):
        return [GUARD + SUB * tile for tile in range(TILES[level])]

    def put(ref, slot, row, value):
        ref[slot, row : row + SUB, :] = value

    def rims(row, slots):
        half, at = divmod((row - GUARD) // SUB, HALF_TILES)
        one, two = (r[SUB * at : SUB * at + SUB, :] for r in (got_first, got_second))
        after, before = jnp.where(odd_y, two, one), jnp.where(odd_y, one, two)
        if half == 0:
            both = jnp.where(even_block, after, before)
        else:
            both = jnp.where(even_block, before, after)
        values = []
        for slot in slots:
            rim = lane_roll(both, HALF - 16 * slot - 8 * half)
            if slot >= 4:
                rim = jnp.where(side_ok > 0, rim, 1.0 if slot < 6 else 0.0)
            values.append(jnp.where(inner, tile_at(held, slot, row), rim))
        return values

    def paired(ref, slot, start):
        return (
            ref[slot, pl.ds(start, SUB, stride=2), :] + ref[slot, pl.ds(start + 1, SUB, stride=2), :]
        )

    takes = [(2 * lane + offset) & (LANES - 1) for offset in (0, 1, -1, 2)]

    def coefficients(level):
        for row in tiles(level):
            if level == 0:
                values = rims(row, (4, 5, 6, 7))
                reaction, viscosity = values[:2], values[2:]
            else:
                start = GUARD + 2 * (row - GUARD)
                ref = sums[level - 1]
                value = 0.0625 * paired(ref, 3, start)
                viscosity = [lane_take(value, t) for t in takes]
                value = 0.25 * paired(ref, 2, start)
                reaction = [lane_take(value, t) for t in takes[:2]]
            for slot, value in enumerate(viscosity):
                put(viscous[level], slot, row, value)
            for slot, value in enumerate(reaction):
                put(reactions[level], slot, row, value)
            put(sums[level], 2, row, reaction[0] + reaction[1])
            put(sums[level], 3, row, viscosity[0] + viscosity[1])

    def faces(level, row):
        here = [tile_at(viscous[level], p, row) for p in range(2)]
        north = [jnp.minimum(here[p], tile_at(viscous[level], p, row - 1)) for p in range(2)]
        south = [jnp.minimum(here[p], tile_at(viscous[level], p, row + 1)) for p in range(2)]
        return here, jnp.minimum(here[0], here[1]), north, south

    def outside(level, row, here):
        if level == 0:
            beyond = [lane_roll(here[1], 1), lane_roll(here[0], -1)]
        else:
            beyond = [tile_at(viscous[level], 2 + p, row) for p in range(2)]
        return [jnp.minimum(h, b) for h, b in zip(here, beyond)]

    def weigh(level):
        for row in tiles(level):
            here, middle, north, south = faces(level, row)
            outer = outside(level, row, here)
            found = []
            for p in range(2):
                diagonal = tile_at(reactions[level], p, row) + (
                    (middle + outer[p]) + (north[p] + south[p])
                )
                found.append(OMEGA / diagonal)
                if level == 0:
                    put(outers, p, row, outer[p])
            if level > 0:
                found += [lane_roll(found[1], 1), lane_roll(found[0], -1)]
            for slot, value in enumerate(found):
                put(weights[level], slot, row, value)

    def take_sources(level):
        for row in tiles(level):
            if level == 0:
                found = rims(row, (0, 1, 2, 3))
            else:
                start = GUARD + 2 * (row - GUARD)
                values = [0.25 * paired(sums[level - 1], comp, start) for comp in range(2)]
                found = [lane_take(value, t) for value in values for t in takes]
            for slot, value in enumerate(found):
                put(sources[level], slot, row, value)

    def kinds(level):
        return 2 if level == 0 else 4

    def first_sweep(level):
        for row in tiles(level):
            for comp in range(2):
                for p in range(2):
                    put(
                        iterates[level],
                        2 * comp + p,
                        row,
                        tile_at(weights[level], p, row)
                        * tile_at(sources[level], kinds(level) * comp + p, row),
                    )

    def residual(level):
        state, iterate, weight, source = (
            states[level],
            iterates[level],
            weights[level],
            sources[level],
        )
        for row in tiles(level):
            _, middle, north, south = faces(level, row)
            if level == 0:
                outer = [tile_at(outers, p, row) for p in range(2)]
            else:
                outer = outside(level, row, [tile_at(viscous[level], p, row) for p in range(2)])
            scale = [tile_at(weight, p, row) for p in range(2)]
            kept = level > 0 or TOP <= row < LOW
            for comp in range(2):
                here = [tile_at(iterate, 2 * comp + p, row) for p in range(2)]
                if level == 0:
                    beyond = [lane_roll(here[1], 1), lane_roll(here[0], -1)]
                else:
                    beyond = [
                        tile_at(weight, 2 + p, row) * tile_at(source, 4 * comp + 2 + p, row)
                        for p in range(2)
                    ]
                total = None
                for p in range(2):
                    slot = 2 * comp + p
                    around = middle * here[1 - p] + outer[p] * beyond[p]
                    around = around + (
                        south[p] * tile_at(iterate, slot, row + 1)
                        + north[p] * tile_at(iterate, slot, row - 1)
                    )
                    left = KEEP * tile_at(source, kinds(level) * comp + p, row) + around
                    if kept:
                        put(state, SWEPT + slot, row, here[p] + scale[p] * left)
                    if level == LOCAL - 1:
                        put(ring, slot, row, left)
                        put(state, ITERATE + slot, row, here[p])
                    total = left if total is None else total + left
                put(sums[level], comp, row, total)
            if kept:
                for p in range(2):
                    within = jnp.where(odd_row, north[p], south[p])
                    across = jnp.where(odd_row, south[p], north[p])
                    put(state, CENTRE + p, row, KEEP + scale[p] * (middle + within))
                    put(state, SIDE + p, row, scale[p] * outer[p])
                    put(state, ACROSS + p, row, scale[p] * across)
                    if level == LOCAL - 1:
                        put(state, WEIGHT + p, row, scale[p])

    coefficients(0)
    take_sources(0)
    weigh(0)
    coefficients(1)
    first_sweep(0)
    residual(0)
    weigh(1)
    coefficients(2)
    take_sources(1)
    weigh(2)
    coefficients(3)
    first_sweep(1)
    residual(1)
    take_sources(2)
    weigh(3)
    first_sweep(2)
    residual(2)
    take_sources(3)
    first_sweep(3)
    residual(3)

    start = GUARD + RIM[LOCAL - 1]
    column = lane & (SUB - 1)
    own = [
        lane_take(scale * paired(sums[LOCAL - 1], slot, start), column)
        for slot, scale in enumerate((0.25, 0.25, 0.25, 0.0625))
    ]
    chosen = ((lane >> 3) & (SUB - 1)) == sub
    edge = (lane >> 4) & 3
    place = lane & 15

    def packed(value):
        return jnp.sum(value, axis=0, keepdims=True)

    def joined(a, b):
        return packed(jnp.where(chosen, jnp.where(inner, a, b), 0.0))

    rims = jnp.zeros((SUB, LANES), F32)
    for p in range(2):
        index = jnp.where(edge < 2, column, 0 if p == 0 else SUB - 1)
        for part in range(2):
            along = (edge == part) & ((place >> 3) == p) & (sub == (0 if part == 0 else SUB - 1))
            up = (edge == 2 + p) & (place == sub + SUB * part)
            row = start + SUB * part
            value = jnp.where(
                inner,
                lane_take(tile_at(ring, p, row), index),
                lane_take(tile_at(ring, 2 + p, row), index),
            )
            rims = jnp.where(along | up, value, rims)
    kind = sub % CHUNK
    tile = jnp.where(
        kind == 0,
        joined(own[0], own[1]),
        jnp.where(kind == 1, joined(own[2], own[3]), jnp.where(kind == 2, packed(rims), 0.0)),
    )
    for block in range(CHUNK * devices // SUB):
        chunks[SUB * block : SUB * block + SUB, :] = tile


def coarse_solve(fields, rows_total, cols_total):
    shape = fields[0].shape
    width = shape[1]
    row, lane = iota(0, shape), iota(1, shape)

    def along(value, amount):
        return pltpu.roll(value, amount % width, 1)

    def down(value, amount):
        return pltpu.roll(value, amount % shape[0], 0)

    sources = fields[:2]
    reaction = jnp.where(lane < cols_total, fields[2], 1.0)
    viscous = fields[3]
    stored = []
    for level in range(COARSE):
        step = 1 << level
        odd_lane, odd_row = (lane & step) != 0, (row & step) != 0

        def paired(value):
            return (
                jnp.where(odd_lane, along(value, step), value),
                jnp.where(odd_lane, value, along(value, -step)),
            )

        def outside(value):
            return (
                jnp.where(odd_lane, along(value, 2 * step), along(value, step)),
                jnp.where(odd_lane, along(value, -step), along(value, -2 * step)),
            )

        here, reactions = paired(viscous), paired(reaction)
        beyond = outside(viscous)
        beyond = (
            jnp.where(lane < 2 * step, 0.0, beyond[0]),
            jnp.where(lane < cols_total - 2 * step, beyond[1], 0.0),
        )
        middle = jnp.minimum(here[0], here[1])
        outer = [jnp.minimum(a, b) for a, b in zip(here, beyond)]
        north, south, weights = [], [], []
        for p in range(2):
            above = jnp.where(row < step, 0.0, down(here[p], step))
            below = jnp.where(row < rows_total - step, down(here[p], -step), 0.0)
            north.append(jnp.minimum(here[p], above))
            south.append(jnp.minimum(here[p], below))
            diagonal = reactions[p] + ((middle + outer[p]) + (north[p] + south[p]))
            weights.append(OMEGA / diagonal)
        weights_beyond = (along(weights[1], 2 * step), along(weights[0], -2 * step))
        swept, remaining = [], []
        for source in sources:
            values, values_beyond = paired(source), outside(source)
            x = [w * s for w, s in zip(weights, values)]
            x_beyond = [w * s for w, s in zip(weights_beyond, values_beyond)]
            total = None
            for p in range(2):
                around = middle * x[1 - p] + outer[p] * x_beyond[p]
                around = around + (south[p] * down(x[p], -step) + north[p] * down(x[p], step))
                left = KEEP * values[p] + around
                swept.append(x[p] + weights[p] * left)
                total = left if total is None else total + left
            remaining.append(total)
        centre, side, across = [], [], []
        for p in range(2):
            within = jnp.where(odd_row, north[p], south[p])
            out = jnp.where(odd_row, south[p], north[p])
            centre.append(KEEP + weights[p] * (middle + within))
            side.append(weights[p] * outer[p])
            across.append(weights[p] * out)
        stored.append((step, odd_lane, odd_row, swept, centre, side, across))

        def folded(value, scale):
            return scale * (value + jnp.where(odd_row, down(value, step), down(value, -step)))

        sources = [folded(total, 0.25) for total in remaining]
        reaction = folded(reactions[0] + reactions[1], 0.25)
        viscous = folded(here[0] + here[1], 0.0625)

    block = 1 << COARSE
    rows_left, cols_left = rows_total // block, cols_total // block
    cells = [(i, j) for i in range(rows_left) for j in range(cols_left)]

    def spread_cells(value):
        found = {}
        for i, j in cells:
            column, place = divmod(block * j, LANES)
            tile = value[block * i : block * i + SUB, LANES * column : LANES * column + LANES]
            found[i, j] = lane_take(tile, jnp.full((SUB, LANES), place, jnp.int32))
        return found

    source_cells = [spread_cells(s) for s in sources]
    reaction_cells, viscous_cells = spread_cells(reaction), spread_cells(viscous)
    pulls, weight_cells = {}, {}
    for i, j in cells:
        near = [c for c in ((i - 1, j), (i + 1, j), (i, j - 1), (i, j + 1)) if c in viscous_cells]
        links = [(c, jnp.minimum(viscous_cells[i, j], viscous_cells[c])) for c in near]
        diagonal = reaction_cells[i, j] + sum(c for _, c in links)
        weight_cells[i, j] = OMEGA / diagonal
        pulls[i, j] = [(c, weight_cells[i, j] * link) for c, link in links]
    solved = []
    for comp in range(2):
        pushed = {c: weight_cells[c] * source_cells[comp][c] for c in cells}
        values = pushed
        for _ in range(COARSE_SWEEPS - 1):
            values = {
                c: (KEEP * values[c] + pushed[c])
                + sum(pull * values[other] for other, pull in pulls[c])
                for c in cells
            }
        solved.append(values)

    def laid(values, di, dj):
        tiles = []
        nothing = jnp.zeros((SUB, LANES), F32)
        for tile in range(shape[0] // SUB):
            i = SUB * tile // block
            if di:
                i += 1 if (SUB * tile // (block // 2)) % 2 else -1
            columns = []
            for column in range(width // LANES):
                place = iota(1) // block + column * (LANES // block)
                value = nothing
                for j in range(cols_left):
                    if (i, j) in values and column * LANES <= (j - dj) * block < (column + 1) * LANES:
                        value = jnp.where(place == j - dj, values[i, j], value)
                columns.append(value)
            tiles.append(columns[0] if len(columns) == 1 else jnp.concatenate(columns, 1))
        return jnp.concatenate(tiles, 0)

    corrections = None
    for step, odd_lane, odd_row, swept, centre, side, across in reversed(stored):
        found = []
        for comp in range(2):
            if corrections is None:
                here = laid(solved[comp], 0, 0)
                beyond = [laid(solved[comp], 0, -1), laid(solved[comp], 0, 1)]
                out = laid(solved[comp], 1, 0)
            else:
                here = corrections[comp]
                beyond = [along(here, 2 * step), along(here, -2 * step)]
                out = jnp.where(odd_row, down(here, -step), down(here, step))
            parts = [
                (swept[2 * comp + p] + centre[p] * here) + (side[p] * beyond[p] + across[p] * out)
                for p in range(2)
            ]
            found.append(jnp.where(odd_lane, parts[1], parts[0]))
        corrections = found
    return corrections


def up_kernel(size_x, size_y, gathered, state0, state1, state2, state3, out, *refs):
    grid, whole, swept3, corr1, corr2, corr3, merged0, merged1, merged2 = refs
    index_x, index_y = lax.axis_index("gx"), lax.axis_index("gy")
    rows_total, cols_total = CELLS * size_x, CELLS * size_y
    width = max(LANES, cols_total)
    columns = width // LANES
    per_column = LANES // CELLS
    lane, sub = iota(1), iota(0)

    tall = iota(1, (2 * size_x, LANES))
    for column in range(columns):
        targets = [[jnp.zeros((2 * size_x, LANES), F32)] * CELLS for _ in range(2)]
        for place in range(min(per_column, size_y - column * per_column)):
            j = column * per_column + place
            chunk = jnp.concatenate(
                [
                    gathered[pl.ds(CHUNK * j + h, size_x, stride=CHUNK * size_y), :]
                    for h in range(2)
                ],
                0,
            )
            mine = (tall // CELLS) == place
            turns = {}
            for half in range(2):
                for r in range(CELLS):
                    shift = (CELLS * (place - r) - half * HALF) % LANES
                    if shift not in turns:
                        turns[shift] = lane_roll(chunk, shift)
                    targets[half][r] = jnp.where(mine, turns[shift], targets[half][r])
        for half in range(2):
            for r in range(CELLS):
                for h in range(2):
                    grid[2 * h + half, column, pl.ds(r, size_x, stride=CELLS), :] = targets[half][r][
                        h * size_x : (h + 1) * size_x
                    ]
    fields = [
        jnp.concatenate([grid[f, c] for c in range(columns)], 1) if columns > 1 else grid[f, 0]
        for f in range(4)
    ]

    def ring_row(dx, dy):
        i = jnp.clip(index_x + dx, 0, size_x - 1)
        j = jnp.clip(index_y + dy, 0, size_y - 1)
        return jnp.broadcast_to(
            gathered[pl.ds(CHUNK * (i * size_y + j) + 2, 1), :], (SUB, LANES)
        )

    beside = {
        (dx, dy): ring_row(dx, dy) for dx in (-1, 0, 1) for dy in (-1, 0, 1) if dx or dy
    }
    start = GUARD + RIM[3]
    for comp in range(2):
        base = comp * HALF
        for p in range(2):
            slot = 2 * comp + p
            end = 7 if p else 0
            corner_lane = LANES - 1 if p else SUB
            dy = -1 if p else 1
            for tile in range(2):
                at = start + SUB * tile
                index = base + (48 if p else 32) + SUB * tile + sub
                ringed = lane_take(beside[0, dy], index)
                swept = jnp.where(
                    lane == corner_lane,
                    tile_at(state3, ITERATE + slot, at) + tile_at(state3, WEIGHT + p, at) * ringed,
                    tile_at(state3, SWEPT + slot, at),
                )
                swept3[slot, at : at + SUB, :] = swept
            for dx, at, edge in ((-1, start - 1, 16), (1, start + 2 * SUB, 0)):
                index = base + edge + 8 * p
                ringed = jnp.where(
                    lane == corner_lane,
                    lane_take(beside[dx, dy], jnp.full((SUB, LANES), index + end, jnp.int32)),
                    lane_take(beside[dx, 0], index + (lane & 7)),
                )
                rows = slice(at, at + 1)
                swept3[slot, rows, :] = (
                    state3[ITERATE + slot, rows, :] + state3[WEIGHT + p, rows, :] * ringed[0:1]
                )

    corrections = coarse_solve(fields, rows_total, cols_total)

    for comp in range(2):
        for kind in range(3):
            shift = (width - CELLS * index_y + (0, -1, 1)[kind] + width) % width
            turned = pltpu.roll(corrections[comp], shift, 1)
            if columns > 1:
                tall_lane = iota(1, (rows_total, LANES))
                turned = jnp.where(
                    tall_lane < HALF, turned[:, :LANES], turned[:, width - LANES :]
                )
            slot = 3 * comp + kind
            whole[slot, 2 * GUARD : 2 * GUARD + rows_total, :] = turned
            whole[slot, 0 : 2 * GUARD, :] = jnp.zeros((2 * GUARD, LANES), F32)
            whole[slot, 2 * GUARD + rows_total :, :] = jnp.zeros((3 * SUB, LANES), F32)

    def swept_rows(ref, level, coarse_row, parity, here, beyond, across, comp):
        at = pl.ds(GUARD + RIM[level] + 2 * coarse_row + parity, SUB, stride=2)
        state = (state0, state1, state2, state3)[level]
        return [
            (ref[SWEPT + 2 * comp + p, at, :] + state[CENTRE + p, at, :] * here)
            + (state[SIDE + p, at, :] * beyond[p] + state[ACROSS + p, at, :] * across)
            for p in range(2)
        ]

    base = pl.multiple_of(CELLS * index_x, SUB)
    for comp in range(2):
        window = [whole[3 * comp + kind, pl.ds(base, 6 * SUB), :] for kind in range(3)]
        for tile in range(2):
            first = SUB * tile - 1
            at = 2 * GUARD + first
            here, right, left = [w[at : at + SUB] for w in window]
            for parity in range(2):
                shifted = at + (1 if parity else -1)
                across = window[0][shifted : shifted + SUB]
                found = swept_rows(swept3, 3, first, parity, here, (left, right), across, comp)
                rows = pl.ds(GUARD + RIM[3] + 2 * first + parity, SUB, stride=2)
                for p in range(2):
                    corr3[2 * comp + p, rows, :] = found[p]

    corrs = [None, corr1, corr2, corr3]
    merged = [merged0, merged1, merged2]
    near = ((((lane + 32) & (LANES - 1)) - 32) >> 1) & (LANES - 1)
    odd_lane = (lane & 1) == 1
    for level in (2, 1, 0):
        coarse = level + 1
        corr, state, whole_rows = corrs[coarse], (state0, state1, state2)[level], merged[level]
        count = (LANES >> coarse) + 2
        origin = GUARD + RIM[coarse]
        sides = {}
        for tile in range(-(-count // SUB)):
            at = origin - 1 + SUB * tile
            for comp in range(2):
                even, odd = tile_at(corr, 2 * comp, at), tile_at(corr, 2 * comp + 1, at)
                even_here, odd_here = lane_take(even, near), lane_take(odd, near)
                even_next = lane_take(even, (near + 1) & (LANES - 1))
                odd_last = lane_take(odd, (near - 1) & (LANES - 1))
                here = jnp.where(odd_lane, odd_here, even_here)
                whole_rows[3 * comp, at : at + SUB, :] = here
                whole_rows[3 * comp + 1, at : at + SUB, :] = jnp.where(
                    odd_lane, even_next, odd_here
                )
                whole_rows[3 * comp + 2, at : at + SUB, :] = jnp.where(
                    odd_lane, even_here, odd_last
                )
        if level > 0:
            first, tiles = -1, -(-count // SUB)
        else:
            first, tiles = 0, (count - 2) // SUB
        for tile in range(tiles):
            coarse_row = first + SUB * tile
            at = origin + coarse_row
            for comp in range(2):
                here, right, left = [tile_at(whole_rows, 3 * comp + k, at) for k in range(3)]
                for parity in range(2):
                    across = tile_at(whole_rows, 3 * comp, at + (1 if parity else -1))
                    found = swept_rows(
                        state, level, coarse_row, parity, here, (left, right), across, comp
                    )
                    if level > 0:
                        rows = pl.ds(GUARD + RIM[level] + 2 * coarse_row + parity, SUB, stride=2)
                        for p in range(2):
                            corrs[level][2 * comp + p, rows, :] = found[p]
                    else:
                        rows = pl.ds(2 * coarse_row + parity, SUB, stride=2)
                        out[comp, rows, :] = jnp.where(
                            odd_lane,
                            lane_take(found[1], lane >> 1),
                            lane_take(found[0], lane >> 1),
                        )


def params():
    return pltpu.CompilerParams(vmem_limit_bytes=VMEM_LIMIT)


VMEM_SPEC = pl.BlockSpec(memory_space=pltpu.VMEM)
SMEM_SPEC = pl.BlockSpec(memory_space=pltpu.SMEM)
HBM_SPEC = pl.BlockSpec(memory_space=pltpu.HBM)


def swap_routes(size_x, size_y):
    def index(i, j):
        return i * size_y + j

    routes = []
    for axis in range(2):
        size = (size_x, size_y)[axis]
        for offset in range(2):
            route = []
            for i in range(size_x):
                for j in range(size_y):
                    here = (i, j)[axis]
                    other = here + 1 if here % 2 == offset else here - 1
                    if 0 <= other < size:
                        peer = (other, j) if axis == 0 else (i, other)
                    else:
                        peer = (i, j ^ 1) if axis == 0 else (i ^ 1, j)
                    route.append((index(i, j), index(*peer)))
            routes.append(route)
    return routes


def per_device(size_x, size_y, right_side, shift_coef, viscosity, wet_tiles):
    axes = ("gx", "gy")
    devices = size_x * size_y
    routes = swap_routes(size_x, size_y)
    band = jax.ShapeDtypeStruct((4 * HALO, LANES), F32)
    held_shape = pltpu.VMEM((4, HELD[0], LANES), F32)
    held, first, second = pl.pallas_call(
        bands_kernel,
        out_shape=(held_shape, band, band),
        in_specs=[SMEM_SPEC] + [HBM_SPEC] * 3,
        out_specs=(VMEM_SPEC,) * 3,
        scratch_shapes=[pltpu.SemaphoreType.DMA((4,))],
        compiler_params=params(),
        name="bands",
    )(
        wet_tiles,
        *[
            pltpu.with_memory_space_constraint(array, pltpu.HBM)
            for array in (right_side, shift_coef, viscosity)
        ],
    )
    second = lax.ppermute(second, axes, routes[1])
    first = lax.ppermute(first, axes, routes[0])
    strip = jax.ShapeDtypeStruct((MESSAGE, LANES), F32)
    got = (first, second)
    first, second = pl.pallas_call(
        functools.partial(strips_kernel, size_x),
        out_shape=(strip, strip),
        in_specs=[SMEM_SPEC] + [VMEM_SPEC] * 3,
        out_specs=(VMEM_SPEC,) * 2,
        compiler_params=params(),
        name="strips",
    )(wet_tiles, held, *got)
    fields = pl.pallas_call(
        functools.partial(halves_kernel, size_x),
        out_shape=pltpu.VMEM((8, HELD[0], LANES), F32),
        in_specs=[SMEM_SPEC] + [VMEM_SPEC] * 3,
        out_specs=VMEM_SPEC,
        cost_estimate=pl.CostEstimate(flops=1 << 20, bytes_accessed=1 << 21, transcendentals=0),
        compiler_params=params(),
        name="halves",
    )(wet_tiles, held, *got)
    second = lax.ppermute(second, axes, routes[3])
    first = lax.ppermute(first, axes, routes[2])

    def buffers(counts):
        return [pltpu.VMEM((n, HELD[level], LANES), F32) for level, n in enumerate(counts)]

    chunks, *states = pl.pallas_call(
        functools.partial(down_kernel, size_y, devices),
        out_shape=(jax.ShapeDtypeStruct((CHUNK * devices, LANES), F32),)
        + tuple(buffers([STATE, STATE, STATE, STATE + 6])),
        in_specs=[VMEM_SPEC] * 3,
        out_specs=(VMEM_SPEC,) * (1 + LOCAL),
        scratch_shapes=buffers([2, 4, 4, 4])
        + buffers([2] * 4)
        + buffers([4, 8, 8, 8])
        + buffers([2, 4, 4, 4])
        + buffers([4] * 4)
        + buffers([4] * 4)
        + [pltpu.VMEM((2, HELD[0], LANES), F32), pltpu.VMEM((4, HELD[3], LANES), F32)],
        compiler_params=params(),
        name="down",
    )(second, first, fields)
    gathered = lax.all_to_all(chunks, axes, 0, 0, tiled=True)
    rows_total = CELLS * size_x
    columns = max(LANES, CELLS * size_y) // LANES
    return pl.pallas_call(
        functools.partial(up_kernel, size_x, size_y),
        out_shape=jax.ShapeDtypeStruct((2, LANES, LANES), F32),
        in_specs=[VMEM_SPEC] * (1 + LOCAL),
        out_specs=VMEM_SPEC,
        scratch_shapes=[
            pltpu.VMEM((4, columns, rows_total, LANES), F32),
            pltpu.VMEM((6, rows_total + 5 * SUB, LANES), F32),
            pltpu.VMEM((4, HELD[3], LANES), F32),
        ]
        + [pltpu.VMEM((4, HELD[level], LANES), F32) for level in (1, 2, 3)]
        + [pltpu.VMEM((6, HELD[level + 1], LANES), F32) for level in (0, 1, 2)],
        compiler_params=params(),
        name="up",
    )(gathered, *states)


def solution(mesh):
    sizes = dict(mesh.shape)
    placed = (P(None, "gx", "gy"), P("gx", "gy"), P("gx", "gy"), P("gx", "gy"))
    return jax.shard_map(
        functools.partial(per_device, sizes["gx"], sizes["gy"]),
        mesh=mesh,
        in_specs=placed,
        out_specs=P(None, "gx", "gy"),
        check_vma=False,
    )
```

```python
import functools

import jax
import jax.numpy as jnp
from jax import lax
from jax.experimental import pallas as pl
from jax.experimental.pallas import tpu as pltpu
from jax.sharding import PartitionSpec as P

LOCAL = 4
COARSE = 4
COARSE_SWEEPS = 8
OMEGA = 0.8
KEEP = 1.0 - OMEGA

LANES = 128
HALF = LANES // 2
SUB = 8
HALO = 16
GUARD = 8
CELLS = LANES >> LOCAL
ROWS = [(LANES + 2 * HALO) >> level for level in range(LOCAL)]
TILES = [-(-rows // SUB) for rows in ROWS]
HELD = [GUARD + SUB * tiles + 16 for tiles in TILES]
RIM = [HALO >> level for level in range(LOCAL)]
TOP = GUARD + HALO
LOW = TOP + LANES
HALF_TILES = TILES[0] // 2
MESSAGE = ROWS[0] // 2
CHUNK = 4
F32 = jnp.float32
VMEM_LIMIT = 48 * 1024 * 1024

SWEPT, CENTRE, SIDE, ACROSS = 0, 4, 6, 8
STATE = 10
ITERATE, WEIGHT = 10, 14


def iota(dim, shape=(SUB, LANES)):
    return lax.broadcasted_iota(jnp.int32, shape, dim)


def lane_take(tile, index):
    return jnp.take_along_axis(tile, index, axis=1)


def lane_roll(tile, shift):
    return pltpu.roll(tile, shift % LANES, 1)


def tile_at(ref, slot, row):
    return ref[slot, row : row + SUB, :]


def bands_kernel(wet, right_side, shift_coef, viscosity, held, first, second, sems):
    odd = lax.axis_index("gx") % 2
    wetness = wet[0, 0].astype(F32)
    own = pl.ds(TOP, LANES)
    sources = (right_side.at[0], right_side.at[1], shift_coef, viscosity)
    copies = [
        pltpu.make_async_copy(sources[field], held.at[field, own, :], sems.at[field])
        for field in range(4)
    ]
    for copy in copies:
        copy.start()
    bottom = LANES - HALO
    starts = (TOP + bottom - bottom * odd, TOP + bottom * odd)
    for field in range(4):
        copies[field].wait()
        for start, out in zip(starts, (first, second)):
            value = held[field, pl.ds(pl.multiple_of(start, SUB), HALO), :]
            out[field * HALO : (field + 1) * HALO, :] = value if field == 2 else value * wetness


def rim_place(half, lane):
    to_left = ((lane >> 3) & 1) == half
    q = jnp.where(to_left, lane, (lane - (56 + 8 * half)) & (LANES - 1)) >> 4
    cell = 2 * (lane & 7) + (q & 1) + jnp.where(to_left, 0, LANES - HALO)
    return to_left, q >> 1, cell


def strips_kernel(size_x, wet, held, got_first, got_second, first, second):
    index_x = lax.axis_index("gx")
    odd_x = index_x % 2 == 1
    odd_y = lax.axis_index("gy") % 2 == 1
    wetness = wet[0, 0].astype(F32)
    above = (index_x > 0).astype(F32)
    below = (index_x < size_x - 1).astype(F32)
    lane = iota(1)
    rim_tiles = HALO // SUB

    def piece(field, tile):
        if rim_tiles <= tile < TILES[0] - rim_tiles:
            row = GUARD + SUB * tile
            return held[field, row : row + SUB, :]
        top = tile < rim_tiles
        row = field * HALO + SUB * (tile if top else tile - (TILES[0] - rim_tiles))
        one, two = got_first[row : row + SUB, :], got_second[row : row + SUB, :]
        return jnp.where(odd_x, one, two) if top else jnp.where(odd_x, two, one)

    places = [rim_place(half, lane) for half in range(2)]
    for tile in range(HALF_TILES):
        found = []
        for half in range(2):
            to_left, owner, cell = places[half]
            at = tile + half * HALF_TILES
            value = None
            for field in range(4):
                part = lane_take(piece(field, at), cell)
                value = part if value is None else jnp.where(owner == field, part, value)
            if rim_tiles <= at < TILES[0] - rim_tiles:
                value = value * jnp.where(owner == 2, 1.0, wetness)
            else:
                value = value * jnp.where(owner == 3, above if at < rim_tiles else below, 1.0)
            found.append(value)
        left = jnp.where(places[0][0], found[0], found[1])
        right = jnp.where(places[0][0], found[1], found[0])
        rows = slice(SUB * tile, SUB * tile + SUB)
        first[rows, :] = jnp.where(odd_y, left, right)
        second[rows, :] = jnp.where(odd_y, right, left)


def halves_kernel(size_x, wet, held, got_first, got_second, fields):
    index_x = lax.axis_index("gx")
    odd_x = index_x % 2 == 1
    wetness = wet[0, 0].astype(F32)
    above = (index_x > 0).astype(F32)
    below = (index_x < size_x - 1).astype(F32)
    lane = iota(1)
    rim_tiles = HALO // SUB
    for tile in range(TILES[0]):
        row = GUARD + SUB * tile
        for field in range(4):
            if rim_tiles <= tile < TILES[0] - rim_tiles:
                value = held[field, row : row + SUB, :]
                if field != 2:
                    value = value * wetness
            else:
                top = tile < rim_tiles
                at = field * HALO + SUB * (tile if top else tile - (TILES[0] - rim_tiles))
                one, two = got_first[at : at + SUB, :], got_second[at : at + SUB, :]
                value = jnp.where(odd_x, one, two) if top else jnp.where(odd_x, two, one)
                if field == 3:
                    value = value * (above if top else below)
            for parity in range(2):
                fields[2 * field + parity, row : row + SUB, :] = lane_take(
                    value, (2 * lane + parity) & (LANES - 1)
                )


def down_kernel(size_y, devices, got_second, got_first, held, chunks, *refs):
    states, refs = refs[:LOCAL], refs[LOCAL:]
    viscous, refs = refs[:LOCAL], refs[LOCAL:]
    reactions, refs = refs[:LOCAL], refs[LOCAL:]
    sources, refs = refs[:LOCAL], refs[LOCAL:]
    weights, refs = refs[:LOCAL], refs[LOCAL:]
    iterates, refs = refs[:LOCAL], refs[LOCAL:]
    sums, (outers, ring) = refs[:LOCAL], refs[LOCAL:]
    index_y = lax.axis_index("gy")
    odd_y = index_y % 2 == 1
    lane, sub = iota(1), iota(0)
    side_ok = jnp.where(
        lane < 96, (index_y < size_y - 1).astype(F32), (index_y > 0).astype(F32)
    )
    odd_row = (sub & 1) == 1
    inner = lane < HALF
    even_block = ((lane >> 3) & 1) == 0

    def tiles(level):
        return [GUARD + SUB * tile for tile in range(TILES[level])]

    def put(ref, slot, row, value):
        ref[slot, row : row + SUB, :] = value

    def rims(row, slots):
        half, at = divmod((row - GUARD) // SUB, HALF_TILES)
        one, two = (r[SUB * at : SUB * at + SUB, :] for r in (got_first, got_second))
        after, before = jnp.where(odd_y, two, one), jnp.where(odd_y, one, two)
        if half == 0:
            both = jnp.where(even_block, after, before)
        else:
            both = jnp.where(even_block, before, after)
        values = []
        for slot in slots:
            rim = lane_roll(both, HALF - 16 * slot - 8 * half)
            if slot >= 4:
                rim = jnp.where(side_ok > 0, rim, 1.0 if slot < 6 else 0.0)
            values.append(jnp.where(inner, tile_at(held, slot, row), rim))
        return values

    def paired(ref, slot, start):
        return (
            ref[slot, pl.ds(start, SUB, stride=2), :] + ref[slot, pl.ds(start + 1, SUB, stride=2), :]
        )

    takes = [(2 * lane + offset) & (LANES - 1) for offset in (0, 1, -1, 2)]

    def coefficients(level):
        for row in tiles(level):
            if level == 0:
                values = rims(row, (4, 5, 6, 7))
                reaction, viscosity = values[:2], values[2:]
            else:
                start = GUARD + 2 * (row - GUARD)
                ref = sums[level - 1]
                value = 0.0625 * paired(ref, 3, start)
                viscosity = [lane_take(value, t) for t in takes]
                value = 0.25 * paired(ref, 2, start)
                reaction = [lane_take(value, t) for t in takes[:2]]
            for slot, value in enumerate(viscosity):
                put(viscous[level], slot, row, value)
            for slot, value in enumerate(reaction):
                put(reactions[level], slot, row, value)
            put(sums[level], 2, row, reaction[0] + reaction[1])
            put(sums[level], 3, row, viscosity[0] + viscosity[1])

    def faces(level, row):
        here = [tile_at(viscous[level], p, row) for p in range(2)]
        north = [jnp.minimum(here[p], tile_at(viscous[level], p, row - 1)) for p in range(2)]
        south = [jnp.minimum(here[p], tile_at(viscous[level], p, row + 1)) for p in range(2)]
        return here, jnp.minimum(here[0], here[1]), north, south

    def outside(level, row, here):
        if level == 0:
            beyond = [lane_roll(here[1], 1), lane_roll(here[0], -1)]
        else:
            beyond = [tile_at(viscous[level], 2 + p, row) for p in range(2)]
        return [jnp.minimum(h, b) for h, b in zip(here, beyond)]

    def weigh(level):
        for row in tiles(level):
            here, middle, north, south = faces(level, row)
            outer = outside(level, row, here)
            found = []
            for p in range(2):
                diagonal = tile_at(reactions[level], p, row) + (
                    (middle + outer[p]) + (north[p] + south[p])
                )
                found.append(OMEGA / diagonal)
                if level == 0:
                    put(outers, p, row, outer[p])
            if level > 0:
                found += [lane_roll(found[1], 1), lane_roll(found[0], -1)]
            for slot, value in enumerate(found):
                put(weights[level], slot, row, value)

    def take_sources(level):
        for row in tiles(level):
            if level == 0:
                found = rims(row, (0, 1, 2, 3))
            else:
                start = GUARD + 2 * (row - GUARD)
                values = [0.25 * paired(sums[level - 1], comp, start) for comp in range(2)]
                found = [lane_take(value, t) for value in values for t in takes]
            for slot, value in enumerate(found):
                put(sources[level], slot, row, value)

    def kinds(level):
        return 2 if level == 0 else 4

    def first_sweep(level):
        for row in tiles(level):
            for comp in range(2):
                for p in range(2):
                    put(
                        iterates[level],
                        2 * comp + p,
                        row,
                        tile_at(weights[level], p, row)
                        * tile_at(sources[level], kinds(level) * comp + p, row),
                    )

    def residual(level):
        state, iterate, weight, source = (
            states[level],
            iterates[level],
            weights[level],
            sources[level],
        )
        for row in tiles(level):
            _, middle, north, south = faces(level, row)
            if level == 0:
                outer = [tile_at(outers, p, row) for p in range(2)]
            else:
                outer = outside(level, row, [tile_at(viscous[level], p, row) for p in range(2)])
            scale = [tile_at(weight, p, row) for p in range(2)]
            kept = level > 0 or TOP <= row < LOW
            for comp in range(2):
                here = [tile_at(iterate, 2 * comp + p, row) for p in range(2)]
                if level == 0:
                    beyond = [lane_roll(here[1], 1), lane_roll(here[0], -1)]
                else:
                    beyond = [
                        tile_at(weight, 2 + p, row) * tile_at(source, 4 * comp + 2 + p, row)
                        for p in range(2)
                    ]
                total = None
                for p in range(2):
                    slot = 2 * comp + p
                    around = middle * here[1 - p] + outer[p] * beyond[p]
                    around = around + (
                        south[p] * tile_at(iterate, slot, row + 1)
                        + north[p] * tile_at(iterate, slot, row - 1)
                    )
                    left = KEEP * tile_at(source, kinds(level) * comp + p, row) + around
                    if kept:
                        put(state, SWEPT + slot, row, here[p] + scale[p] * left)
                    if level == LOCAL - 1:
                        put(ring, slot, row, left)
                        put(state, ITERATE + slot, row, here[p])
                    total = left if total is None else total + left
                put(sums[level], comp, row, total)
            if kept:
                for p in range(2):
                    within = jnp.where(odd_row, north[p], south[p])
                    across = jnp.where(odd_row, south[p], north[p])
                    put(state, CENTRE + p, row, KEEP + scale[p] * (middle + within))
                    put(state, SIDE + p, row, scale[p] * outer[p])
                    put(state, ACROSS + p, row, scale[p] * across)
                    if level == LOCAL - 1:
                        put(state, WEIGHT + p, row, scale[p])

    coefficients(0)
    take_sources(0)
    weigh(0)
    coefficients(1)
    first_sweep(0)
    residual(0)
    weigh(1)
    coefficients(2)
    take_sources(1)
    weigh(2)
    coefficients(3)
    first_sweep(1)
    residual(1)
    take_sources(2)
    weigh(3)
    first_sweep(2)
    residual(2)
    take_sources(3)
    first_sweep(3)
    residual(3)

    start = GUARD + RIM[LOCAL - 1]
    column = lane & (SUB - 1)
    own = [
        lane_take(scale * paired(sums[LOCAL - 1], slot, start), column)
        for slot, scale in enumerate((0.25, 0.25, 0.25, 0.0625))
    ]
    turned = ((lane >> 3) - index_y) & 15
    chosen = (turned & (SUB - 1)) == sub

    def packed(value):
        return jnp.sum(value, axis=0, keepdims=True)

    def joined(a, b):
        return packed(jnp.where(chosen, jnp.where(turned < SUB, a, b), 0.0))

    edge = (lane >> 4) & 3
    place = lane & 15

    rims = jnp.zeros((SUB, LANES), F32)
    for p in range(2):
        index = jnp.where(edge < 2, column, 0 if p == 0 else SUB - 1)
        for part in range(2):
            along = (edge == part) & ((place >> 3) == p) & (sub == (0 if part == 0 else SUB - 1))
            up = (edge == 2 + p) & (place == sub + SUB * part)
            row = start + SUB * part
            value = jnp.where(
                inner,
                lane_take(tile_at(ring, p, row), index),
                lane_take(tile_at(ring, 2 + p, row), index),
            )
            rims = jnp.where(along | up, value, rims)
    kind = sub % CHUNK
    parts = [joined(own[0], own[1]), joined(own[2], own[2]), packed(rims), joined(own[3], own[3])]
    tile = jnp.where(
        kind < 2,
        jnp.where(kind == 0, parts[0], parts[1]),
        jnp.where(kind == 2, parts[2], parts[3]),
    )
    for block in range(CHUNK * devices // SUB):
        chunks[SUB * block : SUB * block + SUB, :] = tile


def write(buffer, slot, rows, value):
    for column in range(buffer.shape[1]):
        buffer[slot, column, rows, :] = value[:, LANES * column : LANES * column + LANES]


def read(buffer, slot, rows):
    parts = [buffer[slot, column, rows, :] for column in range(buffer.shape[1])]
    return parts[0] if len(parts) == 1 else jnp.concatenate(parts, 1)


class Coarse:
    def __init__(self, step, row_step, rows, cols_total, width):
        self.step, self.row_step = step, row_step
        self.shape = (rows, width)
        lane, row = iota(1, self.shape), iota(0, self.shape)
        column = lane & (cols_total - 1)
        self.odd_lane, self.odd_row = (lane & step) != 0, (row & row_step) != 0
        self.leftmost = column < 2 * step
        self.rightmost = column >= cols_total - 2 * step
        self.top, self.bottom = row < row_step, row >= rows - row_step

    def along(self, value, amount):
        return pltpu.roll(value, amount % self.shape[1], 1)

    def down(self, value, amount):
        return pltpu.roll(value, amount % self.shape[0], 0)

    def paired(self, value):
        return (
            jnp.where(self.odd_lane, self.along(value, self.step), value),
            jnp.where(self.odd_lane, value, self.along(value, -self.step)),
        )

    def outside(self, value):
        return (
            jnp.where(
                self.odd_lane, self.along(value, 2 * self.step), self.along(value, self.step)
            ),
            jnp.where(
                self.odd_lane, self.along(value, -self.step), self.along(value, -2 * self.step)
            ),
        )

    def coefficients(self, viscous, reaction):
        here, reactions, beyond = self.paired(viscous), self.paired(reaction), self.outside(viscous)
        self.middle = jnp.minimum(here[0], here[1])
        self.outer = [
            jnp.minimum(here[0], jnp.where(self.leftmost, 0.0, beyond[0])),
            jnp.minimum(here[1], jnp.where(self.rightmost, 0.0, beyond[1])),
        ]
        self.north, self.south, self.weights = [], [], []
        for p in range(2):
            above = jnp.where(self.top, 0.0, self.down(here[p], self.row_step))
            below = jnp.where(self.bottom, 0.0, self.down(here[p], -self.row_step))
            self.north.append(jnp.minimum(here[p], above))
            self.south.append(jnp.minimum(here[p], below))
            diagonal = reactions[p] + (
                (self.middle + self.outer[p]) + (self.north[p] + self.south[p])
            )
            self.weights.append(OMEGA / diagonal)
        return here[0] + here[1], reactions[0] + reactions[1]

    def weigh(self):
        self.weights_beyond = (
            self.along(self.weights[1], 2 * self.step),
            self.along(self.weights[0], -2 * self.step),
        )

    def take(self, source):
        self.values, self.values_beyond = self.paired(source), self.outside(source)

    def residual(self):
        x = [w * s for w, s in zip(self.weights, self.values)]
        x_beyond = [w * s for w, s in zip(self.weights_beyond, self.values_beyond)]
        total, self.swept = None, []
        for p in range(2):
            around = self.middle * x[1 - p] + self.outer[p] * x_beyond[p]
            around = around + (
                self.south[p] * self.down(x[p], -self.row_step)
                + self.north[p] * self.down(x[p], self.row_step)
            )
            left = KEEP * self.values[p] + around
            self.swept.append(x[p] + self.weights[p] * left)
            total = left if total is None else total + left
        return total

    def corrected(self, here, beyond, across):
        parts = []
        for p in range(2):
            within = jnp.where(self.odd_row, self.north[p], self.south[p])
            out = jnp.where(self.odd_row, self.south[p], self.north[p])
            weight = self.weights[p]
            centre = KEEP + weight * (self.middle + within)
            parts.append(
                (self.swept[p] + centre * here)
                + ((weight * self.outer[p]) * beyond[p] + (weight * out) * across)
            )
        return jnp.where(self.odd_lane, parts[1], parts[0])


def coarse_solve(grid, buffer, rows_total, cols_total, width, meanwhile):
    columns = width // LANES

    def whole(slot):
        return jnp.concatenate([grid[slot, c] for c in range(columns)], 1) if columns > 1 else grid[slot, 0]

    levels, rows, row_step = [], rows_total, 1
    for index in range(COARSE + 1):
        levels.append(Coarse(1 << index, row_step, rows, cols_total, width))
        if rows > SUB:
            rows //= 2
        else:
            row_step *= 2

    def folded(index, value, slot, scale):
        level = levels[index]
        rows = level.shape[0]
        if levels[index + 1].shape[0] == rows:
            other = jnp.where(
                level.odd_row, level.down(value, level.row_step), level.down(value, -level.row_step)
            )
            return scale * (value + other)
        write(buffer, slot, slice(0, rows), value)
        first, second = [pl.ds(begin, rows // 2, stride=2) for begin in range(2)]
        return scale * (read(buffer, slot, first) + read(buffer, slot, second))

    def opened(index, value):
        level = levels[index]
        rows = level.shape[0]
        if value.shape[0] == rows:
            return value, jnp.where(
                level.odd_row, level.down(value, -level.row_step), level.down(value, level.row_step)
            )
        half = rows // 2
        blank = jnp.zeros((SUB, width), F32)
        for begin in range(2):
            write(buffer, 0, pl.ds(begin, half, stride=2), value)
        write(buffer, 1, slice(SUB, 2 * SUB), blank)
        write(buffer, 1, slice(rows, rows + SUB), blank)
        for begin in (SUB + 2, SUB - 1):
            write(buffer, 1, pl.ds(begin, half, stride=2), value)
        return read(buffer, 0, slice(0, rows)), read(buffer, 1, slice(SUB, SUB + rows))

    viscous, reaction, source = [None] * 5, [None] * 5, [None] * 5
    viscous[0], reaction[0], source[0] = whole(2), whole(1), whole(0)

    def coefficients(index):
        pair, reactions = levels[index].coefficients(viscous[index], reaction[index])
        viscous[index + 1] = folded(index, pair, 0, 0.0625)
        reaction[index + 1] = folded(index, reactions, 1, 0.25)

    def residual(index):
        source[index + 1] = folded(index, levels[index].residual(), 2, 0.25)

    last = levels[COARSE]
    block = 1 << COARSE
    cols_left = cols_total // block
    rows_left = last.shape[0]
    lane = iota(1, (rows_left, LANES))
    groups = 1 if cols_total < LANES else 2
    per_group = columns // groups

    def spread(value):
        found = []
        for group in range(groups):
            for j in range(cols_left):
                column, place = divmod(block * j, LANES)
                column += group * per_group
                if groups == 1:
                    place = place + (lane & (LANES - cols_total))
                else:
                    place = jnp.full((rows_left, LANES), place, jnp.int32)
                found.append(lane_take(value[:, LANES * column : LANES * column + LANES], place))
        return found

    def flat(values, group, j):
        return values[group * cols_left + j]

    levels[0].take(source[0])
    coefficients(0)
    coefficients(1)
    levels[0].weigh()
    coefficients(2)
    levels[1].weigh()
    residual(0)
    levels[1].take(source[1])
    coefficients(3)
    levels[2].weigh()
    residual(1)
    levels[2].take(source[2])
    meanwhile()
    levels[3].weigh()
    viscous_columns, reaction_columns = spread(viscous[4]), spread(reaction[4])
    residual(2)
    levels[3].take(source[3])

    top, bottom = last.top[:, :LANES], last.bottom[:, :LANES]
    pulls, weights = [], []
    for group in range(groups):
        for j in range(cols_left):
            here = flat(viscous_columns, group, j)
            above = jnp.where(top, 0.0, last.down(here, last.row_step))
            below = jnp.where(bottom, 0.0, last.down(here, -last.row_step))
            links = [jnp.minimum(here, above), jnp.minimum(here, below)]
            links += [
                jnp.minimum(here, flat(viscous_columns, group, other))
                for other in (j - 1, j + 1)
                if 0 <= other < cols_left
            ]
            weight = OMEGA / (flat(reaction_columns, group, j) + sum(links))
            weights.append(weight)
            pulls.append([weight * link for link in links])
    residual(3)
    pushed = [w * s for w, s in zip(weights, spread(source[4]))]
    values = pushed
    for _ in range(COARSE_SWEEPS - 1):
        following = []
        for group in range(groups):
            for j in range(cols_left):
                at = group * cols_left + j
                here, pull = values[at], pulls[at]
                total = (KEEP * here + pushed[at]) + (
                    pull[0] * last.down(here, last.row_step)
                    + pull[1] * last.down(here, -last.row_step)
                )
                sides = [other for other in (j - 1, j + 1) if 0 <= other < cols_left]
                for link, other in zip(pull[2:], sides):
                    total = total + link * flat(values, group, other)
                following.append(total)
        values = following

    def laid(shift):
        found = []
        for column in range(columns):
            group = column // per_group
            place = ((lane & (cols_total - 1)) if groups == 1 else lane) // block
            place = place + (column % per_group) * (LANES // block)
            value = jnp.zeros((rows_left, LANES), F32)
            for j in range(cols_left):
                value = jnp.where(place == j + shift, flat(values, group, j), value)
            found.append(value)
        return found[0] if columns == 1 else jnp.concatenate(found, 1)

    index = COARSE - 1
    here, across = opened(index, laid(0))
    beyond = [opened(index, laid(shift))[0] for shift in (1, -1)]
    correction = levels[index].corrected(here, beyond, across)
    for index in range(COARSE - 2, -1, -1):
        level, next_level = levels[index], levels[index + 1]
        sides = [next_level.along(correction, 2 * level.step), next_level.along(correction, -2 * level.step)]
        here, across = opened(index, correction)
        beyond = [opened_sides(level, buffer, side) for side in sides]
        correction = level.corrected(here, beyond, across)
    return correction


def opened_sides(level, buffer, value):
    rows = level.shape[0]
    if value.shape[0] == rows:
        return value
    for begin in range(2):
        write(buffer, 2, pl.ds(begin, rows // 2, stride=2), value)
    return read(buffer, 2, slice(0, rows))


def up_kernel(size_x, size_y, gathered, state0, state1, state2, state3, out, *refs):
    grid, buffer, whole, window, swept3, corr1, corr2, corr3, merged0, merged1, merged2 = refs
    index_x, index_y = lax.axis_index("gx"), lax.axis_index("gy")
    rows_total, cols_total = CELLS * size_x, CELLS * size_y
    width = 2 * cols_total
    columns = width // LANES
    per_column = LANES // CELLS
    lane, sub = iota(1), iota(0)

    tall = iota(1, (size_x, LANES)) // CELLS
    modulus = min(size_y, per_column)
    for column in range(columns):
        comp = column // (columns // 2) if columns > 1 else 0
        first = (column % (columns // 2)) * per_column if columns > 1 else 0
        for slot, kind in ((2, 3), (1, 1), (0, 0)):
            chunks = [
                gathered[pl.ds(CHUNK * (first + j) + kind, size_x, stride=CHUNK * size_y), :]
                for j in range(modulus)
            ]
            for r in range(CELLS):
                turn = r + CELLS * comp
                value = chunks[0]
                for j in range(1, modulus):
                    value = jnp.where(((tall - turn) & (modulus - 1)) == j, chunks[j], value)
                grid[slot, column, pl.ds(r, size_x, stride=CELLS), :] = lane_roll(
                    value, -CELLS * turn
                )

    def ring_row(dx, dy):
        i = jnp.clip(index_x + dx, 0, size_x - 1)
        j = jnp.clip(index_y + dy, 0, size_y - 1)
        return jnp.broadcast_to(
            gathered[pl.ds(CHUNK * (i * size_y + j) + 2, 1), :], (SUB, LANES)
        )

    start = GUARD + RIM[3]

    def complete_ring():
        beside = {
            (dx, dy): ring_row(dx, dy) for dx in (-1, 0, 1) for dy in (-1, 0, 1) if dx or dy
        }
        for comp in range(2):
            base = comp * HALF
            for p in range(2):
                slot = 2 * comp + p
                end = 7 if p else 0
                corner_lane = LANES - 1 if p else SUB
                dy = -1 if p else 1
                for tile in range(2):
                    at = start + SUB * tile
                    index = base + (48 if p else 32) + SUB * tile + sub
                    ringed = lane_take(beside[0, dy], index)
                    swept = jnp.where(
                        lane == corner_lane,
                        tile_at(state3, ITERATE + slot, at)
                        + tile_at(state3, WEIGHT + p, at) * ringed,
                        tile_at(state3, SWEPT + slot, at),
                    )
                    swept3[slot, at : at + SUB, :] = swept
                for dx, at, edge in ((-1, start - 1, 16), (1, start + 2 * SUB, 0)):
                    index = base + edge + 8 * p
                    ringed = jnp.where(
                        lane == corner_lane,
                        lane_take(beside[dx, dy], jnp.full((SUB, LANES), index + end, jnp.int32)),
                        lane_take(beside[dx, 0], index + (lane & 7)),
                    )
                    rows = slice(at, at + 1)
                    swept3[slot, rows, :] = (
                        state3[ITERATE + slot, rows, :] + state3[WEIGHT + p, rows, :] * ringed[0:1]
                    )

    correction = coarse_solve(grid, buffer, rows_total, cols_total, width, complete_ring)

    whole[GUARD : GUARD + rows_total, :] = correction
    whole[0:GUARD, :] = jnp.zeros((GUARD, width), F32)
    whole[GUARD + rows_total :, :] = jnp.zeros((2 * SUB, width), F32)
    near_rows = whole[pl.ds(pl.multiple_of(CELLS * index_x, SUB), 3 * SUB), :]
    for comp in range(2):
        for kind in range(3):
            shift = (2 * width - cols_total * comp - CELLS * index_y + (0, -1, 1)[kind]) % width
            turned = pltpu.roll(near_rows, shift, 1)
            if columns > 1:
                tall_lane = iota(1, (3 * SUB, LANES))
                turned = jnp.where(
                    tall_lane < HALF, turned[:, :LANES], turned[:, width - LANES :]
                )
            window[3 * comp + kind, 0 : 3 * SUB, :] = turned

    def swept_rows(ref, level, coarse_row, parity, here, beyond, across, comp):
        at = pl.ds(GUARD + RIM[level] + 2 * coarse_row + parity, SUB, stride=2)
        state = (state0, state1, state2, state3)[level]
        return [
            (ref[SWEPT + 2 * comp + p, at, :] + state[CENTRE + p, at, :] * here)
            + (state[SIDE + p, at, :] * beyond[p] + state[ACROSS + p, at, :] * across)
            for p in range(2)
        ]

    for comp in range(2):
        for tile in range(2):
            first = SUB * tile - 1
            at = GUARD + first
            here, right, left = [tile_at(window, 3 * comp + kind, at) for kind in range(3)]
            for parity in range(2):
                across = tile_at(window, 3 * comp, at + (1 if parity else -1))
                found = swept_rows(swept3, 3, first, parity, here, (left, right), across, comp)
                rows = pl.ds(GUARD + RIM[3] + 2 * first + parity, SUB, stride=2)
                for p in range(2):
                    corr3[2 * comp + p, rows, :] = found[p]

    corrs = [None, corr1, corr2, corr3]
    merged = [merged0, merged1, merged2]
    near = ((((lane + 32) & (LANES - 1)) - 32) >> 1) & (LANES - 1)
    odd_lane = (lane & 1) == 1
    for level in (2, 1, 0):
        coarse = level + 1
        corr, state, whole_rows = corrs[coarse], (state0, state1, state2)[level], merged[level]
        count = (LANES >> coarse) + 2
        origin = GUARD + RIM[coarse]
        sides = {}
        for tile in range(-(-count // SUB)):
            at = origin - 1 + SUB * tile
            for comp in range(2):
                even, odd = tile_at(corr, 2 * comp, at), tile_at(corr, 2 * comp + 1, at)
                even_here, odd_here = lane_take(even, near), lane_take(odd, near)
                even_next = lane_take(even, (near + 1) & (LANES - 1))
                odd_last = lane_take(odd, (near - 1) & (LANES - 1))
                here = jnp.where(odd_lane, odd_here, even_here)
                whole_rows[3 * comp, at : at + SUB, :] = here
                whole_rows[3 * comp + 1, at : at + SUB, :] = jnp.where(
                    odd_lane, even_next, odd_here
                )
                whole_rows[3 * comp + 2, at : at + SUB, :] = jnp.where(
                    odd_lane, even_here, odd_last
                )
        if level > 0:
            first, tiles = -1, -(-count // SUB)
        else:
            first, tiles = 0, (count - 2) // SUB
        for tile in range(tiles):
            coarse_row = first + SUB * tile
            at = origin + coarse_row
            for comp in range(2):
                here, right, left = [tile_at(whole_rows, 3 * comp + k, at) for k in range(3)]
                for parity in range(2):
                    across = tile_at(whole_rows, 3 * comp, at + (1 if parity else -1))
                    found = swept_rows(
                        state, level, coarse_row, parity, here, (left, right), across, comp
                    )
                    if level > 0:
                        rows = pl.ds(GUARD + RIM[level] + 2 * coarse_row + parity, SUB, stride=2)
                        for p in range(2):
                            corrs[level][2 * comp + p, rows, :] = found[p]
                    else:
                        rows = pl.ds(2 * coarse_row + parity, SUB, stride=2)
                        out[comp, rows, :] = jnp.where(
                            odd_lane,
                            lane_take(found[1], lane >> 1),
                            lane_take(found[0], lane >> 1),
                        )


def params():
    return pltpu.CompilerParams(vmem_limit_bytes=VMEM_LIMIT)


VMEM_SPEC = pl.BlockSpec(memory_space=pltpu.VMEM)
SMEM_SPEC = pl.BlockSpec(memory_space=pltpu.SMEM)
HBM_SPEC = pl.BlockSpec(memory_space=pltpu.HBM)


def swap_routes(size_x, size_y):
    def index(i, j):
        return i * size_y + j

    routes = []
    for axis in range(2):
        size = (size_x, size_y)[axis]
        for offset in range(2):
            route = []
            for i in range(size_x):
                for j in range(size_y):
                    here = (i, j)[axis]
                    other = here + 1 if here % 2 == offset else here - 1
                    if 0 <= other < size:
                        peer = (other, j) if axis == 0 else (i, other)
                    else:
                        peer = (i, j ^ 1) if axis == 0 else (i ^ 1, j)
                    route.append((index(i, j), index(*peer)))
            routes.append(route)
    return routes


def per_device(size_x, size_y, right_side, shift_coef, viscosity, wet_tiles):
    axes = ("gx", "gy")
    devices = size_x * size_y
    routes = swap_routes(size_x, size_y)
    band = jax.ShapeDtypeStruct((4 * HALO, LANES), F32)
    held_shape = pltpu.VMEM((4, HELD[0], LANES), F32)
    held, first, second = pl.pallas_call(
        bands_kernel,
        out_shape=(held_shape, band, band),
        in_specs=[SMEM_SPEC] + [HBM_SPEC] * 3,
        out_specs=(VMEM_SPEC,) * 3,
        scratch_shapes=[pltpu.SemaphoreType.DMA((4,))],
        compiler_params=params(),
        name="bands",
    )(
        wet_tiles,
        *[
            pltpu.with_memory_space_constraint(array, pltpu.HBM)
            for array in (right_side, shift_coef, viscosity)
        ],
    )
    second = lax.ppermute(second, axes, routes[1])
    first = lax.ppermute(first, axes, routes[0])
    strip = jax.ShapeDtypeStruct((MESSAGE, LANES), F32)
    got = (first, second)
    first, second = pl.pallas_call(
        functools.partial(strips_kernel, size_x),
        out_shape=(strip, strip),
        in_specs=[SMEM_SPEC] + [VMEM_SPEC] * 3,
        out_specs=(VMEM_SPEC,) * 2,
        compiler_params=params(),
        name="strips",
    )(wet_tiles, held, *got)
    fields = pl.pallas_call(
        functools.partial(halves_kernel, size_x),
        out_shape=pltpu.VMEM((8, HELD[0], LANES), F32),
        in_specs=[SMEM_SPEC] + [VMEM_SPEC] * 3,
        out_specs=VMEM_SPEC,
        cost_estimate=pl.CostEstimate(flops=1 << 20, bytes_accessed=1 << 21, transcendentals=0),
        compiler_params=params(),
        name="halves",
    )(wet_tiles, held, *got)
    second = lax.ppermute(second, axes, routes[3])
    first = lax.ppermute(first, axes, routes[2])

    def buffers(counts):
        return [pltpu.VMEM((n, HELD[level], LANES), F32) for level, n in enumerate(counts)]

    chunks, *states = pl.pallas_call(
        functools.partial(down_kernel, size_y, devices),
        out_shape=(jax.ShapeDtypeStruct((CHUNK * devices, LANES), F32),)
        + tuple(buffers([STATE, STATE, STATE, STATE + 6])),
        in_specs=[VMEM_SPEC] * 3,
        out_specs=(VMEM_SPEC,) * (1 + LOCAL),
        scratch_shapes=buffers([2, 4, 4, 4])
        + buffers([2] * 4)
        + buffers([4, 8, 8, 8])
        + buffers([2, 4, 4, 4])
        + buffers([4] * 4)
        + buffers([4] * 4)
        + [pltpu.VMEM((2, HELD[0], LANES), F32), pltpu.VMEM((4, HELD[3], LANES), F32)],
        compiler_params=params(),
        name="down",
    )(second, first, fields)
    gathered = lax.all_to_all(chunks, axes, 0, 0, tiled=True)
    rows_total = CELLS * size_x
    width = 2 * CELLS * size_y
    return pl.pallas_call(
        functools.partial(up_kernel, size_x, size_y),
        out_shape=jax.ShapeDtypeStruct((2, LANES, LANES), F32),
        in_specs=[VMEM_SPEC] * (1 + LOCAL),
        out_specs=VMEM_SPEC,
        scratch_shapes=[
            pltpu.VMEM((3, width // LANES, rows_total, LANES), F32),
            pltpu.VMEM((3, width // LANES, rows_total + 3 * SUB, LANES), F32),
            pltpu.VMEM((rows_total + 3 * SUB, width), F32),
            pltpu.VMEM((6, 5 * SUB, LANES), F32),
            pltpu.VMEM((4, HELD[3], LANES), F32),
        ]
        + [pltpu.VMEM((4, HELD[level], LANES), F32) for level in (1, 2, 3)]
        + [pltpu.VMEM((6, HELD[level + 1], LANES), F32) for level in (0, 1, 2)],
        compiler_params=params(),
        name="up",
    )(gathered, *states)


def solution(mesh):
    sizes = dict(mesh.shape)
    placed = (P(None, "gx", "gy"), P("gx", "gy"), P("gx", "gy"), P("gx", "gy"))
    return jax.shard_map(
        functools.partial(per_device, sizes["gx"], sizes["gy"]),
        mesh=mesh,
        in_specs=placed,
        out_specs=P(None, "gx", "gy"),
        check_vma=False,
    )
```

```python
import functools

import jax
import jax.numpy as jnp
from jax import lax
from jax.experimental import pallas as pl
from jax.experimental.pallas import tpu as pltpu
from jax.sharding import PartitionSpec as P

LOCAL = 4
COARSE = 4
COARSE_SWEEPS = 8
OMEGA = 0.8
KEEP = 1.0 - OMEGA

LANES = 128
HALF = LANES // 2
SUB = 8
HALO = 16
GUARD = 8
CELLS = LANES >> LOCAL
ROWS = [(LANES + 2 * HALO) >> level for level in range(LOCAL)]
TILES = [-(-rows // SUB) for rows in ROWS]
HELD = [GUARD + SUB * tiles + 16 for tiles in TILES]
RIM = [HALO >> level for level in range(LOCAL)]
TOP = GUARD + HALO
LOW = TOP + LANES
HALF_TILES = TILES[0] // 2
MESSAGE = ROWS[0] // 2
CHUNK = 4
F32 = jnp.float32
VMEM_LIMIT = 48 * 1024 * 1024

SWEPT, CENTRE, SIDE, ACROSS = 0, 4, 6, 8
STATE = 10
ITERATE, WEIGHT = 10, 14


def iota(dim, shape=(SUB, LANES)):
    return lax.broadcasted_iota(jnp.int32, shape, dim)


def lane_take(tile, index):
    return jnp.take_along_axis(tile, index, axis=1)


def lane_roll(tile, shift):
    return pltpu.roll(tile, shift % LANES, 1)


def tile_at(ref, slot, row):
    return ref[slot, row : row + SUB, :]


def bands_kernel(wet, right_side, shift_coef, viscosity, held, first, second, sems):
    odd = lax.axis_index("gx") % 2
    wetness = wet[0, 0].astype(F32)
    own = pl.ds(TOP, LANES)
    sources = (right_side.at[0], right_side.at[1], shift_coef, viscosity)
    copies = [
        pltpu.make_async_copy(sources[field], held.at[field, own, :], sems.at[field])
        for field in range(4)
    ]
    for copy in copies:
        copy.start()
    bottom = LANES - HALO
    starts = (TOP + bottom - bottom * odd, TOP + bottom * odd)
    for field in range(4):
        copies[field].wait()
        for start, out in zip(starts, (first, second)):
            value = held[field, pl.ds(pl.multiple_of(start, SUB), HALO), :]
            out[field * HALO : (field + 1) * HALO, :] = value if field == 2 else value * wetness


def rim_place(half, lane):
    to_left = ((lane >> 3) & 1) == half
    q = jnp.where(to_left, lane, (lane - (56 + 8 * half)) & (LANES - 1)) >> 4
    cell = 2 * (lane & 7) + (q & 1) + jnp.where(to_left, 0, LANES - HALO)
    return to_left, q >> 1, cell


def strips_kernel(size_x, wet, got_second, got_first, held, first, second):
    index_x = lax.axis_index("gx")
    odd_x = index_x % 2 == 1
    odd_y = lax.axis_index("gy") % 2 == 1
    wetness = wet[0, 0].astype(F32)
    above = (index_x > 0).astype(F32)
    below = (index_x < size_x - 1).astype(F32)
    lane = iota(1)
    rim_tiles = HALO // SUB

    def piece(field, tile):
        if rim_tiles <= tile < TILES[0] - rim_tiles:
            row = GUARD + SUB * tile
            return held[field, row : row + SUB, :]
        top = tile < rim_tiles
        row = field * HALO + SUB * (tile if top else tile - (TILES[0] - rim_tiles))
        one, two = got_first[row : row + SUB, :], got_second[row : row + SUB, :]
        return jnp.where(odd_x, one, two) if top else jnp.where(odd_x, two, one)

    places = [rim_place(half, lane) for half in range(2)]
    for tile in range(HALF_TILES):
        found = []
        for half in range(2):
            to_left, owner, cell = places[half]
            at = tile + half * HALF_TILES
            value = None
            for field in range(4):
                part = lane_take(piece(field, at), cell)
                value = part if value is None else jnp.where(owner == field, part, value)
            if rim_tiles <= at < TILES[0] - rim_tiles:
                value = value * jnp.where(owner == 2, 1.0, wetness)
            else:
                value = value * jnp.where(owner == 3, above if at < rim_tiles else below, 1.0)
            found.append(value)
        left = jnp.where(places[0][0], found[0], found[1])
        right = jnp.where(places[0][0], found[1], found[0])
        rows = slice(SUB * tile, SUB * tile + SUB)
        first[rows, :] = jnp.where(odd_y, left, right)
        second[rows, :] = jnp.where(odd_y, right, left)


def halves_kernel(size_x, wet, got_second, got_first, held, fields):
    index_x = lax.axis_index("gx")
    odd_x = index_x % 2 == 1
    wetness = wet[0, 0].astype(F32)
    above = (index_x > 0).astype(F32)
    below = (index_x < size_x - 1).astype(F32)
    lane = iota(1)
    rim_tiles = HALO // SUB
    for tile in range(TILES[0]):
        row = GUARD + SUB * tile
        for field in range(4):
            if rim_tiles <= tile < TILES[0] - rim_tiles:
                value = held[field, row : row + SUB, :]
                if field != 2:
                    value = value * wetness
            else:
                top = tile < rim_tiles
                at = field * HALO + SUB * (tile if top else tile - (TILES[0] - rim_tiles))
                one, two = got_first[at : at + SUB, :], got_second[at : at + SUB, :]
                value = jnp.where(odd_x, one, two) if top else jnp.where(odd_x, two, one)
                if field == 3:
                    value = value * (above if top else below)
            for parity in range(2):
                fields[2 * field + parity, row : row + SUB, :] = lane_take(
                    value, (2 * lane + parity) & (LANES - 1)
                )


def down_kernel(size_y, devices, got_second, got_first, held, chunks, *refs):
    states, refs = refs[:LOCAL], refs[LOCAL:]
    viscous, refs = refs[:LOCAL], refs[LOCAL:]
    reactions, refs = refs[:LOCAL], refs[LOCAL:]
    sources, refs = refs[:LOCAL], refs[LOCAL:]
    weights, refs = refs[:LOCAL], refs[LOCAL:]
    iterates, refs = refs[:LOCAL], refs[LOCAL:]
    sums, (outers, ring) = refs[:LOCAL], refs[LOCAL:]
    index_y = lax.axis_index("gy")
    odd_y = index_y % 2 == 1
    lane, sub = iota(1), iota(0)
    side_ok = jnp.where(
        lane < 96, (index_y < size_y - 1).astype(F32), (index_y > 0).astype(F32)
    )
    odd_row = (sub & 1) == 1
    inner = lane < HALF
    even_block = ((lane >> 3) & 1) == 0

    def tiles(level):
        return [GUARD + SUB * tile for tile in range(TILES[level])]

    def put(ref, slot, row, value):
        ref[slot, row : row + SUB, :] = value

    def rims(row, slots):
        half, at = divmod((row - GUARD) // SUB, HALF_TILES)
        one, two = (r[SUB * at : SUB * at + SUB, :] for r in (got_first, got_second))
        after, before = jnp.where(odd_y, two, one), jnp.where(odd_y, one, two)
        if half == 0:
            both = jnp.where(even_block, after, before)
        else:
            both = jnp.where(even_block, before, after)
        values = []
        for slot in slots:
            rim = lane_roll(both, HALF - 16 * slot - 8 * half)
            if slot >= 4:
                rim = jnp.where(side_ok > 0, rim, 1.0 if slot < 6 else 0.0)
            values.append(jnp.where(inner, tile_at(held, slot, row), rim))
        return values

    def paired(ref, slot, start):
        return (
            ref[slot, pl.ds(start, SUB, stride=2), :] + ref[slot, pl.ds(start + 1, SUB, stride=2), :]
        )

    takes = [(2 * lane + offset) & (LANES - 1) for offset in (0, 1, -1, 2)]

    def coefficients(level):
        for row in tiles(level):
            if level == 0:
                values = rims(row, (4, 5, 6, 7))
                reaction, viscosity = values[:2], values[2:]
            else:
                start = GUARD + 2 * (row - GUARD)
                ref = sums[level - 1]
                value = 0.0625 * paired(ref, 3, start)
                viscosity = [lane_take(value, t) for t in takes]
                value = 0.25 * paired(ref, 2, start)
                reaction = [lane_take(value, t) for t in takes[:2]]
            for slot, value in enumerate(viscosity):
                put(viscous[level], slot, row, value)
            for slot, value in enumerate(reaction):
                put(reactions[level], slot, row, value)
            put(sums[level], 2, row, reaction[0] + reaction[1])
            put(sums[level], 3, row, viscosity[0] + viscosity[1])

    def faces(level, row):
        here = [tile_at(viscous[level], p, row) for p in range(2)]
        north = [jnp.minimum(here[p], tile_at(viscous[level], p, row - 1)) for p in range(2)]
        south = [jnp.minimum(here[p], tile_at(viscous[level], p, row + 1)) for p in range(2)]
        return here, jnp.minimum(here[0], here[1]), north, south

    def outside(level, row, here):
        if level == 0:
            beyond = [lane_roll(here[1], 1), lane_roll(here[0], -1)]
        else:
            beyond = [tile_at(viscous[level], 2 + p, row) for p in range(2)]
        return [jnp.minimum(h, b) for h, b in zip(here, beyond)]

    def weigh(level):
        for row in tiles(level):
            here, middle, north, south = faces(level, row)
            outer = outside(level, row, here)
            found = []
            for p in range(2):
                diagonal = tile_at(reactions[level], p, row) + (
                    (middle + outer[p]) + (north[p] + south[p])
                )
                found.append(OMEGA / diagonal)
                if level == 0:
                    put(outers, p, row, outer[p])
            if level > 0:
                found += [lane_roll(found[1], 1), lane_roll(found[0], -1)]
            for slot, value in enumerate(found):
                put(weights[level], slot, row, value)

    def take_sources(level):
        for row in tiles(level):
            if level == 0:
                found = rims(row, (0, 1, 2, 3))
            else:
                start = GUARD + 2 * (row - GUARD)
                values = [0.25 * paired(sums[level - 1], comp, start) for comp in range(2)]
                found = [lane_take(value, t) for value in values for t in takes]
            for slot, value in enumerate(found):
                put(sources[level], slot, row, value)

    def kinds(level):
        return 2 if level == 0 else 4

    def first_sweep(level):
        for row in tiles(level):
            for comp in range(2):
                for p in range(2):
                    put(
                        iterates[level],
                        2 * comp + p,
                        row,
                        tile_at(weights[level], p, row)
                        * tile_at(sources[level], kinds(level) * comp + p, row),
                    )

    def residual(level):
        state, iterate, weight, source = (
            states[level],
            iterates[level],
            weights[level],
            sources[level],
        )
        for row in tiles(level):
            _, middle, north, south = faces(level, row)
            if level == 0:
                outer = [tile_at(outers, p, row) for p in range(2)]
            else:
                outer = outside(level, row, [tile_at(viscous[level], p, row) for p in range(2)])
            scale = [tile_at(weight, p, row) for p in range(2)]
            kept = level > 0 or TOP <= row < LOW
            for comp in range(2):
                here = [tile_at(iterate, 2 * comp + p, row) for p in range(2)]
                if level == 0:
                    beyond = [lane_roll(here[1], 1), lane_roll(here[0], -1)]
                else:
                    beyond = [
                        tile_at(weight, 2 + p, row) * tile_at(source, 4 * comp + 2 + p, row)
                        for p in range(2)
                    ]
                total = None
                for p in range(2):
                    slot = 2 * comp + p
                    around = middle * here[1 - p] + outer[p] * beyond[p]
                    around = around + (
                        south[p] * tile_at(iterate, slot, row + 1)
                        + north[p] * tile_at(iterate, slot, row - 1)
                    )
                    left = KEEP * tile_at(source, kinds(level) * comp + p, row) + around
                    if kept:
                        put(state, SWEPT + slot, row, here[p] + scale[p] * left)
                    if level == LOCAL - 1:
                        put(ring, slot, row, left)
                        put(state, ITERATE + slot, row, here[p])
                    total = left if total is None else total + left
                put(sums[level], comp, row, total)
            if kept:
                for p in range(2):
                    within = jnp.where(odd_row, north[p], south[p])
                    across = jnp.where(odd_row, south[p], north[p])
                    put(state, CENTRE + p, row, KEEP + scale[p] * (middle + within))
                    put(state, SIDE + p, row, scale[p] * outer[p])
                    put(state, ACROSS + p, row, scale[p] * across)
                    if level == LOCAL - 1:
                        put(state, WEIGHT + p, row, scale[p])

    coefficients(0)
    take_sources(0)
    weigh(0)
    coefficients(1)
    first_sweep(0)
    residual(0)
    weigh(1)
    coefficients(2)
    take_sources(1)
    weigh(2)
    coefficients(3)
    first_sweep(1)
    residual(1)
    take_sources(2)
    weigh(3)
    first_sweep(2)
    residual(2)
    take_sources(3)
    first_sweep(3)
    residual(3)

    start = GUARD + RIM[LOCAL - 1]
    column = lane & (SUB - 1)
    own = [
        lane_take(scale * paired(sums[LOCAL - 1], slot, start), column)
        for slot, scale in enumerate((0.25, 0.25, 0.25, 0.0625))
    ]
    turned = ((lane >> 3) - index_y) & 15
    chosen = (turned & (SUB - 1)) == sub

    def packed(value):
        return jnp.sum(value, axis=0, keepdims=True)

    def joined(a, b):
        return packed(jnp.where(chosen, jnp.where(turned < SUB, a, b), 0.0))

    edge = (lane >> 4) & 3
    place = lane & 15

    rims = jnp.zeros((SUB, LANES), F32)
    for p in range(2):
        index = jnp.where(edge < 2, column, 0 if p == 0 else SUB - 1)
        for part in range(2):
            along = (edge == part) & ((place >> 3) == p) & (sub == (0 if part == 0 else SUB - 1))
            up = (edge == 2 + p) & (place == sub + SUB * part)
            row = start + SUB * part
            value = jnp.where(
                inner,
                lane_take(tile_at(ring, p, row), index),
                lane_take(tile_at(ring, 2 + p, row), index),
            )
            rims = jnp.where(along | up, value, rims)
    kind = sub % CHUNK
    parts = [joined(own[0], own[1]), joined(own[2], own[2]), packed(rims), joined(own[3], own[3])]
    tile = jnp.where(
        kind < 2,
        jnp.where(kind == 0, parts[0], parts[1]),
        jnp.where(kind == 2, parts[2], parts[3]),
    )
    for block in range(CHUNK * devices // SUB):
        chunks[SUB * block : SUB * block + SUB, :] = tile


def write(buffer, slot, rows, value):
    for column in range(buffer.shape[1]):
        buffer[slot, column, rows, :] = value[:, LANES * column : LANES * column + LANES]


def read(buffer, slot, rows):
    parts = [buffer[slot, column, rows, :] for column in range(buffer.shape[1])]
    return parts[0] if len(parts) == 1 else jnp.concatenate(parts, 1)


class Coarse:
    def __init__(self, step, row_step, rows, cols_total, width):
        self.step, self.row_step = step, row_step
        self.shape = (rows, width)
        lane, row = iota(1, self.shape), iota(0, self.shape)
        column = lane & (cols_total - 1)
        self.odd_lane, self.odd_row = (lane & step) != 0, (row & row_step) != 0
        self.leftmost = column < 2 * step
        self.rightmost = column >= cols_total - 2 * step
        self.top, self.bottom = row < row_step, row >= rows - row_step

    def along(self, value, amount):
        return pltpu.roll(value, amount % self.shape[1], 1)

    def down(self, value, amount):
        return pltpu.roll(value, amount % self.shape[0], 0)

    def paired(self, value):
        return (
            jnp.where(self.odd_lane, self.along(value, self.step), value),
            jnp.where(self.odd_lane, value, self.along(value, -self.step)),
        )

    def outside(self, value):
        return (
            jnp.where(
                self.odd_lane, self.along(value, 2 * self.step), self.along(value, self.step)
            ),
            jnp.where(
                self.odd_lane, self.along(value, -self.step), self.along(value, -2 * self.step)
            ),
        )

    def coefficients(self, viscous, reaction):
        here, reactions, beyond = self.paired(viscous), self.paired(reaction), self.outside(viscous)
        self.middle = jnp.minimum(here[0], here[1])
        self.outer = [
            jnp.minimum(here[0], jnp.where(self.leftmost, 0.0, beyond[0])),
            jnp.minimum(here[1], jnp.where(self.rightmost, 0.0, beyond[1])),
        ]
        self.north, self.south, self.weights = [], [], []
        for p in range(2):
            above = jnp.where(self.top, 0.0, self.down(here[p], self.row_step))
            below = jnp.where(self.bottom, 0.0, self.down(here[p], -self.row_step))
            self.north.append(jnp.minimum(here[p], above))
            self.south.append(jnp.minimum(here[p], below))
            diagonal = reactions[p] + (
                (self.middle + self.outer[p]) + (self.north[p] + self.south[p])
            )
            self.weights.append(OMEGA / diagonal)
        return here[0] + here[1], reactions[0] + reactions[1]

    def weigh(self):
        self.weights_beyond = (
            self.along(self.weights[1], 2 * self.step),
            self.along(self.weights[0], -2 * self.step),
        )

    def take(self, source):
        self.values, self.values_beyond = self.paired(source), self.outside(source)

    def residual(self):
        x = [w * s for w, s in zip(self.weights, self.values)]
        x_beyond = [w * s for w, s in zip(self.weights_beyond, self.values_beyond)]
        total, self.swept = None, []
        for p in range(2):
            around = self.middle * x[1 - p] + self.outer[p] * x_beyond[p]
            around = around + (
                self.south[p] * self.down(x[p], -self.row_step)
                + self.north[p] * self.down(x[p], self.row_step)
            )
            left = KEEP * self.values[p] + around
            self.swept.append(x[p] + self.weights[p] * left)
            total = left if total is None else total + left
        return total

    def corrected(self, here, beyond, across):
        parts = []
        for p in range(2):
            within = jnp.where(self.odd_row, self.north[p], self.south[p])
            out = jnp.where(self.odd_row, self.south[p], self.north[p])
            weight = self.weights[p]
            centre = KEEP + weight * (self.middle + within)
            parts.append(
                (self.swept[p] + centre * here)
                + ((weight * self.outer[p]) * beyond[p] + (weight * out) * across)
            )
        return jnp.where(self.odd_lane, parts[1], parts[0])


def coarse_solve(grid, buffer, rows_total, cols_total, width, meanwhile):
    columns = width // LANES

    def whole(slot):
        return jnp.concatenate([grid[slot, c] for c in range(columns)], 1) if columns > 1 else grid[slot, 0]

    levels, rows, row_step = [], rows_total, 1
    for index in range(COARSE + 1):
        levels.append(Coarse(1 << index, row_step, rows, cols_total, width))
        if rows > SUB:
            rows //= 2
        else:
            row_step *= 2

    def folded(index, value, slot, scale):
        level = levels[index]
        rows = level.shape[0]
        if levels[index + 1].shape[0] == rows:
            other = jnp.where(
                level.odd_row, level.down(value, level.row_step), level.down(value, -level.row_step)
            )
            return scale * (value + other)
        write(buffer, slot, slice(0, rows), value)
        first, second = [pl.ds(begin, rows // 2, stride=2) for begin in range(2)]
        return scale * (read(buffer, slot, first) + read(buffer, slot, second))

    def opened(index, value):
        level = levels[index]
        rows = level.shape[0]
        if value.shape[0] == rows:
            return value, jnp.where(
                level.odd_row, level.down(value, -level.row_step), level.down(value, level.row_step)
            )
        half = rows // 2
        blank = jnp.zeros((SUB, width), F32)
        for begin in range(2):
            write(buffer, 0, pl.ds(begin, half, stride=2), value)
        write(buffer, 1, slice(SUB, 2 * SUB), blank)
        write(buffer, 1, slice(rows, rows + SUB), blank)
        for begin in (SUB + 2, SUB - 1):
            write(buffer, 1, pl.ds(begin, half, stride=2), value)
        return read(buffer, 0, slice(0, rows)), read(buffer, 1, slice(SUB, SUB + rows))

    viscous, reaction, source = [None] * 5, [None] * 5, [None] * 5
    viscous[0], reaction[0], source[0] = whole(2), whole(1), whole(0)

    def coefficients(index):
        pair, reactions = levels[index].coefficients(viscous[index], reaction[index])
        viscous[index + 1] = folded(index, pair, 0, 0.0625)
        reaction[index + 1] = folded(index, reactions, 1, 0.25)

    def residual(index):
        source[index + 1] = folded(index, levels[index].residual(), 2, 0.25)

    last = levels[COARSE]
    block = 1 << COARSE
    cols_left = cols_total // block
    rows_left = last.shape[0]
    lane = iota(1, (rows_left, LANES))
    groups = 1 if cols_total < LANES else 2
    per_group = columns // groups

    def spread(value):
        found = []
        for group in range(groups):
            for j in range(cols_left):
                column, place = divmod(block * j, LANES)
                column += group * per_group
                if groups == 1:
                    place = place + (lane & (LANES - cols_total))
                else:
                    place = jnp.full((rows_left, LANES), place, jnp.int32)
                found.append(lane_take(value[:, LANES * column : LANES * column + LANES], place))
        return found

    def flat(values, group, j):
        return values[group * cols_left + j]

    levels[0].take(source[0])
    coefficients(0)
    coefficients(1)
    levels[0].weigh()
    coefficients(2)
    levels[1].weigh()
    residual(0)
    levels[1].take(source[1])
    coefficients(3)
    levels[2].weigh()
    residual(1)
    levels[2].take(source[2])
    meanwhile()
    levels[3].weigh()
    viscous_columns, reaction_columns = spread(viscous[4]), spread(reaction[4])
    residual(2)
    levels[3].take(source[3])

    top, bottom = last.top[:, :LANES], last.bottom[:, :LANES]
    pulls, weights = [], []
    for group in range(groups):
        for j in range(cols_left):
            here = flat(viscous_columns, group, j)
            above = jnp.where(top, 0.0, last.down(here, last.row_step))
            below = jnp.where(bottom, 0.0, last.down(here, -last.row_step))
            links = [jnp.minimum(here, above), jnp.minimum(here, below)]
            links += [
                jnp.minimum(here, flat(viscous_columns, group, other))
                for other in (j - 1, j + 1)
                if 0 <= other < cols_left
            ]
            weight = OMEGA / (flat(reaction_columns, group, j) + sum(links))
            weights.append(weight)
            pulls.append([weight * link for link in links])
    residual(3)
    pushed = [w * s for w, s in zip(weights, spread(source[4]))]
    values = pushed
    for _ in range(COARSE_SWEEPS - 1):
        following = []
        for group in range(groups):
            for j in range(cols_left):
                at = group * cols_left + j
                here, pull = values[at], pulls[at]
                total = (KEEP * here + pushed[at]) + (
                    pull[0] * last.down(here, last.row_step)
                    + pull[1] * last.down(here, -last.row_step)
                )
                sides = [other for other in (j - 1, j + 1) if 0 <= other < cols_left]
                for link, other in zip(pull[2:], sides):
                    total = total + link * flat(values, group, other)
                following.append(total)
        values = following

    def laid(shift):
        found = []
        for column in range(columns):
            group = column // per_group
            place = ((lane & (cols_total - 1)) if groups == 1 else lane) // block
            place = place + (column % per_group) * (LANES // block)
            value = jnp.zeros((rows_left, LANES), F32)
            for j in range(cols_left):
                value = jnp.where(place == j + shift, flat(values, group, j), value)
            found.append(value)
        return found[0] if columns == 1 else jnp.concatenate(found, 1)

    index = COARSE - 1
    here, across = opened(index, laid(0))
    beyond = [opened(index, laid(shift))[0] for shift in (1, -1)]
    correction = levels[index].corrected(here, beyond, across)
    for index in range(COARSE - 2, -1, -1):
        level, next_level = levels[index], levels[index + 1]
        sides = [next_level.along(correction, 2 * level.step), next_level.along(correction, -2 * level.step)]
        here, across = opened(index, correction)
        beyond = [opened_sides(level, buffer, side) for side in sides]
        correction = level.corrected(here, beyond, across)
    return correction


def opened_sides(level, buffer, value):
    rows = level.shape[0]
    if value.shape[0] == rows:
        return value
    for begin in range(2):
        write(buffer, 2, pl.ds(begin, rows // 2, stride=2), value)
    return read(buffer, 2, slice(0, rows))


def up_kernel(size_x, size_y, gathered, state0, state1, state2, state3, out, *refs):
    grid, buffer, whole, window, swept3, corr1, corr2, corr3, merged0, merged1, merged2 = refs
    index_x, index_y = lax.axis_index("gx"), lax.axis_index("gy")
    rows_total, cols_total = CELLS * size_x, CELLS * size_y
    width = 2 * cols_total
    columns = width // LANES
    per_column = LANES // CELLS
    lane, sub = iota(1), iota(0)

    tall = iota(1, (size_x, LANES)) // CELLS
    modulus = min(size_y, per_column)
    for column in range(columns):
        comp = column // (columns // 2) if columns > 1 else 0
        first = (column % (columns // 2)) * per_column if columns > 1 else 0
        for slot, kind in ((2, 3), (1, 1), (0, 0)):
            chunks = [
                gathered[pl.ds(CHUNK * (first + j) + kind, size_x, stride=CHUNK * size_y), :]
                for j in range(modulus)
            ]
            for r in range(CELLS):
                turn = r + CELLS * comp
                value = chunks[0]
                for j in range(1, modulus):
                    value = jnp.where(((tall - turn) & (modulus - 1)) == j, chunks[j], value)
                grid[slot, column, pl.ds(r, size_x, stride=CELLS), :] = lane_roll(
                    value, -CELLS * turn
                )

    def ring_row(dx, dy):
        i = jnp.clip(index_x + dx, 0, size_x - 1)
        j = jnp.clip(index_y + dy, 0, size_y - 1)
        return jnp.broadcast_to(
            gathered[pl.ds(CHUNK * (i * size_y + j) + 2, 1), :], (SUB, LANES)
        )

    start = GUARD + RIM[3]

    def complete_ring():
        beside = {
            (dx, dy): ring_row(dx, dy) for dx in (-1, 0, 1) for dy in (-1, 0, 1) if dx or dy
        }
        for comp in range(2):
            base = comp * HALF
            for p in range(2):
                slot = 2 * comp + p
                end = 7 if p else 0
                corner_lane = LANES - 1 if p else SUB
                dy = -1 if p else 1
                for tile in range(2):
                    at = start + SUB * tile
                    index = base + (48 if p else 32) + SUB * tile + sub
                    ringed = lane_take(beside[0, dy], index)
                    swept = jnp.where(
                        lane == corner_lane,
                        tile_at(state3, ITERATE + slot, at)
                        + tile_at(state3, WEIGHT + p, at) * ringed,
                        tile_at(state3, SWEPT + slot, at),
                    )
                    swept3[slot, at : at + SUB, :] = swept
                for dx, at, edge in ((-1, start - 1, 16), (1, start + 2 * SUB, 0)):
                    index = base + edge + 8 * p
                    ringed = jnp.where(
                        lane == corner_lane,
                        lane_take(beside[dx, dy], jnp.full((SUB, LANES), index + end, jnp.int32)),
                        lane_take(beside[dx, 0], index + (lane & 7)),
                    )
                    rows = slice(at, at + 1)
                    swept3[slot, rows, :] = (
                        state3[ITERATE + slot, rows, :] + state3[WEIGHT + p, rows, :] * ringed[0:1]
                    )

    correction = coarse_solve(grid, buffer, rows_total, cols_total, width, complete_ring)

    whole[GUARD : GUARD + rows_total, :] = correction
    whole[0:GUARD, :] = jnp.zeros((GUARD, width), F32)
    whole[GUARD + rows_total :, :] = jnp.zeros((2 * SUB, width), F32)
    near_rows = whole[pl.ds(pl.multiple_of(CELLS * index_x, SUB), 3 * SUB), :]
    for comp in range(2):
        for kind in range(3):
            shift = (2 * width - cols_total * comp - CELLS * index_y + (0, -1, 1)[kind]) % width
            turned = pltpu.roll(near_rows, shift, 1)
            if columns > 1:
                tall_lane = iota(1, (3 * SUB, LANES))
                turned = jnp.where(
                    tall_lane < HALF, turned[:, :LANES], turned[:, width - LANES :]
                )
            window[3 * comp + kind, 0 : 3 * SUB, :] = turned

    def swept_rows(ref, level, coarse_row, parity, here, beyond, across, comp):
        at = pl.ds(GUARD + RIM[level] + 2 * coarse_row + parity, SUB, stride=2)
        state = (state0, state1, state2, state3)[level]
        return [
            (ref[SWEPT + 2 * comp + p, at, :] + state[CENTRE + p, at, :] * here)
            + (state[SIDE + p, at, :] * beyond[p] + state[ACROSS + p, at, :] * across)
            for p in range(2)
        ]

    for comp in range(2):
        for tile in range(2):
            first = SUB * tile - 1
            at = GUARD + first
            here, right, left = [tile_at(window, 3 * comp + kind, at) for kind in range(3)]
            for parity in range(2):
                across = tile_at(window, 3 * comp, at + (1 if parity else -1))
                found = swept_rows(swept3, 3, first, parity, here, (left, right), across, comp)
                rows = pl.ds(GUARD + RIM[3] + 2 * first + parity, SUB, stride=2)
                for p in range(2):
                    corr3[2 * comp + p, rows, :] = found[p]

    corrs = [None, corr1, corr2, corr3]
    merged = [merged0, merged1, merged2]
    near = ((((lane + 32) & (LANES - 1)) - 32) >> 1) & (LANES - 1)
    odd_lane = (lane & 1) == 1
    for level in (2, 1, 0):
        coarse = level + 1
        corr, state, whole_rows = corrs[coarse], (state0, state1, state2)[level], merged[level]
        count = (LANES >> coarse) + 2
        origin = GUARD + RIM[coarse]
        sides = {}
        for tile in range(-(-count // SUB)):
            at = origin - 1 + SUB * tile
            for comp in range(2):
                even, odd = tile_at(corr, 2 * comp, at), tile_at(corr, 2 * comp + 1, at)
                even_here, odd_here = lane_take(even, near), lane_take(odd, near)
                even_next = lane_take(even, (near + 1) & (LANES - 1))
                odd_last = lane_take(odd, (near - 1) & (LANES - 1))
                here = jnp.where(odd_lane, odd_here, even_here)
                whole_rows[3 * comp, at : at + SUB, :] = here
                whole_rows[3 * comp + 1, at : at + SUB, :] = jnp.where(
                    odd_lane, even_next, odd_here
                )
                whole_rows[3 * comp + 2, at : at + SUB, :] = jnp.where(
                    odd_lane, even_here, odd_last
                )
        if level > 0:
            first, tiles = -1, -(-count // SUB)
        else:
            first, tiles = 0, (count - 2) // SUB
        for tile in range(tiles):
            coarse_row = first + SUB * tile
            at = origin + coarse_row
            for comp in range(2):
                here, right, left = [tile_at(whole_rows, 3 * comp + k, at) for k in range(3)]
                for parity in range(2):
                    across = tile_at(whole_rows, 3 * comp, at + (1 if parity else -1))
                    found = swept_rows(
                        state, level, coarse_row, parity, here, (left, right), across, comp
                    )
                    if level > 0:
                        rows = pl.ds(GUARD + RIM[level] + 2 * coarse_row + parity, SUB, stride=2)
                        for p in range(2):
                            corrs[level][2 * comp + p, rows, :] = found[p]
                    else:
                        rows = pl.ds(2 * coarse_row + parity, SUB, stride=2)
                        out[comp, rows, :] = jnp.where(
                            odd_lane,
                            lane_take(found[1], lane >> 1),
                            lane_take(found[0], lane >> 1),
                        )


def params():
    return pltpu.CompilerParams(vmem_limit_bytes=VMEM_LIMIT)


VMEM_SPEC = pl.BlockSpec(memory_space=pltpu.VMEM)
SMEM_SPEC = pl.BlockSpec(memory_space=pltpu.SMEM)
HBM_SPEC = pl.BlockSpec(memory_space=pltpu.HBM)


def swap_routes(size_x, size_y):
    def index(i, j):
        return i * size_y + j

    routes = []
    for axis in range(2):
        size = (size_x, size_y)[axis]
        for offset in range(2):
            route = []
            for i in range(size_x):
                for j in range(size_y):
                    here = (i, j)[axis]
                    other = here + 1 if here % 2 == offset else here - 1
                    if 0 <= other < size:
                        peer = (other, j) if axis == 0 else (i, other)
                    else:
                        peer = (i, j ^ 1) if axis == 0 else (i ^ 1, j)
                    route.append((index(i, j), index(*peer)))
            routes.append(route)
    return routes


def per_device(size_x, size_y, right_side, shift_coef, viscosity, wet_tiles):
    axes = ("gx", "gy")
    devices = size_x * size_y
    routes = swap_routes(size_x, size_y)
    band = jax.ShapeDtypeStruct((4 * HALO, LANES), F32)
    held_shape = pltpu.VMEM((4, HELD[0], LANES), F32)
    held, first, second = pl.pallas_call(
        bands_kernel,
        out_shape=(held_shape, band, band),
        in_specs=[SMEM_SPEC] + [HBM_SPEC] * 3,
        out_specs=(VMEM_SPEC,) * 3,
        scratch_shapes=[pltpu.SemaphoreType.DMA((4,))],
        compiler_params=params(),
        name="bands",
    )(
        wet_tiles,
        *[
            pltpu.with_memory_space_constraint(array, pltpu.HBM)
            for array in (right_side, shift_coef, viscosity)
        ],
    )
    second = lax.ppermute(second, axes, routes[1])
    first = lax.ppermute(first, axes, routes[0])
    strip = jax.ShapeDtypeStruct((MESSAGE, LANES), F32)
    got = (second, first)
    first, second = pl.pallas_call(
        functools.partial(strips_kernel, size_x),
        out_shape=(strip, strip),
        in_specs=[SMEM_SPEC] + [VMEM_SPEC] * 3,
        out_specs=(VMEM_SPEC,) * 2,
        compiler_params=params(),
        name="strips",
    )(wet_tiles, *got, held)
    fields = pl.pallas_call(
        functools.partial(halves_kernel, size_x),
        out_shape=pltpu.VMEM((8, HELD[0], LANES), F32),
        in_specs=[SMEM_SPEC] + [VMEM_SPEC] * 3,
        out_specs=VMEM_SPEC,
        cost_estimate=pl.CostEstimate(flops=1 << 20, bytes_accessed=1 << 21, transcendentals=0),
        compiler_params=params(),
        name="halves",
    )(wet_tiles, *got, held)
    second = lax.ppermute(second, axes, routes[3])
    first = lax.ppermute(first, axes, routes[2])

    def buffers(counts):
        return [pltpu.VMEM((n, HELD[level], LANES), F32) for level, n in enumerate(counts)]

    chunks, *states = pl.pallas_call(
        functools.partial(down_kernel, size_y, devices),
        out_shape=(jax.ShapeDtypeStruct((CHUNK * devices, LANES), F32),)
        + tuple(buffers([STATE, STATE, STATE, STATE + 6])),
        in_specs=[VMEM_SPEC] * 3,
        out_specs=(VMEM_SPEC,) * (1 + LOCAL),
        scratch_shapes=buffers([2, 4, 4, 4])
        + buffers([2] * 4)
        + buffers([4, 8, 8, 8])
        + buffers([2, 4, 4, 4])
        + buffers([4] * 4)
        + buffers([4] * 4)
        + [pltpu.VMEM((2, HELD[0], LANES), F32), pltpu.VMEM((4, HELD[3], LANES), F32)],
        compiler_params=params(),
        name="down",
    )(second, first, fields)
    gathered = lax.all_to_all(chunks, axes, 0, 0, tiled=True)
    rows_total = CELLS * size_x
    width = 2 * CELLS * size_y
    return pl.pallas_call(
        functools.partial(up_kernel, size_x, size_y),
        out_shape=jax.ShapeDtypeStruct((2, LANES, LANES), F32),
        in_specs=[VMEM_SPEC] * (1 + LOCAL),
        out_specs=VMEM_SPEC,
        scratch_shapes=[
            pltpu.VMEM((3, width // LANES, rows_total, LANES), F32),
            pltpu.VMEM((3, width // LANES, rows_total + 3 * SUB, LANES), F32),
            pltpu.VMEM((rows_total + 3 * SUB, width), F32),
            pltpu.VMEM((6, 5 * SUB, LANES), F32),
            pltpu.VMEM((4, HELD[3], LANES), F32),
        ]
        + [pltpu.VMEM((4, HELD[level], LANES), F32) for level in (1, 2, 3)]
        + [pltpu.VMEM((6, HELD[level + 1], LANES), F32) for level in (0, 1, 2)],
        compiler_params=params(),
        name="up",
    )(gathered, *states)


def solution(mesh):
    sizes = dict(mesh.shape)
    placed = (P(None, "gx", "gy"), P("gx", "gy"), P("gx", "gy"), P("gx", "gy"))
    return jax.shard_map(
        functools.partial(per_device, sizes["gx"], sizes["gy"]),
        mesh=mesh,
        in_specs=placed,
        out_specs=P(None, "gx", "gy"),
        check_vma=False,
    )
```

```python
import functools

import jax
import jax.numpy as jnp
from jax import lax
from jax.experimental import pallas as pl
from jax.experimental.pallas import tpu as pltpu
from jax.sharding import PartitionSpec as P

LOCAL = 4
COARSE = 4
COARSE_SWEEPS = 8
OMEGA = 0.8
KEEP = 1.0 - OMEGA

LANES = 128
HALF = LANES // 2
SUB = 8
HALO = 16
GUARD = 8
CELLS = LANES >> LOCAL
ROWS = [(LANES + 2 * HALO) >> level for level in range(LOCAL)]
TILES = [-(-rows // SUB) for rows in ROWS]
HELD = [GUARD + SUB * tiles + 16 for tiles in TILES]
RIM = [HALO >> level for level in range(LOCAL)]
TOP = GUARD + HALO
LOW = TOP + LANES
HALF_TILES = TILES[0] // 2
MESSAGE = ROWS[0] // 2
CHUNK = 4
F32 = jnp.float32
VMEM_LIMIT = 48 * 1024 * 1024

SWEPT, CENTRE, SIDE, ACROSS = 0, 4, 6, 8
STATE = 10
ITERATE, WEIGHT = 10, 14


def iota(dim, shape=(SUB, LANES)):
    return lax.broadcasted_iota(jnp.int32, shape, dim)


def lane_take(tile, index):
    return jnp.take_along_axis(tile, index, axis=1)


def lane_roll(tile, shift):
    return pltpu.roll(tile, shift % LANES, 1)


def tile_at(ref, slot, row):
    return ref[slot, row : row + SUB, :]


def bands_kernel(wet, right_side, shift_coef, viscosity, held, first, second, sems):
    odd = lax.axis_index("gx") % 2
    wetness = wet[0, 0].astype(F32)
    own = pl.ds(TOP, LANES)
    sources = (right_side.at[0], right_side.at[1], shift_coef, viscosity)
    copies = [
        pltpu.make_async_copy(sources[field], held.at[field, own, :], sems.at[field])
        for field in range(4)
    ]
    for copy in copies:
        copy.start()
    bottom = LANES - HALO
    starts = (TOP + bottom - bottom * odd, TOP + bottom * odd)
    for field in range(4):
        copies[field].wait()
        for start, out in zip(starts, (first, second)):
            value = held[field, pl.ds(pl.multiple_of(start, SUB), HALO), :]
            out[field * HALO : (field + 1) * HALO, :] = value if field == 2 else value * wetness


def rim_place(half, lane):
    to_left = ((lane >> 3) & 1) == half
    q = jnp.where(to_left, lane, (lane - (56 + 8 * half)) & (LANES - 1)) >> 4
    cell = 2 * (lane & 7) + (q & 1) + jnp.where(to_left, 0, LANES - HALO)
    return to_left, q >> 1, cell


def strips_kernel(size_x, wet, got_second, got_first, held, first, second):
    index_x = lax.axis_index("gx")
    odd_x = index_x % 2 == 1
    odd_y = lax.axis_index("gy") % 2 == 1
    wetness = wet[0, 0].astype(F32)
    above = (index_x > 0).astype(F32)
    below = (index_x < size_x - 1).astype(F32)
    lane = iota(1)
    rim_tiles = HALO // SUB

    def piece(field, tile):
        if rim_tiles <= tile < TILES[0] - rim_tiles:
            row = GUARD + SUB * tile
            return held[field, row : row + SUB, :]
        top = tile < rim_tiles
        row = field * HALO + SUB * (tile if top else tile - (TILES[0] - rim_tiles))
        one, two = got_first[row : row + SUB, :], got_second[row : row + SUB, :]
        return jnp.where(odd_x, one, two) if top else jnp.where(odd_x, two, one)

    places = [rim_place(half, lane) for half in range(2)]
    for tile in range(HALF_TILES):
        found = []
        for half in range(2):
            to_left, owner, cell = places[half]
            at = tile + half * HALF_TILES
            value = None
            for field in range(4):
                part = lane_take(piece(field, at), cell)
                value = part if value is None else jnp.where(owner == field, part, value)
            if rim_tiles <= at < TILES[0] - rim_tiles:
                value = value * jnp.where(owner == 2, 1.0, wetness)
            else:
                value = value * jnp.where(owner == 3, above if at < rim_tiles else below, 1.0)
            found.append(value)
        left = jnp.where(places[0][0], found[0], found[1])
        right = jnp.where(places[0][0], found[1], found[0])
        rows = slice(SUB * tile, SUB * tile + SUB)
        first[rows, :] = jnp.where(odd_y, left, right)
        second[rows, :] = jnp.where(odd_y, right, left)


def halves_kernel(size_x, wet, got_second, got_first, held, fields):
    index_x = lax.axis_index("gx")
    odd_x = index_x % 2 == 1
    wetness = wet[0, 0].astype(F32)
    above = (index_x > 0).astype(F32)
    below = (index_x < size_x - 1).astype(F32)
    lane = iota(1)
    rim_tiles = HALO // SUB
    for tile in range(TILES[0]):
        row = GUARD + SUB * tile
        for field in range(4):
            if rim_tiles <= tile < TILES[0] - rim_tiles:
                value = held[field, row : row + SUB, :]
                if field != 2:
                    value = value * wetness
            else:
                top = tile < rim_tiles
                at = field * HALO + SUB * (tile if top else tile - (TILES[0] - rim_tiles))
                one, two = got_first[at : at + SUB, :], got_second[at : at + SUB, :]
                value = jnp.where(odd_x, one, two) if top else jnp.where(odd_x, two, one)
                if field == 3:
                    value = value * (above if top else below)
            for parity in range(2):
                fields[2 * field + parity, row : row + SUB, :] = lane_take(
                    value, (2 * lane + parity) & (LANES - 1)
                )


def down_kernel(size_y, devices, got_second, got_first, held, chunks, *refs):
    states, refs = refs[:LOCAL], refs[LOCAL:]
    viscous, refs = refs[:LOCAL], refs[LOCAL:]
    reactions, refs = refs[:LOCAL], refs[LOCAL:]
    sources, refs = refs[:LOCAL], refs[LOCAL:]
    weights, refs = refs[:LOCAL], refs[LOCAL:]
    iterates, refs = refs[:LOCAL], refs[LOCAL:]
    sums, (outers, ring) = refs[:LOCAL], refs[LOCAL:]
    index_y = lax.axis_index("gy")
    odd_y = index_y % 2 == 1
    lane, sub = iota(1), iota(0)
    side_ok = jnp.where(
        lane < 96, (index_y < size_y - 1).astype(F32), (index_y > 0).astype(F32)
    )
    odd_row = (sub & 1) == 1
    inner = lane < HALF
    even_block = ((lane >> 3) & 1) == 0

    def tiles(level):
        return [GUARD + SUB * tile for tile in range(TILES[level])]

    def put(ref, slot, row, value):
        ref[slot, row : row + SUB, :] = value

    def rims(row, slots):
        half, at = divmod((row - GUARD) // SUB, HALF_TILES)
        one, two = (r[SUB * at : SUB * at + SUB, :] for r in (got_first, got_second))
        after, before = jnp.where(odd_y, two, one), jnp.where(odd_y, one, two)
        if half == 0:
            both = jnp.where(even_block, after, before)
        else:
            both = jnp.where(even_block, before, after)
        values = []
        for slot in slots:
            rim = lane_roll(both, HALF - 16 * slot - 8 * half)
            if slot >= 4:
                rim = jnp.where(side_ok > 0, rim, 1.0 if slot < 6 else 0.0)
            values.append(jnp.where(inner, tile_at(held, slot, row), rim))
        return values

    def paired(ref, slot, start):
        return (
            ref[slot, pl.ds(start, SUB, stride=2), :] + ref[slot, pl.ds(start + 1, SUB, stride=2), :]
        )

    takes = [(2 * lane + offset) & (LANES - 1) for offset in (0, 1, -1, 2)]

    def coefficients(level):
        for row in tiles(level):
            if level == 0:
                values = rims(row, (4, 5, 6, 7))
                reaction, viscosity = values[:2], values[2:]
            else:
                start = GUARD + 2 * (row - GUARD)
                ref = sums[level - 1]
                value = 0.0625 * paired(ref, 3, start)
                viscosity = [lane_take(value, t) for t in takes]
                value = 0.25 * paired(ref, 2, start)
                reaction = [lane_take(value, t) for t in takes[:2]]
            for slot, value in enumerate(viscosity):
                put(viscous[level], slot, row, value)
            for slot, value in enumerate(reaction):
                put(reactions[level], slot, row, value)
            put(sums[level], 2, row, reaction[0] + reaction[1])
            put(sums[level], 3, row, viscosity[0] + viscosity[1])

    def faces(level, row):
        here = [tile_at(viscous[level], p, row) for p in range(2)]
        north = [jnp.minimum(here[p], tile_at(viscous[level], p, row - 1)) for p in range(2)]
        south = [jnp.minimum(here[p], tile_at(viscous[level], p, row + 1)) for p in range(2)]
        return here, jnp.minimum(here[0], here[1]), north, south

    def outside(level, row, here):
        if level == 0:
            beyond = [lane_roll(here[1], 1), lane_roll(here[0], -1)]
        else:
            beyond = [tile_at(viscous[level], 2 + p, row) for p in range(2)]
        return [jnp.minimum(h, b) for h, b in zip(here, beyond)]

    def weigh(level):
        for row in tiles(level):
            here, middle, north, south = faces(level, row)
            outer = outside(level, row, here)
            found = []
            for p in range(2):
                diagonal = tile_at(reactions[level], p, row) + (
                    (middle + outer[p]) + (north[p] + south[p])
                )
                found.append(OMEGA / diagonal)
                if level == 0:
                    put(outers, p, row, outer[p])
            if level > 0:
                found += [lane_roll(found[1], 1), lane_roll(found[0], -1)]
            for slot, value in enumerate(found):
                put(weights[level], slot, row, value)

    def take_sources(level):
        for row in tiles(level):
            if level == 0:
                found = rims(row, (0, 1, 2, 3))
            else:
                start = GUARD + 2 * (row - GUARD)
                values = [0.25 * paired(sums[level - 1], comp, start) for comp in range(2)]
                found = [lane_take(value, t) for value in values for t in takes]
            for slot, value in enumerate(found):
                put(sources[level], slot, row, value)

    def kinds(level):
        return 2 if level == 0 else 4

    def first_sweep(level):
        for row in tiles(level):
            for comp in range(2):
                for p in range(2):
                    put(
                        iterates[level],
                        2 * comp + p,
                        row,
                        tile_at(weights[level], p, row)
                        * tile_at(sources[level], kinds(level) * comp + p, row),
                    )

    def residual(level):
        state, iterate, weight, source = (
            states[level],
            iterates[level],
            weights[level],
            sources[level],
        )
        for row in tiles(level):
            _, middle, north, south = faces(level, row)
            if level == 0:
                outer = [tile_at(outers, p, row) for p in range(2)]
            else:
                outer = outside(level, row, [tile_at(viscous[level], p, row) for p in range(2)])
            scale = [tile_at(weight, p, row) for p in range(2)]
            kept = level > 0 or TOP <= row < LOW
            for comp in range(2):
                here = [tile_at(iterate, 2 * comp + p, row) for p in range(2)]
                if level == 0:
                    beyond = [lane_roll(here[1], 1), lane_roll(here[0], -1)]
                else:
                    beyond = [
                        tile_at(weight, 2 + p, row) * tile_at(source, 4 * comp + 2 + p, row)
                        for p in range(2)
                    ]
                total = None
                for p in range(2):
                    slot = 2 * comp + p
                    around = middle * here[1 - p] + outer[p] * beyond[p]
                    around = around + (
                        south[p] * tile_at(iterate, slot, row + 1)
                        + north[p] * tile_at(iterate, slot, row - 1)
                    )
                    left = KEEP * tile_at(source, kinds(level) * comp + p, row) + around
                    if kept:
                        put(state, SWEPT + slot, row, here[p] + scale[p] * left)
                    if level == LOCAL - 1:
                        put(ring, slot, row, left)
                        put(state, ITERATE + slot, row, here[p])
                    total = left if total is None else total + left
                put(sums[level], comp, row, total)
            if kept:
                for p in range(2):
                    within = jnp.where(odd_row, north[p], south[p])
                    across = jnp.where(odd_row, south[p], north[p])
                    put(state, CENTRE + p, row, KEEP + scale[p] * (middle + within))
                    put(state, SIDE + p, row, scale[p] * outer[p])
                    put(state, ACROSS + p, row, scale[p] * across)
                    if level == LOCAL - 1:
                        put(state, WEIGHT + p, row, scale[p])

    coefficients(0)
    take_sources(0)
    weigh(0)
    coefficients(1)
    first_sweep(0)
    residual(0)
    weigh(1)
    coefficients(2)
    take_sources(1)
    weigh(2)
    coefficients(3)
    first_sweep(1)
    residual(1)
    take_sources(2)
    weigh(3)
    first_sweep(2)
    residual(2)
    take_sources(3)
    first_sweep(3)
    residual(3)

    start = GUARD + RIM[LOCAL - 1]
    column = lane & (SUB - 1)
    own = [
        lane_take(scale * paired(sums[LOCAL - 1], slot, start), column)
        for slot, scale in enumerate((0.25, 0.25, 0.25, 0.0625))
    ]
    turned = ((lane >> 3) - index_y) & 15
    chosen = (turned & (SUB - 1)) == sub

    def packed(value):
        return jnp.sum(value, axis=0, keepdims=True)

    def joined(a, b):
        return packed(jnp.where(chosen, jnp.where(turned < SUB, a, b), 0.0))

    edge = (lane >> 4) & 3
    place = lane & 15

    rims = jnp.zeros((SUB, LANES), F32)
    for p in range(2):
        index = jnp.where(edge < 2, column, 0 if p == 0 else SUB - 1)
        for part in range(2):
            along = (edge == part) & ((place >> 3) == p) & (sub == (0 if part == 0 else SUB - 1))
            up = (edge == 2 + p) & (place == sub + SUB * part)
            row = start + SUB * part
            value = jnp.where(
                inner,
                lane_take(tile_at(ring, p, row), index),
                lane_take(tile_at(ring, 2 + p, row), index),
            )
            rims = jnp.where(along | up, value, rims)
    kind = sub % CHUNK
    parts = [joined(own[0], own[1]), joined(own[2], own[2]), packed(rims), joined(own[3], own[3])]
    tile = jnp.where(
        kind < 2,
        jnp.where(kind == 0, parts[0], parts[1]),
        jnp.where(kind == 2, parts[2], parts[3]),
    )
    for block in range(CHUNK * devices // SUB):
        chunks[SUB * block : SUB * block + SUB, :] = tile


def write(buffer, slot, rows, value):
    for column in range(buffer.shape[1]):
        buffer[slot, column, rows, :] = value[:, LANES * column : LANES * column + LANES]


def read(buffer, slot, rows):
    parts = [buffer[slot, column, rows, :] for column in range(buffer.shape[1])]
    return parts[0] if len(parts) == 1 else jnp.concatenate(parts, 1)


class Coarse:
    def __init__(self, step, row_step, rows, cols_total, width):
        self.step, self.row_step = step, row_step
        self.shape = (rows, width)
        lane, row = iota(1, self.shape), iota(0, self.shape)
        column = lane & (cols_total - 1)
        self.odd_lane, self.odd_row = (lane & step) != 0, (row & row_step) != 0
        self.leftmost = column < 2 * step
        self.rightmost = column >= cols_total - 2 * step
        self.top, self.bottom = row < row_step, row >= rows - row_step

    def along(self, value, amount):
        return pltpu.roll(value, amount % self.shape[1], 1)

    def down(self, value, amount):
        return pltpu.roll(value, amount % self.shape[0], 0)

    def paired(self, value):
        return (
            jnp.where(self.odd_lane, self.along(value, self.step), value),
            jnp.where(self.odd_lane, value, self.along(value, -self.step)),
        )

    def outside(self, value):
        return (
            jnp.where(
                self.odd_lane, self.along(value, 2 * self.step), self.along(value, self.step)
            ),
            jnp.where(
                self.odd_lane, self.along(value, -self.step), self.along(value, -2 * self.step)
            ),
        )

    def farther(self, value):
        return (
            jnp.where(
                self.odd_lane, self.along(value, 3 * self.step), self.along(value, 2 * self.step)
            ),
            jnp.where(
                self.odd_lane, self.along(value, -2 * self.step), self.along(value, -3 * self.step)
            ),
        )

    def rows_beside(self, here):
        above = jnp.where(self.top, 0.0, self.down(here, self.row_step))
        below = jnp.where(self.bottom, 0.0, self.down(here, -self.row_step))
        return jnp.minimum(here, above), jnp.minimum(here, below)

    def coefficients(self, viscous, reaction):
        here, beyond, far = self.paired(viscous), self.outside(viscous), self.farther(viscous)
        reactions, reactions_beyond = self.paired(reaction), self.outside(reaction)
        edges = (self.leftmost, self.rightmost)
        self.middle = jnp.minimum(here[0], here[1])
        self.outer, self.north, self.south = [], [], []
        self.weights, self.weights_beyond = [], []
        for p in range(2):
            outer = jnp.minimum(here[p], jnp.where(edges[p], 0.0, beyond[p]))
            north, south = self.rows_beside(here[p])
            diagonal = reactions[p] + ((self.middle + outer) + (north + south))
            self.weights.append(OMEGA / diagonal)
            self.outer.append(outer)
            self.north.append(north)
            self.south.append(south)
            next_outer = jnp.minimum(beyond[p], far[p])
            north, south = self.rows_beside(beyond[p])
            diagonal = reactions_beyond[p] + ((outer + next_outer) + (north + south))
            self.weights_beyond.append(OMEGA / diagonal)
        return here[0] + here[1], reactions[0] + reactions[1]

    def take(self, source):
        self.values, self.values_beyond = self.paired(source), self.outside(source)

    def residual(self):
        x = [w * s for w, s in zip(self.weights, self.values)]
        x_beyond = [w * s for w, s in zip(self.weights_beyond, self.values_beyond)]
        total, self.swept = None, []
        for p in range(2):
            around = self.middle * x[1 - p] + self.outer[p] * x_beyond[p]
            around = around + (
                self.south[p] * self.down(x[p], -self.row_step)
                + self.north[p] * self.down(x[p], self.row_step)
            )
            left = KEEP * self.values[p] + around
            self.swept.append(x[p] + self.weights[p] * left)
            total = left if total is None else total + left
        return total

    def prepare(self):
        parts = []
        for p in range(2):
            within = jnp.where(self.odd_row, self.north[p], self.south[p])
            out = jnp.where(self.odd_row, self.south[p], self.north[p])
            weight = self.weights[p]
            centre = KEEP + weight * (self.middle + within)
            parts.append((self.swept[p], centre, weight * self.outer[p], weight * out))
        self.parts = parts
        self.left_parts = [self.along(value, 2 * self.step) for value in parts[1]]
        self.right_parts = [self.along(value, -2 * self.step) for value in parts[0]]

    def corrected(self, here, left, right):
        def swept(part, own, side):
            return (part[0] + part[1] * own[0]) + (part[2] * side[0] + part[3] * own[1])

        even, odd = swept(self.parts[0], here, left), swept(self.parts[1], here, right)
        before, after = swept(self.left_parts, left, here), swept(self.right_parts, right, here)
        return (
            jnp.where(self.odd_lane, odd, even),
            jnp.where(self.odd_lane, even, before),
            jnp.where(self.odd_lane, after, odd),
        )


def coarse_solve(grid, buffer, rows_total, cols_total, width, meanwhile):
    columns = width // LANES

    def whole(slot):
        return jnp.concatenate([grid[slot, c] for c in range(columns)], 1) if columns > 1 else grid[slot, 0]

    levels, rows, row_step = [], rows_total, 1
    for index in range(COARSE + 1):
        levels.append(Coarse(1 << index, row_step, rows, cols_total, width))
        if rows > SUB:
            rows //= 2
        else:
            row_step *= 2

    def folded(index, value, slot, scale):
        level = levels[index]
        rows = level.shape[0]
        if levels[index + 1].shape[0] == rows:
            other = jnp.where(
                level.odd_row, level.down(value, level.row_step), level.down(value, -level.row_step)
            )
            return scale * (value + other)
        write(buffer, slot, slice(0, rows), value)
        first, second = [pl.ds(begin, rows // 2, stride=2) for begin in range(2)]
        return scale * (read(buffer, slot, first) + read(buffer, slot, second))

    def opened(index, value, slot):
        level = levels[index]
        rows = level.shape[0]
        if value.shape[0] == rows:
            return value, jnp.where(
                level.odd_row, level.down(value, -level.row_step), level.down(value, level.row_step)
            )
        half = rows // 2
        blank = jnp.zeros((SUB, width), F32)
        for begin in range(2):
            write(buffer, slot, pl.ds(begin, half, stride=2), value)
        write(buffer, slot + 1, slice(SUB, 2 * SUB), blank)
        write(buffer, slot + 1, slice(rows, rows + SUB), blank)
        for begin in (SUB + 2, SUB - 1):
            write(buffer, slot + 1, pl.ds(begin, half, stride=2), value)
        return read(buffer, slot, slice(0, rows)), read(buffer, slot + 1, slice(SUB, SUB + rows))

    viscous, reaction, source = [None] * 5, [None] * 5, [None] * 5
    viscous[0], reaction[0], source[0] = whole(2), whole(1), whole(0)

    def coefficients(index):
        pair, reactions = levels[index].coefficients(viscous[index], reaction[index])
        viscous[index + 1] = folded(index, pair, 0, 0.0625)
        reaction[index + 1] = folded(index, reactions, 1, 0.25)

    def residual(index):
        source[index + 1] = folded(index, levels[index].residual(), 2, 0.25)

    last = levels[COARSE]
    block = 1 << COARSE
    cols_left = cols_total // block
    rows_left = last.shape[0]
    lane = iota(1, (rows_left, LANES))
    groups = 1 if cols_total < LANES else 2
    per_group = columns // groups

    def spread(value):
        found = []
        for group in range(groups):
            for j in range(cols_left):
                column, place = divmod(block * j, LANES)
                column += group * per_group
                if groups == 1:
                    place = place + (lane & (LANES - cols_total))
                else:
                    place = jnp.full((rows_left, LANES), place, jnp.int32)
                found.append(lane_take(value[:, LANES * column : LANES * column + LANES], place))
        return found

    def flat(values, group, j):
        return values[group * cols_left + j]

    levels[0].take(source[0])
    coefficients(0)
    coefficients(1)
    residual(0)
    levels[1].take(source[1])
    coefficients(2)
    residual(1)
    levels[2].take(source[2])
    coefficients(3)
    residual(2)
    levels[3].take(source[3])
    viscous_columns, reaction_columns = spread(viscous[4]), spread(reaction[4])

    top, bottom = last.top[:, :LANES], last.bottom[:, :LANES]
    pulls, weights = [], []
    for group in range(groups):
        for j in range(cols_left):
            here = flat(viscous_columns, group, j)
            above = jnp.where(top, 0.0, last.down(here, last.row_step))
            below = jnp.where(bottom, 0.0, last.down(here, -last.row_step))
            links = [jnp.minimum(here, above), jnp.minimum(here, below)]
            links += [
                jnp.minimum(here, flat(viscous_columns, group, other))
                for other in (j - 1, j + 1)
                if 0 <= other < cols_left
            ]
            weight = OMEGA / (flat(reaction_columns, group, j) + sum(links))
            weights.append(weight)
            pulls.append([weight * link for link in links])
    residual(3)
    pushed = [w * s for w, s in zip(weights, spread(source[4]))]
    meanwhile()
    for index in range(COARSE - 1, -1, -1):
        levels[index].prepare()
    values = pushed
    for _ in range(COARSE_SWEEPS - 1):
        following = []
        for group in range(groups):
            for j in range(cols_left):
                at = group * cols_left + j
                here, pull = values[at], pulls[at]
                total = (KEEP * here + pushed[at]) + (
                    pull[0] * last.down(here, last.row_step)
                    + pull[1] * last.down(here, -last.row_step)
                )
                sides = [other for other in (j - 1, j + 1) if 0 <= other < cols_left]
                for link, other in zip(pull[2:], sides):
                    total = total + link * flat(values, group, other)
                following.append(total)
        values = following

    def laid(shift):
        found = []
        for column in range(columns):
            group = column // per_group
            place = ((lane & (cols_total - 1)) if groups == 1 else lane) // block
            place = place + (column % per_group) * (LANES // block)
            value = jnp.zeros((rows_left, LANES), F32)
            for j in range(cols_left):
                value = jnp.where(place == j + shift, flat(values, group, j), value)
            found.append(value)
        return found[0] if columns == 1 else jnp.concatenate(found, 1)

    corrections = [laid(shift) for shift in (0, 1, -1)]
    for index in range(COARSE - 1, -1, -1):
        corrections = levels[index].corrected(
            *[opened(index, value, 2 * at) for at, value in enumerate(corrections)]
        )
    return corrections


def up_kernel(size_x, size_y, gathered, state0, state1, state2, state3, out, *refs):
    grid, buffer, whole, window, swept3, corr1, corr2, corr3, merged0, merged1, merged2 = refs
    index_x, index_y = lax.axis_index("gx"), lax.axis_index("gy")
    rows_total, cols_total = CELLS * size_x, CELLS * size_y
    width = 2 * cols_total
    columns = width // LANES
    per_column = LANES // CELLS
    lane, sub = iota(1), iota(0)

    tall = iota(1, (size_x, LANES)) // CELLS
    modulus = min(size_y, per_column)
    for column in range(columns):
        comp = column // (columns // 2) if columns > 1 else 0
        first = (column % (columns // 2)) * per_column if columns > 1 else 0
        for slot, kind in ((2, 3), (1, 1), (0, 0)):
            chunks = [
                gathered[pl.ds(CHUNK * (first + j) + kind, size_x, stride=CHUNK * size_y), :]
                for j in range(modulus)
            ]
            for r in range(CELLS):
                turn = r + CELLS * comp
                value = chunks[0]
                for j in range(1, modulus):
                    value = jnp.where(((tall - turn) & (modulus - 1)) == j, chunks[j], value)
                grid[slot, column, pl.ds(r, size_x, stride=CELLS), :] = lane_roll(
                    value, -CELLS * turn
                )

    def ring_row(dx, dy):
        i = jnp.clip(index_x + dx, 0, size_x - 1)
        j = jnp.clip(index_y + dy, 0, size_y - 1)
        return jnp.broadcast_to(
            gathered[pl.ds(CHUNK * (i * size_y + j) + 2, 1), :], (SUB, LANES)
        )

    start = GUARD + RIM[3]

    def complete_ring():
        beside = {
            (dx, dy): ring_row(dx, dy) for dx in (-1, 0, 1) for dy in (-1, 0, 1) if dx or dy
        }
        for comp in range(2):
            base = comp * HALF
            for p in range(2):
                slot = 2 * comp + p
                end = 7 if p else 0
                corner_lane = LANES - 1 if p else SUB
                dy = -1 if p else 1
                for tile in range(2):
                    at = start + SUB * tile
                    index = base + (48 if p else 32) + SUB * tile + sub
                    ringed = lane_take(beside[0, dy], index)
                    swept = jnp.where(
                        lane == corner_lane,
                        tile_at(state3, ITERATE + slot, at)
                        + tile_at(state3, WEIGHT + p, at) * ringed,
                        tile_at(state3, SWEPT + slot, at),
                    )
                    swept3[slot, at : at + SUB, :] = swept
                for dx, at, edge in ((-1, start - 1, 16), (1, start + 2 * SUB, 0)):
                    index = base + edge + 8 * p
                    ringed = jnp.where(
                        lane == corner_lane,
                        lane_take(beside[dx, dy], jnp.full((SUB, LANES), index + end, jnp.int32)),
                        lane_take(beside[dx, 0], index + (lane & 7)),
                    )
                    rows = slice(at, at + 1)
                    swept3[slot, rows, :] = (
                        state3[ITERATE + slot, rows, :] + state3[WEIGHT + p, rows, :] * ringed[0:1]
                    )

    corrections = coarse_solve(grid, buffer, rows_total, cols_total, width, complete_ring)

    blank = jnp.zeros((SUB, width), F32)
    for kind, correction in enumerate(corrections):
        whole[kind, GUARD : GUARD + rows_total, :] = correction
        whole[kind, 0:GUARD, :] = blank
        whole[kind, GUARD + rows_total : GUARD + rows_total + SUB, :] = blank
    near_rows = pl.ds(pl.multiple_of(CELLS * index_x, SUB), 3 * SUB)
    for comp in range(2):
        shift = (2 * width - cols_total * comp - CELLS * index_y) % width
        for kind in range(3):
            turned = pltpu.roll(whole[kind, near_rows, :], shift, 1)
            if columns > 1:
                tall_lane = iota(1, (3 * SUB, LANES))
                turned = jnp.where(
                    tall_lane < HALF, turned[:, :LANES], turned[:, width - LANES :]
                )
            window[3 * comp + kind, 0 : 3 * SUB, :] = turned

    def swept_rows(ref, level, coarse_row, parity, here, beyond, across, comp):
        at = pl.ds(GUARD + RIM[level] + 2 * coarse_row + parity, SUB, stride=2)
        state = (state0, state1, state2, state3)[level]
        return [
            (ref[SWEPT + 2 * comp + p, at, :] + state[CENTRE + p, at, :] * here)
            + (state[SIDE + p, at, :] * beyond[p] + state[ACROSS + p, at, :] * across)
            for p in range(2)
        ]

    for comp in range(2):
        for tile in range(2):
            first = SUB * tile - 1
            at = GUARD + first
            here, left, right = [tile_at(window, 3 * comp + kind, at) for kind in range(3)]
            for parity in range(2):
                across = tile_at(window, 3 * comp, at + (1 if parity else -1))
                found = swept_rows(swept3, 3, first, parity, here, (left, right), across, comp)
                rows = pl.ds(GUARD + RIM[3] + 2 * first + parity, SUB, stride=2)
                for p in range(2):
                    corr3[2 * comp + p, rows, :] = found[p]

    corrs = [None, corr1, corr2, corr3]
    merged = [merged0, merged1, merged2]
    near = ((((lane + 32) & (LANES - 1)) - 32) >> 1) & (LANES - 1)
    odd_lane = (lane & 1) == 1
    for level in (2, 1, 0):
        coarse = level + 1
        corr, state, whole_rows = corrs[coarse], (state0, state1, state2)[level], merged[level]
        count = (LANES >> coarse) + 2
        origin = GUARD + RIM[coarse]
        sides = {}
        for tile in range(-(-count // SUB)):
            at = origin - 1 + SUB * tile
            for comp in range(2):
                even, odd = tile_at(corr, 2 * comp, at), tile_at(corr, 2 * comp + 1, at)
                even_here, odd_here = lane_take(even, near), lane_take(odd, near)
                even_next = lane_take(even, (near + 1) & (LANES - 1))
                odd_last = lane_take(odd, (near - 1) & (LANES - 1))
                here = jnp.where(odd_lane, odd_here, even_here)
                whole_rows[3 * comp, at : at + SUB, :] = here
                whole_rows[3 * comp + 1, at : at + SUB, :] = jnp.where(
                    odd_lane, even_next, odd_here
                )
                whole_rows[3 * comp + 2, at : at + SUB, :] = jnp.where(
                    odd_lane, even_here, odd_last
                )
        if level > 0:
            first, tiles = -1, -(-count // SUB)
        else:
            first, tiles = 0, (count - 2) // SUB
        for tile in range(tiles):
            coarse_row = first + SUB * tile
            at = origin + coarse_row
            for comp in range(2):
                here, right, left = [tile_at(whole_rows, 3 * comp + k, at) for k in range(3)]
                for parity in range(2):
                    across = tile_at(whole_rows, 3 * comp, at + (1 if parity else -1))
                    found = swept_rows(
                        state, level, coarse_row, parity, here, (left, right), across, comp
                    )
                    if level > 0:
                        rows = pl.ds(GUARD + RIM[level] + 2 * coarse_row + parity, SUB, stride=2)
                        for p in range(2):
                            corrs[level][2 * comp + p, rows, :] = found[p]
                    else:
                        rows = pl.ds(2 * coarse_row + parity, SUB, stride=2)
                        out[comp, rows, :] = jnp.where(
                            odd_lane,
                            lane_take(found[1], lane >> 1),
                            lane_take(found[0], lane >> 1),
                        )


def params():
    return pltpu.CompilerParams(vmem_limit_bytes=VMEM_LIMIT)


VMEM_SPEC = pl.BlockSpec(memory_space=pltpu.VMEM)
SMEM_SPEC = pl.BlockSpec(memory_space=pltpu.SMEM)
HBM_SPEC = pl.BlockSpec(memory_space=pltpu.HBM)


def swap_routes(size_x, size_y):
    def index(i, j):
        return i * size_y + j

    routes = []
    for axis in range(2):
        size = (size_x, size_y)[axis]
        for offset in range(2):
            route = []
            for i in range(size_x):
                for j in range(size_y):
                    here = (i, j)[axis]
                    other = here + 1 if here % 2 == offset else here - 1
                    if 0 <= other < size:
                        peer = (other, j) if axis == 0 else (i, other)
                    else:
                        peer = (i, j ^ 1) if axis == 0 else (i ^ 1, j)
                    route.append((index(i, j), index(*peer)))
            routes.append(route)
    return routes


def per_device(size_x, size_y, right_side, shift_coef, viscosity, wet_tiles):
    axes = ("gx", "gy")
    devices = size_x * size_y
    routes = swap_routes(size_x, size_y)
    band = jax.ShapeDtypeStruct((4 * HALO, LANES), F32)
    held_shape = pltpu.VMEM((4, HELD[0], LANES), F32)
    held, first, second = pl.pallas_call(
        bands_kernel,
        out_shape=(held_shape, band, band),
        in_specs=[SMEM_SPEC] + [HBM_SPEC] * 3,
        out_specs=(VMEM_SPEC,) * 3,
        scratch_shapes=[pltpu.SemaphoreType.DMA((4,))],
        compiler_params=params(),
        name="bands",
    )(
        wet_tiles,
        *[
            pltpu.with_memory_space_constraint(array, pltpu.HBM)
            for array in (right_side, shift_coef, viscosity)
        ],
    )
    second = lax.ppermute(second, axes, routes[1])
    first = lax.ppermute(first, axes, routes[0])
    strip = jax.ShapeDtypeStruct((MESSAGE, LANES), F32)
    got = (second, first)
    first, second = pl.pallas_call(
        functools.partial(strips_kernel, size_x),
        out_shape=(strip, strip),
        in_specs=[SMEM_SPEC] + [VMEM_SPEC] * 3,
        out_specs=(VMEM_SPEC,) * 2,
        compiler_params=params(),
        name="strips",
    )(wet_tiles, *got, held)
    fields = pl.pallas_call(
        functools.partial(halves_kernel, size_x),
        out_shape=pltpu.VMEM((8, HELD[0], LANES), F32),
        in_specs=[SMEM_SPEC] + [VMEM_SPEC] * 3,
        out_specs=VMEM_SPEC,
        cost_estimate=pl.CostEstimate(flops=1 << 20, bytes_accessed=1 << 21, transcendentals=0),
        compiler_params=params(),
        name="halves",
    )(wet_tiles, *got, held)
    second = lax.ppermute(second, axes, routes[3])
    first = lax.ppermute(first, axes, routes[2])

    def buffers(counts):
        return [pltpu.VMEM((n, HELD[level], LANES), F32) for level, n in enumerate(counts)]

    chunks, *states = pl.pallas_call(
        functools.partial(down_kernel, size_y, devices),
        out_shape=(jax.ShapeDtypeStruct((CHUNK * devices, LANES), F32),)
        + tuple(buffers([STATE, STATE, STATE, STATE + 6])),
        in_specs=[VMEM_SPEC] * 3,
        out_specs=(VMEM_SPEC,) * (1 + LOCAL),
        scratch_shapes=buffers([2, 4, 4, 4])
        + buffers([2] * 4)
        + buffers([4, 8, 8, 8])
        + buffers([2, 4, 4, 4])
        + buffers([4] * 4)
        + buffers([4] * 4)
        + [pltpu.VMEM((2, HELD[0], LANES), F32), pltpu.VMEM((4, HELD[3], LANES), F32)],
        compiler_params=params(),
        name="down",
    )(second, first, fields)
    gathered = lax.all_to_all(chunks, axes, 0, 0, tiled=True)
    rows_total = CELLS * size_x
    width = 2 * CELLS * size_y
    return pl.pallas_call(
        functools.partial(up_kernel, size_x, size_y),
        out_shape=jax.ShapeDtypeStruct((2, LANES, LANES), F32),
        in_specs=[VMEM_SPEC] * (1 + LOCAL),
        out_specs=VMEM_SPEC,
        scratch_shapes=[
            pltpu.VMEM((3, width // LANES, rows_total, LANES), F32),
            pltpu.VMEM((6, width // LANES, rows_total + 3 * SUB, LANES), F32),
            pltpu.VMEM((3, rows_total + 2 * SUB, width), F32),
            pltpu.VMEM((6, 5 * SUB, LANES), F32),
            pltpu.VMEM((4, HELD[3], LANES), F32),
        ]
        + [pltpu.VMEM((4, HELD[level], LANES), F32) for level in (1, 2, 3)]
        + [pltpu.VMEM((6, HELD[level + 1], LANES), F32) for level in (0, 1, 2)],
        compiler_params=params(),
        name="up",
    )(gathered, *states)


def solution(mesh):
    sizes = dict(mesh.shape)
    placed = (P(None, "gx", "gy"), P("gx", "gy"), P("gx", "gy"), P("gx", "gy"))
    return jax.shard_map(
        functools.partial(per_device, sizes["gx"], sizes["gy"]),
        mesh=mesh,
        in_specs=placed,
        out_specs=P(None, "gx", "gy"),
        check_vma=False,
    )
```

```python
import functools

import jax
import jax.numpy as jnp
from jax import lax
from jax.experimental import pallas as pl
from jax.experimental.pallas import tpu as pltpu
from jax.sharding import PartitionSpec as P

LOCAL = 4
COARSE = 4
COARSE_SWEEPS = 8
OMEGA = 0.8
KEEP = 1.0 - OMEGA

LANES = 128
HALF = LANES // 2
SUB = 8
HALO = 16
GUARD = 8
CELLS = LANES >> LOCAL
ROWS = [(LANES + 2 * HALO) >> level for level in range(LOCAL)]
TILES = [-(-rows // SUB) for rows in ROWS]
HELD = [GUARD + SUB * tiles + 16 for tiles in TILES]
RIM = [HALO >> level for level in range(LOCAL)]
TOP = GUARD + HALO
LOW = TOP + LANES
HALF_TILES = TILES[0] // 2
MESSAGE = ROWS[0] // 2
CHUNK = 4
F32 = jnp.float32
VMEM_LIMIT = 48 * 1024 * 1024

SWEPT, CENTRE, SIDE, ACROSS = 0, 4, 6, 8
STATE = 10
ITERATE, WEIGHT = 10, 14


def iota(dim, shape=(SUB, LANES)):
    return lax.broadcasted_iota(jnp.int32, shape, dim)


def lane_take(tile, index):
    return jnp.take_along_axis(tile, index, axis=1)


def lane_roll(tile, shift):
    return pltpu.roll(tile, shift % LANES, 1)


def tile_at(ref, slot, row):
    return ref[slot, row : row + SUB, :]


def bands_kernel(wet, right_side, shift_coef, viscosity, held, first, second, sems):
    odd = lax.axis_index("gx") % 2
    wetness = wet[0, 0].astype(F32)
    own = pl.ds(TOP, LANES)
    sources = (right_side.at[0], right_side.at[1], shift_coef, viscosity)
    copies = [
        pltpu.make_async_copy(sources[field], held.at[field, own, :], sems.at[field])
        for field in range(4)
    ]
    for copy in copies:
        copy.start()
    bottom = LANES - HALO
    starts = (TOP + bottom - bottom * odd, TOP + bottom * odd)
    for field in range(4):
        copies[field].wait()
        for start, out in zip(starts, (first, second)):
            value = held[field, pl.ds(pl.multiple_of(start, SUB), HALO), :]
            out[field * HALO : (field + 1) * HALO, :] = value if field == 2 else value * wetness


def rim_place(half, lane):
    to_left = ((lane >> 3) & 1) == half
    q = jnp.where(to_left, lane, (lane - (56 + 8 * half)) & (LANES - 1)) >> 4
    cell = 2 * (lane & 7) + (q & 1) + jnp.where(to_left, 0, LANES - HALO)
    return to_left, q >> 1, cell


def strips_kernel(size_x, wet, got_second, got_first, held, first, second):
    index_x = lax.axis_index("gx")
    odd_x = index_x % 2 == 1
    odd_y = lax.axis_index("gy") % 2 == 1
    wetness = wet[0, 0].astype(F32)
    above = (index_x > 0).astype(F32)
    below = (index_x < size_x - 1).astype(F32)
    lane = iota(1)
    rim_tiles = HALO // SUB

    def piece(field, tile):
        if rim_tiles <= tile < TILES[0] - rim_tiles:
            row = GUARD + SUB * tile
            return held[field, row : row + SUB, :]
        top = tile < rim_tiles
        row = field * HALO + SUB * (tile if top else tile - (TILES[0] - rim_tiles))
        one, two = got_first[row : row + SUB, :], got_second[row : row + SUB, :]
        return jnp.where(odd_x, one, two) if top else jnp.where(odd_x, two, one)

    places = [rim_place(half, lane) for half in range(2)]
    found = {}
    for half in range(2):
        _, owner, cell = places[half]
        for tile in range(HALF_TILES):
            at = tile + half * HALF_TILES
            value = None
            for field in range(4):
                part = lane_take(piece(field, at), cell)
                value = part if value is None else jnp.where(owner == field, part, value)
            if rim_tiles <= at < TILES[0] - rim_tiles:
                value = value * jnp.where(owner == 2, 1.0, wetness)
            else:
                value = value * jnp.where(owner == 3, above if at < rim_tiles else below, 1.0)
            found[half, tile] = value
    for tile in range(HALF_TILES):
        left = jnp.where(places[0][0], found[0, tile], found[1, tile])
        right = jnp.where(places[0][0], found[1, tile], found[0, tile])
        rows = slice(SUB * tile, SUB * tile + SUB)
        first[rows, :] = jnp.where(odd_y, left, right)
        second[rows, :] = jnp.where(odd_y, right, left)


def halves_kernel(size_x, wet, got_second, got_first, held, fields):
    index_x = lax.axis_index("gx")
    odd_x = index_x % 2 == 1
    wetness = wet[0, 0].astype(F32)
    above = (index_x > 0).astype(F32)
    below = (index_x < size_x - 1).astype(F32)
    lane = iota(1)
    rim_tiles = HALO // SUB
    for tile in range(TILES[0]):
        row = GUARD + SUB * tile
        for field in range(4):
            if rim_tiles <= tile < TILES[0] - rim_tiles:
                value = held[field, row : row + SUB, :]
                if field != 2:
                    value = value * wetness
            else:
                top = tile < rim_tiles
                at = field * HALO + SUB * (tile if top else tile - (TILES[0] - rim_tiles))
                one, two = got_first[at : at + SUB, :], got_second[at : at + SUB, :]
                value = jnp.where(odd_x, one, two) if top else jnp.where(odd_x, two, one)
                if field == 3:
                    value = value * (above if top else below)
            for parity in range(2):
                fields[2 * field + parity, row : row + SUB, :] = lane_take(
                    value, (2 * lane + parity) & (LANES - 1)
                )


def down_kernel(size_y, devices, got_second, got_first, held, chunks, *refs):
    states, refs = refs[:LOCAL], refs[LOCAL:]
    viscous, refs = refs[:LOCAL], refs[LOCAL:]
    reactions, refs = refs[:LOCAL], refs[LOCAL:]
    sources, refs = refs[:LOCAL], refs[LOCAL:]
    weights, refs = refs[:LOCAL], refs[LOCAL:]
    iterates, refs = refs[:LOCAL], refs[LOCAL:]
    sums, (outers, ring) = refs[:LOCAL], refs[LOCAL:]
    index_y = lax.axis_index("gy")
    odd_y = index_y % 2 == 1
    lane, sub = iota(1), iota(0)
    side_ok = jnp.where(
        lane < 96, (index_y < size_y - 1).astype(F32), (index_y > 0).astype(F32)
    )
    odd_row = (sub & 1) == 1
    inner = lane < HALF
    even_block = ((lane >> 3) & 1) == 0

    def tiles(level):
        return [GUARD + SUB * tile for tile in range(TILES[level])]

    def put(ref, slot, row, value):
        ref[slot, row : row + SUB, :] = value

    def rims(row, slots):
        half, at = divmod((row - GUARD) // SUB, HALF_TILES)
        one, two = (r[SUB * at : SUB * at + SUB, :] for r in (got_first, got_second))
        after, before = jnp.where(odd_y, two, one), jnp.where(odd_y, one, two)
        if half == 0:
            both = jnp.where(even_block, after, before)
        else:
            both = jnp.where(even_block, before, after)
        values = []
        for slot in slots:
            rim = lane_roll(both, HALF - 16 * slot - 8 * half)
            if slot >= 4:
                rim = jnp.where(side_ok > 0, rim, 1.0 if slot < 6 else 0.0)
            values.append(jnp.where(inner, tile_at(held, slot, row), rim))
        return values

    def paired(ref, slot, start):
        return (
            ref[slot, pl.ds(start, SUB, stride=2), :] + ref[slot, pl.ds(start + 1, SUB, stride=2), :]
        )

    takes = [(2 * lane + offset) & (LANES - 1) for offset in (0, 1, -1, 2)]

    def coefficients(level):
        if level == 0:
            for row in tiles(level):
                values = rims(row, (4, 5, 6, 7))
                for slot, value in enumerate(values[:2]):
                    put(reactions[level], slot, row, value)
                for slot, value in enumerate(values[2:]):
                    put(viscous[level], slot, row, value)
                put(sums[level], 2, row, values[0] + values[1])
                put(sums[level], 3, row, values[2] + values[3])
            return
        ref = sums[level - 1]
        loaded = {
            row: [
                scale * paired(ref, slot, GUARD + 2 * (row - GUARD))
                for slot, scale in ((2, 0.25), (3, 0.0625))
            ]
            for row in tiles(level)
        }
        found = {row: ([], []) for row in loaded}
        for kind, index in enumerate(takes):
            for row, (reaction, viscosity) in loaded.items():
                value = lane_take(viscosity, index)
                put(viscous[level], kind, row, value)
                found[row][1].append(value)
                if kind < 2:
                    value = lane_take(reaction, index)
                    put(reactions[level], kind, row, value)
                    found[row][0].append(value)
        for row, (reaction, viscosity) in found.items():
            put(sums[level], 2, row, reaction[0] + reaction[1])
            put(sums[level], 3, row, viscosity[0] + viscosity[1])

    def faces(level, row):
        here = [tile_at(viscous[level], p, row) for p in range(2)]
        north = [jnp.minimum(here[p], tile_at(viscous[level], p, row - 1)) for p in range(2)]
        south = [jnp.minimum(here[p], tile_at(viscous[level], p, row + 1)) for p in range(2)]
        return here, jnp.minimum(here[0], here[1]), north, south

    def outside(level, row, here):
        if level == 0:
            beyond = [lane_roll(here[1], 1), lane_roll(here[0], -1)]
        else:
            beyond = [tile_at(viscous[level], 2 + p, row) for p in range(2)]
        return [jnp.minimum(h, b) for h, b in zip(here, beyond)]

    def weigh(level):
        for row in tiles(level):
            here, middle, north, south = faces(level, row)
            outer = outside(level, row, here)
            found = []
            for p in range(2):
                diagonal = tile_at(reactions[level], p, row) + (
                    (middle + outer[p]) + (north[p] + south[p])
                )
                found.append(OMEGA / diagonal)
                if level == 0:
                    put(outers, p, row, outer[p])
            if level > 0:
                found += [lane_roll(found[1], 1), lane_roll(found[0], -1)]
            for slot, value in enumerate(found):
                put(weights[level], slot, row, value)

    def take_sources(level):
        if level == 0:
            for row in tiles(level):
                for slot, value in enumerate(rims(row, (0, 1, 2, 3))):
                    put(sources[level], slot, row, value)
            return
        loaded = {
            row: [
                0.25 * paired(sums[level - 1], comp, GUARD + 2 * (row - GUARD))
                for comp in range(2)
            ]
            for row in tiles(level)
        }
        for kind, index in enumerate(takes):
            for row, values in loaded.items():
                for comp in range(2):
                    put(sources[level], 4 * comp + kind, row, lane_take(values[comp], index))

    def kinds(level):
        return 2 if level == 0 else 4

    def first_sweep(level):
        for row in tiles(level):
            for comp in range(2):
                for p in range(2):
                    put(
                        iterates[level],
                        2 * comp + p,
                        row,
                        tile_at(weights[level], p, row)
                        * tile_at(sources[level], kinds(level) * comp + p, row),
                    )

    def residual(level):
        state, iterate, weight, source = (
            states[level],
            iterates[level],
            weights[level],
            sources[level],
        )
        for row in tiles(level):
            _, middle, north, south = faces(level, row)
            if level == 0:
                outer = [tile_at(outers, p, row) for p in range(2)]
            else:
                outer = outside(level, row, [tile_at(viscous[level], p, row) for p in range(2)])
            scale = [tile_at(weight, p, row) for p in range(2)]
            kept = level > 0 or TOP <= row < LOW
            for comp in range(2):
                here = [tile_at(iterate, 2 * comp + p, row) for p in range(2)]
                if level == 0:
                    beyond = [lane_roll(here[1], 1), lane_roll(here[0], -1)]
                else:
                    beyond = [
                        tile_at(weight, 2 + p, row) * tile_at(source, 4 * comp + 2 + p, row)
                        for p in range(2)
                    ]
                total = None
                for p in range(2):
                    slot = 2 * comp + p
                    around = middle * here[1 - p] + outer[p] * beyond[p]
                    around = around + (
                        south[p] * tile_at(iterate, slot, row + 1)
                        + north[p] * tile_at(iterate, slot, row - 1)
                    )
                    left = KEEP * tile_at(source, kinds(level) * comp + p, row) + around
                    if kept:
                        put(state, SWEPT + slot, row, here[p] + scale[p] * left)
                    if level == LOCAL - 1:
                        put(ring, slot, row, left)
                        put(state, ITERATE + slot, row, here[p])
                    total = left if total is None else total + left
                put(sums[level], comp, row, total)
            if kept:
                for p in range(2):
                    within = jnp.where(odd_row, north[p], south[p])
                    across = jnp.where(odd_row, south[p], north[p])
                    put(state, CENTRE + p, row, KEEP + scale[p] * (middle + within))
                    put(state, SIDE + p, row, scale[p] * outer[p])
                    put(state, ACROSS + p, row, scale[p] * across)
                    if level == LOCAL - 1:
                        put(state, WEIGHT + p, row, scale[p])

    coefficients(0)
    take_sources(0)
    weigh(0)
    coefficients(1)
    first_sweep(0)
    residual(0)
    weigh(1)
    coefficients(2)
    take_sources(1)
    weigh(2)
    coefficients(3)
    first_sweep(1)
    residual(1)
    take_sources(2)
    weigh(3)
    first_sweep(2)
    residual(2)
    take_sources(3)
    first_sweep(3)
    residual(3)

    start = GUARD + RIM[LOCAL - 1]
    column = lane & (SUB - 1)
    own = [
        lane_take(scale * paired(sums[LOCAL - 1], slot, start), column)
        for slot, scale in enumerate((0.25, 0.25, 0.25, 0.0625))
    ]
    turned = ((lane >> 3) - index_y) & 15
    chosen = (turned & (SUB - 1)) == sub

    def packed(value):
        return jnp.sum(value, axis=0, keepdims=True)

    def joined(a, b):
        return packed(jnp.where(chosen, jnp.where(turned < SUB, a, b), 0.0))

    edge = (lane >> 4) & 3
    place = lane & 15

    rims = jnp.zeros((SUB, LANES), F32)
    for p in range(2):
        index = jnp.where(edge < 2, column, 0 if p == 0 else SUB - 1)
        for part in range(2):
            along = (edge == part) & ((place >> 3) == p) & (sub == (0 if part == 0 else SUB - 1))
            up = (edge == 2 + p) & (place == sub + SUB * part)
            row = start + SUB * part
            value = jnp.where(
                inner,
                lane_take(tile_at(ring, p, row), index),
                lane_take(tile_at(ring, 2 + p, row), index),
            )
            rims = jnp.where(along | up, value, rims)
    kind = sub % CHUNK
    parts = [joined(own[0], own[1]), joined(own[2], own[2]), packed(rims), joined(own[3], own[3])]
    tile = jnp.where(
        kind < 2,
        jnp.where(kind == 0, parts[0], parts[1]),
        jnp.where(kind == 2, parts[2], parts[3]),
    )
    for block in range(CHUNK * devices // SUB):
        chunks[SUB * block : SUB * block + SUB, :] = tile


def write(buffer, slot, rows, value):
    for column in range(buffer.shape[1]):
        buffer[slot, column, rows, :] = value[:, LANES * column : LANES * column + LANES]


def read(buffer, slot, rows):
    parts = [buffer[slot, column, rows, :] for column in range(buffer.shape[1])]
    return parts[0] if len(parts) == 1 else jnp.concatenate(parts, 1)


class Coarse:
    def __init__(self, step, row_step, rows, cols_total, width):
        self.step, self.row_step = step, row_step
        self.shape = (rows, width)
        lane, row = iota(1, self.shape), iota(0, self.shape)
        column = lane & (cols_total - 1)
        self.odd_lane, self.odd_row = (lane & step) != 0, (row & row_step) != 0
        self.leftmost = column < 2 * step
        self.rightmost = column >= cols_total - 2 * step
        self.top, self.bottom = row < row_step, row >= rows - row_step

    def along(self, value, amount):
        return pltpu.roll(value, amount % self.shape[1], 1)

    def down(self, value, amount):
        return pltpu.roll(value, amount % self.shape[0], 0)

    def paired(self, value):
        return (
            jnp.where(self.odd_lane, self.along(value, self.step), value),
            jnp.where(self.odd_lane, value, self.along(value, -self.step)),
        )

    def outside(self, value):
        return (
            jnp.where(
                self.odd_lane, self.along(value, 2 * self.step), self.along(value, self.step)
            ),
            jnp.where(
                self.odd_lane, self.along(value, -self.step), self.along(value, -2 * self.step)
            ),
        )

    def farther(self, value):
        return (
            jnp.where(
                self.odd_lane, self.along(value, 3 * self.step), self.along(value, 2 * self.step)
            ),
            jnp.where(
                self.odd_lane, self.along(value, -2 * self.step), self.along(value, -3 * self.step)
            ),
        )

    def rows_beside(self, here):
        above = jnp.where(self.top, 0.0, self.down(here, self.row_step))
        below = jnp.where(self.bottom, 0.0, self.down(here, -self.row_step))
        return jnp.minimum(here, above), jnp.minimum(here, below)

    def coefficients(self, viscous, reaction):
        here, beyond, far = self.paired(viscous), self.outside(viscous), self.farther(viscous)
        reactions, reactions_beyond = self.paired(reaction), self.outside(reaction)
        edges = (self.leftmost, self.rightmost)
        self.middle = jnp.minimum(here[0], here[1])
        self.outer, self.north, self.south = [], [], []
        self.weights, self.weights_beyond = [], []
        for p in range(2):
            outer = jnp.minimum(here[p], jnp.where(edges[p], 0.0, beyond[p]))
            north, south = self.rows_beside(here[p])
            diagonal = reactions[p] + ((self.middle + outer) + (north + south))
            self.weights.append(OMEGA / diagonal)
            self.outer.append(outer)
            self.north.append(north)
            self.south.append(south)
            next_outer = jnp.minimum(beyond[p], far[p])
            north, south = self.rows_beside(beyond[p])
            diagonal = reactions_beyond[p] + ((outer + next_outer) + (north + south))
            self.weights_beyond.append(OMEGA / diagonal)
        return here[0] + here[1], reactions[0] + reactions[1]

    def take(self, source):
        self.values, self.values_beyond = self.paired(source), self.outside(source)

    def residual(self):
        x = [w * s for w, s in zip(self.weights, self.values)]
        x_beyond = [w * s for w, s in zip(self.weights_beyond, self.values_beyond)]
        total, self.swept = None, []
        for p in range(2):
            around = self.middle * x[1 - p] + self.outer[p] * x_beyond[p]
            around = around + (
                self.south[p] * self.down(x[p], -self.row_step)
                + self.north[p] * self.down(x[p], self.row_step)
            )
            left = KEEP * self.values[p] + around
            self.swept.append(x[p] + self.weights[p] * left)
            total = left if total is None else total + left
        return total

    def prepare(self):
        parts = []
        for p in range(2):
            within = jnp.where(self.odd_row, self.north[p], self.south[p])
            out = jnp.where(self.odd_row, self.south[p], self.north[p])
            weight = self.weights[p]
            centre = KEEP + weight * (self.middle + within)
            parts.append((self.swept[p], centre, weight * self.outer[p], weight * out))
        self.parts = parts
        self.left_parts = [self.along(value, 2 * self.step) for value in parts[1]]
        self.right_parts = [self.along(value, -2 * self.step) for value in parts[0]]

    def corrected(self, here, left, right):
        def swept(part, own, side):
            return (part[0] + part[1] * own[0]) + (part[2] * side[0] + part[3] * own[1])

        even, odd = swept(self.parts[0], here, left), swept(self.parts[1], here, right)
        before, after = swept(self.left_parts, left, here), swept(self.right_parts, right, here)
        return (
            jnp.where(self.odd_lane, odd, even),
            jnp.where(self.odd_lane, even, before),
            jnp.where(self.odd_lane, after, odd),
        )


def coarse_solve(grid, buffer, rows_total, cols_total, width, meanwhile):
    columns = width // LANES

    def whole(slot):
        return jnp.concatenate([grid[slot, c] for c in range(columns)], 1) if columns > 1 else grid[slot, 0]

    levels, rows, row_step = [], rows_total, 1
    for index in range(COARSE + 1):
        levels.append(Coarse(1 << index, row_step, rows, cols_total, width))
        if rows > SUB:
            rows //= 2
        else:
            row_step *= 2

    def folded(index, value, slot, scale):
        level = levels[index]
        rows = level.shape[0]
        if levels[index + 1].shape[0] == rows:
            other = jnp.where(
                level.odd_row, level.down(value, level.row_step), level.down(value, -level.row_step)
            )
            return scale * (value + other)
        write(buffer, slot, slice(0, rows), value)
        first, second = [pl.ds(begin, rows // 2, stride=2) for begin in range(2)]
        return scale * (read(buffer, slot, first) + read(buffer, slot, second))

    def opened(index, value, slot):
        level = levels[index]
        rows = level.shape[0]
        if value.shape[0] == rows:
            return value, jnp.where(
                level.odd_row, level.down(value, -level.row_step), level.down(value, level.row_step)
            )
        half = rows // 2
        blank = jnp.zeros((SUB, width), F32)
        for begin in range(2):
            write(buffer, slot, pl.ds(begin, half, stride=2), value)
        write(buffer, slot + 1, slice(SUB, 2 * SUB), blank)
        write(buffer, slot + 1, slice(rows, rows + SUB), blank)
        for begin in (SUB + 2, SUB - 1):
            write(buffer, slot + 1, pl.ds(begin, half, stride=2), value)
        return read(buffer, slot, slice(0, rows)), read(buffer, slot + 1, slice(SUB, SUB + rows))

    viscous, reaction, source = [None] * 5, [None] * 5, [None] * 5
    viscous[0], reaction[0], source[0] = whole(2), whole(1), whole(0)

    def coefficients(index):
        pair, reactions = levels[index].coefficients(viscous[index], reaction[index])
        viscous[index + 1] = folded(index, pair, 0, 0.0625)
        reaction[index + 1] = folded(index, reactions, 1, 0.25)

    def residual(index):
        source[index + 1] = folded(index, levels[index].residual(), 2, 0.25)

    last = levels[COARSE]
    block = 1 << COARSE
    cols_left = cols_total // block
    rows_left = last.shape[0]
    lane = iota(1, (rows_left, LANES))
    groups = 1 if cols_total < LANES else 2
    per_group = columns // groups

    def spread(*arrays):
        found = [[] for _ in arrays]
        for group in range(groups):
            for j in range(cols_left):
                column, place = divmod(block * j, LANES)
                column += group * per_group
                if groups == 1:
                    place = place + (lane & (LANES - cols_total))
                else:
                    place = jnp.full((rows_left, LANES), place, jnp.int32)
                for value, columns_found in zip(arrays, found):
                    tile = value[:, LANES * column : LANES * column + LANES]
                    columns_found.append(lane_take(tile, place))
        return found

    def flat(values, group, j):
        return values[group * cols_left + j]

    levels[0].take(source[0])
    coefficients(0)
    coefficients(1)
    residual(0)
    levels[1].take(source[1])
    coefficients(2)
    residual(1)
    levels[2].take(source[2])
    coefficients(3)
    residual(2)
    levels[3].take(source[3])
    viscous_columns, reaction_columns = spread(viscous[4], reaction[4])

    top, bottom = last.top[:, :LANES], last.bottom[:, :LANES]
    pulls, weights = [], []
    for group in range(groups):
        for j in range(cols_left):
            here = flat(viscous_columns, group, j)
            above = jnp.where(top, 0.0, last.down(here, last.row_step))
            below = jnp.where(bottom, 0.0, last.down(here, -last.row_step))
            links = [jnp.minimum(here, above), jnp.minimum(here, below)]
            links += [
                jnp.minimum(here, flat(viscous_columns, group, other))
                for other in (j - 1, j + 1)
                if 0 <= other < cols_left
            ]
            weight = OMEGA / (flat(reaction_columns, group, j) + sum(links))
            weights.append(weight)
            pulls.append([weight * link for link in links])
    residual(3)
    pushed = [w * s for w, s in zip(weights, spread(source[4])[0])]
    meanwhile()
    for index in range(COARSE - 1, -1, -1):
        levels[index].prepare()
    values = pushed
    for _ in range(COARSE_SWEEPS - 1):
        following = []
        for group in range(groups):
            for j in range(cols_left):
                at = group * cols_left + j
                here, pull = values[at], pulls[at]
                total = (KEEP * here + pushed[at]) + (
                    pull[0] * last.down(here, last.row_step)
                    + pull[1] * last.down(here, -last.row_step)
                )
                sides = [other for other in (j - 1, j + 1) if 0 <= other < cols_left]
                for link, other in zip(pull[2:], sides):
                    total = total + link * flat(values, group, other)
                following.append(total)
        values = following

    def laid(shift):
        found = []
        for column in range(columns):
            group = column // per_group
            place = ((lane & (cols_total - 1)) if groups == 1 else lane) // block
            place = place + (column % per_group) * (LANES // block)
            value = jnp.zeros((rows_left, LANES), F32)
            for j in range(cols_left):
                value = jnp.where(place == j + shift, flat(values, group, j), value)
            found.append(value)
        return found[0] if columns == 1 else jnp.concatenate(found, 1)

    corrections = [laid(shift) for shift in (0, 1, -1)]
    for index in range(COARSE - 1, -1, -1):
        corrections = levels[index].corrected(
            *[opened(index, value, 2 * at) for at, value in enumerate(corrections)]
        )
    return corrections


def up_kernel(size_x, size_y, gathered, state0, state1, state2, state3, out, *refs):
    grid, buffer, whole, window, swept3, corr1, corr2, corr3, merged0, merged1, merged2 = refs
    index_x, index_y = lax.axis_index("gx"), lax.axis_index("gy")
    rows_total, cols_total = CELLS * size_x, CELLS * size_y
    width = 2 * cols_total
    columns = width // LANES
    per_column = LANES // CELLS
    lane, sub = iota(1), iota(0)

    tall = iota(1, (size_x, LANES)) // CELLS
    modulus = min(size_y, per_column)
    for column in range(columns):
        comp = column // (columns // 2) if columns > 1 else 0
        first = (column % (columns // 2)) * per_column if columns > 1 else 0
        for slot, kind in ((2, 3), (1, 1), (0, 0)):
            chunks = [
                gathered[pl.ds(CHUNK * (first + j) + kind, size_x, stride=CHUNK * size_y), :]
                for j in range(modulus)
            ]
            for r in range(CELLS):
                turn = r + CELLS * comp
                value = chunks[0]
                for j in range(1, modulus):
                    value = jnp.where(((tall - turn) & (modulus - 1)) == j, chunks[j], value)
                grid[slot, column, pl.ds(r, size_x, stride=CELLS), :] = lane_roll(
                    value, -CELLS * turn
                )

    def ring_row(dx, dy):
        i = jnp.clip(index_x + dx, 0, size_x - 1)
        j = jnp.clip(index_y + dy, 0, size_y - 1)
        return jnp.broadcast_to(
            gathered[pl.ds(CHUNK * (i * size_y + j) + 2, 1), :], (SUB, LANES)
        )

    start = GUARD + RIM[3]

    def complete_ring():
        beside = {
            (dx, dy): ring_row(dx, dy) for dx in (-1, 0, 1) for dy in (-1, 0, 1) if dx or dy
        }
        for comp in range(2):
            base = comp * HALF
            for p in range(2):
                slot = 2 * comp + p
                end = 7 if p else 0
                corner_lane = LANES - 1 if p else SUB
                dy = -1 if p else 1
                for tile in range(2):
                    at = start + SUB * tile
                    index = base + (48 if p else 32) + SUB * tile + sub
                    ringed = lane_take(beside[0, dy], index)
                    swept = jnp.where(
                        lane == corner_lane,
                        tile_at(state3, ITERATE + slot, at)
                        + tile_at(state3, WEIGHT + p, at) * ringed,
                        tile_at(state3, SWEPT + slot, at),
                    )
                    swept3[slot, at : at + SUB, :] = swept
                for dx, at, edge in ((-1, start - 1, 16), (1, start + 2 * SUB, 0)):
                    index = base + edge + 8 * p
                    ringed = jnp.where(
                        lane == corner_lane,
                        lane_take(beside[dx, dy], jnp.full((SUB, LANES), index + end, jnp.int32)),
                        lane_take(beside[dx, 0], index + (lane & 7)),
                    )
                    rows = slice(at, at + 1)
                    swept3[slot, rows, :] = (
                        state3[ITERATE + slot, rows, :] + state3[WEIGHT + p, rows, :] * ringed[0:1]
                    )

    corrections = coarse_solve(grid, buffer, rows_total, cols_total, width, complete_ring)

    blank = jnp.zeros((SUB, width), F32)
    for kind, correction in enumerate(corrections):
        whole[kind, GUARD : GUARD + rows_total, :] = correction
        whole[kind, 0:GUARD, :] = blank
        whole[kind, GUARD + rows_total : GUARD + rows_total + SUB, :] = blank
    near_rows = pl.ds(pl.multiple_of(CELLS * index_x, SUB), 3 * SUB)
    for comp in range(2):
        shift = (2 * width - cols_total * comp - CELLS * index_y) % width
        for kind in range(3):
            turned = pltpu.roll(whole[kind, near_rows, :], shift, 1)
            if columns > 1:
                tall_lane = iota(1, (3 * SUB, LANES))
                turned = jnp.where(
                    tall_lane < HALF, turned[:, :LANES], turned[:, width - LANES :]
                )
            window[3 * comp + kind, 0 : 3 * SUB, :] = turned

    def swept_rows(ref, level, coarse_row, parity, here, beyond, across, comp):
        at = pl.ds(GUARD + RIM[level] + 2 * coarse_row + parity, SUB, stride=2)
        state = (state0, state1, state2, state3)[level]
        return [
            (ref[SWEPT + 2 * comp + p, at, :] + state[CENTRE + p, at, :] * here)
            + (state[SIDE + p, at, :] * beyond[p] + state[ACROSS + p, at, :] * across)
            for p in range(2)
        ]

    for comp in range(2):
        for tile in range(2):
            first = SUB * tile - 1
            at = GUARD + first
            here, left, right = [tile_at(window, 3 * comp + kind, at) for kind in range(3)]
            for parity in range(2):
                across = tile_at(window, 3 * comp, at + (1 if parity else -1))
                found = swept_rows(swept3, 3, first, parity, here, (left, right), across, comp)
                rows = pl.ds(GUARD + RIM[3] + 2 * first + parity, SUB, stride=2)
                for p in range(2):
                    corr3[2 * comp + p, rows, :] = found[p]

    corrs = [None, corr1, corr2, corr3]
    merged = [merged0, merged1, merged2]
    near = ((((lane + 32) & (LANES - 1)) - 32) >> 1) & (LANES - 1)
    odd_lane = (lane & 1) == 1
    for level in (2, 1, 0):
        coarse = level + 1
        corr, state, whole_rows = corrs[coarse], (state0, state1, state2)[level], merged[level]
        count = (LANES >> coarse) + 2
        origin = GUARD + RIM[coarse]
        places = [
            (comp, origin - 1 + SUB * tile)
            for tile in range(-(-count // SUB))
            for comp in range(2)
        ]
        pairs = {
            (comp, at): (tile_at(corr, 2 * comp, at), tile_at(corr, 2 * comp + 1, at))
            for comp, at in places
        }
        moved = {
            place: [lane_take(even, near), lane_take(odd, near)]
            for place, (even, odd) in pairs.items()
        }
        for place, (even, _) in pairs.items():
            moved[place].append(lane_take(even, (near + 1) & (LANES - 1)))
        for place, (_, odd) in pairs.items():
            moved[place].append(lane_take(odd, (near - 1) & (LANES - 1)))
        for (comp, at), (even_here, odd_here, even_next, odd_last) in moved.items():
            rows = slice(at, at + SUB)
            whole_rows[3 * comp, rows, :] = jnp.where(odd_lane, odd_here, even_here)
            whole_rows[3 * comp + 1, rows, :] = jnp.where(odd_lane, even_next, odd_here)
            whole_rows[3 * comp + 2, rows, :] = jnp.where(odd_lane, even_here, odd_last)
        if level > 0:
            first, tiles = -1, -(-count // SUB)
        else:
            first, tiles = 0, (count - 2) // SUB
        for tile in range(tiles):
            coarse_row = first + SUB * tile
            at = origin + coarse_row
            for comp in range(2):
                here, right, left = [tile_at(whole_rows, 3 * comp + k, at) for k in range(3)]
                for parity in range(2):
                    across = tile_at(whole_rows, 3 * comp, at + (1 if parity else -1))
                    found = swept_rows(
                        state, level, coarse_row, parity, here, (left, right), across, comp
                    )
                    if level > 0:
                        rows = pl.ds(GUARD + RIM[level] + 2 * coarse_row + parity, SUB, stride=2)
                        for p in range(2):
                            corrs[level][2 * comp + p, rows, :] = found[p]
                    else:
                        rows = pl.ds(2 * coarse_row + parity, SUB, stride=2)
                        out[comp, rows, :] = jnp.where(
                            odd_lane,
                            lane_take(found[1], lane >> 1),
                            lane_take(found[0], lane >> 1),
                        )


def params():
    return pltpu.CompilerParams(vmem_limit_bytes=VMEM_LIMIT)


VMEM_SPEC = pl.BlockSpec(memory_space=pltpu.VMEM)
SMEM_SPEC = pl.BlockSpec(memory_space=pltpu.SMEM)
HBM_SPEC = pl.BlockSpec(memory_space=pltpu.HBM)


def swap_routes(size_x, size_y):
    def index(i, j):
        return i * size_y + j

    routes = []
    for axis in range(2):
        size = (size_x, size_y)[axis]
        for offset in range(2):
            route = []
            for i in range(size_x):
                for j in range(size_y):
                    here = (i, j)[axis]
                    other = here + 1 if here % 2 == offset else here - 1
                    if 0 <= other < size:
                        peer = (other, j) if axis == 0 else (i, other)
                    else:
                        peer = (i, j ^ 1) if axis == 0 else (i ^ 1, j)
                    route.append((index(i, j), index(*peer)))
            routes.append(route)
    return routes


def per_device(size_x, size_y, right_side, shift_coef, viscosity, wet_tiles):
    axes = ("gx", "gy")
    devices = size_x * size_y
    routes = swap_routes(size_x, size_y)
    band = jax.ShapeDtypeStruct((4 * HALO, LANES), F32)
    held_shape = pltpu.VMEM((4, HELD[0], LANES), F32)
    held, first, second = pl.pallas_call(
        bands_kernel,
        out_shape=(held_shape, band, band),
        in_specs=[SMEM_SPEC] + [HBM_SPEC] * 3,
        out_specs=(VMEM_SPEC,) * 3,
        scratch_shapes=[pltpu.SemaphoreType.DMA((4,))],
        compiler_params=params(),
        name="bands",
    )(
        wet_tiles,
        *[
            pltpu.with_memory_space_constraint(array, pltpu.HBM)
            for array in (right_side, shift_coef, viscosity)
        ],
    )
    second = lax.ppermute(second, axes, routes[1])
    first = lax.ppermute(first, axes, routes[0])
    strip = jax.ShapeDtypeStruct((MESSAGE, LANES), F32)
    got = (second, first)
    first, second = pl.pallas_call(
        functools.partial(strips_kernel, size_x),
        out_shape=(strip, strip),
        in_specs=[SMEM_SPEC] + [VMEM_SPEC] * 3,
        out_specs=(VMEM_SPEC,) * 2,
        compiler_params=params(),
        name="strips",
    )(wet_tiles, *got, held)
    fields = pl.pallas_call(
        functools.partial(halves_kernel, size_x),
        out_shape=pltpu.VMEM((8, HELD[0], LANES), F32),
        in_specs=[SMEM_SPEC] + [VMEM_SPEC] * 3,
        out_specs=VMEM_SPEC,
        cost_estimate=pl.CostEstimate(flops=1 << 20, bytes_accessed=1 << 21, transcendentals=0),
        compiler_params=params(),
        name="halves",
    )(wet_tiles, *got, held)
    second = lax.ppermute(second, axes, routes[3])
    first = lax.ppermute(first, axes, routes[2])

    def buffers(counts):
        return [pltpu.VMEM((n, HELD[level], LANES), F32) for level, n in enumerate(counts)]

    chunks, *states = pl.pallas_call(
        functools.partial(down_kernel, size_y, devices),
        out_shape=(jax.ShapeDtypeStruct((CHUNK * devices, LANES), F32),)
        + tuple(buffers([STATE, STATE, STATE, STATE + 6])),
        in_specs=[VMEM_SPEC] * 3,
        out_specs=(VMEM_SPEC,) * (1 + LOCAL),
        scratch_shapes=buffers([2, 4, 4, 4])
        + buffers([2] * 4)
        + buffers([4, 8, 8, 8])
        + buffers([2, 4, 4, 4])
        + buffers([4] * 4)
        + buffers([4] * 4)
        + [pltpu.VMEM((2, HELD[0], LANES), F32), pltpu.VMEM((4, HELD[3], LANES), F32)],
        compiler_params=params(),
        name="down",
    )(second, first, fields)
    gathered = lax.all_to_all(chunks, axes, 0, 0, tiled=True)
    rows_total = CELLS * size_x
    width = 2 * CELLS * size_y
    return pl.pallas_call(
        functools.partial(up_kernel, size_x, size_y),
        out_shape=jax.ShapeDtypeStruct((2, LANES, LANES), F32),
        in_specs=[VMEM_SPEC] * (1 + LOCAL),
        out_specs=VMEM_SPEC,
        scratch_shapes=[
            pltpu.VMEM((3, width // LANES, rows_total, LANES), F32),
            pltpu.VMEM((6, width // LANES, rows_total + 3 * SUB, LANES), F32),
            pltpu.VMEM((3, rows_total + 2 * SUB, width), F32),
            pltpu.VMEM((6, 5 * SUB, LANES), F32),
            pltpu.VMEM((4, HELD[3], LANES), F32),
        ]
        + [pltpu.VMEM((4, HELD[level], LANES), F32) for level in (1, 2, 3)]
        + [pltpu.VMEM((6, HELD[level + 1], LANES), F32) for level in (0, 1, 2)],
        compiler_params=params(),
        name="up",
    )(gathered, *states)


def solution(mesh):
    sizes = dict(mesh.shape)
    placed = (P(None, "gx", "gy"), P("gx", "gy"), P("gx", "gy"), P("gx", "gy"))
    return jax.shard_map(
        functools.partial(per_device, sizes["gx"], sizes["gy"]),
        mesh=mesh,
        in_specs=placed,
        out_specs=P(None, "gx", "gy"),
        check_vma=False,
    )
```

```python
import functools

import jax
import jax.numpy as jnp
from jax import lax
from jax.experimental import pallas as pl
from jax.experimental.pallas import tpu as pltpu
from jax.sharding import PartitionSpec as P

LOCAL = 4
COARSE = 4
COARSE_SWEEPS = 8
OMEGA = 0.8
KEEP = 1.0 - OMEGA

LANES = 128
HALF = LANES // 2
SUB = 8
HALO = 16
GUARD = 8
CELLS = LANES >> LOCAL
ROWS = [(LANES + 2 * HALO) >> level for level in range(LOCAL)]
TILES = [-(-rows // SUB) for rows in ROWS]
HELD = [GUARD + SUB * tiles + 16 for tiles in TILES]
RIM = [HALO >> level for level in range(LOCAL)]
TOP = GUARD + HALO
LOW = TOP + LANES
HALF_TILES = TILES[0] // 2
MESSAGE = ROWS[0] // 2
CHUNK = 4
F32 = jnp.float32
VMEM_LIMIT = 48 * 1024 * 1024

SWEPT, CENTRE, SIDE, ACROSS = 0, 4, 6, 8
STATE = 10
ITERATE, WEIGHT = 10, 14


def iota(dim, shape=(SUB, LANES)):
    return lax.broadcasted_iota(jnp.int32, shape, dim)


def lane_take(tile, index):
    return jnp.take_along_axis(tile, index, axis=1)


def lane_roll(tile, shift):
    return pltpu.roll(tile, shift % LANES, 1)


def tile_at(ref, slot, row):
    return ref[slot, row : row + SUB, :]


def bands_kernel(wet, right_side, shift_coef, viscosity, first, second, sems):
    odd = lax.axis_index("gx") % 2
    wetness = wet[0, 0].astype(F32)
    bottom = LANES - HALO
    copies = []
    for slot, (start, out) in enumerate(((bottom - bottom * odd, first), (bottom * odd, second))):
        rows = pl.ds(pl.multiple_of(start, SUB), HALO)
        for kind, (source, target) in enumerate(
            (
                (right_side.at[:, rows, :], out.at[0:2]),
                (shift_coef.at[rows, :], out.at[2]),
                (viscosity.at[rows, :], out.at[3]),
            )
        ):
            copies.append(pltpu.make_async_copy(source, target, sems.at[3 * slot + kind]))
    for copy in copies:
        copy.start()
    for copy in copies:
        copy.wait()
    for out in (first, second):
        for field in (0, 1, 3):
            out[field] = out[field] * wetness


def own_rows(right_side, shift_coef, viscosity, field, tile):
    rows = slice(SUB * tile, SUB * tile + SUB)
    if field < 2:
        return right_side[field, rows, :]
    return shift_coef[rows, :] if field == 2 else viscosity[rows, :]


def rim_place(half, lane):
    to_left = ((lane >> 3) & 1) == half
    q = jnp.where(to_left, lane, (lane - (56 + 8 * half)) & (LANES - 1)) >> 4
    cell = 2 * (lane & 7) + (q & 1) + jnp.where(to_left, 0, LANES - HALO)
    return to_left, q >> 1, cell


def strips_kernel(
    size_x, wet, got_second, got_first, right_side, shift_coef, viscosity, first, second
):
    index_x = lax.axis_index("gx")
    odd_x = index_x % 2 == 1
    odd_y = lax.axis_index("gy") % 2 == 1
    wetness = wet[0, 0].astype(F32)
    above = (index_x > 0).astype(F32)
    below = (index_x < size_x - 1).astype(F32)
    lane = iota(1)
    rim_tiles = HALO // SUB

    def piece(field, tile):
        if rim_tiles <= tile < TILES[0] - rim_tiles:
            return own_rows(right_side, shift_coef, viscosity, field, tile - rim_tiles)
        top = tile < rim_tiles
        row = SUB * (tile if top else tile - (TILES[0] - rim_tiles))
        one, two = tile_at(got_first, field, row), tile_at(got_second, field, row)
        return jnp.where(odd_x, one, two) if top else jnp.where(odd_x, two, one)

    places = [rim_place(half, lane) for half in range(2)]
    found = {}
    for half in range(2):
        _, owner, cell = places[half]
        for tile in range(HALF_TILES):
            at = tile + half * HALF_TILES
            value = None
            for field in range(4):
                part = lane_take(piece(field, at), cell)
                value = part if value is None else jnp.where(owner == field, part, value)
            if rim_tiles <= at < TILES[0] - rim_tiles:
                value = value * jnp.where(owner == 2, 1.0, wetness)
            else:
                value = value * jnp.where(owner == 3, above if at < rim_tiles else below, 1.0)
            found[half, tile] = value
    for tile in range(HALF_TILES):
        left = jnp.where(places[0][0], found[0, tile], found[1, tile])
        right = jnp.where(places[0][0], found[1, tile], found[0, tile])
        rows = slice(SUB * tile, SUB * tile + SUB)
        first[rows, :] = jnp.where(odd_y, left, right)
        second[rows, :] = jnp.where(odd_y, right, left)


def halves_kernel(
    size_x, wet, got_second, got_first, right_side, shift_coef, viscosity, fields
):
    index_x = lax.axis_index("gx")
    odd_x = index_x % 2 == 1
    wetness = wet[0, 0].astype(F32)
    above = (index_x > 0).astype(F32)
    below = (index_x < size_x - 1).astype(F32)
    lane = iota(1)
    rim_tiles = HALO // SUB
    for tile in range(TILES[0]):
        row = GUARD + SUB * tile
        for field in range(4):
            if rim_tiles <= tile < TILES[0] - rim_tiles:
                value = own_rows(right_side, shift_coef, viscosity, field, tile - rim_tiles)
                if field != 2:
                    value = value * wetness
            else:
                top = tile < rim_tiles
                at = SUB * (tile if top else tile - (TILES[0] - rim_tiles))
                one, two = tile_at(got_first, field, at), tile_at(got_second, field, at)
                value = jnp.where(odd_x, one, two) if top else jnp.where(odd_x, two, one)
                if field == 3:
                    value = value * (above if top else below)
            for parity in range(2):
                fields[2 * field + parity, row : row + SUB, :] = lane_take(
                    value, (2 * lane + parity) & (LANES - 1)
                )


def down_kernel(size_y, devices, got_second, got_first, held, chunks, *refs):
    states, refs = refs[:LOCAL], refs[LOCAL:]
    viscous, refs = refs[:LOCAL], refs[LOCAL:]
    reactions, refs = refs[:LOCAL], refs[LOCAL:]
    sources, refs = refs[:LOCAL], refs[LOCAL:]
    weights, refs = refs[:LOCAL], refs[LOCAL:]
    iterates, refs = refs[:LOCAL], refs[LOCAL:]
    sums, (outers, ring) = refs[:LOCAL], refs[LOCAL:]
    index_y = lax.axis_index("gy")
    odd_y = index_y % 2 == 1
    lane, sub = iota(1), iota(0)
    side_ok = jnp.where(
        lane < 96, (index_y < size_y - 1).astype(F32), (index_y > 0).astype(F32)
    )
    odd_row = (sub & 1) == 1
    inner = lane < HALF
    even_block = ((lane >> 3) & 1) == 0

    def tiles(level):
        return [GUARD + SUB * tile for tile in range(TILES[level])]

    def put(ref, slot, row, value):
        ref[slot, row : row + SUB, :] = value

    def rims(row, slots):
        half, at = divmod((row - GUARD) // SUB, HALF_TILES)
        one, two = (r[SUB * at : SUB * at + SUB, :] for r in (got_first, got_second))
        after, before = jnp.where(odd_y, two, one), jnp.where(odd_y, one, two)
        if half == 0:
            both = jnp.where(even_block, after, before)
        else:
            both = jnp.where(even_block, before, after)
        values = []
        for slot in slots:
            rim = lane_roll(both, HALF - 16 * slot - 8 * half)
            if slot >= 4:
                rim = jnp.where(side_ok > 0, rim, 1.0 if slot < 6 else 0.0)
            values.append(jnp.where(inner, tile_at(held, slot, row), rim))
        return values

    def paired(ref, slot, start):
        return (
            ref[slot, pl.ds(start, SUB, stride=2), :] + ref[slot, pl.ds(start + 1, SUB, stride=2), :]
        )

    takes = [(2 * lane + offset) & (LANES - 1) for offset in (0, 1, -1, 2)]

    def coefficients(level):
        if level == 0:
            for row in tiles(level):
                values = rims(row, (4, 5, 6, 7))
                for slot, value in enumerate(values[:2]):
                    put(reactions[level], slot, row, value)
                for slot, value in enumerate(values[2:]):
                    put(viscous[level], slot, row, value)
                put(sums[level], 2, row, values[0] + values[1])
                put(sums[level], 3, row, values[2] + values[3])
            return
        ref = sums[level - 1]
        loaded = {
            row: [
                scale * paired(ref, slot, GUARD + 2 * (row - GUARD))
                for slot, scale in ((2, 0.25), (3, 0.0625))
            ]
            for row in tiles(level)
        }
        found = {row: ([], []) for row in loaded}
        for kind, index in enumerate(takes):
            for row, (reaction, viscosity) in loaded.items():
                value = lane_take(viscosity, index)
                put(viscous[level], kind, row, value)
                found[row][1].append(value)
                if kind < 2:
                    value = lane_take(reaction, index)
                    put(reactions[level], kind, row, value)
                    found[row][0].append(value)
        for row, (reaction, viscosity) in found.items():
            put(sums[level], 2, row, reaction[0] + reaction[1])
            put(sums[level], 3, row, viscosity[0] + viscosity[1])

    def faces(level, row):
        here = [tile_at(viscous[level], p, row) for p in range(2)]
        north = [jnp.minimum(here[p], tile_at(viscous[level], p, row - 1)) for p in range(2)]
        south = [jnp.minimum(here[p], tile_at(viscous[level], p, row + 1)) for p in range(2)]
        return here, jnp.minimum(here[0], here[1]), north, south

    def outside(level, row, here):
        if level == 0:
            beyond = [lane_roll(here[1], 1), lane_roll(here[0], -1)]
        else:
            beyond = [tile_at(viscous[level], 2 + p, row) for p in range(2)]
        return [jnp.minimum(h, b) for h, b in zip(here, beyond)]

    def weigh(level):
        for row in tiles(level):
            here, middle, north, south = faces(level, row)
            outer = outside(level, row, here)
            found = []
            for p in range(2):
                diagonal = tile_at(reactions[level], p, row) + (
                    (middle + outer[p]) + (north[p] + south[p])
                )
                found.append(OMEGA / diagonal)
                if level == 0:
                    put(outers, p, row, outer[p])
            if level > 0:
                found += [lane_roll(found[1], 1), lane_roll(found[0], -1)]
            for slot, value in enumerate(found):
                put(weights[level], slot, row, value)

    def take_sources(level):
        if level == 0:
            for row in tiles(level):
                for slot, value in enumerate(rims(row, (0, 1, 2, 3))):
                    put(sources[level], slot, row, value)
            return
        loaded = {
            row: [
                0.25 * paired(sums[level - 1], comp, GUARD + 2 * (row - GUARD))
                for comp in range(2)
            ]
            for row in tiles(level)
        }
        for kind, index in enumerate(takes):
            for row, values in loaded.items():
                for comp in range(2):
                    put(sources[level], 4 * comp + kind, row, lane_take(values[comp], index))

    def kinds(level):
        return 2 if level == 0 else 4

    def first_sweep(level):
        for row in tiles(level):
            for comp in range(2):
                for p in range(2):
                    put(
                        iterates[level],
                        2 * comp + p,
                        row,
                        tile_at(weights[level], p, row)
                        * tile_at(sources[level], kinds(level) * comp + p, row),
                    )

    def residual(level):
        state, iterate, weight, source = (
            states[level],
            iterates[level],
            weights[level],
            sources[level],
        )
        for row in tiles(level):
            _, middle, north, south = faces(level, row)
            if level == 0:
                outer = [tile_at(outers, p, row) for p in range(2)]
            else:
                outer = outside(level, row, [tile_at(viscous[level], p, row) for p in range(2)])
            scale = [tile_at(weight, p, row) for p in range(2)]
            kept = level > 0 or TOP <= row < LOW
            for comp in range(2):
                here = [tile_at(iterate, 2 * comp + p, row) for p in range(2)]
                if level == 0:
                    beyond = [lane_roll(here[1], 1), lane_roll(here[0], -1)]
                else:
                    beyond = [
                        tile_at(weight, 2 + p, row) * tile_at(source, 4 * comp + 2 + p, row)
                        for p in range(2)
                    ]
                total = None
                for p in range(2):
                    slot = 2 * comp + p
                    around = middle * here[1 - p] + outer[p] * beyond[p]
                    around = around + (
                        south[p] * tile_at(iterate, slot, row + 1)
                        + north[p] * tile_at(iterate, slot, row - 1)
                    )
                    left = KEEP * tile_at(source, kinds(level) * comp + p, row) + around
                    if kept:
                        put(state, SWEPT + slot, row, here[p] + scale[p] * left)
                    if level == LOCAL - 1:
                        put(ring, slot, row, left)
                        put(state, ITERATE + slot, row, here[p])
                    total = left if total is None else total + left
                put(sums[level], comp, row, total)
            if kept:
                for p in range(2):
                    within = jnp.where(odd_row, north[p], south[p])
                    across = jnp.where(odd_row, south[p], north[p])
                    put(state, CENTRE + p, row, KEEP + scale[p] * (middle + within))
                    put(state, SIDE + p, row, scale[p] * outer[p])
                    put(state, ACROSS + p, row, scale[p] * across)
                    if level == LOCAL - 1:
                        put(state, WEIGHT + p, row, scale[p])

    coefficients(0)
    take_sources(0)
    weigh(0)
    coefficients(1)
    first_sweep(0)
    residual(0)
    weigh(1)
    coefficients(2)
    take_sources(1)
    weigh(2)
    coefficients(3)
    first_sweep(1)
    residual(1)
    take_sources(2)
    weigh(3)
    first_sweep(2)
    residual(2)
    take_sources(3)
    first_sweep(3)
    residual(3)

    start = GUARD + RIM[LOCAL - 1]
    column = lane & (SUB - 1)
    own = [
        lane_take(scale * paired(sums[LOCAL - 1], slot, start), column)
        for slot, scale in enumerate((0.25, 0.25, 0.25, 0.0625))
    ]
    turned = ((lane >> 3) - index_y) & 15
    chosen = (turned & (SUB - 1)) == sub

    def packed(value):
        return jnp.sum(value, axis=0, keepdims=True)

    def joined(a, b):
        return packed(jnp.where(chosen, jnp.where(turned < SUB, a, b), 0.0))

    edge = (lane >> 4) & 3
    place = lane & 15

    rims = jnp.zeros((SUB, LANES), F32)
    for p in range(2):
        index = jnp.where(edge < 2, column, 0 if p == 0 else SUB - 1)
        for part in range(2):
            along = (edge == part) & ((place >> 3) == p) & (sub == (0 if part == 0 else SUB - 1))
            up = (edge == 2 + p) & (place == sub + SUB * part)
            row = start + SUB * part
            value = jnp.where(
                inner,
                lane_take(tile_at(ring, p, row), index),
                lane_take(tile_at(ring, 2 + p, row), index),
            )
            rims = jnp.where(along | up, value, rims)
    kind = sub % CHUNK
    parts = [joined(own[0], own[1]), joined(own[2], own[2]), packed(rims), joined(own[3], own[3])]
    tile = jnp.where(
        kind < 2,
        jnp.where(kind == 0, parts[0], parts[1]),
        jnp.where(kind == 2, parts[2], parts[3]),
    )
    for block in range(CHUNK * devices // SUB):
        chunks[SUB * block : SUB * block + SUB, :] = tile


def write(buffer, slot, rows, value):
    for column in range(buffer.shape[1]):
        buffer[slot, column, rows, :] = value[:, LANES * column : LANES * column + LANES]


def read(buffer, slot, rows):
    parts = [buffer[slot, column, rows, :] for column in range(buffer.shape[1])]
    return parts[0] if len(parts) == 1 else jnp.concatenate(parts, 1)


class Coarse:
    def __init__(self, step, row_step, rows, cols_total, width):
        self.step, self.row_step = step, row_step
        self.shape = (rows, width)
        lane, row = iota(1, self.shape), iota(0, self.shape)
        column = lane & (cols_total - 1)
        self.odd_lane, self.odd_row = (lane & step) != 0, (row & row_step) != 0
        self.leftmost = column < 2 * step
        self.rightmost = column >= cols_total - 2 * step
        self.top, self.bottom = row < row_step, row >= rows - row_step

    def along(self, value, amount):
        return pltpu.roll(value, amount % self.shape[1], 1)

    def down(self, value, amount):
        return pltpu.roll(value, amount % self.shape[0], 0)

    def paired(self, value):
        return (
            jnp.where(self.odd_lane, self.along(value, self.step), value),
            jnp.where(self.odd_lane, value, self.along(value, -self.step)),
        )

    def outside(self, value):
        return (
            jnp.where(
                self.odd_lane, self.along(value, 2 * self.step), self.along(value, self.step)
            ),
            jnp.where(
                self.odd_lane, self.along(value, -self.step), self.along(value, -2 * self.step)
            ),
        )

    def farther(self, value):
        return (
            jnp.where(
                self.odd_lane, self.along(value, 3 * self.step), self.along(value, 2 * self.step)
            ),
            jnp.where(
                self.odd_lane, self.along(value, -2 * self.step), self.along(value, -3 * self.step)
            ),
        )

    def rows_beside(self, here):
        above = jnp.where(self.top, 0.0, self.down(here, self.row_step))
        below = jnp.where(self.bottom, 0.0, self.down(here, -self.row_step))
        return jnp.minimum(here, above), jnp.minimum(here, below)

    def coefficients(self, viscous, reaction):
        here, beyond, far = self.paired(viscous), self.outside(viscous), self.farther(viscous)
        reactions, reactions_beyond = self.paired(reaction), self.outside(reaction)
        edges = (self.leftmost, self.rightmost)
        self.middle = jnp.minimum(here[0], here[1])
        self.outer, self.north, self.south = [], [], []
        self.weights, self.weights_beyond = [], []
        for p in range(2):
            outer = jnp.minimum(here[p], jnp.where(edges[p], 0.0, beyond[p]))
            north, south = self.rows_beside(here[p])
            diagonal = reactions[p] + ((self.middle + outer) + (north + south))
            self.weights.append(OMEGA / diagonal)
            self.outer.append(outer)
            self.north.append(north)
            self.south.append(south)
            next_outer = jnp.minimum(beyond[p], far[p])
            north, south = self.rows_beside(beyond[p])
            diagonal = reactions_beyond[p] + ((outer + next_outer) + (north + south))
            self.weights_beyond.append(OMEGA / diagonal)
        return here[0] + here[1], reactions[0] + reactions[1]

    def take(self, source):
        self.values, self.values_beyond = self.paired(source), self.outside(source)

    def residual(self):
        x = [w * s for w, s in zip(self.weights, self.values)]
        x_beyond = [w * s for w, s in zip(self.weights_beyond, self.values_beyond)]
        total, self.swept = None, []
        for p in range(2):
            around = self.middle * x[1 - p] + self.outer[p] * x_beyond[p]
            around = around + (
                self.south[p] * self.down(x[p], -self.row_step)
                + self.north[p] * self.down(x[p], self.row_step)
            )
            left = KEEP * self.values[p] + around
            self.swept.append(x[p] + self.weights[p] * left)
            total = left if total is None else total + left
        return total

    def prepare(self):
        parts = []
        for p in range(2):
            within = jnp.where(self.odd_row, self.north[p], self.south[p])
            out = jnp.where(self.odd_row, self.south[p], self.north[p])
            weight = self.weights[p]
            centre = KEEP + weight * (self.middle + within)
            parts.append((self.swept[p], centre, weight * self.outer[p], weight * out))
        self.parts = parts
        self.left_parts = [self.along(value, 2 * self.step) for value in parts[1]]
        self.right_parts = [self.along(value, -2 * self.step) for value in parts[0]]

    def corrected(self, here, left, right):
        def swept(part, own, side):
            return (part[0] + part[1] * own[0]) + (part[2] * side[0] + part[3] * own[1])

        even, odd = swept(self.parts[0], here, left), swept(self.parts[1], here, right)
        before, after = swept(self.left_parts, left, here), swept(self.right_parts, right, here)
        return (
            jnp.where(self.odd_lane, odd, even),
            jnp.where(self.odd_lane, even, before),
            jnp.where(self.odd_lane, after, odd),
        )


def coarse_solve(grid, buffer, rows_total, cols_total, width, meanwhile):
    columns = width // LANES

    def whole(slot):
        return jnp.concatenate([grid[slot, c] for c in range(columns)], 1) if columns > 1 else grid[slot, 0]

    levels, rows, row_step = [], rows_total, 1
    for index in range(COARSE + 1):
        levels.append(Coarse(1 << index, row_step, rows, cols_total, width))
        if rows > SUB:
            rows //= 2
        else:
            row_step *= 2

    def folded(index, value, slot, scale):
        level = levels[index]
        rows = level.shape[0]
        if levels[index + 1].shape[0] == rows:
            other = jnp.where(
                level.odd_row, level.down(value, level.row_step), level.down(value, -level.row_step)
            )
            return scale * (value + other)
        write(buffer, slot, slice(0, rows), value)
        first, second = [pl.ds(begin, rows // 2, stride=2) for begin in range(2)]
        return scale * (read(buffer, slot, first) + read(buffer, slot, second))

    def opened(index, value, slot):
        level = levels[index]
        rows = level.shape[0]
        if value.shape[0] == rows:
            return value, jnp.where(
                level.odd_row, level.down(value, -level.row_step), level.down(value, level.row_step)
            )
        half = rows // 2
        blank = jnp.zeros((SUB, width), F32)
        for begin in range(2):
            write(buffer, slot, pl.ds(begin, half, stride=2), value)
        write(buffer, slot + 1, slice(SUB, 2 * SUB), blank)
        write(buffer, slot + 1, slice(rows, rows + SUB), blank)
        for begin in (SUB + 2, SUB - 1):
            write(buffer, slot + 1, pl.ds(begin, half, stride=2), value)
        return read(buffer, slot, slice(0, rows)), read(buffer, slot + 1, slice(SUB, SUB + rows))

    viscous, reaction, source = [None] * 5, [None] * 5, [None] * 5
    viscous[0], reaction[0], source[0] = whole(2), whole(1), whole(0)

    def coefficients(index):
        pair, reactions = levels[index].coefficients(viscous[index], reaction[index])
        viscous[index + 1] = folded(index, pair, 0, 0.0625)
        reaction[index + 1] = folded(index, reactions, 1, 0.25)

    def residual(index):
        source[index + 1] = folded(index, levels[index].residual(), 2, 0.25)

    last = levels[COARSE]
    block = 1 << COARSE
    cols_left = cols_total // block
    rows_left = last.shape[0]
    lane = iota(1, (rows_left, LANES))
    groups = 1 if cols_total < LANES else 2
    per_group = columns // groups

    def spread(*arrays):
        found = [[] for _ in arrays]
        for group in range(groups):
            for j in range(cols_left):
                column, place = divmod(block * j, LANES)
                column += group * per_group
                if groups == 1:
                    place = place + (lane & (LANES - cols_total))
                else:
                    place = jnp.full((rows_left, LANES), place, jnp.int32)
                for value, columns_found in zip(arrays, found):
                    tile = value[:, LANES * column : LANES * column + LANES]
                    columns_found.append(lane_take(tile, place))
        return found

    def flat(values, group, j):
        return values[group * cols_left + j]

    levels[0].take(source[0])
    coefficients(0)
    coefficients(1)
    residual(0)
    levels[1].take(source[1])
    coefficients(2)
    residual(1)
    levels[2].take(source[2])
    coefficients(3)
    residual(2)
    levels[3].take(source[3])
    viscous_columns, reaction_columns = spread(viscous[4], reaction[4])

    top, bottom = last.top[:, :LANES], last.bottom[:, :LANES]
    pulls, weights = [], []
    for group in range(groups):
        for j in range(cols_left):
            here = flat(viscous_columns, group, j)
            above = jnp.where(top, 0.0, last.down(here, last.row_step))
            below = jnp.where(bottom, 0.0, last.down(here, -last.row_step))
            links = [jnp.minimum(here, above), jnp.minimum(here, below)]
            links += [
                jnp.minimum(here, flat(viscous_columns, group, other))
                for other in (j - 1, j + 1)
                if 0 <= other < cols_left
            ]
            weight = OMEGA / (flat(reaction_columns, group, j) + sum(links))
            weights.append(weight)
            pulls.append([weight * link for link in links])
    residual(3)
    pushed = [w * s for w, s in zip(weights, spread(source[4])[0])]
    meanwhile()
    for index in range(COARSE - 1, -1, -1):
        levels[index].prepare()
    values = pushed
    for _ in range(COARSE_SWEEPS - 1):
        following = []
        for group in range(groups):
            for j in range(cols_left):
                at = group * cols_left + j
                here, pull = values[at], pulls[at]
                total = (KEEP * here + pushed[at]) + (
                    pull[0] * last.down(here, last.row_step)
                    + pull[1] * last.down(here, -last.row_step)
                )
                sides = [other for other in (j - 1, j + 1) if 0 <= other < cols_left]
                for link, other in zip(pull[2:], sides):
                    total = total + link * flat(values, group, other)
                following.append(total)
        values = following

    def laid(shift):
        found = []
        for column in range(columns):
            group = column // per_group
            place = ((lane & (cols_total - 1)) if groups == 1 else lane) // block
            place = place + (column % per_group) * (LANES // block)
            value = jnp.zeros((rows_left, LANES), F32)
            for j in range(cols_left):
                value = jnp.where(place == j + shift, flat(values, group, j), value)
            found.append(value)
        return found[0] if columns == 1 else jnp.concatenate(found, 1)

    corrections = [laid(shift) for shift in (0, 1, -1)]
    for index in range(COARSE - 1, -1, -1):
        corrections = levels[index].corrected(
            *[opened(index, value, 2 * at) for at, value in enumerate(corrections)]
        )
    return corrections


def up_kernel(size_x, size_y, gathered, state0, state1, state2, state3, out, *refs):
    grid, buffer, whole, window, swept3, corr1, corr2, corr3, merged0, merged1, merged2 = refs
    index_x, index_y = lax.axis_index("gx"), lax.axis_index("gy")
    rows_total, cols_total = CELLS * size_x, CELLS * size_y
    width = 2 * cols_total
    columns = width // LANES
    per_column = LANES // CELLS
    lane, sub = iota(1), iota(0)

    tall = iota(1, (size_x, LANES)) // CELLS
    modulus = min(size_y, per_column)
    for column in range(columns):
        comp = column // (columns // 2) if columns > 1 else 0
        first = (column % (columns // 2)) * per_column if columns > 1 else 0
        for slot, kind in ((2, 3), (1, 1), (0, 0)):
            chunks = [
                gathered[pl.ds(CHUNK * (first + j) + kind, size_x, stride=CHUNK * size_y), :]
                for j in range(modulus)
            ]
            for r in range(CELLS):
                turn = r + CELLS * comp
                value = chunks[0]
                for j in range(1, modulus):
                    value = jnp.where(((tall - turn) & (modulus - 1)) == j, chunks[j], value)
                grid[slot, column, pl.ds(r, size_x, stride=CELLS), :] = lane_roll(
                    value, -CELLS * turn
                )

    def ring_row(dx, dy):
        i = jnp.clip(index_x + dx, 0, size_x - 1)
        j = jnp.clip(index_y + dy, 0, size_y - 1)
        return jnp.broadcast_to(
            gathered[pl.ds(CHUNK * (i * size_y + j) + 2, 1), :], (SUB, LANES)
        )

    start = GUARD + RIM[3]

    def complete_ring():
        beside = {
            (dx, dy): ring_row(dx, dy) for dx in (-1, 0, 1) for dy in (-1, 0, 1) if dx or dy
        }
        for comp in range(2):
            base = comp * HALF
            for p in range(2):
                slot = 2 * comp + p
                end = 7 if p else 0
                corner_lane = LANES - 1 if p else SUB
                dy = -1 if p else 1
                for tile in range(2):
                    at = start + SUB * tile
                    index = base + (48 if p else 32) + SUB * tile + sub
                    ringed = lane_take(beside[0, dy], index)
                    swept = jnp.where(
                        lane == corner_lane,
                        tile_at(state3, ITERATE + slot, at)
                        + tile_at(state3, WEIGHT + p, at) * ringed,
                        tile_at(state3, SWEPT + slot, at),
                    )
                    swept3[slot, at : at + SUB, :] = swept
                for dx, at, edge in ((-1, start - 1, 16), (1, start + 2 * SUB, 0)):
                    index = base + edge + 8 * p
                    ringed = jnp.where(
                        lane == corner_lane,
                        lane_take(beside[dx, dy], jnp.full((SUB, LANES), index + end, jnp.int32)),
                        lane_take(beside[dx, 0], index + (lane & 7)),
                    )
                    rows = slice(at, at + 1)
                    swept3[slot, rows, :] = (
                        state3[ITERATE + slot, rows, :] + state3[WEIGHT + p, rows, :] * ringed[0:1]
                    )

    corrections = coarse_solve(grid, buffer, rows_total, cols_total, width, complete_ring)

    blank = jnp.zeros((SUB, width), F32)
    for kind, correction in enumerate(corrections):
        whole[kind, GUARD : GUARD + rows_total, :] = correction
        whole[kind, 0:GUARD, :] = blank
        whole[kind, GUARD + rows_total : GUARD + rows_total + SUB, :] = blank
    near_rows = pl.ds(pl.multiple_of(CELLS * index_x, SUB), 3 * SUB)
    for comp in range(2):
        shift = (2 * width - cols_total * comp - CELLS * index_y) % width
        for kind in range(3):
            turned = pltpu.roll(whole[kind, near_rows, :], shift, 1)
            if columns > 1:
                tall_lane = iota(1, (3 * SUB, LANES))
                turned = jnp.where(
                    tall_lane < HALF, turned[:, :LANES], turned[:, width - LANES :]
                )
            window[3 * comp + kind, 0 : 3 * SUB, :] = turned

    def swept_rows(ref, level, coarse_row, parity, here, beyond, across, comp):
        at = pl.ds(GUARD + RIM[level] + 2 * coarse_row + parity, SUB, stride=2)
        state = (state0, state1, state2, state3)[level]
        return [
            (ref[SWEPT + 2 * comp + p, at, :] + state[CENTRE + p, at, :] * here)
            + (state[SIDE + p, at, :] * beyond[p] + state[ACROSS + p, at, :] * across)
            for p in range(2)
        ]

    for comp in range(2):
        for tile in range(2):
            first = SUB * tile - 1
            at = GUARD + first
            here, left, right = [tile_at(window, 3 * comp + kind, at) for kind in range(3)]
            for parity in range(2):
                across = tile_at(window, 3 * comp, at + (1 if parity else -1))
                found = swept_rows(swept3, 3, first, parity, here, (left, right), across, comp)
                rows = pl.ds(GUARD + RIM[3] + 2 * first + parity, SUB, stride=2)
                for p in range(2):
                    corr3[2 * comp + p, rows, :] = found[p]

    corrs = [None, corr1, corr2, corr3]
    merged = [merged0, merged1, merged2]
    near = ((((lane + 32) & (LANES - 1)) - 32) >> 1) & (LANES - 1)
    odd_lane = (lane & 1) == 1
    for level in (2, 1, 0):
        coarse = level + 1
        corr, state, whole_rows = corrs[coarse], (state0, state1, state2)[level], merged[level]
        count = (LANES >> coarse) + 2
        origin = GUARD + RIM[coarse]
        places = [
            (comp, origin - 1 + SUB * tile)
            for tile in range(-(-count // SUB))
            for comp in range(2)
        ]
        pairs = {
            (comp, at): (tile_at(corr, 2 * comp, at), tile_at(corr, 2 * comp + 1, at))
            for comp, at in places
        }
        moved = {
            place: [lane_take(even, near), lane_take(odd, near)]
            for place, (even, odd) in pairs.items()
        }
        for place, (even, _) in pairs.items():
            moved[place].append(lane_take(even, (near + 1) & (LANES - 1)))
        for place, (_, odd) in pairs.items():
            moved[place].append(lane_take(odd, (near - 1) & (LANES - 1)))
        for (comp, at), (even_here, odd_here, even_next, odd_last) in moved.items():
            rows = slice(at, at + SUB)
            whole_rows[3 * comp, rows, :] = jnp.where(odd_lane, odd_here, even_here)
            whole_rows[3 * comp + 1, rows, :] = jnp.where(odd_lane, even_next, odd_here)
            whole_rows[3 * comp + 2, rows, :] = jnp.where(odd_lane, even_here, odd_last)
        if level > 0:
            first, tiles = -1, -(-count // SUB)
        else:
            first, tiles = 0, (count - 2) // SUB
        for tile in range(tiles):
            coarse_row = first + SUB * tile
            at = origin + coarse_row
            for comp in range(2):
                here, right, left = [tile_at(whole_rows, 3 * comp + k, at) for k in range(3)]
                for parity in range(2):
                    across = tile_at(whole_rows, 3 * comp, at + (1 if parity else -1))
                    found = swept_rows(
                        state, level, coarse_row, parity, here, (left, right), across, comp
                    )
                    if level > 0:
                        rows = pl.ds(GUARD + RIM[level] + 2 * coarse_row + parity, SUB, stride=2)
                        for p in range(2):
                            corrs[level][2 * comp + p, rows, :] = found[p]
                    else:
                        rows = pl.ds(2 * coarse_row + parity, SUB, stride=2)
                        out[comp, rows, :] = jnp.where(
                            odd_lane,
                            lane_take(found[1], lane >> 1),
                            lane_take(found[0], lane >> 1),
                        )


def params():
    return pltpu.CompilerParams(vmem_limit_bytes=VMEM_LIMIT)


VMEM_SPEC = pl.BlockSpec(memory_space=pltpu.VMEM)
SMEM_SPEC = pl.BlockSpec(memory_space=pltpu.SMEM)
HBM_SPEC = pl.BlockSpec(memory_space=pltpu.HBM)


def swap_routes(size_x, size_y):
    def index(i, j):
        return i * size_y + j

    routes = []
    for axis in range(2):
        size = (size_x, size_y)[axis]
        for offset in range(2):
            route = []
            for i in range(size_x):
                for j in range(size_y):
                    here = (i, j)[axis]
                    other = here + 1 if here % 2 == offset else here - 1
                    if 0 <= other < size:
                        peer = (other, j) if axis == 0 else (i, other)
                    else:
                        peer = (i, j ^ 1) if axis == 0 else (i ^ 1, j)
                    route.append((index(i, j), index(*peer)))
            routes.append(route)
    return routes


def per_device(size_x, size_y, right_side, shift_coef, viscosity, wet_tiles):
    axes = ("gx", "gy")
    devices = size_x * size_y
    routes = swap_routes(size_x, size_y)
    band = pltpu.VMEM((4, HALO, LANES), F32)
    own = (right_side, shift_coef, viscosity)
    first, second = pl.pallas_call(
        bands_kernel,
        out_shape=(band, band),
        in_specs=[SMEM_SPEC] + [HBM_SPEC] * 3,
        out_specs=(VMEM_SPEC,) * 2,
        scratch_shapes=[pltpu.SemaphoreType.DMA((6,))],
        compiler_params=params(),
        name="bands",
    )(wet_tiles, *[pltpu.with_memory_space_constraint(array, pltpu.HBM) for array in own])
    second = lax.ppermute(second, axes, routes[1])
    first = lax.ppermute(first, axes, routes[0])
    strip = jax.ShapeDtypeStruct((MESSAGE, LANES), F32)
    got = (second, first)
    first, second = pl.pallas_call(
        functools.partial(strips_kernel, size_x),
        out_shape=(strip, strip),
        in_specs=[SMEM_SPEC] + [VMEM_SPEC] * 5,
        out_specs=(VMEM_SPEC,) * 2,
        compiler_params=params(),
        name="strips",
    )(wet_tiles, *got, *own)
    fields = pl.pallas_call(
        functools.partial(halves_kernel, size_x),
        out_shape=pltpu.VMEM((8, HELD[0], LANES), F32),
        in_specs=[SMEM_SPEC] + [VMEM_SPEC] * 5,
        out_specs=VMEM_SPEC,
        cost_estimate=pl.CostEstimate(flops=1 << 20, bytes_accessed=1 << 21, transcendentals=0),
        compiler_params=params(),
        name="halves",
    )(wet_tiles, *got, *own)
    second = lax.ppermute(second, axes, routes[3])
    first = lax.ppermute(first, axes, routes[2])

    def buffers(counts):
        return [pltpu.VMEM((n, HELD[level], LANES), F32) for level, n in enumerate(counts)]

    chunks, *states = pl.pallas_call(
        functools.partial(down_kernel, size_y, devices),
        out_shape=(jax.ShapeDtypeStruct((CHUNK * devices, LANES), F32),)
        + tuple(buffers([STATE, STATE, STATE, STATE + 6])),
        in_specs=[VMEM_SPEC] * 3,
        out_specs=(VMEM_SPEC,) * (1 + LOCAL),
        scratch_shapes=buffers([2, 4, 4, 4])
        + buffers([2] * 4)
        + buffers([4, 8, 8, 8])
        + buffers([2, 4, 4, 4])
        + buffers([4] * 4)
        + buffers([4] * 4)
        + [pltpu.VMEM((2, HELD[0], LANES), F32), pltpu.VMEM((4, HELD[3], LANES), F32)],
        compiler_params=params(),
        name="down",
    )(second, first, fields)
    gathered = lax.all_to_all(chunks, axes, 0, 0, tiled=True)
    rows_total = CELLS * size_x
    width = 2 * CELLS * size_y
    return pl.pallas_call(
        functools.partial(up_kernel, size_x, size_y),
        out_shape=jax.ShapeDtypeStruct((2, LANES, LANES), F32),
        in_specs=[VMEM_SPEC] * (1 + LOCAL),
        out_specs=VMEM_SPEC,
        scratch_shapes=[
            pltpu.VMEM((3, width // LANES, rows_total, LANES), F32),
            pltpu.VMEM((6, width // LANES, rows_total + 3 * SUB, LANES), F32),
            pltpu.VMEM((3, rows_total + 2 * SUB, width), F32),
            pltpu.VMEM((6, 5 * SUB, LANES), F32),
            pltpu.VMEM((4, HELD[3], LANES), F32),
        ]
        + [pltpu.VMEM((4, HELD[level], LANES), F32) for level in (1, 2, 3)]
        + [pltpu.VMEM((6, HELD[level + 1], LANES), F32) for level in (0, 1, 2)],
        compiler_params=params(),
        name="up",
    )(gathered, *states)


def solution(mesh):
    sizes = dict(mesh.shape)
    placed = (P(None, "gx", "gy"), P("gx", "gy"), P("gx", "gy"), P("gx", "gy"))
    return jax.shard_map(
        functools.partial(per_device, sizes["gx"], sizes["gy"]),
        mesh=mesh,
        in_specs=placed,
        out_specs=P(None, "gx", "gy"),
        check_vma=False,
    )
```

```python
import functools

import jax
import jax.numpy as jnp
from jax import lax
from jax.experimental import pallas as pl
from jax.experimental.pallas import tpu as pltpu
from jax.sharding import PartitionSpec as P

LOCAL = 4
COARSE = 4
COARSE_SWEEPS = 8
OMEGA = 0.8
KEEP = 1.0 - OMEGA

LANES = 128
HALF = LANES // 2
SUB = 8
HALO = 16
GUARD = 8
CELLS = LANES >> LOCAL
ROWS = [(LANES + 2 * HALO) >> level for level in range(LOCAL)]
TILES = [-(-rows // SUB) for rows in ROWS]
HELD = [GUARD + SUB * tiles + 16 for tiles in TILES]
RIM = [HALO >> level for level in range(LOCAL)]
TOP = GUARD + HALO
LOW = TOP + LANES
HALF_TILES = TILES[0] // 2
MESSAGE = ROWS[0] // 2
CHUNK = 4
PIECES = (4, 8)
F32 = jnp.float32
VMEM_LIMIT = 48 * 1024 * 1024

SWEPT, CENTRE, SIDE, ACROSS = 0, 4, 6, 8
STATE = 10
ITERATE, WEIGHT = 10, 14


def iota(dim, shape=(SUB, LANES)):
    return lax.broadcasted_iota(jnp.int32, shape, dim)


def lane_take(tile, index):
    return jnp.take_along_axis(tile, index, axis=1)


def lane_roll(tile, shift):
    return pltpu.roll(tile, shift % LANES, 1)


def tile_at(ref, slot, row):
    return ref[slot, row : row + SUB, :]


def bands_kernel(wet, right_side, shift_coef, viscosity, first, second, sems):
    odd = lax.axis_index("gx") % 2
    wetness = wet[0, 0].astype(F32)
    bottom = LANES - HALO
    copies = []
    for slot, (start, out) in enumerate(((bottom - bottom * odd, first), (bottom * odd, second))):
        rows = pl.ds(pl.multiple_of(start, SUB), HALO)
        for kind, (source, target) in enumerate(
            (
                (right_side.at[:, rows, :], out.at[0:2]),
                (shift_coef.at[rows, :], out.at[2]),
                (viscosity.at[rows, :], out.at[3]),
            )
        ):
            copies.append(pltpu.make_async_copy(source, target, sems.at[3 * slot + kind]))
    for copy in copies:
        copy.start()
    for copy in copies:
        copy.wait()
    for out in (first, second):
        for field in (0, 1, 3):
            out[field] = out[field] * wetness


def own_rows(right_side, shift_coef, viscosity, field, tile):
    rows = slice(SUB * tile, SUB * tile + SUB)
    if field < 2:
        return right_side[field, rows, :]
    return shift_coef[rows, :] if field == 2 else viscosity[rows, :]


def rim_place(half, lane):
    to_left = ((lane >> 3) & 1) == half
    q = jnp.where(to_left, lane, (lane - (56 + 8 * half)) & (LANES - 1)) >> 4
    cell = 2 * (lane & 7) + (q & 1) + jnp.where(to_left, 0, LANES - HALO)
    return to_left, q >> 1, cell


def strips_kernel(
    size_x, wet, got_second, got_first, right_side, shift_coef, viscosity, first, second
):
    index_x = lax.axis_index("gx")
    odd_x = index_x % 2 == 1
    odd_y = lax.axis_index("gy") % 2 == 1
    wetness = wet[0, 0].astype(F32)
    above = (index_x > 0).astype(F32)
    below = (index_x < size_x - 1).astype(F32)
    lane = iota(1)
    rim_tiles = HALO // SUB

    def piece(field, tile):
        if rim_tiles <= tile < TILES[0] - rim_tiles:
            return own_rows(right_side, shift_coef, viscosity, field, tile - rim_tiles)
        top = tile < rim_tiles
        row = SUB * (tile if top else tile - (TILES[0] - rim_tiles))
        one, two = tile_at(got_first, field, row), tile_at(got_second, field, row)
        return jnp.where(odd_x, one, two) if top else jnp.where(odd_x, two, one)

    places = [rim_place(half, lane) for half in range(2)]
    found = {}
    for half in range(2):
        _, owner, cell = places[half]
        for tile in range(HALF_TILES):
            at = tile + half * HALF_TILES
            value = None
            for field in range(4):
                part = lane_take(piece(field, at), cell)
                value = part if value is None else jnp.where(owner == field, part, value)
            if rim_tiles <= at < TILES[0] - rim_tiles:
                value = value * jnp.where(owner == 2, 1.0, wetness)
            else:
                value = value * jnp.where(owner == 3, above if at < rim_tiles else below, 1.0)
            found[half, tile] = value
    for tile in range(HALF_TILES):
        left = jnp.where(places[0][0], found[0, tile], found[1, tile])
        right = jnp.where(places[0][0], found[1, tile], found[0, tile])
        rows = slice(SUB * tile, SUB * tile + SUB)
        first[rows, :] = jnp.where(odd_y, left, right)
        second[rows, :] = jnp.where(odd_y, right, left)


def halves_kernel(
    size_x, wet, got_second, got_first, right_side, shift_coef, viscosity, fields
):
    index_x = lax.axis_index("gx")
    odd_x = index_x % 2 == 1
    wetness = wet[0, 0].astype(F32)
    above = (index_x > 0).astype(F32)
    below = (index_x < size_x - 1).astype(F32)
    lane = iota(1)
    rim_tiles = HALO // SUB
    for tile in range(TILES[0]):
        row = GUARD + SUB * tile
        for field in range(4):
            if rim_tiles <= tile < TILES[0] - rim_tiles:
                value = own_rows(right_side, shift_coef, viscosity, field, tile - rim_tiles)
                if field != 2:
                    value = value * wetness
            else:
                top = tile < rim_tiles
                at = SUB * (tile if top else tile - (TILES[0] - rim_tiles))
                one, two = tile_at(got_first, field, at), tile_at(got_second, field, at)
                value = jnp.where(odd_x, one, two) if top else jnp.where(odd_x, two, one)
                if field == 3:
                    value = value * (above if top else below)
            for parity in range(2):
                fields[2 * field + parity, row : row + SUB, :] = lane_take(
                    value, (2 * lane + parity) & (LANES - 1)
                )


def down_kernel(size_y, devices, got_second, got_first, held, chunks, *refs):
    states, refs = refs[:LOCAL], refs[LOCAL:]
    viscous, refs = refs[:LOCAL], refs[LOCAL:]
    reactions, refs = refs[:LOCAL], refs[LOCAL:]
    sources, refs = refs[:LOCAL], refs[LOCAL:]
    weights, refs = refs[:LOCAL], refs[LOCAL:]
    iterates, refs = refs[:LOCAL], refs[LOCAL:]
    sums, (outers, ring) = refs[:LOCAL], refs[LOCAL:]
    index_y = lax.axis_index("gy")
    odd_y = index_y % 2 == 1
    lane, sub = iota(1), iota(0)
    side_ok = jnp.where(
        lane < 96, (index_y < size_y - 1).astype(F32), (index_y > 0).astype(F32)
    )
    odd_row = (sub & 1) == 1
    inner = lane < HALF
    even_block = ((lane >> 3) & 1) == 0

    def tiles(level):
        return [GUARD + SUB * tile for tile in range(TILES[level])]

    def put(ref, slot, row, value):
        ref[slot, row : row + SUB, :] = value

    def rims(row, slots):
        half, at = divmod((row - GUARD) // SUB, HALF_TILES)
        one, two = (r[SUB * at : SUB * at + SUB, :] for r in (got_first, got_second))
        after, before = jnp.where(odd_y, two, one), jnp.where(odd_y, one, two)
        if half == 0:
            both = jnp.where(even_block, after, before)
        else:
            both = jnp.where(even_block, before, after)
        values = []
        for slot in slots:
            rim = lane_roll(both, HALF - 16 * slot - 8 * half)
            if slot >= 4:
                rim = jnp.where(side_ok > 0, rim, 1.0 if slot < 6 else 0.0)
            values.append(jnp.where(inner, tile_at(held, slot, row), rim))
        return values

    def paired(ref, slot, start):
        return (
            ref[slot, pl.ds(start, SUB, stride=2), :] + ref[slot, pl.ds(start + 1, SUB, stride=2), :]
        )

    takes = [(2 * lane + offset) & (LANES - 1) for offset in (0, 1, -1, 2)]

    def coefficients(level):
        if level == 0:
            for row in tiles(level):
                values = rims(row, (4, 5, 6, 7))
                for slot, value in enumerate(values[:2]):
                    put(reactions[level], slot, row, value)
                for slot, value in enumerate(values[2:]):
                    put(viscous[level], slot, row, value)
                put(sums[level], 2, row, values[0] + values[1])
                put(sums[level], 3, row, values[2] + values[3])
            return
        ref = sums[level - 1]
        loaded = {
            row: [
                scale * paired(ref, slot, GUARD + 2 * (row - GUARD))
                for slot, scale in ((2, 0.25), (3, 0.0625))
            ]
            for row in tiles(level)
        }
        found = {row: ([], []) for row in loaded}
        for kind, index in enumerate(takes):
            for row, (reaction, viscosity) in loaded.items():
                value = lane_take(viscosity, index)
                put(viscous[level], kind, row, value)
                found[row][1].append(value)
                if kind < 2:
                    value = lane_take(reaction, index)
                    put(reactions[level], kind, row, value)
                    found[row][0].append(value)
        for row, (reaction, viscosity) in found.items():
            put(sums[level], 2, row, reaction[0] + reaction[1])
            put(sums[level], 3, row, viscosity[0] + viscosity[1])

    def faces(level, row):
        here = [tile_at(viscous[level], p, row) for p in range(2)]
        north = [jnp.minimum(here[p], tile_at(viscous[level], p, row - 1)) for p in range(2)]
        south = [jnp.minimum(here[p], tile_at(viscous[level], p, row + 1)) for p in range(2)]
        return here, jnp.minimum(here[0], here[1]), north, south

    def outside(level, row, here):
        if level == 0:
            beyond = [lane_roll(here[1], 1), lane_roll(here[0], -1)]
        else:
            beyond = [tile_at(viscous[level], 2 + p, row) for p in range(2)]
        return [jnp.minimum(h, b) for h, b in zip(here, beyond)]

    def weigh(level):
        for row in tiles(level):
            here, middle, north, south = faces(level, row)
            outer = outside(level, row, here)
            found = []
            for p in range(2):
                diagonal = tile_at(reactions[level], p, row) + (
                    (middle + outer[p]) + (north[p] + south[p])
                )
                found.append(OMEGA / diagonal)
                if level == 0:
                    put(outers, p, row, outer[p])
            if level > 0:
                found += [lane_roll(found[1], 1), lane_roll(found[0], -1)]
            for slot, value in enumerate(found):
                put(weights[level], slot, row, value)

    def take_sources(level):
        if level == 0:
            for row in tiles(level):
                for slot, value in enumerate(rims(row, (0, 1, 2, 3))):
                    put(sources[level], slot, row, value)
            return
        loaded = {
            row: [
                0.25 * paired(sums[level - 1], comp, GUARD + 2 * (row - GUARD))
                for comp in range(2)
            ]
            for row in tiles(level)
        }
        for kind, index in enumerate(takes):
            for row, values in loaded.items():
                for comp in range(2):
                    put(sources[level], 4 * comp + kind, row, lane_take(values[comp], index))

    def kinds(level):
        return 2 if level == 0 else 4

    def first_sweep(level):
        for row in tiles(level):
            for comp in range(2):
                for p in range(2):
                    put(
                        iterates[level],
                        2 * comp + p,
                        row,
                        tile_at(weights[level], p, row)
                        * tile_at(sources[level], kinds(level) * comp + p, row),
                    )

    def residual(level):
        state, iterate, weight, source = (
            states[level],
            iterates[level],
            weights[level],
            sources[level],
        )
        for row in tiles(level):
            _, middle, north, south = faces(level, row)
            if level == 0:
                outer = [tile_at(outers, p, row) for p in range(2)]
            else:
                outer = outside(level, row, [tile_at(viscous[level], p, row) for p in range(2)])
            scale = [tile_at(weight, p, row) for p in range(2)]
            kept = level > 0 or TOP <= row < LOW
            for comp in range(2):
                here = [tile_at(iterate, 2 * comp + p, row) for p in range(2)]
                if level == 0:
                    beyond = [lane_roll(here[1], 1), lane_roll(here[0], -1)]
                else:
                    beyond = [
                        tile_at(weight, 2 + p, row) * tile_at(source, 4 * comp + 2 + p, row)
                        for p in range(2)
                    ]
                total = None
                for p in range(2):
                    slot = 2 * comp + p
                    around = middle * here[1 - p] + outer[p] * beyond[p]
                    around = around + (
                        south[p] * tile_at(iterate, slot, row + 1)
                        + north[p] * tile_at(iterate, slot, row - 1)
                    )
                    left = KEEP * tile_at(source, kinds(level) * comp + p, row) + around
                    if kept:
                        put(state, SWEPT + slot, row, here[p] + scale[p] * left)
                    if level == LOCAL - 1:
                        put(ring, slot, row, left)
                        put(state, ITERATE + slot, row, here[p])
                    total = left if total is None else total + left
                put(sums[level], comp, row, total)
            if kept:
                for p in range(2):
                    within = jnp.where(odd_row, north[p], south[p])
                    across = jnp.where(odd_row, south[p], north[p])
                    put(state, CENTRE + p, row, KEEP + scale[p] * (middle + within))
                    put(state, SIDE + p, row, scale[p] * outer[p])
                    put(state, ACROSS + p, row, scale[p] * across)
                    if level == LOCAL - 1:
                        put(state, WEIGHT + p, row, scale[p])

    coefficients(0)
    take_sources(0)
    weigh(0)
    coefficients(1)
    first_sweep(0)
    residual(0)
    weigh(1)
    coefficients(2)
    take_sources(1)
    weigh(2)
    coefficients(3)
    first_sweep(1)
    residual(1)
    take_sources(2)
    weigh(3)
    first_sweep(2)
    residual(2)
    take_sources(3)
    first_sweep(3)
    residual(3)

    start = GUARD + RIM[LOCAL - 1]
    column = lane & (SUB - 1)
    own = [
        lane_take(scale * paired(sums[LOCAL - 1], slot, start), column)
        for slot, scale in enumerate((0.25, 0.25, 0.25, 0.0625))
    ]
    turned = ((lane >> 3) - index_y) & 15
    chosen = (turned & (SUB - 1)) == sub

    def packed(value):
        return jnp.sum(value, axis=0, keepdims=True)

    def joined(a, b):
        return packed(jnp.where(chosen, jnp.where(turned < SUB, a, b), 0.0))

    edge = (lane >> 4) & 3
    place = lane & 15

    rims = jnp.zeros((SUB, LANES), F32)
    for p in range(2):
        index = jnp.where(edge < 2, column, 0 if p == 0 else SUB - 1)
        for part in range(2):
            along = (edge == part) & ((place >> 3) == p) & (sub == (0 if part == 0 else SUB - 1))
            up = (edge == 2 + p) & (place == sub + SUB * part)
            row = start + SUB * part
            value = jnp.where(
                inner,
                lane_take(tile_at(ring, p, row), index),
                lane_take(tile_at(ring, 2 + p, row), index),
            )
            rims = jnp.where(along | up, value, rims)
    kind = sub % CHUNK
    parts = [joined(own[0], own[1]), joined(own[2], own[2]), packed(rims), joined(own[3], own[3])]
    tile = jnp.where(
        kind < 2,
        jnp.where(kind == 0, parts[0], parts[1]),
        jnp.where(kind == 2, parts[2], parts[3]),
    )
    for block in range(CHUNK * devices // SUB):
        chunks[SUB * block : SUB * block + SUB, :] = tile


def write(buffer, slot, rows, value):
    for column in range(buffer.shape[1]):
        buffer[slot, column, rows, :] = value[:, LANES * column : LANES * column + LANES]


def read(buffer, slot, rows):
    parts = [buffer[slot, column, rows, :] for column in range(buffer.shape[1])]
    return parts[0] if len(parts) == 1 else jnp.concatenate(parts, 1)


class Coarse:
    def __init__(self, step, row_step, rows, cols_total, width):
        self.step, self.row_step = step, row_step
        self.shape = (rows, width)
        lane, row = iota(1, self.shape), iota(0, self.shape)
        column = lane & (cols_total - 1)
        self.odd_lane, self.odd_row = (lane & step) != 0, (row & row_step) != 0
        self.leftmost = column < 2 * step
        self.rightmost = column >= cols_total - 2 * step
        self.top, self.bottom = row < row_step, row >= rows - row_step

    def along(self, value, amount):
        return pltpu.roll(value, amount % self.shape[1], 1)

    def down(self, value, amount):
        return pltpu.roll(value, amount % self.shape[0], 0)

    def paired(self, value):
        return (
            jnp.where(self.odd_lane, self.along(value, self.step), value),
            jnp.where(self.odd_lane, value, self.along(value, -self.step)),
        )

    def outside(self, value):
        return (
            jnp.where(
                self.odd_lane, self.along(value, 2 * self.step), self.along(value, self.step)
            ),
            jnp.where(
                self.odd_lane, self.along(value, -self.step), self.along(value, -2 * self.step)
            ),
        )

    def farther(self, value):
        return (
            jnp.where(
                self.odd_lane, self.along(value, 3 * self.step), self.along(value, 2 * self.step)
            ),
            jnp.where(
                self.odd_lane, self.along(value, -2 * self.step), self.along(value, -3 * self.step)
            ),
        )

    def rows_beside(self, here):
        above = jnp.where(self.top, 0.0, self.down(here, self.row_step))
        below = jnp.where(self.bottom, 0.0, self.down(here, -self.row_step))
        return jnp.minimum(here, above), jnp.minimum(here, below)

    def coefficients(self, viscous, reaction):
        here, beyond, far = self.paired(viscous), self.outside(viscous), self.farther(viscous)
        reactions, reactions_beyond = self.paired(reaction), self.outside(reaction)
        edges = (self.leftmost, self.rightmost)
        self.middle = jnp.minimum(here[0], here[1])
        self.outer, self.north, self.south = [], [], []
        self.weights, self.weights_beyond = [], []
        for p in range(2):
            outer = jnp.minimum(here[p], jnp.where(edges[p], 0.0, beyond[p]))
            north, south = self.rows_beside(here[p])
            diagonal = reactions[p] + ((self.middle + outer) + (north + south))
            self.weights.append(OMEGA / diagonal)
            self.outer.append(outer)
            self.north.append(north)
            self.south.append(south)
            next_outer = jnp.minimum(beyond[p], far[p])
            north, south = self.rows_beside(beyond[p])
            diagonal = reactions_beyond[p] + ((outer + next_outer) + (north + south))
            self.weights_beyond.append(OMEGA / diagonal)
        return here[0] + here[1], reactions[0] + reactions[1]

    def take(self, source):
        self.values, self.values_beyond = self.paired(source), self.outside(source)

    def residual(self):
        x = [w * s for w, s in zip(self.weights, self.values)]
        x_beyond = [w * s for w, s in zip(self.weights_beyond, self.values_beyond)]
        total, self.swept = None, []
        for p in range(2):
            around = self.middle * x[1 - p] + self.outer[p] * x_beyond[p]
            around = around + (
                self.south[p] * self.down(x[p], -self.row_step)
                + self.north[p] * self.down(x[p], self.row_step)
            )
            left = KEEP * self.values[p] + around
            self.swept.append(x[p] + self.weights[p] * left)
            total = left if total is None else total + left
        return total

    def prepare(self):
        parts = []
        for p in range(2):
            within = jnp.where(self.odd_row, self.north[p], self.south[p])
            out = jnp.where(self.odd_row, self.south[p], self.north[p])
            weight = self.weights[p]
            centre = KEEP + weight * (self.middle + within)
            parts.append((self.swept[p], centre, weight * self.outer[p], weight * out))
        self.parts = parts
        self.left_parts = [self.along(value, 2 * self.step) for value in parts[1]]
        self.right_parts = [self.along(value, -2 * self.step) for value in parts[0]]

    def corrected(self, here, left, right):
        def swept(part, own, side):
            return (part[0] + part[1] * own[0]) + (part[2] * side[0] + part[3] * own[1])

        even, odd = swept(self.parts[0], here, left), swept(self.parts[1], here, right)
        before, after = swept(self.left_parts, left, here), swept(self.right_parts, right, here)
        return (
            jnp.where(self.odd_lane, odd, even),
            jnp.where(self.odd_lane, even, before),
            jnp.where(self.odd_lane, after, odd),
        )


def coarse_solve(grid, buffer, rows_total, cols_total, width, meanwhile):
    columns = width // LANES

    def whole(slot):
        return jnp.concatenate([grid[slot, c] for c in range(columns)], 1) if columns > 1 else grid[slot, 0]

    levels, rows, row_step = [], rows_total, 1
    for index in range(COARSE + 1):
        levels.append(Coarse(1 << index, row_step, rows, cols_total, width))
        if rows > SUB:
            rows //= 2
        else:
            row_step *= 2

    def folded(index, value, slot, scale):
        level = levels[index]
        rows = level.shape[0]
        if levels[index + 1].shape[0] == rows:
            other = jnp.where(
                level.odd_row, level.down(value, level.row_step), level.down(value, -level.row_step)
            )
            return scale * (value + other)
        write(buffer, slot, slice(0, rows), value)
        first, second = [pl.ds(begin, rows // 2, stride=2) for begin in range(2)]
        return scale * (read(buffer, slot, first) + read(buffer, slot, second))

    def opened(index, value, slot):
        level = levels[index]
        rows = level.shape[0]
        if value.shape[0] == rows:
            return value, jnp.where(
                level.odd_row, level.down(value, -level.row_step), level.down(value, level.row_step)
            )
        half = rows // 2
        blank = jnp.zeros((SUB, width), F32)
        for begin in range(2):
            write(buffer, slot, pl.ds(begin, half, stride=2), value)
        write(buffer, slot + 1, slice(SUB, 2 * SUB), blank)
        write(buffer, slot + 1, slice(rows, rows + SUB), blank)
        for begin in (SUB + 2, SUB - 1):
            write(buffer, slot + 1, pl.ds(begin, half, stride=2), value)
        return read(buffer, slot, slice(0, rows)), read(buffer, slot + 1, slice(SUB, SUB + rows))

    viscous, reaction, source = [None] * 5, [None] * 5, [None] * 5
    viscous[0], reaction[0], source[0] = whole(2), whole(1), whole(0)

    def coefficients(index):
        pair, reactions = levels[index].coefficients(viscous[index], reaction[index])
        viscous[index + 1] = folded(index, pair, 0, 0.0625)
        reaction[index + 1] = folded(index, reactions, 1, 0.25)

    def residual(index):
        source[index + 1] = folded(index, levels[index].residual(), 2, 0.25)

    last = levels[COARSE]
    block = 1 << COARSE
    cols_left = cols_total // block
    rows_left = last.shape[0]
    lane = iota(1, (rows_left, LANES))
    groups = 1 if cols_total < LANES else 2
    per_group = columns // groups

    def spread(*arrays):
        found = [[] for _ in arrays]
        for group in range(groups):
            for j in range(cols_left):
                column, place = divmod(block * j, LANES)
                column += group * per_group
                if groups == 1:
                    place = place + (lane & (LANES - cols_total))
                else:
                    place = jnp.full((rows_left, LANES), place, jnp.int32)
                for value, columns_found in zip(arrays, found):
                    tile = value[:, LANES * column : LANES * column + LANES]
                    columns_found.append(lane_take(tile, place))
        return found

    def flat(values, group, j):
        return values[group * cols_left + j]

    levels[0].take(source[0])
    coefficients(0)
    coefficients(1)
    residual(0)
    levels[1].take(source[1])
    coefficients(2)
    residual(1)
    levels[2].take(source[2])
    coefficients(3)
    residual(2)
    levels[3].take(source[3])
    viscous_columns, reaction_columns = spread(viscous[4], reaction[4])

    top, bottom = last.top[:, :LANES], last.bottom[:, :LANES]
    pulls, weights = [], []
    for group in range(groups):
        for j in range(cols_left):
            here = flat(viscous_columns, group, j)
            above = jnp.where(top, 0.0, last.down(here, last.row_step))
            below = jnp.where(bottom, 0.0, last.down(here, -last.row_step))
            links = [jnp.minimum(here, above), jnp.minimum(here, below)]
            links += [
                jnp.minimum(here, flat(viscous_columns, group, other))
                for other in (j - 1, j + 1)
                if 0 <= other < cols_left
            ]
            weight = OMEGA / (flat(reaction_columns, group, j) + sum(links))
            weights.append(weight)
            pulls.append([weight * link for link in links])
    residual(3)
    pushed = [w * s for w, s in zip(weights, spread(source[4])[0])]
    meanwhile()
    for index in range(COARSE - 1, -1, -1):
        levels[index].prepare()
    values = pushed
    for _ in range(COARSE_SWEEPS - 1):
        following = []
        for group in range(groups):
            for j in range(cols_left):
                at = group * cols_left + j
                here, pull = values[at], pulls[at]
                total = (KEEP * here + pushed[at]) + (
                    pull[0] * last.down(here, last.row_step)
                    + pull[1] * last.down(here, -last.row_step)
                )
                sides = [other for other in (j - 1, j + 1) if 0 <= other < cols_left]
                for link, other in zip(pull[2:], sides):
                    total = total + link * flat(values, group, other)
                following.append(total)
        values = following

    def laid(shift):
        found = []
        for column in range(columns):
            group = column // per_group
            place = ((lane & (cols_total - 1)) if groups == 1 else lane) // block
            place = place + (column % per_group) * (LANES // block)
            value = jnp.zeros((rows_left, LANES), F32)
            for j in range(cols_left):
                value = jnp.where(place == j + shift, flat(values, group, j), value)
            found.append(value)
        return found[0] if columns == 1 else jnp.concatenate(found, 1)

    corrections = [laid(shift) for shift in (0, 1, -1)]
    for index in range(COARSE - 1, -1, -1):
        corrections = levels[index].corrected(
            *[opened(index, value, 2 * at) for at, value in enumerate(corrections)]
        )
    return corrections


def up_kernel(size_x, size_y, gathered, state0, state1, state2, state3, out, *refs):
    grid, buffer, whole, window, swept3, corr1, corr2, corr3, merged0, merged1, merged2 = refs[:11]
    finished, sems = refs[11:]
    index_x, index_y = lax.axis_index("gx"), lax.axis_index("gy")
    rows_total, cols_total = CELLS * size_x, CELLS * size_y
    width = 2 * cols_total
    columns = width // LANES
    per_column = LANES // CELLS
    lane, sub = iota(1), iota(0)

    tall = iota(1, (size_x, LANES)) // CELLS
    modulus = min(size_y, per_column)
    for column in range(columns):
        comp = column // (columns // 2) if columns > 1 else 0
        first = (column % (columns // 2)) * per_column if columns > 1 else 0
        for slot, kind in ((2, 3), (1, 1), (0, 0)):
            chunks = [
                gathered[pl.ds(CHUNK * (first + j) + kind, size_x, stride=CHUNK * size_y), :]
                for j in range(modulus)
            ]
            for r in range(CELLS):
                turn = r + CELLS * comp
                value = chunks[0]
                for j in range(1, modulus):
                    value = jnp.where(((tall - turn) & (modulus - 1)) == j, chunks[j], value)
                grid[slot, column, pl.ds(r, size_x, stride=CELLS), :] = lane_roll(
                    value, -CELLS * turn
                )

    def ring_row(dx, dy):
        i = jnp.clip(index_x + dx, 0, size_x - 1)
        j = jnp.clip(index_y + dy, 0, size_y - 1)
        return jnp.broadcast_to(
            gathered[pl.ds(CHUNK * (i * size_y + j) + 2, 1), :], (SUB, LANES)
        )

    start = GUARD + RIM[3]

    def complete_ring():
        beside = {
            (dx, dy): ring_row(dx, dy) for dx in (-1, 0, 1) for dy in (-1, 0, 1) if dx or dy
        }
        for comp in range(2):
            base = comp * HALF
            for p in range(2):
                slot = 2 * comp + p
                end = 7 if p else 0
                corner_lane = LANES - 1 if p else SUB
                dy = -1 if p else 1
                for tile in range(2):
                    at = start + SUB * tile
                    index = base + (48 if p else 32) + SUB * tile + sub
                    ringed = lane_take(beside[0, dy], index)
                    swept = jnp.where(
                        lane == corner_lane,
                        tile_at(state3, ITERATE + slot, at)
                        + tile_at(state3, WEIGHT + p, at) * ringed,
                        tile_at(state3, SWEPT + slot, at),
                    )
                    swept3[slot, at : at + SUB, :] = swept
                for dx, at, edge in ((-1, start - 1, 16), (1, start + 2 * SUB, 0)):
                    index = base + edge + 8 * p
                    ringed = jnp.where(
                        lane == corner_lane,
                        lane_take(beside[dx, dy], jnp.full((SUB, LANES), index + end, jnp.int32)),
                        lane_take(beside[dx, 0], index + (lane & 7)),
                    )
                    rows = slice(at, at + 1)
                    swept3[slot, rows, :] = (
                        state3[ITERATE + slot, rows, :] + state3[WEIGHT + p, rows, :] * ringed[0:1]
                    )

    corrections = coarse_solve(grid, buffer, rows_total, cols_total, width, complete_ring)

    blank = jnp.zeros((SUB, width), F32)
    for kind, correction in enumerate(corrections):
        whole[kind, GUARD : GUARD + rows_total, :] = correction
        whole[kind, 0:GUARD, :] = blank
        whole[kind, GUARD + rows_total : GUARD + rows_total + SUB, :] = blank
    near_rows = pl.ds(pl.multiple_of(CELLS * index_x, SUB), 3 * SUB)
    for comp in range(2):
        shift = (2 * width - cols_total * comp - CELLS * index_y) % width
        for kind in range(3):
            turned = pltpu.roll(whole[kind, near_rows, :], shift, 1)
            if columns > 1:
                tall_lane = iota(1, (3 * SUB, LANES))
                turned = jnp.where(
                    tall_lane < HALF, turned[:, :LANES], turned[:, width - LANES :]
                )
            window[3 * comp + kind, 0 : 3 * SUB, :] = turned

    def swept_rows(ref, level, coarse_row, parity, here, beyond, across, comp):
        at = pl.ds(GUARD + RIM[level] + 2 * coarse_row + parity, SUB, stride=2)
        state = (state0, state1, state2, state3)[level]
        return [
            (ref[SWEPT + 2 * comp + p, at, :] + state[CENTRE + p, at, :] * here)
            + (state[SIDE + p, at, :] * beyond[p] + state[ACROSS + p, at, :] * across)
            for p in range(2)
        ]

    for comp in range(2):
        for tile in range(2):
            first = SUB * tile - 1
            at = GUARD + first
            here, left, right = [tile_at(window, 3 * comp + kind, at) for kind in range(3)]
            for parity in range(2):
                across = tile_at(window, 3 * comp, at + (1 if parity else -1))
                found = swept_rows(swept3, 3, first, parity, here, (left, right), across, comp)
                rows = pl.ds(GUARD + RIM[3] + 2 * first + parity, SUB, stride=2)
                for p in range(2):
                    corr3[2 * comp + p, rows, :] = found[p]

    corrs = [None, corr1, corr2, corr3]
    merged = [merged0, merged1, merged2]
    near = ((((lane + 32) & (LANES - 1)) - 32) >> 1) & (LANES - 1)
    odd_lane = (lane & 1) == 1
    for level in (2, 1, 0):
        coarse = level + 1
        corr, state, whole_rows = corrs[coarse], (state0, state1, state2)[level], merged[level]
        count = (LANES >> coarse) + 2
        origin = GUARD + RIM[coarse]
        places = [
            (comp, origin - 1 + SUB * tile)
            for tile in range(-(-count // SUB))
            for comp in range(2)
        ]
        pairs = {
            (comp, at): (tile_at(corr, 2 * comp, at), tile_at(corr, 2 * comp + 1, at))
            for comp, at in places
        }
        moved = {
            place: [lane_take(even, near), lane_take(odd, near)]
            for place, (even, odd) in pairs.items()
        }
        for place, (even, _) in pairs.items():
            moved[place].append(lane_take(even, (near + 1) & (LANES - 1)))
        for place, (_, odd) in pairs.items():
            moved[place].append(lane_take(odd, (near - 1) & (LANES - 1)))
        for (comp, at), (even_here, odd_here, even_next, odd_last) in moved.items():
            rows = slice(at, at + SUB)
            whole_rows[3 * comp, rows, :] = jnp.where(odd_lane, odd_here, even_here)
            whole_rows[3 * comp + 1, rows, :] = jnp.where(odd_lane, even_next, odd_here)
            whole_rows[3 * comp + 2, rows, :] = jnp.where(odd_lane, even_here, odd_last)
        if level > 0:
            first, tiles = -1, -(-count // SUB)
        else:
            first, tiles = 0, (count - 2) // SUB
        copies = []
        for tile in range(tiles):
            coarse_row = first + SUB * tile
            at = origin + coarse_row
            for comp in range(2):
                here, right, left = [tile_at(whole_rows, 3 * comp + k, at) for k in range(3)]
                for parity in range(2):
                    across = tile_at(whole_rows, 3 * comp, at + (1 if parity else -1))
                    found = swept_rows(
                        state, level, coarse_row, parity, here, (left, right), across, comp
                    )
                    if level > 0:
                        rows = pl.ds(GUARD + RIM[level] + 2 * coarse_row + parity, SUB, stride=2)
                        for p in range(2):
                            corrs[level][2 * comp + p, rows, :] = found[p]
                    else:
                        rows = pl.ds(2 * coarse_row + parity, SUB, stride=2)
                        finished[comp, rows, :] = jnp.where(
                            odd_lane,
                            lane_take(found[1], lane >> 1),
                            lane_take(found[0], lane >> 1),
                        )
            if level == 0 and tile + 1 in PIECES:
                piece = len(copies)
                begin = 2 * SUB * PIECES[piece - 1] if piece else 0
                rows = pl.ds(begin, 2 * SUB * (tile + 1) - begin)
                copy = pltpu.make_async_copy(
                    finished.at[:, rows, :], out.at[:, rows, :], sems.at[piece]
                )
                copy.start()
                copies.append(copy)
        for copy in copies:
            copy.wait()


def params():
    return pltpu.CompilerParams(vmem_limit_bytes=VMEM_LIMIT)


VMEM_SPEC = pl.BlockSpec(memory_space=pltpu.VMEM)
SMEM_SPEC = pl.BlockSpec(memory_space=pltpu.SMEM)
HBM_SPEC = pl.BlockSpec(memory_space=pltpu.HBM)


def swap_routes(size_x, size_y):
    def index(i, j):
        return i * size_y + j

    routes = []
    for axis in range(2):
        size = (size_x, size_y)[axis]
        for offset in range(2):
            route = []
            for i in range(size_x):
                for j in range(size_y):
                    here = (i, j)[axis]
                    other = here + 1 if here % 2 == offset else here - 1
                    if 0 <= other < size:
                        peer = (other, j) if axis == 0 else (i, other)
                    else:
                        peer = (i, j ^ 1) if axis == 0 else (i ^ 1, j)
                    route.append((index(i, j), index(*peer)))
            routes.append(route)
    return routes


def per_device(size_x, size_y, right_side, shift_coef, viscosity, wet_tiles):
    axes = ("gx", "gy")
    devices = size_x * size_y
    routes = swap_routes(size_x, size_y)
    band = pltpu.VMEM((4, HALO, LANES), F32)
    own = (right_side, shift_coef, viscosity)
    first, second = pl.pallas_call(
        bands_kernel,
        out_shape=(band, band),
        in_specs=[SMEM_SPEC] + [HBM_SPEC] * 3,
        out_specs=(VMEM_SPEC,) * 2,
        scratch_shapes=[pltpu.SemaphoreType.DMA((6,))],
        compiler_params=params(),
        name="bands",
    )(wet_tiles, *[pltpu.with_memory_space_constraint(array, pltpu.HBM) for array in own])
    second = lax.ppermute(second, axes, routes[1])
    first = lax.ppermute(first, axes, routes[0])
    strip = jax.ShapeDtypeStruct((MESSAGE, LANES), F32)
    got = (second, first)
    first, second = pl.pallas_call(
        functools.partial(strips_kernel, size_x),
        out_shape=(strip, strip),
        in_specs=[SMEM_SPEC] + [VMEM_SPEC] * 5,
        out_specs=(VMEM_SPEC,) * 2,
        compiler_params=params(),
        name="strips",
    )(wet_tiles, *got, *own)
    fields = pl.pallas_call(
        functools.partial(halves_kernel, size_x),
        out_shape=pltpu.VMEM((8, HELD[0], LANES), F32),
        in_specs=[SMEM_SPEC] + [VMEM_SPEC] * 5,
        out_specs=VMEM_SPEC,
        cost_estimate=pl.CostEstimate(flops=1 << 20, bytes_accessed=1 << 21, transcendentals=0),
        compiler_params=params(),
        name="halves",
    )(wet_tiles, *got, *own)
    second = lax.ppermute(second, axes, routes[3])
    first = lax.ppermute(first, axes, routes[2])

    def buffers(counts):
        return [pltpu.VMEM((n, HELD[level], LANES), F32) for level, n in enumerate(counts)]

    chunks, *states = pl.pallas_call(
        functools.partial(down_kernel, size_y, devices),
        out_shape=(jax.ShapeDtypeStruct((CHUNK * devices, LANES), F32),)
        + tuple(buffers([STATE, STATE, STATE, STATE + 6])),
        in_specs=[VMEM_SPEC] * 3,
        out_specs=(VMEM_SPEC,) * (1 + LOCAL),
        scratch_shapes=buffers([2, 4, 4, 4])
        + buffers([2] * 4)
        + buffers([4, 8, 8, 8])
        + buffers([2, 4, 4, 4])
        + buffers([4] * 4)
        + buffers([4] * 4)
        + [pltpu.VMEM((2, HELD[0], LANES), F32), pltpu.VMEM((4, HELD[3], LANES), F32)],
        compiler_params=params(),
        name="down",
    )(second, first, fields)
    gathered = lax.all_to_all(chunks, axes, 0, 0, tiled=True)
    rows_total = CELLS * size_x
    width = 2 * CELLS * size_y
    return pl.pallas_call(
        functools.partial(up_kernel, size_x, size_y),
        out_shape=jax.ShapeDtypeStruct((2, LANES, LANES), F32),
        in_specs=[VMEM_SPEC] * (1 + LOCAL),
        out_specs=HBM_SPEC,
        scratch_shapes=[
            pltpu.VMEM((3, width // LANES, rows_total, LANES), F32),
            pltpu.VMEM((6, width // LANES, rows_total + 3 * SUB, LANES), F32),
            pltpu.VMEM((3, rows_total + 2 * SUB, width), F32),
            pltpu.VMEM((6, 5 * SUB, LANES), F32),
            pltpu.VMEM((4, HELD[3], LANES), F32),
        ]
        + [pltpu.VMEM((4, HELD[level], LANES), F32) for level in (1, 2, 3)]
        + [pltpu.VMEM((6, HELD[level + 1], LANES), F32) for level in (0, 1, 2)]
        + [pltpu.VMEM((2, LANES, LANES), F32), pltpu.SemaphoreType.DMA((len(PIECES),))],
        compiler_params=params(),
        name="up",
    )(gathered, *states)


def solution(mesh):
    sizes = dict(mesh.shape)
    placed = (P(None, "gx", "gy"), P("gx", "gy"), P("gx", "gy"), P("gx", "gy"))
    return jax.shard_map(
        functools.partial(per_device, sizes["gx"], sizes["gy"]),
        mesh=mesh,
        in_specs=placed,
        out_specs=P(None, "gx", "gy"),
        check_vma=False,
    )
```

```python
import functools

import jax
import jax.numpy as jnp
from jax import lax
from jax.experimental import pallas as pl
from jax.experimental.pallas import tpu as pltpu
from jax.sharding import PartitionSpec as P

LOCAL = 4
COARSE = 4
COARSE_SWEEPS = 8
OMEGA = 0.8
KEEP = 1.0 - OMEGA

LANES = 128
HALF = LANES // 2
SUB = 8
HALO = 16
GUARD = 8
CELLS = LANES >> LOCAL
ROWS = [(LANES + 2 * HALO) >> level for level in range(LOCAL)]
TILES = [-(-rows // SUB) for rows in ROWS]
HELD = [GUARD + SUB * tiles + 16 for tiles in TILES]
RIM = [HALO >> level for level in range(LOCAL)]
TOP = GUARD + HALO
LOW = TOP + LANES
HALF_TILES = TILES[0] // 2
MESSAGE = ROWS[0] // 2
CHUNK = 4
PIECES = (4, 8)
F32 = jnp.float32
VMEM_LIMIT = 48 * 1024 * 1024

SWEPT, CENTRE, SIDE, ACROSS = 0, 4, 6, 8
STATE = 10
ITERATE, WEIGHT = 10, 14


def iota(dim, shape=(SUB, LANES)):
    return lax.broadcasted_iota(jnp.int32, shape, dim)


def lane_take(tile, index):
    return jnp.take_along_axis(tile, index, axis=1)


def lane_roll(tile, shift):
    return pltpu.roll(tile, shift % LANES, 1)


def tile_at(ref, slot, row):
    return ref[slot, row : row + SUB, :]


def bands_kernel(right_side, shift_coef, viscosity, first, second, sems):
    odd = lax.axis_index("gx") % 2
    bottom = LANES - HALO
    copies = []
    for slot, (start, out) in enumerate(((bottom - bottom * odd, first), (bottom * odd, second))):
        rows = pl.ds(pl.multiple_of(start, SUB), HALO)
        for kind, (source, target) in enumerate(
            (
                (right_side.at[:, rows, :], out.at[0:2]),
                (shift_coef.at[rows, :], out.at[2]),
                (viscosity.at[rows, :], out.at[3]),
            )
        ):
            copies.append(pltpu.make_async_copy(source, target, sems.at[3 * slot + kind]))
    for copy in copies:
        copy.start()
    for copy in copies:
        copy.wait()


def own_rows(right_side, shift_coef, viscosity, field, tile):
    rows = slice(SUB * tile, SUB * tile + SUB)
    if field < 2:
        return right_side[field, rows, :]
    return shift_coef[rows, :] if field == 2 else viscosity[rows, :]


def rim_place(half, lane):
    to_left = ((lane >> 3) & 1) == half
    q = jnp.where(to_left, lane, (lane - (56 + 8 * half)) & (LANES - 1)) >> 4
    cell = 2 * (lane & 7) + (q & 1) + jnp.where(to_left, 0, LANES - HALO)
    return to_left, q >> 1, cell


def strips_kernel(
    size_x,
    wet,
    got_second,
    got_first,
    wet_second,
    wet_first,
    right_side,
    shift_coef,
    viscosity,
    first,
    second,
):
    index_x = lax.axis_index("gx")
    odd_x = index_x % 2 == 1
    odd_y = lax.axis_index("gy") % 2 == 1
    wetness = wet[...]
    wet_above = jnp.where(odd_x, wet_first[...], wet_second[...])
    wet_below = jnp.where(odd_x, wet_second[...], wet_first[...])
    above = wet_above * (index_x > 0).astype(F32)
    below = wet_below * (index_x < size_x - 1).astype(F32)
    lane = iota(1)
    rim_tiles = HALO // SUB

    def piece(field, tile):
        if rim_tiles <= tile < TILES[0] - rim_tiles:
            return own_rows(right_side, shift_coef, viscosity, field, tile - rim_tiles)
        top = tile < rim_tiles
        row = SUB * (tile if top else tile - (TILES[0] - rim_tiles))
        one, two = tile_at(got_first, field, row), tile_at(got_second, field, row)
        return jnp.where(odd_x, one, two) if top else jnp.where(odd_x, two, one)

    places = [rim_place(half, lane) for half in range(2)]
    found = {}
    for half in range(2):
        _, owner, cell = places[half]
        for tile in range(HALF_TILES):
            at = tile + half * HALF_TILES
            value = None
            for field in range(4):
                part = lane_take(piece(field, at), cell)
                value = part if value is None else jnp.where(owner == field, part, value)
            if rim_tiles <= at < TILES[0] - rim_tiles:
                value = value * jnp.where(owner == 2, 1.0, wetness)
            else:
                flags = (wet_above, above) if at < rim_tiles else (wet_below, below)
                value = value * jnp.where(
                    owner == 2, 1.0, jnp.where(owner == 3, flags[1], flags[0])
                )
            found[half, tile] = value
    for tile in range(HALF_TILES):
        left = jnp.where(places[0][0], found[0, tile], found[1, tile])
        right = jnp.where(places[0][0], found[1, tile], found[0, tile])
        rows = slice(SUB * tile, SUB * tile + SUB)
        first[rows, :] = jnp.where(odd_y, left, right)
        second[rows, :] = jnp.where(odd_y, right, left)


def halves_kernel(
    size_x,
    wet,
    got_second,
    got_first,
    wet_second,
    wet_first,
    right_side,
    shift_coef,
    viscosity,
    fields,
):
    index_x = lax.axis_index("gx")
    odd_x = index_x % 2 == 1
    wetness = wet[...]
    wet_above = jnp.where(odd_x, wet_first[...], wet_second[...])
    wet_below = jnp.where(odd_x, wet_second[...], wet_first[...])
    above = wet_above * (index_x > 0).astype(F32)
    below = wet_below * (index_x < size_x - 1).astype(F32)
    lane = iota(1)
    rim_tiles = HALO // SUB
    for tile in range(TILES[0]):
        row = GUARD + SUB * tile
        for field in range(4):
            if rim_tiles <= tile < TILES[0] - rim_tiles:
                value = own_rows(right_side, shift_coef, viscosity, field, tile - rim_tiles)
                if field != 2:
                    value = value * wetness
            else:
                top = tile < rim_tiles
                at = SUB * (tile if top else tile - (TILES[0] - rim_tiles))
                one, two = tile_at(got_first, field, at), tile_at(got_second, field, at)
                value = jnp.where(odd_x, one, two) if top else jnp.where(odd_x, two, one)
                if field == 3:
                    value = value * (above if top else below)
                elif field < 2:
                    value = value * (wet_above if top else wet_below)
            for parity in range(2):
                fields[2 * field + parity, row : row + SUB, :] = lane_take(
                    value, (2 * lane + parity) & (LANES - 1)
                )


def down_kernel(size_y, devices, got_second, got_first, held, chunks, *refs):
    states, refs = refs[:LOCAL], refs[LOCAL:]
    viscous, refs = refs[:LOCAL], refs[LOCAL:]
    reactions, refs = refs[:LOCAL], refs[LOCAL:]
    sources, refs = refs[:LOCAL], refs[LOCAL:]
    weights, refs = refs[:LOCAL], refs[LOCAL:]
    iterates, refs = refs[:LOCAL], refs[LOCAL:]
    sums, (outers, ring) = refs[:LOCAL], refs[LOCAL:]
    index_y = lax.axis_index("gy")
    odd_y = index_y % 2 == 1
    lane, sub = iota(1), iota(0)
    side_ok = jnp.where(
        lane < 96, (index_y < size_y - 1).astype(F32), (index_y > 0).astype(F32)
    )
    odd_row = (sub & 1) == 1
    inner = lane < HALF
    even_block = ((lane >> 3) & 1) == 0

    def tiles(level):
        return [GUARD + SUB * tile for tile in range(TILES[level])]

    def put(ref, slot, row, value):
        ref[slot, row : row + SUB, :] = value

    def rims(row, slots):
        half, at = divmod((row - GUARD) // SUB, HALF_TILES)
        one, two = (r[SUB * at : SUB * at + SUB, :] for r in (got_first, got_second))
        after, before = jnp.where(odd_y, two, one), jnp.where(odd_y, one, two)
        if half == 0:
            both = jnp.where(even_block, after, before)
        else:
            both = jnp.where(even_block, before, after)
        values = []
        for slot in slots:
            rim = lane_roll(both, HALF - 16 * slot - 8 * half)
            if slot >= 4:
                rim = jnp.where(side_ok > 0, rim, 1.0 if slot < 6 else 0.0)
            values.append(jnp.where(inner, tile_at(held, slot, row), rim))
        return values

    def paired(ref, slot, start):
        return (
            ref[slot, pl.ds(start, SUB, stride=2), :] + ref[slot, pl.ds(start + 1, SUB, stride=2), :]
        )

    takes = [(2 * lane + offset) & (LANES - 1) for offset in (0, 1, -1, 2)]

    def coefficients(level):
        if level == 0:
            for row in tiles(level):
                values = rims(row, (4, 5, 6, 7))
                for slot, value in enumerate(values[:2]):
                    put(reactions[level], slot, row, value)
                for slot, value in enumerate(values[2:]):
                    put(viscous[level], slot, row, value)
                put(sums[level], 2, row, values[0] + values[1])
                put(sums[level], 3, row, values[2] + values[3])
            return
        ref = sums[level - 1]
        loaded = {
            row: [
                scale * paired(ref, slot, GUARD + 2 * (row - GUARD))
                for slot, scale in ((2, 0.25), (3, 0.0625))
            ]
            for row in tiles(level)
        }
        found = {row: ([], []) for row in loaded}
        for kind, index in enumerate(takes):
            for row, (reaction, viscosity) in loaded.items():
                value = lane_take(viscosity, index)
                put(viscous[level], kind, row, value)
                found[row][1].append(value)
                if kind < 2:
                    value = lane_take(reaction, index)
                    put(reactions[level], kind, row, value)
                    found[row][0].append(value)
        for row, (reaction, viscosity) in found.items():
            put(sums[level], 2, row, reaction[0] + reaction[1])
            put(sums[level], 3, row, viscosity[0] + viscosity[1])

    def faces(level, row):
        here = [tile_at(viscous[level], p, row) for p in range(2)]
        north = [jnp.minimum(here[p], tile_at(viscous[level], p, row - 1)) for p in range(2)]
        south = [jnp.minimum(here[p], tile_at(viscous[level], p, row + 1)) for p in range(2)]
        return here, jnp.minimum(here[0], here[1]), north, south

    def outside(level, row, here):
        if level == 0:
            beyond = [lane_roll(here[1], 1), lane_roll(here[0], -1)]
        else:
            beyond = [tile_at(viscous[level], 2 + p, row) for p in range(2)]
        return [jnp.minimum(h, b) for h, b in zip(here, beyond)]

    def weigh(level):
        for row in tiles(level):
            here, middle, north, south = faces(level, row)
            outer = outside(level, row, here)
            found = []
            for p in range(2):
                diagonal = tile_at(reactions[level], p, row) + (
                    (middle + outer[p]) + (north[p] + south[p])
                )
                found.append(OMEGA / diagonal)
                if level == 0:
                    put(outers, p, row, outer[p])
            if level > 0:
                found += [lane_roll(found[1], 1), lane_roll(found[0], -1)]
            for slot, value in enumerate(found):
                put(weights[level], slot, row, value)

    def take_sources(level):
        if level == 0:
            for row in tiles(level):
                for slot, value in enumerate(rims(row, (0, 1, 2, 3))):
                    put(sources[level], slot, row, value)
            return
        loaded = {
            row: [
                0.25 * paired(sums[level - 1], comp, GUARD + 2 * (row - GUARD))
                for comp in range(2)
            ]
            for row in tiles(level)
        }
        for kind, index in enumerate(takes):
            for row, values in loaded.items():
                for comp in range(2):
                    put(sources[level], 4 * comp + kind, row, lane_take(values[comp], index))

    def kinds(level):
        return 2 if level == 0 else 4

    def first_sweep(level):
        for row in tiles(level):
            for comp in range(2):
                for p in range(2):
                    put(
                        iterates[level],
                        2 * comp + p,
                        row,
                        tile_at(weights[level], p, row)
                        * tile_at(sources[level], kinds(level) * comp + p, row),
                    )

    def residual(level):
        state, iterate, weight, source = (
            states[level],
            iterates[level],
            weights[level],
            sources[level],
        )
        for row in tiles(level):
            _, middle, north, south = faces(level, row)
            if level == 0:
                outer = [tile_at(outers, p, row) for p in range(2)]
            else:
                outer = outside(level, row, [tile_at(viscous[level], p, row) for p in range(2)])
            scale = [tile_at(weight, p, row) for p in range(2)]
            kept = level > 0 or TOP <= row < LOW
            for comp in range(2):
                here = [tile_at(iterate, 2 * comp + p, row) for p in range(2)]
                if level == 0:
                    beyond = [lane_roll(here[1], 1), lane_roll(here[0], -1)]
                else:
                    beyond = [
                        tile_at(weight, 2 + p, row) * tile_at(source, 4 * comp + 2 + p, row)
                        for p in range(2)
                    ]
                total = None
                for p in range(2):
                    slot = 2 * comp + p
                    around = middle * here[1 - p] + outer[p] * beyond[p]
                    around = around + (
                        south[p] * tile_at(iterate, slot, row + 1)
                        + north[p] * tile_at(iterate, slot, row - 1)
                    )
                    left = KEEP * tile_at(source, kinds(level) * comp + p, row) + around
                    if kept:
                        put(state, SWEPT + slot, row, here[p] + scale[p] * left)
                    if level == LOCAL - 1:
                        put(ring, slot, row, left)
                        put(state, ITERATE + slot, row, here[p])
                    total = left if total is None else total + left
                put(sums[level], comp, row, total)
            if kept:
                for p in range(2):
                    within = jnp.where(odd_row, north[p], south[p])
                    across = jnp.where(odd_row, south[p], north[p])
                    put(state, CENTRE + p, row, KEEP + scale[p] * (middle + within))
                    put(state, SIDE + p, row, scale[p] * outer[p])
                    put(state, ACROSS + p, row, scale[p] * across)
                    if level == LOCAL - 1:
                        put(state, WEIGHT + p, row, scale[p])

    coefficients(0)
    take_sources(0)
    weigh(0)
    coefficients(1)
    first_sweep(0)
    residual(0)
    weigh(1)
    coefficients(2)
    take_sources(1)
    weigh(2)
    coefficients(3)
    first_sweep(1)
    residual(1)
    take_sources(2)
    weigh(3)
    first_sweep(2)
    residual(2)
    take_sources(3)
    first_sweep(3)
    residual(3)

    start = GUARD + RIM[LOCAL - 1]
    column = lane & (SUB - 1)
    own = [
        lane_take(scale * paired(sums[LOCAL - 1], slot, start), column)
        for slot, scale in enumerate((0.25, 0.25, 0.25, 0.0625))
    ]
    turned = ((lane >> 3) - index_y) & 15
    chosen = (turned & (SUB - 1)) == sub

    def packed(value):
        return jnp.sum(value, axis=0, keepdims=True)

    def joined(a, b):
        return packed(jnp.where(chosen, jnp.where(turned < SUB, a, b), 0.0))

    edge = (lane >> 4) & 3
    place = lane & 15

    rims = jnp.zeros((SUB, LANES), F32)
    for p in range(2):
        index = jnp.where(edge < 2, column, 0 if p == 0 else SUB - 1)
        for part in range(2):
            along = (edge == part) & ((place >> 3) == p) & (sub == (0 if part == 0 else SUB - 1))
            up = (edge == 2 + p) & (place == sub + SUB * part)
            row = start + SUB * part
            value = jnp.where(
                inner,
                lane_take(tile_at(ring, p, row), index),
                lane_take(tile_at(ring, 2 + p, row), index),
            )
            rims = jnp.where(along | up, value, rims)
    kind = sub % CHUNK
    parts = [joined(own[0], own[1]), joined(own[2], own[2]), packed(rims), joined(own[3], own[3])]
    tile = jnp.where(
        kind < 2,
        jnp.where(kind == 0, parts[0], parts[1]),
        jnp.where(kind == 2, parts[2], parts[3]),
    )
    for block in range(CHUNK * devices // SUB):
        chunks[SUB * block : SUB * block + SUB, :] = tile


def write(buffer, slot, rows, value):
    for column in range(buffer.shape[1]):
        buffer[slot, column, rows, :] = value[:, LANES * column : LANES * column + LANES]


def read(buffer, slot, rows):
    parts = [buffer[slot, column, rows, :] for column in range(buffer.shape[1])]
    return parts[0] if len(parts) == 1 else jnp.concatenate(parts, 1)


class Coarse:
    def __init__(self, step, row_step, rows, cols_total, width):
        self.step, self.row_step = step, row_step
        self.shape = (rows, width)
        lane, row = iota(1, self.shape), iota(0, self.shape)
        column = lane & (cols_total - 1)
        self.odd_lane, self.odd_row = (lane & step) != 0, (row & row_step) != 0
        self.leftmost = column < 2 * step
        self.rightmost = column >= cols_total - 2 * step
        self.top, self.bottom = row < row_step, row >= rows - row_step

    def along(self, value, amount):
        return pltpu.roll(value, amount % self.shape[1], 1)

    def down(self, value, amount):
        return pltpu.roll(value, amount % self.shape[0], 0)

    def paired(self, value):
        return (
            jnp.where(self.odd_lane, self.along(value, self.step), value),
            jnp.where(self.odd_lane, value, self.along(value, -self.step)),
        )

    def outside(self, value):
        return (
            jnp.where(
                self.odd_lane, self.along(value, 2 * self.step), self.along(value, self.step)
            ),
            jnp.where(
                self.odd_lane, self.along(value, -self.step), self.along(value, -2 * self.step)
            ),
        )

    def farther(self, value):
        return (
            jnp.where(
                self.odd_lane, self.along(value, 3 * self.step), self.along(value, 2 * self.step)
            ),
            jnp.where(
                self.odd_lane, self.along(value, -2 * self.step), self.along(value, -3 * self.step)
            ),
        )

    def rows_beside(self, here):
        above = jnp.where(self.top, 0.0, self.down(here, self.row_step))
        below = jnp.where(self.bottom, 0.0, self.down(here, -self.row_step))
        return jnp.minimum(here, above), jnp.minimum(here, below)

    def coefficients(self, viscous, reaction):
        here, beyond, far = self.paired(viscous), self.outside(viscous), self.farther(viscous)
        reactions, reactions_beyond = self.paired(reaction), self.outside(reaction)
        edges = (self.leftmost, self.rightmost)
        self.middle = jnp.minimum(here[0], here[1])
        self.outer, self.north, self.south = [], [], []
        self.weights, self.weights_beyond = [], []
        for p in range(2):
            outer = jnp.minimum(here[p], jnp.where(edges[p], 0.0, beyond[p]))
            north, south = self.rows_beside(here[p])
            diagonal = reactions[p] + ((self.middle + outer) + (north + south))
            self.weights.append(OMEGA / diagonal)
            self.outer.append(outer)
            self.north.append(north)
            self.south.append(south)
            next_outer = jnp.minimum(beyond[p], far[p])
            north, south = self.rows_beside(beyond[p])
            diagonal = reactions_beyond[p] + ((outer + next_outer) + (north + south))
            self.weights_beyond.append(OMEGA / diagonal)
        return here[0] + here[1], reactions[0] + reactions[1]

    def take(self, source):
        self.values, self.values_beyond = self.paired(source), self.outside(source)

    def residual(self):
        x = [w * s for w, s in zip(self.weights, self.values)]
        x_beyond = [w * s for w, s in zip(self.weights_beyond, self.values_beyond)]
        total, self.swept = None, []
        for p in range(2):
            around = self.middle * x[1 - p] + self.outer[p] * x_beyond[p]
            around = around + (
                self.south[p] * self.down(x[p], -self.row_step)
                + self.north[p] * self.down(x[p], self.row_step)
            )
            left = KEEP * self.values[p] + around
            self.swept.append(x[p] + self.weights[p] * left)
            total = left if total is None else total + left
        return total

    def prepare(self):
        parts = []
        for p in range(2):
            within = jnp.where(self.odd_row, self.north[p], self.south[p])
            out = jnp.where(self.odd_row, self.south[p], self.north[p])
            weight = self.weights[p]
            centre = KEEP + weight * (self.middle + within)
            parts.append((self.swept[p], centre, weight * self.outer[p], weight * out))
        self.parts = parts
        self.left_parts = [self.along(value, 2 * self.step) for value in parts[1]]
        self.right_parts = [self.along(value, -2 * self.step) for value in parts[0]]

    def corrected(self, here, left, right):
        def swept(part, own, side):
            return (part[0] + part[1] * own[0]) + (part[2] * side[0] + part[3] * own[1])

        even, odd = swept(self.parts[0], here, left), swept(self.parts[1], here, right)
        before, after = swept(self.left_parts, left, here), swept(self.right_parts, right, here)
        return (
            jnp.where(self.odd_lane, odd, even),
            jnp.where(self.odd_lane, even, before),
            jnp.where(self.odd_lane, after, odd),
        )


def coarse_solve(grid, buffer, rows_total, cols_total, width, meanwhile):
    columns = width // LANES

    def whole(slot):
        return jnp.concatenate([grid[slot, c] for c in range(columns)], 1) if columns > 1 else grid[slot, 0]

    levels, rows, row_step = [], rows_total, 1
    for index in range(COARSE + 1):
        levels.append(Coarse(1 << index, row_step, rows, cols_total, width))
        if rows > SUB:
            rows //= 2
        else:
            row_step *= 2

    def folded(index, value, slot, scale):
        level = levels[index]
        rows = level.shape[0]
        if levels[index + 1].shape[0] == rows:
            other = jnp.where(
                level.odd_row, level.down(value, level.row_step), level.down(value, -level.row_step)
            )
            return scale * (value + other)
        write(buffer, slot, slice(0, rows), value)
        first, second = [pl.ds(begin, rows // 2, stride=2) for begin in range(2)]
        return scale * (read(buffer, slot, first) + read(buffer, slot, second))

    def opened(index, value, slot):
        level = levels[index]
        rows = level.shape[0]
        if value.shape[0] == rows:
            return value, jnp.where(
                level.odd_row, level.down(value, -level.row_step), level.down(value, level.row_step)
            )
        half = rows // 2
        blank = jnp.zeros((SUB, width), F32)
        for begin in range(2):
            write(buffer, slot, pl.ds(begin, half, stride=2), value)
        write(buffer, slot + 1, slice(SUB, 2 * SUB), blank)
        write(buffer, slot + 1, slice(rows, rows + SUB), blank)
        for begin in (SUB + 2, SUB - 1):
            write(buffer, slot + 1, pl.ds(begin, half, stride=2), value)
        return read(buffer, slot, slice(0, rows)), read(buffer, slot + 1, slice(SUB, SUB + rows))

    viscous, reaction, source = [None] * 5, [None] * 5, [None] * 5
    viscous[0], reaction[0], source[0] = whole(2), whole(1), whole(0)

    def coefficients(index):
        pair, reactions = levels[index].coefficients(viscous[index], reaction[index])
        viscous[index + 1] = folded(index, pair, 0, 0.0625)
        reaction[index + 1] = folded(index, reactions, 1, 0.25)

    def residual(index):
        source[index + 1] = folded(index, levels[index].residual(), 2, 0.25)

    last = levels[COARSE]
    block = 1 << COARSE
    cols_left = cols_total // block
    rows_left = last.shape[0]
    lane = iota(1, (rows_left, LANES))
    groups = 1 if cols_total < LANES else 2
    per_group = columns // groups

    def spread(*arrays):
        found = [[] for _ in arrays]
        for group in range(groups):
            for j in range(cols_left):
                column, place = divmod(block * j, LANES)
                column += group * per_group
                if groups == 1:
                    place = place + (lane & (LANES - cols_total))
                else:
                    place = jnp.full((rows_left, LANES), place, jnp.int32)
                for value, columns_found in zip(arrays, found):
                    tile = value[:, LANES * column : LANES * column + LANES]
                    columns_found.append(lane_take(tile, place))
        return found

    def flat(values, group, j):
        return values[group * cols_left + j]

    levels[0].take(source[0])
    coefficients(0)
    coefficients(1)
    residual(0)
    levels[1].take(source[1])
    coefficients(2)
    residual(1)
    levels[2].take(source[2])
    coefficients(3)
    residual(2)
    levels[3].take(source[3])
    viscous_columns, reaction_columns = spread(viscous[4], reaction[4])

    top, bottom = last.top[:, :LANES], last.bottom[:, :LANES]
    pulls, weights = [], []
    for group in range(groups):
        for j in range(cols_left):
            here = flat(viscous_columns, group, j)
            above = jnp.where(top, 0.0, last.down(here, last.row_step))
            below = jnp.where(bottom, 0.0, last.down(here, -last.row_step))
            links = [jnp.minimum(here, above), jnp.minimum(here, below)]
            links += [
                jnp.minimum(here, flat(viscous_columns, group, other))
                for other in (j - 1, j + 1)
                if 0 <= other < cols_left
            ]
            weight = OMEGA / (flat(reaction_columns, group, j) + sum(links))
            weights.append(weight)
            pulls.append([weight * link for link in links])
    residual(3)
    pushed = [w * s for w, s in zip(weights, spread(source[4])[0])]
    meanwhile()
    for index in range(COARSE - 1, -1, -1):
        levels[index].prepare()
    values = pushed
    for _ in range(COARSE_SWEEPS - 1):
        following = []
        for group in range(groups):
            for j in range(cols_left):
                at = group * cols_left + j
                here, pull = values[at], pulls[at]
                total = (KEEP * here + pushed[at]) + (
                    pull[0] * last.down(here, last.row_step)
                    + pull[1] * last.down(here, -last.row_step)
                )
                sides = [other for other in (j - 1, j + 1) if 0 <= other < cols_left]
                for link, other in zip(pull[2:], sides):
                    total = total + link * flat(values, group, other)
                following.append(total)
        values = following

    def laid(shift):
        found = []
        for column in range(columns):
            group = column // per_group
            place = ((lane & (cols_total - 1)) if groups == 1 else lane) // block
            place = place + (column % per_group) * (LANES // block)
            value = jnp.zeros((rows_left, LANES), F32)
            for j in range(cols_left):
                value = jnp.where(place == j + shift, flat(values, group, j), value)
            found.append(value)
        return found[0] if columns == 1 else jnp.concatenate(found, 1)

    corrections = [laid(shift) for shift in (0, 1, -1)]
    for index in range(COARSE - 1, -1, -1):
        corrections = levels[index].corrected(
            *[opened(index, value, 2 * at) for at, value in enumerate(corrections)]
        )
    return corrections


def up_kernel(size_x, size_y, gathered, state0, state1, state2, state3, out, *refs):
    grid, buffer, whole, window, swept3, corr1, corr2, corr3, merged0, merged1, merged2 = refs[:11]
    finished, sems = refs[11:]
    index_x, index_y = lax.axis_index("gx"), lax.axis_index("gy")
    rows_total, cols_total = CELLS * size_x, CELLS * size_y
    width = 2 * cols_total
    columns = width // LANES
    per_column = LANES // CELLS
    lane, sub = iota(1), iota(0)

    tall = iota(1, (size_x, LANES)) // CELLS
    modulus = min(size_y, per_column)
    for column in range(columns):
        comp = column // (columns // 2) if columns > 1 else 0
        first = (column % (columns // 2)) * per_column if columns > 1 else 0
        for slot, kind in ((2, 3), (1, 1), (0, 0)):
            chunks = [
                gathered[pl.ds(CHUNK * (first + j) + kind, size_x, stride=CHUNK * size_y), :]
                for j in range(modulus)
            ]
            for r in range(CELLS):
                turn = r + CELLS * comp
                value = chunks[0]
                for j in range(1, modulus):
                    value = jnp.where(((tall - turn) & (modulus - 1)) == j, chunks[j], value)
                grid[slot, column, pl.ds(r, size_x, stride=CELLS), :] = lane_roll(
                    value, -CELLS * turn
                )

    def ring_row(dx, dy):
        i = jnp.clip(index_x + dx, 0, size_x - 1)
        j = jnp.clip(index_y + dy, 0, size_y - 1)
        return jnp.broadcast_to(
            gathered[pl.ds(CHUNK * (i * size_y + j) + 2, 1), :], (SUB, LANES)
        )

    start = GUARD + RIM[3]

    def complete_ring():
        beside = {
            (dx, dy): ring_row(dx, dy) for dx in (-1, 0, 1) for dy in (-1, 0, 1) if dx or dy
        }
        for comp in range(2):
            base = comp * HALF
            for p in range(2):
                slot = 2 * comp + p
                end = 7 if p else 0
                corner_lane = LANES - 1 if p else SUB
                dy = -1 if p else 1
                for tile in range(2):
                    at = start + SUB * tile
                    index = base + (48 if p else 32) + SUB * tile + sub
                    ringed = lane_take(beside[0, dy], index)
                    swept = jnp.where(
                        lane == corner_lane,
                        tile_at(state3, ITERATE + slot, at)
                        + tile_at(state3, WEIGHT + p, at) * ringed,
                        tile_at(state3, SWEPT + slot, at),
                    )
                    swept3[slot, at : at + SUB, :] = swept
                for dx, at, edge in ((-1, start - 1, 16), (1, start + 2 * SUB, 0)):
                    index = base + edge + 8 * p
                    ringed = jnp.where(
                        lane == corner_lane,
                        lane_take(beside[dx, dy], jnp.full((SUB, LANES), index + end, jnp.int32)),
                        lane_take(beside[dx, 0], index + (lane & 7)),
                    )
                    rows = slice(at, at + 1)
                    swept3[slot, rows, :] = (
                        state3[ITERATE + slot, rows, :] + state3[WEIGHT + p, rows, :] * ringed[0:1]
                    )

    corrections = coarse_solve(grid, buffer, rows_total, cols_total, width, complete_ring)

    blank = jnp.zeros((SUB, width), F32)
    for kind, correction in enumerate(corrections):
        whole[kind, GUARD : GUARD + rows_total, :] = correction
        whole[kind, 0:GUARD, :] = blank
        whole[kind, GUARD + rows_total : GUARD + rows_total + SUB, :] = blank
    near_rows = pl.ds(pl.multiple_of(CELLS * index_x, SUB), 3 * SUB)
    for comp in range(2):
        shift = (2 * width - cols_total * comp - CELLS * index_y) % width
        for kind in range(3):
            turned = pltpu.roll(whole[kind, near_rows, :], shift, 1)
            if columns > 1:
                tall_lane = iota(1, (3 * SUB, LANES))
                turned = jnp.where(
                    tall_lane < HALF, turned[:, :LANES], turned[:, width - LANES :]
                )
            window[3 * comp + kind, 0 : 3 * SUB, :] = turned

    def swept_rows(ref, level, coarse_row, parity, here, beyond, across, comp):
        at = pl.ds(GUARD + RIM[level] + 2 * coarse_row + parity, SUB, stride=2)
        state = (state0, state1, state2, state3)[level]
        return [
            (ref[SWEPT + 2 * comp + p, at, :] + state[CENTRE + p, at, :] * here)
            + (state[SIDE + p, at, :] * beyond[p] + state[ACROSS + p, at, :] * across)
            for p in range(2)
        ]

    for comp in range(2):
        for tile in range(2):
            first = SUB * tile - 1
            at = GUARD + first
            here, left, right = [tile_at(window, 3 * comp + kind, at) for kind in range(3)]
            for parity in range(2):
                across = tile_at(window, 3 * comp, at + (1 if parity else -1))
                found = swept_rows(swept3, 3, first, parity, here, (left, right), across, comp)
                rows = pl.ds(GUARD + RIM[3] + 2 * first + parity, SUB, stride=2)
                for p in range(2):
                    corr3[2 * comp + p, rows, :] = found[p]

    corrs = [None, corr1, corr2, corr3]
    merged = [merged0, merged1, merged2]
    near = ((((lane + 32) & (LANES - 1)) - 32) >> 1) & (LANES - 1)
    odd_lane = (lane & 1) == 1
    for level in (2, 1, 0):
        coarse = level + 1
        corr, state, whole_rows = corrs[coarse], (state0, state1, state2)[level], merged[level]
        count = (LANES >> coarse) + 2
        origin = GUARD + RIM[coarse]
        places = [
            (comp, origin - 1 + SUB * tile)
            for tile in range(-(-count // SUB))
            for comp in range(2)
        ]
        pairs = {
            (comp, at): (tile_at(corr, 2 * comp, at), tile_at(corr, 2 * comp + 1, at))
            for comp, at in places
        }
        moved = {
            place: [lane_take(even, near), lane_take(odd, near)]
            for place, (even, odd) in pairs.items()
        }
        for place, (even, _) in pairs.items():
            moved[place].append(lane_take(even, (near + 1) & (LANES - 1)))
        for place, (_, odd) in pairs.items():
            moved[place].append(lane_take(odd, (near - 1) & (LANES - 1)))
        for (comp, at), (even_here, odd_here, even_next, odd_last) in moved.items():
            rows = slice(at, at + SUB)
            whole_rows[3 * comp, rows, :] = jnp.where(odd_lane, odd_here, even_here)
            whole_rows[3 * comp + 1, rows, :] = jnp.where(odd_lane, even_next, odd_here)
            whole_rows[3 * comp + 2, rows, :] = jnp.where(odd_lane, even_here, odd_last)
        if level > 0:
            first, tiles = -1, -(-count // SUB)
        else:
            first, tiles = 0, (count - 2) // SUB
        copies = []
        for tile in range(tiles):
            coarse_row = first + SUB * tile
            at = origin + coarse_row
            for comp in range(2):
                here, right, left = [tile_at(whole_rows, 3 * comp + k, at) for k in range(3)]
                for parity in range(2):
                    across = tile_at(whole_rows, 3 * comp, at + (1 if parity else -1))
                    found = swept_rows(
                        state, level, coarse_row, parity, here, (left, right), across, comp
                    )
                    if level > 0:
                        rows = pl.ds(GUARD + RIM[level] + 2 * coarse_row + parity, SUB, stride=2)
                        for p in range(2):
                            corrs[level][2 * comp + p, rows, :] = found[p]
                    else:
                        rows = pl.ds(2 * coarse_row + parity, SUB, stride=2)
                        finished[comp, rows, :] = jnp.where(
                            odd_lane,
                            lane_take(found[1], lane >> 1),
                            lane_take(found[0], lane >> 1),
                        )
            if level == 0 and tile + 1 in PIECES:
                piece = len(copies)
                begin = 2 * SUB * PIECES[piece - 1] if piece else 0
                rows = pl.ds(begin, 2 * SUB * (tile + 1) - begin)
                copy = pltpu.make_async_copy(
                    finished.at[:, rows, :], out.at[:, rows, :], sems.at[piece]
                )
                copy.start()
                copies.append(copy)
        for copy in copies:
            copy.wait()


def params():
    return pltpu.CompilerParams(vmem_limit_bytes=VMEM_LIMIT)


VMEM_SPEC = pl.BlockSpec(memory_space=pltpu.VMEM)
HBM_SPEC = pl.BlockSpec(memory_space=pltpu.HBM)


def swap_routes(size_x, size_y):
    def index(i, j):
        return i * size_y + j

    routes = []
    for axis in range(2):
        size = (size_x, size_y)[axis]
        for offset in range(2):
            route = []
            for i in range(size_x):
                for j in range(size_y):
                    here = (i, j)[axis]
                    other = here + 1 if here % 2 == offset else here - 1
                    if 0 <= other < size:
                        peer = (other, j) if axis == 0 else (i, other)
                    else:
                        peer = (i, j ^ 1) if axis == 0 else (i ^ 1, j)
                    route.append((index(i, j), index(*peer)))
            routes.append(route)
    return routes


def per_device(size_x, size_y, right_side, shift_coef, viscosity, wet_tiles):
    axes = ("gx", "gy")
    devices = size_x * size_y
    routes = swap_routes(size_x, size_y)
    band = pltpu.VMEM((4, HALO, LANES), F32)
    own = (right_side, shift_coef, viscosity)
    first, second = pl.pallas_call(
        bands_kernel,
        out_shape=(band, band),
        in_specs=[HBM_SPEC] * 3,
        out_specs=(VMEM_SPEC,) * 2,
        scratch_shapes=[pltpu.SemaphoreType.DMA((6,))],
        compiler_params=params(),
        name="bands",
    )(*[pltpu.with_memory_space_constraint(array, pltpu.HBM) for array in own])
    flag, _ = lax.optimization_barrier((wet_tiles, first))
    wet = jnp.broadcast_to(flag.astype(F32), (SUB, LANES))
    second = lax.ppermute(second, axes, routes[1])
    first = lax.ppermute(first, axes, routes[0])
    wet_second = lax.ppermute(wet, axes, routes[1])
    wet_first = lax.ppermute(wet, axes, routes[0])
    strip = jax.ShapeDtypeStruct((MESSAGE, LANES), F32)
    got = (second, first, wet_second, wet_first)
    first, second = pl.pallas_call(
        functools.partial(strips_kernel, size_x),
        out_shape=(strip, strip),
        in_specs=[VMEM_SPEC] * 8,
        out_specs=(VMEM_SPEC,) * 2,
        compiler_params=params(),
        name="strips",
    )(wet, *got, *own)
    fields = pl.pallas_call(
        functools.partial(halves_kernel, size_x),
        out_shape=pltpu.VMEM((8, HELD[0], LANES), F32),
        in_specs=[VMEM_SPEC] * 8,
        out_specs=VMEM_SPEC,
        cost_estimate=pl.CostEstimate(flops=1 << 20, bytes_accessed=1 << 21, transcendentals=0),
        compiler_params=params(),
        name="halves",
    )(wet, *got, *own)
    second = lax.ppermute(second, axes, routes[3])
    first = lax.ppermute(first, axes, routes[2])

    def buffers(counts):
        return [pltpu.VMEM((n, HELD[level], LANES), F32) for level, n in enumerate(counts)]

    chunks, *states = pl.pallas_call(
        functools.partial(down_kernel, size_y, devices),
        out_shape=(jax.ShapeDtypeStruct((CHUNK * devices, LANES), F32),)
        + tuple(buffers([STATE, STATE, STATE, STATE + 6])),
        in_specs=[VMEM_SPEC] * 3,
        out_specs=(VMEM_SPEC,) * (1 + LOCAL),
        scratch_shapes=buffers([2, 4, 4, 4])
        + buffers([2] * 4)
        + buffers([4, 8, 8, 8])
        + buffers([2, 4, 4, 4])
        + buffers([4] * 4)
        + buffers([4] * 4)
        + [pltpu.VMEM((2, HELD[0], LANES), F32), pltpu.VMEM((4, HELD[3], LANES), F32)],
        compiler_params=params(),
        name="down",
    )(second, first, fields)
    gathered = lax.all_to_all(chunks, axes, 0, 0, tiled=True)
    rows_total = CELLS * size_x
    width = 2 * CELLS * size_y
    return pl.pallas_call(
        functools.partial(up_kernel, size_x, size_y),
        out_shape=jax.ShapeDtypeStruct((2, LANES, LANES), F32),
        in_specs=[VMEM_SPEC] * (1 + LOCAL),
        out_specs=HBM_SPEC,
        scratch_shapes=[
            pltpu.VMEM((3, width // LANES, rows_total, LANES), F32),
            pltpu.VMEM((6, width // LANES, rows_total + 3 * SUB, LANES), F32),
            pltpu.VMEM((3, rows_total + 2 * SUB, width), F32),
            pltpu.VMEM((6, 5 * SUB, LANES), F32),
            pltpu.VMEM((4, HELD[3], LANES), F32),
        ]
        + [pltpu.VMEM((4, HELD[level], LANES), F32) for level in (1, 2, 3)]
        + [pltpu.VMEM((6, HELD[level + 1], LANES), F32) for level in (0, 1, 2)]
        + [pltpu.VMEM((2, LANES, LANES), F32), pltpu.SemaphoreType.DMA((len(PIECES),))],
        compiler_params=params(),
        name="up",
    )(gathered, *states)


def solution(mesh):
    sizes = dict(mesh.shape)
    placed = (P(None, "gx", "gy"), P("gx", "gy"), P("gx", "gy"), P("gx", "gy"))
    return jax.shard_map(
        functools.partial(per_device, sizes["gx"], sizes["gy"]),
        mesh=mesh,
        in_specs=placed,
        out_specs=P(None, "gx", "gy"),
        check_vma=False,
    )
```

```python
import functools

import jax
import jax.numpy as jnp
from jax import lax
from jax.experimental import pallas as pl
from jax.experimental.pallas import tpu as pltpu
from jax.sharding import PartitionSpec as P

LOCAL = 4
COARSE = 4
COARSE_SWEEPS = 8
OMEGA = 0.8
KEEP = 1.0 - OMEGA

LANES = 128
HALF = LANES // 2
SUB = 8
HALO = 16
GUARD = 8
CELLS = LANES >> LOCAL
ROWS = [(LANES + 2 * HALO) >> level for level in range(LOCAL)]
TILES = [-(-rows // SUB) for rows in ROWS]
HELD = [GUARD + SUB * tiles + 16 for tiles in TILES]
RIM = [HALO >> level for level in range(LOCAL)]
TOP = GUARD + HALO
LOW = TOP + LANES
HALF_TILES = TILES[0] // 2
MESSAGE = ROWS[0] // 2
CHUNK = 4
PIECES = (4, 8)
F32 = jnp.float32
FIRST_COST = 1 << 31
VMEM_LIMIT = 48 * 1024 * 1024

SWEPT, CENTRE, SIDE, ACROSS = 0, 4, 6, 8
STATE = 10
ITERATE, WEIGHT = 10, 14


def iota(dim, shape=(SUB, LANES)):
    return lax.broadcasted_iota(jnp.int32, shape, dim)


def lane_take(tile, index):
    return jnp.take_along_axis(tile, index, axis=1)


def lane_roll(tile, shift):
    return pltpu.roll(tile, shift % LANES, 1)


def tile_at(ref, slot, row):
    return ref[slot, row : row + SUB, :]


def first_kernel(blank):
    blank[...] = jnp.zeros((SUB, LANES), F32)


def bands_kernel(wet, blank, right_side, shift_coef, viscosity, first, second):
    odd = lax.axis_index("gx") % 2
    wetness = wet[0, 0].astype(F32)
    bottom = LANES - HALO
    for start, out in ((bottom - bottom * odd, first), (bottom * odd, second)):
        rows = pl.ds(pl.multiple_of(start, SUB), HALO)
        out[0] = right_side[0, rows, :] * wetness
        out[1] = right_side[1, rows, :] * wetness
        out[2] = shift_coef[rows, :]
        out[3] = viscosity[rows, :] * wetness


def own_rows(right_side, shift_coef, viscosity, field, tile):
    rows = slice(SUB * tile, SUB * tile + SUB)
    if field < 2:
        return right_side[field, rows, :]
    return shift_coef[rows, :] if field == 2 else viscosity[rows, :]


def rim_place(half, lane):
    to_left = ((lane >> 3) & 1) == half
    q = jnp.where(to_left, lane, (lane - (56 + 8 * half)) & (LANES - 1)) >> 4
    cell = 2 * (lane & 7) + (q & 1) + jnp.where(to_left, 0, LANES - HALO)
    return to_left, q >> 1, cell


def strips_kernel(
    size_x, wet, got_second, got_first, right_side, shift_coef, viscosity, first, second
):
    index_x = lax.axis_index("gx")
    odd_x = index_x % 2 == 1
    odd_y = lax.axis_index("gy") % 2 == 1
    wetness = wet[0, 0].astype(F32)
    above = (index_x > 0).astype(F32)
    below = (index_x < size_x - 1).astype(F32)
    lane = iota(1)
    rim_tiles = HALO // SUB

    def piece(field, tile):
        if rim_tiles <= tile < TILES[0] - rim_tiles:
            return own_rows(right_side, shift_coef, viscosity, field, tile - rim_tiles)
        top = tile < rim_tiles
        row = SUB * (tile if top else tile - (TILES[0] - rim_tiles))
        one, two = tile_at(got_first, field, row), tile_at(got_second, field, row)
        return jnp.where(odd_x, one, two) if top else jnp.where(odd_x, two, one)

    places = [rim_place(half, lane) for half in range(2)]
    found = {}
    for half in range(2):
        _, owner, cell = places[half]
        for tile in range(HALF_TILES):
            at = tile + half * HALF_TILES
            value = None
            for field in range(4):
                part = lane_take(piece(field, at), cell)
                value = part if value is None else jnp.where(owner == field, part, value)
            if rim_tiles <= at < TILES[0] - rim_tiles:
                value = value * jnp.where(owner == 2, 1.0, wetness)
            else:
                value = value * jnp.where(owner == 3, above if at < rim_tiles else below, 1.0)
            found[half, tile] = value
    for tile in range(HALF_TILES):
        left = jnp.where(places[0][0], found[0, tile], found[1, tile])
        right = jnp.where(places[0][0], found[1, tile], found[0, tile])
        rows = slice(SUB * tile, SUB * tile + SUB)
        first[rows, :] = jnp.where(odd_y, left, right)
        second[rows, :] = jnp.where(odd_y, right, left)


def halves_kernel(
    size_x, wet, got_second, got_first, right_side, shift_coef, viscosity, fields
):
    index_x = lax.axis_index("gx")
    odd_x = index_x % 2 == 1
    wetness = wet[0, 0].astype(F32)
    above = (index_x > 0).astype(F32)
    below = (index_x < size_x - 1).astype(F32)
    lane = iota(1)
    rim_tiles = HALO // SUB
    for tile in range(TILES[0]):
        row = GUARD + SUB * tile
        for field in range(4):
            if rim_tiles <= tile < TILES[0] - rim_tiles:
                value = own_rows(right_side, shift_coef, viscosity, field, tile - rim_tiles)
                if field != 2:
                    value = value * wetness
            else:
                top = tile < rim_tiles
                at = SUB * (tile if top else tile - (TILES[0] - rim_tiles))
                one, two = tile_at(got_first, field, at), tile_at(got_second, field, at)
                value = jnp.where(odd_x, one, two) if top else jnp.where(odd_x, two, one)
                if field == 3:
                    value = value * (above if top else below)
            for parity in range(2):
                fields[2 * field + parity, row : row + SUB, :] = lane_take(
                    value, (2 * lane + parity) & (LANES - 1)
                )


def down_kernel(size_y, devices, got_second, got_first, held, chunks, *refs):
    states, refs = refs[:LOCAL], refs[LOCAL:]
    viscous, refs = refs[:LOCAL], refs[LOCAL:]
    reactions, refs = refs[:LOCAL], refs[LOCAL:]
    sources, refs = refs[:LOCAL], refs[LOCAL:]
    weights, refs = refs[:LOCAL], refs[LOCAL:]
    iterates, refs = refs[:LOCAL], refs[LOCAL:]
    sums, (outers, ring) = refs[:LOCAL], refs[LOCAL:]
    index_y = lax.axis_index("gy")
    odd_y = index_y % 2 == 1
    lane, sub = iota(1), iota(0)
    side_ok = jnp.where(
        lane < 96, (index_y < size_y - 1).astype(F32), (index_y > 0).astype(F32)
    )
    odd_row = (sub & 1) == 1
    inner = lane < HALF
    even_block = ((lane >> 3) & 1) == 0

    def tiles(level):
        return [GUARD + SUB * tile for tile in range(TILES[level])]

    def put(ref, slot, row, value):
        ref[slot, row : row + SUB, :] = value

    def rims(row, slots):
        half, at = divmod((row - GUARD) // SUB, HALF_TILES)
        one, two = (r[SUB * at : SUB * at + SUB, :] for r in (got_first, got_second))
        after, before = jnp.where(odd_y, two, one), jnp.where(odd_y, one, two)
        if half == 0:
            both = jnp.where(even_block, after, before)
        else:
            both = jnp.where(even_block, before, after)
        values = []
        for slot in slots:
            rim = lane_roll(both, HALF - 16 * slot - 8 * half)
            if slot >= 4:
                rim = jnp.where(side_ok > 0, rim, 1.0 if slot < 6 else 0.0)
            values.append(jnp.where(inner, tile_at(held, slot, row), rim))
        return values

    def paired(ref, slot, start):
        return (
            ref[slot, pl.ds(start, SUB, stride=2), :] + ref[slot, pl.ds(start + 1, SUB, stride=2), :]
        )

    takes = [(2 * lane + offset) & (LANES - 1) for offset in (0, 1, -1, 2)]

    def coefficients(level):
        if level == 0:
            for row in tiles(level):
                values = rims(row, (4, 5, 6, 7))
                for slot, value in enumerate(values[:2]):
                    put(reactions[level], slot, row, value)
                for slot, value in enumerate(values[2:]):
                    put(viscous[level], slot, row, value)
                put(sums[level], 2, row, values[0] + values[1])
                put(sums[level], 3, row, values[2] + values[3])
            return
        ref = sums[level - 1]
        loaded = {
            row: [
                scale * paired(ref, slot, GUARD + 2 * (row - GUARD))
                for slot, scale in ((2, 0.25), (3, 0.0625))
            ]
            for row in tiles(level)
        }
        found = {row: ([], []) for row in loaded}
        for kind, index in enumerate(takes):
            for row, (reaction, viscosity) in loaded.items():
                value = lane_take(viscosity, index)
                put(viscous[level], kind, row, value)
                found[row][1].append(value)
                if kind < 2:
                    value = lane_take(reaction, index)
                    put(reactions[level], kind, row, value)
                    found[row][0].append(value)
        for row, (reaction, viscosity) in found.items():
            put(sums[level], 2, row, reaction[0] + reaction[1])
            put(sums[level], 3, row, viscosity[0] + viscosity[1])

    def faces(level, row):
        here = [tile_at(viscous[level], p, row) for p in range(2)]
        north = [jnp.minimum(here[p], tile_at(viscous[level], p, row - 1)) for p in range(2)]
        south = [jnp.minimum(here[p], tile_at(viscous[level], p, row + 1)) for p in range(2)]
        return here, jnp.minimum(here[0], here[1]), north, south

    def outside(level, row, here):
        if level == 0:
            beyond = [lane_roll(here[1], 1), lane_roll(here[0], -1)]
        else:
            beyond = [tile_at(viscous[level], 2 + p, row) for p in range(2)]
        return [jnp.minimum(h, b) for h, b in zip(here, beyond)]

    def weigh(level):
        for row in tiles(level):
            here, middle, north, south = faces(level, row)
            outer = outside(level, row, here)
            found = []
            for p in range(2):
                diagonal = tile_at(reactions[level], p, row) + (
                    (middle + outer[p]) + (north[p] + south[p])
                )
                found.append(OMEGA / diagonal)
                if level == 0:
                    put(outers, p, row, outer[p])
            if level > 0:
                found += [lane_roll(found[1], 1), lane_roll(found[0], -1)]
            for slot, value in enumerate(found):
                put(weights[level], slot, row, value)

    def take_sources(level):
        if level == 0:
            for row in tiles(level):
                for slot, value in enumerate(rims(row, (0, 1, 2, 3))):
                    put(sources[level], slot, row, value)
            return
        loaded = {
            row: [
                0.25 * paired(sums[level - 1], comp, GUARD + 2 * (row - GUARD))
                for comp in range(2)
            ]
            for row in tiles(level)
        }
        for kind, index in enumerate(takes):
            for row, values in loaded.items():
                for comp in range(2):
                    put(sources[level], 4 * comp + kind, row, lane_take(values[comp], index))

    def kinds(level):
        return 2 if level == 0 else 4

    def first_sweep(level):
        for row in tiles(level):
            for comp in range(2):
                for p in range(2):
                    put(
                        iterates[level],
                        2 * comp + p,
                        row,
                        tile_at(weights[level], p, row)
                        * tile_at(sources[level], kinds(level) * comp + p, row),
                    )

    def residual(level):
        state, iterate, weight, source = (
            states[level],
            iterates[level],
            weights[level],
            sources[level],
        )
        for row in tiles(level):
            _, middle, north, south = faces(level, row)
            if level == 0:
                outer = [tile_at(outers, p, row) for p in range(2)]
            else:
                outer = outside(level, row, [tile_at(viscous[level], p, row) for p in range(2)])
            scale = [tile_at(weight, p, row) for p in range(2)]
            kept = level > 0 or TOP <= row < LOW
            for comp in range(2):
                here = [tile_at(iterate, 2 * comp + p, row) for p in range(2)]
                if level == 0:
                    beyond = [lane_roll(here[1], 1), lane_roll(here[0], -1)]
                else:
                    beyond = [
                        tile_at(weight, 2 + p, row) * tile_at(source, 4 * comp + 2 + p, row)
                        for p in range(2)
                    ]
                total = None
                for p in range(2):
                    slot = 2 * comp + p
                    around = middle * here[1 - p] + outer[p] * beyond[p]
                    around = around + (
                        south[p] * tile_at(iterate, slot, row + 1)
                        + north[p] * tile_at(iterate, slot, row - 1)
                    )
                    left = KEEP * tile_at(source, kinds(level) * comp + p, row) + around
                    if kept:
                        put(state, SWEPT + slot, row, here[p] + scale[p] * left)
                    if level == LOCAL - 1:
                        put(ring, slot, row, left)
                        put(state, ITERATE + slot, row, here[p])
                    total = left if total is None else total + left
                put(sums[level], comp, row, total)
            if kept:
                for p in range(2):
                    within = jnp.where(odd_row, north[p], south[p])
                    across = jnp.where(odd_row, south[p], north[p])
                    put(state, CENTRE + p, row, KEEP + scale[p] * (middle + within))
                    put(state, SIDE + p, row, scale[p] * outer[p])
                    put(state, ACROSS + p, row, scale[p] * across)
                    if level == LOCAL - 1:
                        put(state, WEIGHT + p, row, scale[p])

    coefficients(0)
    take_sources(0)
    weigh(0)
    coefficients(1)
    first_sweep(0)
    residual(0)
    weigh(1)
    coefficients(2)
    take_sources(1)
    weigh(2)
    coefficients(3)
    first_sweep(1)
    residual(1)
    take_sources(2)
    weigh(3)
    first_sweep(2)
    residual(2)
    take_sources(3)
    first_sweep(3)
    residual(3)

    start = GUARD + RIM[LOCAL - 1]
    column = lane & (SUB - 1)
    own = [
        lane_take(scale * paired(sums[LOCAL - 1], slot, start), column)
        for slot, scale in enumerate((0.25, 0.25, 0.25, 0.0625))
    ]
    turned = ((lane >> 3) - index_y) & 15
    chosen = (turned & (SUB - 1)) == sub

    def packed(value):
        return jnp.sum(value, axis=0, keepdims=True)

    def joined(a, b):
        return packed(jnp.where(chosen, jnp.where(turned < SUB, a, b), 0.0))

    edge = (lane >> 4) & 3
    place = lane & 15

    rims = jnp.zeros((SUB, LANES), F32)
    for p in range(2):
        index = jnp.where(edge < 2, column, 0 if p == 0 else SUB - 1)
        for part in range(2):
            along = (edge == part) & ((place >> 3) == p) & (sub == (0 if part == 0 else SUB - 1))
            up = (edge == 2 + p) & (place == sub + SUB * part)
            row = start + SUB * part
            value = jnp.where(
                inner,
                lane_take(tile_at(ring, p, row), index),
                lane_take(tile_at(ring, 2 + p, row), index),
            )
            rims = jnp.where(along | up, value, rims)
    kind = sub % CHUNK
    parts = [joined(own[0], own[1]), joined(own[2], own[2]), packed(rims), joined(own[3], own[3])]
    tile = jnp.where(
        kind < 2,
        jnp.where(kind == 0, parts[0], parts[1]),
        jnp.where(kind == 2, parts[2], parts[3]),
    )
    for block in range(CHUNK * devices // SUB):
        chunks[SUB * block : SUB * block + SUB, :] = tile


def write(buffer, slot, rows, value):
    for column in range(buffer.shape[1]):
        buffer[slot, column, rows, :] = value[:, LANES * column : LANES * column + LANES]


def read(buffer, slot, rows):
    parts = [buffer[slot, column, rows, :] for column in range(buffer.shape[1])]
    return parts[0] if len(parts) == 1 else jnp.concatenate(parts, 1)


class Coarse:
    def __init__(self, step, row_step, rows, cols_total, width):
        self.step, self.row_step = step, row_step
        self.shape = (rows, width)
        lane, row = iota(1, self.shape), iota(0, self.shape)
        column = lane & (cols_total - 1)
        self.odd_lane, self.odd_row = (lane & step) != 0, (row & row_step) != 0
        self.leftmost = column < 2 * step
        self.rightmost = column >= cols_total - 2 * step
        self.top, self.bottom = row < row_step, row >= rows - row_step

    def along(self, value, amount):
        return pltpu.roll(value, amount % self.shape[1], 1)

    def down(self, value, amount):
        return pltpu.roll(value, amount % self.shape[0], 0)

    def paired(self, value):
        return (
            jnp.where(self.odd_lane, self.along(value, self.step), value),
            jnp.where(self.odd_lane, value, self.along(value, -self.step)),
        )

    def outside(self, value):
        return (
            jnp.where(
                self.odd_lane, self.along(value, 2 * self.step), self.along(value, self.step)
            ),
            jnp.where(
                self.odd_lane, self.along(value, -self.step), self.along(value, -2 * self.step)
            ),
        )

    def farther(self, value):
        return (
            jnp.where(
                self.odd_lane, self.along(value, 3 * self.step), self.along(value, 2 * self.step)
            ),
            jnp.where(
                self.odd_lane, self.along(value, -2 * self.step), self.along(value, -3 * self.step)
            ),
        )

    def rows_beside(self, here):
        above = jnp.where(self.top, 0.0, self.down(here, self.row_step))
        below = jnp.where(self.bottom, 0.0, self.down(here, -self.row_step))
        return jnp.minimum(here, above), jnp.minimum(here, below)

    def coefficients(self, viscous, reaction):
        here, beyond, far = self.paired(viscous), self.outside(viscous), self.farther(viscous)
        reactions, reactions_beyond = self.paired(reaction), self.outside(reaction)
        edges = (self.leftmost, self.rightmost)
        self.middle = jnp.minimum(here[0], here[1])
        self.outer, self.north, self.south = [], [], []
        self.weights, self.weights_beyond = [], []
        for p in range(2):
            outer = jnp.minimum(here[p], jnp.where(edges[p], 0.0, beyond[p]))
            north, south = self.rows_beside(here[p])
            diagonal = reactions[p] + ((self.middle + outer) + (north + south))
            self.weights.append(OMEGA / diagonal)
            self.outer.append(outer)
            self.north.append(north)
            self.south.append(south)
            next_outer = jnp.minimum(beyond[p], far[p])
            north, south = self.rows_beside(beyond[p])
            diagonal = reactions_beyond[p] + ((outer + next_outer) + (north + south))
            self.weights_beyond.append(OMEGA / diagonal)
        return here[0] + here[1], reactions[0] + reactions[1]

    def take(self, source):
        self.values, self.values_beyond = self.paired(source), self.outside(source)

    def residual(self):
        x = [w * s for w, s in zip(self.weights, self.values)]
        x_beyond = [w * s for w, s in zip(self.weights_beyond, self.values_beyond)]
        total, self.swept = None, []
        for p in range(2):
            around = self.middle * x[1 - p] + self.outer[p] * x_beyond[p]
            around = around + (
                self.south[p] * self.down(x[p], -self.row_step)
                + self.north[p] * self.down(x[p], self.row_step)
            )
            left = KEEP * self.values[p] + around
            self.swept.append(x[p] + self.weights[p] * left)
            total = left if total is None else total + left
        return total

    def prepare(self):
        parts = []
        for p in range(2):
            within = jnp.where(self.odd_row, self.north[p], self.south[p])
            out = jnp.where(self.odd_row, self.south[p], self.north[p])
            weight = self.weights[p]
            centre = KEEP + weight * (self.middle + within)
            parts.append((self.swept[p], centre, weight * self.outer[p], weight * out))
        self.parts = parts
        self.left_parts = [self.along(value, 2 * self.step) for value in parts[1]]
        self.right_parts = [self.along(value, -2 * self.step) for value in parts[0]]

    def corrected(self, here, left, right):
        def swept(part, own, side):
            return (part[0] + part[1] * own[0]) + (part[2] * side[0] + part[3] * own[1])

        even, odd = swept(self.parts[0], here, left), swept(self.parts[1], here, right)
        before, after = swept(self.left_parts, left, here), swept(self.right_parts, right, here)
        return (
            jnp.where(self.odd_lane, odd, even),
            jnp.where(self.odd_lane, even, before),
            jnp.where(self.odd_lane, after, odd),
        )


def coarse_solve(grid, buffer, rows_total, cols_total, width, meanwhile):
    columns = width // LANES

    def whole(slot):
        return jnp.concatenate([grid[slot, c] for c in range(columns)], 1) if columns > 1 else grid[slot, 0]

    levels, rows, row_step = [], rows_total, 1
    for index in range(COARSE + 1):
        levels.append(Coarse(1 << index, row_step, rows, cols_total, width))
        if rows > SUB:
            rows //= 2
        else:
            row_step *= 2

    def folded(index, value, slot, scale):
        level = levels[index]
        rows = level.shape[0]
        if levels[index + 1].shape[0] == rows:
            other = jnp.where(
                level.odd_row, level.down(value, level.row_step), level.down(value, -level.row_step)
            )
            return scale * (value + other)
        write(buffer, slot, slice(0, rows), value)
        first, second = [pl.ds(begin, rows // 2, stride=2) for begin in range(2)]
        return scale * (read(buffer, slot, first) + read(buffer, slot, second))

    def opened(index, value, slot):
        level = levels[index]
        rows = level.shape[0]
        if value.shape[0] == rows:
            return value, jnp.where(
                level.odd_row, level.down(value, -level.row_step), level.down(value, level.row_step)
            )
        half = rows // 2
        blank = jnp.zeros((SUB, width), F32)
        for begin in range(2):
            write(buffer, slot, pl.ds(begin, half, stride=2), value)
        write(buffer, slot + 1, slice(SUB, 2 * SUB), blank)
        write(buffer, slot + 1, slice(rows, rows + SUB), blank)
        for begin in (SUB + 2, SUB - 1):
            write(buffer, slot + 1, pl.ds(begin, half, stride=2), value)
        return read(buffer, slot, slice(0, rows)), read(buffer, slot + 1, slice(SUB, SUB + rows))

    viscous, reaction, source = [None] * 5, [None] * 5, [None] * 5
    viscous[0], reaction[0], source[0] = whole(2), whole(1), whole(0)

    def coefficients(index):
        pair, reactions = levels[index].coefficients(viscous[index], reaction[index])
        viscous[index + 1] = folded(index, pair, 0, 0.0625)
        reaction[index + 1] = folded(index, reactions, 1, 0.25)

    def residual(index):
        source[index + 1] = folded(index, levels[index].residual(), 2, 0.25)

    last = levels[COARSE]
    block = 1 << COARSE
    cols_left = cols_total // block
    rows_left = last.shape[0]
    lane = iota(1, (rows_left, LANES))
    groups = 1 if cols_total < LANES else 2
    per_group = columns // groups

    def spread(*arrays):
        found = [[] for _ in arrays]
        for group in range(groups):
            for j in range(cols_left):
                column, place = divmod(block * j, LANES)
                column += group * per_group
                if groups == 1:
                    place = place + (lane & (LANES - cols_total))
                else:
                    place = jnp.full((rows_left, LANES), place, jnp.int32)
                for value, columns_found in zip(arrays, found):
                    tile = value[:, LANES * column : LANES * column + LANES]
                    columns_found.append(lane_take(tile, place))
        return found

    def flat(values, group, j):
        return values[group * cols_left + j]

    levels[0].take(source[0])
    coefficients(0)
    coefficients(1)
    residual(0)
    levels[1].take(source[1])
    coefficients(2)
    residual(1)
    levels[2].take(source[2])
    coefficients(3)
    residual(2)
    levels[3].take(source[3])
    viscous_columns, reaction_columns = spread(viscous[4], reaction[4])

    top, bottom = last.top[:, :LANES], last.bottom[:, :LANES]
    pulls, weights = [], []
    for group in range(groups):
        for j in range(cols_left):
            here = flat(viscous_columns, group, j)
            above = jnp.where(top, 0.0, last.down(here, last.row_step))
            below = jnp.where(bottom, 0.0, last.down(here, -last.row_step))
            links = [jnp.minimum(here, above), jnp.minimum(here, below)]
            links += [
                jnp.minimum(here, flat(viscous_columns, group, other))
                for other in (j - 1, j + 1)
                if 0 <= other < cols_left
            ]
            weight = OMEGA / (flat(reaction_columns, group, j) + sum(links))
            weights.append(weight)
            pulls.append([weight * link for link in links])
    residual(3)
    pushed = [w * s for w, s in zip(weights, spread(source[4])[0])]
    meanwhile()
    for index in range(COARSE - 1, -1, -1):
        levels[index].prepare()
    values = pushed
    for _ in range(COARSE_SWEEPS - 1):
        following = []
        for group in range(groups):
            for j in range(cols_left):
                at = group * cols_left + j
                here, pull = values[at], pulls[at]
                total = (KEEP * here + pushed[at]) + (
                    pull[0] * last.down(here, last.row_step)
                    + pull[1] * last.down(here, -last.row_step)
                )
                sides = [other for other in (j - 1, j + 1) if 0 <= other < cols_left]
                for link, other in zip(pull[2:], sides):
                    total = total + link * flat(values, group, other)
                following.append(total)
        values = following

    def laid(shift):
        found = []
        for column in range(columns):
            group = column // per_group
            place = ((lane & (cols_total - 1)) if groups == 1 else lane) // block
            place = place + (column % per_group) * (LANES // block)
            value = jnp.zeros((rows_left, LANES), F32)
            for j in range(cols_left):
                value = jnp.where(place == j + shift, flat(values, group, j), value)
            found.append(value)
        return found[0] if columns == 1 else jnp.concatenate(found, 1)

    corrections = [laid(shift) for shift in (0, 1, -1)]
    for index in range(COARSE - 1, -1, -1):
        corrections = levels[index].corrected(
            *[opened(index, value, 2 * at) for at, value in enumerate(corrections)]
        )
    return corrections


def up_kernel(size_x, size_y, gathered, state0, state1, state2, state3, out, *refs):
    grid, buffer, whole, window, swept3, corr1, corr2, corr3, merged0, merged1, merged2 = refs[:11]
    finished, sems = refs[11:]
    index_x, index_y = lax.axis_index("gx"), lax.axis_index("gy")
    rows_total, cols_total = CELLS * size_x, CELLS * size_y
    width = 2 * cols_total
    columns = width // LANES
    per_column = LANES // CELLS
    lane, sub = iota(1), iota(0)

    tall = iota(1, (size_x, LANES)) // CELLS
    modulus = min(size_y, per_column)
    for column in range(columns):
        comp = column // (columns // 2) if columns > 1 else 0
        first = (column % (columns // 2)) * per_column if columns > 1 else 0
        for slot, kind in ((2, 3), (1, 1), (0, 0)):
            chunks = [
                gathered[pl.ds(CHUNK * (first + j) + kind, size_x, stride=CHUNK * size_y), :]
                for j in range(modulus)
            ]
            for r in range(CELLS):
                turn = r + CELLS * comp
                value = chunks[0]
                for j in range(1, modulus):
                    value = jnp.where(((tall - turn) & (modulus - 1)) == j, chunks[j], value)
                grid[slot, column, pl.ds(r, size_x, stride=CELLS), :] = lane_roll(
                    value, -CELLS * turn
                )

    def ring_row(dx, dy):
        i = jnp.clip(index_x + dx, 0, size_x - 1)
        j = jnp.clip(index_y + dy, 0, size_y - 1)
        return jnp.broadcast_to(
            gathered[pl.ds(CHUNK * (i * size_y + j) + 2, 1), :], (SUB, LANES)
        )

    start = GUARD + RIM[3]

    def complete_ring():
        beside = {
            (dx, dy): ring_row(dx, dy) for dx in (-1, 0, 1) for dy in (-1, 0, 1) if dx or dy
        }
        for comp in range(2):
            base = comp * HALF
            for p in range(2):
                slot = 2 * comp + p
                end = 7 if p else 0
                corner_lane = LANES - 1 if p else SUB
                dy = -1 if p else 1
                for tile in range(2):
                    at = start + SUB * tile
                    index = base + (48 if p else 32) + SUB * tile + sub
                    ringed = lane_take(beside[0, dy], index)
                    swept = jnp.where(
                        lane == corner_lane,
                        tile_at(state3, ITERATE + slot, at)
                        + tile_at(state3, WEIGHT + p, at) * ringed,
                        tile_at(state3, SWEPT + slot, at),
                    )
                    swept3[slot, at : at + SUB, :] = swept
                for dx, at, edge in ((-1, start - 1, 16), (1, start + 2 * SUB, 0)):
                    index = base + edge + 8 * p
                    ringed = jnp.where(
                        lane == corner_lane,
                        lane_take(beside[dx, dy], jnp.full((SUB, LANES), index + end, jnp.int32)),
                        lane_take(beside[dx, 0], index + (lane & 7)),
                    )
                    rows = slice(at, at + 1)
                    swept3[slot, rows, :] = (
                        state3[ITERATE + slot, rows, :] + state3[WEIGHT + p, rows, :] * ringed[0:1]
                    )

    corrections = coarse_solve(grid, buffer, rows_total, cols_total, width, complete_ring)

    blank = jnp.zeros((SUB, width), F32)
    for kind, correction in enumerate(corrections):
        whole[kind, GUARD : GUARD + rows_total, :] = correction
        whole[kind, 0:GUARD, :] = blank
        whole[kind, GUARD + rows_total : GUARD + rows_total + SUB, :] = blank
    near_rows = pl.ds(pl.multiple_of(CELLS * index_x, SUB), 3 * SUB)
    for comp in range(2):
        shift = (2 * width - cols_total * comp - CELLS * index_y) % width
        for kind in range(3):
            turned = pltpu.roll(whole[kind, near_rows, :], shift, 1)
            if columns > 1:
                tall_lane = iota(1, (3 * SUB, LANES))
                turned = jnp.where(
                    tall_lane < HALF, turned[:, :LANES], turned[:, width - LANES :]
                )
            window[3 * comp + kind, 0 : 3 * SUB, :] = turned

    def swept_rows(ref, level, coarse_row, parity, here, beyond, across, comp):
        at = pl.ds(GUARD + RIM[level] + 2 * coarse_row + parity, SUB, stride=2)
        state = (state0, state1, state2, state3)[level]
        return [
            (ref[SWEPT + 2 * comp + p, at, :] + state[CENTRE + p, at, :] * here)
            + (state[SIDE + p, at, :] * beyond[p] + state[ACROSS + p, at, :] * across)
            for p in range(2)
        ]

    for comp in range(2):
        for tile in range(2):
            first = SUB * tile - 1
            at = GUARD + first
            here, left, right = [tile_at(window, 3 * comp + kind, at) for kind in range(3)]
            for parity in range(2):
                across = tile_at(window, 3 * comp, at + (1 if parity else -1))
                found = swept_rows(swept3, 3, first, parity, here, (left, right), across, comp)
                rows = pl.ds(GUARD + RIM[3] + 2 * first + parity, SUB, stride=2)
                for p in range(2):
                    corr3[2 * comp + p, rows, :] = found[p]

    corrs = [None, corr1, corr2, corr3]
    merged = [merged0, merged1, merged2]
    near = ((((lane + 32) & (LANES - 1)) - 32) >> 1) & (LANES - 1)
    odd_lane = (lane & 1) == 1
    for level in (2, 1, 0):
        coarse = level + 1
        corr, state, whole_rows = corrs[coarse], (state0, state1, state2)[level], merged[level]
        count = (LANES >> coarse) + 2
        origin = GUARD + RIM[coarse]
        places = [
            (comp, origin - 1 + SUB * tile)
            for tile in range(-(-count // SUB))
            for comp in range(2)
        ]
        pairs = {
            (comp, at): (tile_at(corr, 2 * comp, at), tile_at(corr, 2 * comp + 1, at))
            for comp, at in places
        }
        moved = {
            place: [lane_take(even, near), lane_take(odd, near)]
            for place, (even, odd) in pairs.items()
        }
        for place, (even, _) in pairs.items():
            moved[place].append(lane_take(even, (near + 1) & (LANES - 1)))
        for place, (_, odd) in pairs.items():
            moved[place].append(lane_take(odd, (near - 1) & (LANES - 1)))
        for (comp, at), (even_here, odd_here, even_next, odd_last) in moved.items():
            rows = slice(at, at + SUB)
            whole_rows[3 * comp, rows, :] = jnp.where(odd_lane, odd_here, even_here)
            whole_rows[3 * comp + 1, rows, :] = jnp.where(odd_lane, even_next, odd_here)
            whole_rows[3 * comp + 2, rows, :] = jnp.where(odd_lane, even_here, odd_last)
        if level > 0:
            first, tiles = -1, -(-count // SUB)
        else:
            first, tiles = 0, (count - 2) // SUB
        copies = []
        for tile in range(tiles):
            coarse_row = first + SUB * tile
            at = origin + coarse_row
            for comp in range(2):
                here, right, left = [tile_at(whole_rows, 3 * comp + k, at) for k in range(3)]
                for parity in range(2):
                    across = tile_at(whole_rows, 3 * comp, at + (1 if parity else -1))
                    found = swept_rows(
                        state, level, coarse_row, parity, here, (left, right), across, comp
                    )
                    if level > 0:
                        rows = pl.ds(GUARD + RIM[level] + 2 * coarse_row + parity, SUB, stride=2)
                        for p in range(2):
                            corrs[level][2 * comp + p, rows, :] = found[p]
                    else:
                        rows = pl.ds(2 * coarse_row + parity, SUB, stride=2)
                        finished[comp, rows, :] = jnp.where(
                            odd_lane,
                            lane_take(found[1], lane >> 1),
                            lane_take(found[0], lane >> 1),
                        )
            if level == 0 and tile + 1 in PIECES:
                piece = len(copies)
                begin = 2 * SUB * PIECES[piece - 1] if piece else 0
                rows = pl.ds(begin, 2 * SUB * (tile + 1) - begin)
                copy = pltpu.make_async_copy(
                    finished.at[:, rows, :], out.at[:, rows, :], sems.at[piece]
                )
                copy.start()
                copies.append(copy)
        for copy in copies:
            copy.wait()


def params():
    return pltpu.CompilerParams(vmem_limit_bytes=VMEM_LIMIT)


VMEM_SPEC = pl.BlockSpec(memory_space=pltpu.VMEM)
SMEM_SPEC = pl.BlockSpec(memory_space=pltpu.SMEM)
HBM_SPEC = pl.BlockSpec(memory_space=pltpu.HBM)


def swap_routes(size_x, size_y):
    def index(i, j):
        return i * size_y + j

    routes = []
    for axis in range(2):
        size = (size_x, size_y)[axis]
        for offset in range(2):
            route = []
            for i in range(size_x):
                for j in range(size_y):
                    here = (i, j)[axis]
                    other = here + 1 if here % 2 == offset else here - 1
                    if 0 <= other < size:
                        peer = (other, j) if axis == 0 else (i, other)
                    else:
                        peer = (i, j ^ 1) if axis == 0 else (i ^ 1, j)
                    route.append((index(i, j), index(*peer)))
            routes.append(route)
    return routes


def per_device(size_x, size_y, right_side, shift_coef, viscosity, wet_tiles):
    axes = ("gx", "gy")
    devices = size_x * size_y
    routes = swap_routes(size_x, size_y)
    band = pltpu.VMEM((4, HALO, LANES), F32)
    own = (right_side, shift_coef, viscosity)
    blank = pl.pallas_call(
        first_kernel,
        out_shape=pltpu.VMEM((SUB, LANES), F32),
        out_specs=VMEM_SPEC,
        cost_estimate=pl.CostEstimate(flops=FIRST_COST, bytes_accessed=FIRST_COST // 16, transcendentals=0),
        compiler_params=params(),
        name="first",
    )()
    wet_tiles, blank = lax.optimization_barrier((wet_tiles, blank))
    first, second = pl.pallas_call(
        bands_kernel,
        out_shape=(band, band),
        in_specs=[SMEM_SPEC] + [VMEM_SPEC] * 4,
        out_specs=(VMEM_SPEC,) * 2,
        compiler_params=params(),
        name="bands",
    )(wet_tiles, blank, *own)
    second = lax.ppermute(second, axes, routes[1])
    first = lax.ppermute(first, axes, routes[0])
    strip = jax.ShapeDtypeStruct((MESSAGE, LANES), F32)
    got = (second, first)
    first, second = pl.pallas_call(
        functools.partial(strips_kernel, size_x),
        out_shape=(strip, strip),
        in_specs=[SMEM_SPEC] + [VMEM_SPEC] * 5,
        out_specs=(VMEM_SPEC,) * 2,
        compiler_params=params(),
        name="strips",
    )(wet_tiles, *got, *own)
    fields = pl.pallas_call(
        functools.partial(halves_kernel, size_x),
        out_shape=pltpu.VMEM((8, HELD[0], LANES), F32),
        in_specs=[SMEM_SPEC] + [VMEM_SPEC] * 5,
        out_specs=VMEM_SPEC,
        cost_estimate=pl.CostEstimate(flops=1 << 20, bytes_accessed=1 << 21, transcendentals=0),
        compiler_params=params(),
        name="halves",
    )(wet_tiles, *got, *own)
    second = lax.ppermute(second, axes, routes[3])
    first = lax.ppermute(first, axes, routes[2])

    def buffers(counts):
        return [pltpu.VMEM((n, HELD[level], LANES), F32) for level, n in enumerate(counts)]

    chunks, *states = pl.pallas_call(
        functools.partial(down_kernel, size_y, devices),
        out_shape=(jax.ShapeDtypeStruct((CHUNK * devices, LANES), F32),)
        + tuple(buffers([STATE, STATE, STATE, STATE + 6])),
        in_specs=[VMEM_SPEC] * 3,
        out_specs=(VMEM_SPEC,) * (1 + LOCAL),
        scratch_shapes=buffers([2, 4, 4, 4])
        + buffers([2] * 4)
        + buffers([4, 8, 8, 8])
        + buffers([2, 4, 4, 4])
        + buffers([4] * 4)
        + buffers([4] * 4)
        + [pltpu.VMEM((2, HELD[0], LANES), F32), pltpu.VMEM((4, HELD[3], LANES), F32)],
        compiler_params=params(),
        name="down",
    )(second, first, fields)
    gathered = lax.all_to_all(chunks, axes, 0, 0, tiled=True)
    rows_total = CELLS * size_x
    width = 2 * CELLS * size_y
    return pl.pallas_call(
        functools.partial(up_kernel, size_x, size_y),
        out_shape=jax.ShapeDtypeStruct((2, LANES, LANES), F32),
        in_specs=[VMEM_SPEC] * (1 + LOCAL),
        out_specs=HBM_SPEC,
        scratch_shapes=[
            pltpu.VMEM((3, width // LANES, rows_total, LANES), F32),
            pltpu.VMEM((6, width // LANES, rows_total + 3 * SUB, LANES), F32),
            pltpu.VMEM((3, rows_total + 2 * SUB, width), F32),
            pltpu.VMEM((6, 5 * SUB, LANES), F32),
            pltpu.VMEM((4, HELD[3], LANES), F32),
        ]
        + [pltpu.VMEM((4, HELD[level], LANES), F32) for level in (1, 2, 3)]
        + [pltpu.VMEM((6, HELD[level + 1], LANES), F32) for level in (0, 1, 2)]
        + [pltpu.VMEM((2, LANES, LANES), F32), pltpu.SemaphoreType.DMA((len(PIECES),))],
        compiler_params=params(),
        name="up",
    )(gathered, *states)


def solution(mesh):
    sizes = dict(mesh.shape)
    placed = (P(None, "gx", "gy"), P("gx", "gy"), P("gx", "gy"), P("gx", "gy"))
    return jax.shard_map(
        functools.partial(per_device, sizes["gx"], sizes["gy"]),
        mesh=mesh,
        in_specs=placed,
        out_specs=P(None, "gx", "gy"),
        check_vma=False,
    )
```

```python
import functools

import jax
import jax.numpy as jnp
from jax import lax
from jax.experimental import pallas as pl
from jax.experimental.pallas import tpu as pltpu
from jax.sharding import PartitionSpec as P

LOCAL = 4
COARSE = 4
COARSE_SWEEPS = 8
OMEGA = 0.8
KEEP = 1.0 - OMEGA

LANES = 128
HALF = LANES // 2
SUB = 8
HALO = 16
GUARD = 8
CELLS = LANES >> LOCAL
ROWS = [(LANES + 2 * HALO) >> level for level in range(LOCAL)]
TILES = [-(-rows // SUB) for rows in ROWS]
HELD = [GUARD + SUB * tiles + 16 for tiles in TILES]
RIM = [HALO >> level for level in range(LOCAL)]
TOP = GUARD + HALO
LOW = TOP + LANES
HALF_TILES = TILES[0] // 2
MESSAGE = ROWS[0] // 2
CHUNK = 4
PIECES = (4, 8)
F32 = jnp.float32
FIRST_COST = 1 << 31
VMEM_LIMIT = 48 * 1024 * 1024

SWEPT, CENTRE, SIDE, ACROSS = 0, 4, 6, 8
STATE = 10
ITERATE, WEIGHT = 10, 14


def iota(dim, shape=(SUB, LANES)):
    return lax.broadcasted_iota(jnp.int32, shape, dim)


def lane_take(tile, index):
    return jnp.take_along_axis(tile, index, axis=1)


def lane_roll(tile, shift):
    return pltpu.roll(tile, shift % LANES, 1)


def tile_at(ref, slot, row):
    return ref[slot, row : row + SUB, :]


def first_kernel(blank):
    blank[...] = jnp.zeros((SUB, LANES), F32)


def bands_kernel(wet, blank, right_side, shift_coef, viscosity, first, second):
    odd = lax.axis_index("gx") % 2
    wetness = wet[0, 0].astype(F32)
    bottom = LANES - HALO
    for start, out in ((bottom - bottom * odd, first), (bottom * odd, second)):
        rows = pl.ds(pl.multiple_of(start, SUB), HALO)
        out[0] = right_side[0, rows, :] * wetness
        out[1] = right_side[1, rows, :] * wetness
        out[2] = shift_coef[rows, :]
        out[3] = viscosity[rows, :] * wetness


def own_rows(right_side, shift_coef, viscosity, field, tile):
    rows = slice(SUB * tile, SUB * tile + SUB)
    if field < 2:
        return right_side[field, rows, :]
    return shift_coef[rows, :] if field == 2 else viscosity[rows, :]


def rim_place(half, lane):
    to_left = ((lane >> 3) & 1) == half
    q = jnp.where(to_left, lane, (lane - (56 + 8 * half)) & (LANES - 1)) >> 4
    cell = 2 * (lane & 7) + (q & 1) + jnp.where(to_left, 0, LANES - HALO)
    return to_left, q >> 1, cell


def rim_value(pieces, place):
    _, owner, cell = place
    value = None
    for field in range(4):
        part = lane_take(pieces[field], cell)
        value = part if value is None else jnp.where(owner == field, part, value)
    return value


RIM_TILES = HALO // SUB


def edges_kernel(wet, right_side, shift_coef, viscosity, lefts, rights):
    wetness = wet[0, 0].astype(F32)
    lane = iota(1)
    places = [rim_place(half, lane) for half in range(2)]
    found = {}
    for half in range(2):
        mask = jnp.where(places[half][1] == 2, 1.0, wetness)
        for tile in range(HALF_TILES):
            at = tile + half * HALF_TILES - RIM_TILES
            if 0 <= at < LANES // SUB:
                pieces = [own_rows(right_side, shift_coef, viscosity, f, at) for f in range(4)]
                found[half, tile] = rim_value(pieces, places[half]) * mask
    blank = jnp.zeros((SUB, LANES), F32)
    for tile in range(HALF_TILES):
        upper, lower = (found.get((half, tile), blank) for half in range(2))
        rows = slice(SUB * tile, SUB * tile + SUB)
        lefts[rows, :] = jnp.where(places[0][0], upper, lower)
        rights[rows, :] = jnp.where(places[0][0], lower, upper)


def strips_kernel(size_x, got_second, got_first, lefts, rights, first, second):
    index_x = lax.axis_index("gx")
    odd_x = index_x % 2 == 1
    odd_y = lax.axis_index("gy") % 2 == 1
    above = (index_x > 0).astype(F32)
    below = (index_x < size_x - 1).astype(F32)
    lane = iota(1)
    places = [rim_place(half, lane) for half in range(2)]
    found = {}
    for half in range(2):
        mask = jnp.where(places[half][1] == 3, below if half else above, 1.0)
        for tile in range(RIM_TILES):
            row = SUB * tile
            pieces = []
            for field in range(4):
                one, two = tile_at(got_first, field, row), tile_at(got_second, field, row)
                pieces.append(jnp.where(odd_x, two, one) if half else jnp.where(odd_x, one, two))
            at = HALF_TILES - RIM_TILES + tile if half else tile
            found[at] = (half, rim_value(pieces, places[half]) * mask)
    for tile in range(HALF_TILES):
        rows = slice(SUB * tile, SUB * tile + SUB)
        left, right = lefts[rows, :], rights[rows, :]
        if tile in found:
            half, value = found[tile]
            left = jnp.where(places[half][0], value, left)
            right = jnp.where(places[half][0], right, value)
        first[rows, :] = jnp.where(odd_y, left, right)
        second[rows, :] = jnp.where(odd_y, right, left)


def halves_kernel(
    size_x, wet, got_second, got_first, right_side, shift_coef, viscosity, fields
):
    index_x = lax.axis_index("gx")
    odd_x = index_x % 2 == 1
    wetness = wet[0, 0].astype(F32)
    above = (index_x > 0).astype(F32)
    below = (index_x < size_x - 1).astype(F32)
    lane = iota(1)
    rim_tiles = HALO // SUB
    for tile in range(TILES[0]):
        row = GUARD + SUB * tile
        for field in range(4):
            if rim_tiles <= tile < TILES[0] - rim_tiles:
                value = own_rows(right_side, shift_coef, viscosity, field, tile - rim_tiles)
                if field != 2:
                    value = value * wetness
            else:
                top = tile < rim_tiles
                at = SUB * (tile if top else tile - (TILES[0] - rim_tiles))
                one, two = tile_at(got_first, field, at), tile_at(got_second, field, at)
                value = jnp.where(odd_x, one, two) if top else jnp.where(odd_x, two, one)
                if field == 3:
                    value = value * (above if top else below)
            for parity in range(2):
                fields[2 * field + parity, row : row + SUB, :] = lane_take(
                    value, (2 * lane + parity) & (LANES - 1)
                )


def down_kernel(size_y, devices, got_second, got_first, held, chunks, *refs):
    states, refs = refs[:LOCAL], refs[LOCAL:]
    viscous, refs = refs[:LOCAL], refs[LOCAL:]
    reactions, refs = refs[:LOCAL], refs[LOCAL:]
    sources, refs = refs[:LOCAL], refs[LOCAL:]
    weights, refs = refs[:LOCAL], refs[LOCAL:]
    iterates, refs = refs[:LOCAL], refs[LOCAL:]
    sums, (outers, ring) = refs[:LOCAL], refs[LOCAL:]
    index_y = lax.axis_index("gy")
    odd_y = index_y % 2 == 1
    lane, sub = iota(1), iota(0)
    side_ok = jnp.where(
        lane < 96, (index_y < size_y - 1).astype(F32), (index_y > 0).astype(F32)
    )
    odd_row = (sub & 1) == 1
    inner = lane < HALF
    even_block = ((lane >> 3) & 1) == 0

    def tiles(level):
        return [GUARD + SUB * tile for tile in range(TILES[level])]

    def put(ref, slot, row, value):
        ref[slot, row : row + SUB, :] = value

    def rims(row, slots):
        half, at = divmod((row - GUARD) // SUB, HALF_TILES)
        one, two = (r[SUB * at : SUB * at + SUB, :] for r in (got_first, got_second))
        after, before = jnp.where(odd_y, two, one), jnp.where(odd_y, one, two)
        if half == 0:
            both = jnp.where(even_block, after, before)
        else:
            both = jnp.where(even_block, before, after)
        values = []
        for slot in slots:
            rim = lane_roll(both, HALF - 16 * slot - 8 * half)
            if slot >= 4:
                rim = jnp.where(side_ok > 0, rim, 1.0 if slot < 6 else 0.0)
            values.append(jnp.where(inner, tile_at(held, slot, row), rim))
        return values

    def paired(ref, slot, start):
        return (
            ref[slot, pl.ds(start, SUB, stride=2), :] + ref[slot, pl.ds(start + 1, SUB, stride=2), :]
        )

    takes = [(2 * lane + offset) & (LANES - 1) for offset in (0, 1, -1, 2)]

    def coefficients(level):
        if level == 0:
            for row in tiles(level):
                values = rims(row, (4, 5, 6, 7))
                for slot, value in enumerate(values[:2]):
                    put(reactions[level], slot, row, value)
                for slot, value in enumerate(values[2:]):
                    put(viscous[level], slot, row, value)
                put(sums[level], 2, row, values[0] + values[1])
                put(sums[level], 3, row, values[2] + values[3])
            return
        ref = sums[level - 1]
        loaded = {
            row: [
                scale * paired(ref, slot, GUARD + 2 * (row - GUARD))
                for slot, scale in ((2, 0.25), (3, 0.0625))
            ]
            for row in tiles(level)
        }
        found = {row: ([], []) for row in loaded}
        for kind, index in enumerate(takes):
            for row, (reaction, viscosity) in loaded.items():
                value = lane_take(viscosity, index)
                put(viscous[level], kind, row, value)
                found[row][1].append(value)
                if kind < 2:
                    value = lane_take(reaction, index)
                    put(reactions[level], kind, row, value)
                    found[row][0].append(value)
        for row, (reaction, viscosity) in found.items():
            put(sums[level], 2, row, reaction[0] + reaction[1])
            put(sums[level], 3, row, viscosity[0] + viscosity[1])

    def faces(level, row):
        here = [tile_at(viscous[level], p, row) for p in range(2)]
        north = [jnp.minimum(here[p], tile_at(viscous[level], p, row - 1)) for p in range(2)]
        south = [jnp.minimum(here[p], tile_at(viscous[level], p, row + 1)) for p in range(2)]
        return here, jnp.minimum(here[0], here[1]), north, south

    def outside(level, row, here):
        if level == 0:
            beyond = [lane_roll(here[1], 1), lane_roll(here[0], -1)]
        else:
            beyond = [tile_at(viscous[level], 2 + p, row) for p in range(2)]
        return [jnp.minimum(h, b) for h, b in zip(here, beyond)]

    def weigh(level):
        for row in tiles(level):
            here, middle, north, south = faces(level, row)
            outer = outside(level, row, here)
            found = []
            for p in range(2):
                diagonal = tile_at(reactions[level], p, row) + (
                    (middle + outer[p]) + (north[p] + south[p])
                )
                found.append(OMEGA / diagonal)
                if level == 0:
                    put(outers, p, row, outer[p])
            if level > 0:
                found += [lane_roll(found[1], 1), lane_roll(found[0], -1)]
            for slot, value in enumerate(found):
                put(weights[level], slot, row, value)

    def take_sources(level):
        if level == 0:
            for row in tiles(level):
                for slot, value in enumerate(rims(row, (0, 1, 2, 3))):
                    put(sources[level], slot, row, value)
            return
        loaded = {
            row: [
                0.25 * paired(sums[level - 1], comp, GUARD + 2 * (row - GUARD))
                for comp in range(2)
            ]
            for row in tiles(level)
        }
        for kind, index in enumerate(takes):
            for row, values in loaded.items():
                for comp in range(2):
                    put(sources[level], 4 * comp + kind, row, lane_take(values[comp], index))

    def kinds(level):
        return 2 if level == 0 else 4

    def first_sweep(level):
        for row in tiles(level):
            for comp in range(2):
                for p in range(2):
                    put(
                        iterates[level],
                        2 * comp + p,
                        row,
                        tile_at(weights[level], p, row)
                        * tile_at(sources[level], kinds(level) * comp + p, row),
                    )

    def residual(level):
        state, iterate, weight, source = (
            states[level],
            iterates[level],
            weights[level],
            sources[level],
        )
        for row in tiles(level):
            _, middle, north, south = faces(level, row)
            if level == 0:
                outer = [tile_at(outers, p, row) for p in range(2)]
            else:
                outer = outside(level, row, [tile_at(viscous[level], p, row) for p in range(2)])
            scale = [tile_at(weight, p, row) for p in range(2)]
            kept = level > 0 or TOP <= row < LOW
            for comp in range(2):
                here = [tile_at(iterate, 2 * comp + p, row) for p in range(2)]
                if level == 0:
                    beyond = [lane_roll(here[1], 1), lane_roll(here[0], -1)]
                else:
                    beyond = [
                        tile_at(weight, 2 + p, row) * tile_at(source, 4 * comp + 2 + p, row)
                        for p in range(2)
                    ]
                total = None
                for p in range(2):
                    slot = 2 * comp + p
                    around = middle * here[1 - p] + outer[p] * beyond[p]
                    around = around + (
                        south[p] * tile_at(iterate, slot, row + 1)
                        + north[p] * tile_at(iterate, slot, row - 1)
                    )
                    left = KEEP * tile_at(source, kinds(level) * comp + p, row) + around
                    if kept:
                        put(state, SWEPT + slot, row, here[p] + scale[p] * left)
                    if level == LOCAL - 1:
                        put(ring, slot, row, left)
                        put(state, ITERATE + slot, row, here[p])
                    total = left if total is None else total + left
                put(sums[level], comp, row, total)
            if kept:
                for p in range(2):
                    within = jnp.where(odd_row, north[p], south[p])
                    across = jnp.where(odd_row, south[p], north[p])
                    put(state, CENTRE + p, row, KEEP + scale[p] * (middle + within))
                    put(state, SIDE + p, row, scale[p] * outer[p])
                    put(state, ACROSS + p, row, scale[p] * across)
                    if level == LOCAL - 1:
                        put(state, WEIGHT + p, row, scale[p])

    coefficients(0)
    take_sources(0)
    weigh(0)
    coefficients(1)
    first_sweep(0)
    residual(0)
    weigh(1)
    coefficients(2)
    take_sources(1)
    weigh(2)
    coefficients(3)
    first_sweep(1)
    residual(1)
    take_sources(2)
    weigh(3)
    first_sweep(2)
    residual(2)
    take_sources(3)
    first_sweep(3)
    residual(3)

    start = GUARD + RIM[LOCAL - 1]
    column = lane & (SUB - 1)
    own = [
        lane_take(scale * paired(sums[LOCAL - 1], slot, start), column)
        for slot, scale in enumerate((0.25, 0.25, 0.25, 0.0625))
    ]
    turned = ((lane >> 3) - index_y) & 15
    chosen = (turned & (SUB - 1)) == sub

    def packed(value):
        return jnp.sum(value, axis=0, keepdims=True)

    def joined(a, b):
        return packed(jnp.where(chosen, jnp.where(turned < SUB, a, b), 0.0))

    edge = (lane >> 4) & 3
    place = lane & 15

    rims = jnp.zeros((SUB, LANES), F32)
    for p in range(2):
        index = jnp.where(edge < 2, column, 0 if p == 0 else SUB - 1)
        for part in range(2):
            along = (edge == part) & ((place >> 3) == p) & (sub == (0 if part == 0 else SUB - 1))
            up = (edge == 2 + p) & (place == sub + SUB * part)
            row = start + SUB * part
            value = jnp.where(
                inner,
                lane_take(tile_at(ring, p, row), index),
                lane_take(tile_at(ring, 2 + p, row), index),
            )
            rims = jnp.where(along | up, value, rims)
    kind = sub % CHUNK
    parts = [joined(own[0], own[1]), joined(own[2], own[2]), packed(rims), joined(own[3], own[3])]
    tile = jnp.where(
        kind < 2,
        jnp.where(kind == 0, parts[0], parts[1]),
        jnp.where(kind == 2, parts[2], parts[3]),
    )
    for block in range(CHUNK * devices // SUB):
        chunks[SUB * block : SUB * block + SUB, :] = tile


def write(buffer, slot, rows, value):
    for column in range(buffer.shape[1]):
        buffer[slot, column, rows, :] = value[:, LANES * column : LANES * column + LANES]


def read(buffer, slot, rows):
    parts = [buffer[slot, column, rows, :] for column in range(buffer.shape[1])]
    return parts[0] if len(parts) == 1 else jnp.concatenate(parts, 1)


class Coarse:
    def __init__(self, step, row_step, rows, cols_total, width):
        self.step, self.row_step = step, row_step
        self.shape = (rows, width)
        lane, row = iota(1, self.shape), iota(0, self.shape)
        column = lane & (cols_total - 1)
        self.odd_lane, self.odd_row = (lane & step) != 0, (row & row_step) != 0
        self.leftmost = column < 2 * step
        self.rightmost = column >= cols_total - 2 * step
        self.top, self.bottom = row < row_step, row >= rows - row_step

    def along(self, value, amount):
        return pltpu.roll(value, amount % self.shape[1], 1)

    def down(self, value, amount):
        return pltpu.roll(value, amount % self.shape[0], 0)

    def paired(self, value):
        return (
            jnp.where(self.odd_lane, self.along(value, self.step), value),
            jnp.where(self.odd_lane, value, self.along(value, -self.step)),
        )

    def outside(self, value):
        return (
            jnp.where(
                self.odd_lane, self.along(value, 2 * self.step), self.along(value, self.step)
            ),
            jnp.where(
                self.odd_lane, self.along(value, -self.step), self.along(value, -2 * self.step)
            ),
        )

    def farther(self, value):
        return (
            jnp.where(
                self.odd_lane, self.along(value, 3 * self.step), self.along(value, 2 * self.step)
            ),
            jnp.where(
                self.odd_lane, self.along(value, -2 * self.step), self.along(value, -3 * self.step)
            ),
        )

    def rows_beside(self, here):
        above = jnp.where(self.top, 0.0, self.down(here, self.row_step))
        below = jnp.where(self.bottom, 0.0, self.down(here, -self.row_step))
        return jnp.minimum(here, above), jnp.minimum(here, below)

    def coefficients(self, viscous, reaction):
        here, beyond, far = self.paired(viscous), self.outside(viscous), self.farther(viscous)
        reactions, reactions_beyond = self.paired(reaction), self.outside(reaction)
        edges = (self.leftmost, self.rightmost)
        self.middle = jnp.minimum(here[0], here[1])
        self.outer, self.north, self.south = [], [], []
        self.weights, self.weights_beyond = [], []
        for p in range(2):
            outer = jnp.minimum(here[p], jnp.where(edges[p], 0.0, beyond[p]))
            north, south = self.rows_beside(here[p])
            diagonal = reactions[p] + ((self.middle + outer) + (north + south))
            self.weights.append(OMEGA / diagonal)
            self.outer.append(outer)
            self.north.append(north)
            self.south.append(south)
            next_outer = jnp.minimum(beyond[p], far[p])
            north, south = self.rows_beside(beyond[p])
            diagonal = reactions_beyond[p] + ((outer + next_outer) + (north + south))
            self.weights_beyond.append(OMEGA / diagonal)
        return here[0] + here[1], reactions[0] + reactions[1]

    def take(self, source):
        self.values, self.values_beyond = self.paired(source), self.outside(source)

    def residual(self):
        x = [w * s for w, s in zip(self.weights, self.values)]
        x_beyond = [w * s for w, s in zip(self.weights_beyond, self.values_beyond)]
        total, self.swept = None, []
        for p in range(2):
            around = self.middle * x[1 - p] + self.outer[p] * x_beyond[p]
            around = around + (
                self.south[p] * self.down(x[p], -self.row_step)
                + self.north[p] * self.down(x[p], self.row_step)
            )
            left = KEEP * self.values[p] + around
            self.swept.append(x[p] + self.weights[p] * left)
            total = left if total is None else total + left
        return total

    def prepare(self):
        parts = []
        for p in range(2):
            within = jnp.where(self.odd_row, self.north[p], self.south[p])
            out = jnp.where(self.odd_row, self.south[p], self.north[p])
            weight = self.weights[p]
            centre = KEEP + weight * (self.middle + within)
            parts.append((self.swept[p], centre, weight * self.outer[p], weight * out))
        self.parts = parts
        self.left_parts = [self.along(value, 2 * self.step) for value in parts[1]]
        self.right_parts = [self.along(value, -2 * self.step) for value in parts[0]]

    def corrected(self, here, left, right):
        def swept(part, own, side):
            return (part[0] + part[1] * own[0]) + (part[2] * side[0] + part[3] * own[1])

        even, odd = swept(self.parts[0], here, left), swept(self.parts[1], here, right)
        before, after = swept(self.left_parts, left, here), swept(self.right_parts, right, here)
        return (
            jnp.where(self.odd_lane, odd, even),
            jnp.where(self.odd_lane, even, before),
            jnp.where(self.odd_lane, after, odd),
        )


def coarse_solve(grid, buffer, rows_total, cols_total, width, meanwhile):
    columns = width // LANES

    def whole(slot):
        return jnp.concatenate([grid[slot, c] for c in range(columns)], 1) if columns > 1 else grid[slot, 0]

    levels, rows, row_step = [], rows_total, 1
    for index in range(COARSE + 1):
        levels.append(Coarse(1 << index, row_step, rows, cols_total, width))
        if rows > SUB:
            rows //= 2
        else:
            row_step *= 2

    def folded(index, value, slot, scale):
        level = levels[index]
        rows = level.shape[0]
        if levels[index + 1].shape[0] == rows:
            other = jnp.where(
                level.odd_row, level.down(value, level.row_step), level.down(value, -level.row_step)
            )
            return scale * (value + other)
        write(buffer, slot, slice(0, rows), value)
        first, second = [pl.ds(begin, rows // 2, stride=2) for begin in range(2)]
        return scale * (read(buffer, slot, first) + read(buffer, slot, second))

    def opened(index, value, slot):
        level = levels[index]
        rows = level.shape[0]
        if value.shape[0] == rows:
            return value, jnp.where(
                level.odd_row, level.down(value, -level.row_step), level.down(value, level.row_step)
            )
        half = rows // 2
        blank = jnp.zeros((SUB, width), F32)
        for begin in range(2):
            write(buffer, slot, pl.ds(begin, half, stride=2), value)
        write(buffer, slot + 1, slice(SUB, 2 * SUB), blank)
        write(buffer, slot + 1, slice(rows, rows + SUB), blank)
        for begin in (SUB + 2, SUB - 1):
            write(buffer, slot + 1, pl.ds(begin, half, stride=2), value)
        return read(buffer, slot, slice(0, rows)), read(buffer, slot + 1, slice(SUB, SUB + rows))

    viscous, reaction, source = [None] * 5, [None] * 5, [None] * 5
    viscous[0], reaction[0], source[0] = whole(2), whole(1), whole(0)

    def coefficients(index):
        pair, reactions = levels[index].coefficients(viscous[index], reaction[index])
        viscous[index + 1] = folded(index, pair, 0, 0.0625)
        reaction[index + 1] = folded(index, reactions, 1, 0.25)

    def residual(index):
        source[index + 1] = folded(index, levels[index].residual(), 2, 0.25)

    last = levels[COARSE]
    block = 1 << COARSE
    cols_left = cols_total // block
    rows_left = last.shape[0]
    lane = iota(1, (rows_left, LANES))
    groups = 1 if cols_total < LANES else 2
    per_group = columns // groups

    def spread(*arrays):
        found = [[] for _ in arrays]
        for group in range(groups):
            for j in range(cols_left):
                column, place = divmod(block * j, LANES)
                column += group * per_group
                if groups == 1:
                    place = place + (lane & (LANES - cols_total))
                else:
                    place = jnp.full((rows_left, LANES), place, jnp.int32)
                for value, columns_found in zip(arrays, found):
                    tile = value[:, LANES * column : LANES * column + LANES]
                    columns_found.append(lane_take(tile, place))
        return found

    def flat(values, group, j):
        return values[group * cols_left + j]

    levels[0].take(source[0])
    coefficients(0)
    coefficients(1)
    residual(0)
    levels[1].take(source[1])
    coefficients(2)
    residual(1)
    levels[2].take(source[2])
    coefficients(3)
    residual(2)
    levels[3].take(source[3])
    viscous_columns, reaction_columns = spread(viscous[4], reaction[4])

    top, bottom = last.top[:, :LANES], last.bottom[:, :LANES]
    pulls, weights = [], []
    for group in range(groups):
        for j in range(cols_left):
            here = flat(viscous_columns, group, j)
            above = jnp.where(top, 0.0, last.down(here, last.row_step))
            below = jnp.where(bottom, 0.0, last.down(here, -last.row_step))
            links = [jnp.minimum(here, above), jnp.minimum(here, below)]
            links += [
                jnp.minimum(here, flat(viscous_columns, group, other))
                for other in (j - 1, j + 1)
                if 0 <= other < cols_left
            ]
            weight = OMEGA / (flat(reaction_columns, group, j) + sum(links))
            weights.append(weight)
            pulls.append([weight * link for link in links])
    residual(3)
    pushed = [w * s for w, s in zip(weights, spread(source[4])[0])]
    meanwhile()
    for index in range(COARSE - 1, -1, -1):
        levels[index].prepare()
    values = pushed
    for _ in range(COARSE_SWEEPS - 1):
        following = []
        for group in range(groups):
            for j in range(cols_left):
                at = group * cols_left + j
                here, pull = values[at], pulls[at]
                total = (KEEP * here + pushed[at]) + (
                    pull[0] * last.down(here, last.row_step)
                    + pull[1] * last.down(here, -last.row_step)
                )
                sides = [other for other in (j - 1, j + 1) if 0 <= other < cols_left]
                for link, other in zip(pull[2:], sides):
                    total = total + link * flat(values, group, other)
                following.append(total)
        values = following

    def laid(shift):
        found = []
        for column in range(columns):
            group = column // per_group
            place = ((lane & (cols_total - 1)) if groups == 1 else lane) // block
            place = place + (column % per_group) * (LANES // block)
            value = jnp.zeros((rows_left, LANES), F32)
            for j in range(cols_left):
                value = jnp.where(place == j + shift, flat(values, group, j), value)
            found.append(value)
        return found[0] if columns == 1 else jnp.concatenate(found, 1)

    corrections = [laid(shift) for shift in (0, 1, -1)]
    for index in range(COARSE - 1, -1, -1):
        corrections = levels[index].corrected(
            *[opened(index, value, 2 * at) for at, value in enumerate(corrections)]
        )
    return corrections


def up_kernel(size_x, size_y, gathered, state0, state1, state2, state3, out, *refs):
    grid, buffer, whole, window, swept3, corr1, corr2, corr3, merged0, merged1, merged2 = refs[:11]
    finished, sems = refs[11:]
    index_x, index_y = lax.axis_index("gx"), lax.axis_index("gy")
    rows_total, cols_total = CELLS * size_x, CELLS * size_y
    width = 2 * cols_total
    columns = width // LANES
    per_column = LANES // CELLS
    lane, sub = iota(1), iota(0)

    tall = iota(1, (size_x, LANES)) // CELLS
    modulus = min(size_y, per_column)
    for column in range(columns):
        comp = column // (columns // 2) if columns > 1 else 0
        first = (column % (columns // 2)) * per_column if columns > 1 else 0
        for slot, kind in ((2, 3), (1, 1), (0, 0)):
            chunks = [
                gathered[pl.ds(CHUNK * (first + j) + kind, size_x, stride=CHUNK * size_y), :]
                for j in range(modulus)
            ]
            for r in range(CELLS):
                turn = r + CELLS * comp
                value = chunks[0]
                for j in range(1, modulus):
                    value = jnp.where(((tall - turn) & (modulus - 1)) == j, chunks[j], value)
                grid[slot, column, pl.ds(r, size_x, stride=CELLS), :] = lane_roll(
                    value, -CELLS * turn
                )

    def ring_row(dx, dy):
        i = jnp.clip(index_x + dx, 0, size_x - 1)
        j = jnp.clip(index_y + dy, 0, size_y - 1)
        return jnp.broadcast_to(
            gathered[pl.ds(CHUNK * (i * size_y + j) + 2, 1), :], (SUB, LANES)
        )

    start = GUARD + RIM[3]

    def complete_ring():
        beside = {
            (dx, dy): ring_row(dx, dy) for dx in (-1, 0, 1) for dy in (-1, 0, 1) if dx or dy
        }
        for comp in range(2):
            base = comp * HALF
            for p in range(2):
                slot = 2 * comp + p
                end = 7 if p else 0
                corner_lane = LANES - 1 if p else SUB
                dy = -1 if p else 1
                for tile in range(2):
                    at = start + SUB * tile
                    index = base + (48 if p else 32) + SUB * tile + sub
                    ringed = lane_take(beside[0, dy], index)
                    swept = jnp.where(
                        lane == corner_lane,
                        tile_at(state3, ITERATE + slot, at)
                        + tile_at(state3, WEIGHT + p, at) * ringed,
                        tile_at(state3, SWEPT + slot, at),
                    )
                    swept3[slot, at : at + SUB, :] = swept
                for dx, at, edge in ((-1, start - 1, 16), (1, start + 2 * SUB, 0)):
                    index = base + edge + 8 * p
                    ringed = jnp.where(
                        lane == corner_lane,
                        lane_take(beside[dx, dy], jnp.full((SUB, LANES), index + end, jnp.int32)),
                        lane_take(beside[dx, 0], index + (lane & 7)),
                    )
                    rows = slice(at, at + 1)
                    swept3[slot, rows, :] = (
                        state3[ITERATE + slot, rows, :] + state3[WEIGHT + p, rows, :] * ringed[0:1]
                    )

    corrections = coarse_solve(grid, buffer, rows_total, cols_total, width, complete_ring)

    blank = jnp.zeros((SUB, width), F32)
    for kind, correction in enumerate(corrections):
        whole[kind, GUARD : GUARD + rows_total, :] = correction
        whole[kind, 0:GUARD, :] = blank
        whole[kind, GUARD + rows_total : GUARD + rows_total + SUB, :] = blank
    near_rows = pl.ds(pl.multiple_of(CELLS * index_x, SUB), 3 * SUB)
    for comp in range(2):
        shift = (2 * width - cols_total * comp - CELLS * index_y) % width
        for kind in range(3):
            turned = pltpu.roll(whole[kind, near_rows, :], shift, 1)
            if columns > 1:
                tall_lane = iota(1, (3 * SUB, LANES))
                turned = jnp.where(
                    tall_lane < HALF, turned[:, :LANES], turned[:, width - LANES :]
                )
            window[3 * comp + kind, 0 : 3 * SUB, :] = turned

    def swept_rows(ref, level, coarse_row, parity, here, beyond, across, comp):
        at = pl.ds(GUARD + RIM[level] + 2 * coarse_row + parity, SUB, stride=2)
        state = (state0, state1, state2, state3)[level]
        return [
            (ref[SWEPT + 2 * comp + p, at, :] + state[CENTRE + p, at, :] * here)
            + (state[SIDE + p, at, :] * beyond[p] + state[ACROSS + p, at, :] * across)
            for p in range(2)
        ]

    for comp in range(2):
        for tile in range(2):
            first = SUB * tile - 1
            at = GUARD + first
            here, left, right = [tile_at(window, 3 * comp + kind, at) for kind in range(3)]
            for parity in range(2):
                across = tile_at(window, 3 * comp, at + (1 if parity else -1))
                found = swept_rows(swept3, 3, first, parity, here, (left, right), across, comp)
                rows = pl.ds(GUARD + RIM[3] + 2 * first + parity, SUB, stride=2)
                for p in range(2):
                    corr3[2 * comp + p, rows, :] = found[p]

    corrs = [None, corr1, corr2, corr3]
    merged = [merged0, merged1, merged2]
    near = ((((lane + 32) & (LANES - 1)) - 32) >> 1) & (LANES - 1)
    odd_lane = (lane & 1) == 1
    for level in (2, 1, 0):
        coarse = level + 1
        corr, state, whole_rows = corrs[coarse], (state0, state1, state2)[level], merged[level]
        count = (LANES >> coarse) + 2
        origin = GUARD + RIM[coarse]
        places = [
            (comp, origin - 1 + SUB * tile)
            for tile in range(-(-count // SUB))
            for comp in range(2)
        ]
        pairs = {
            (comp, at): (tile_at(corr, 2 * comp, at), tile_at(corr, 2 * comp + 1, at))
            for comp, at in places
        }
        moved = {
            place: [lane_take(even, near), lane_take(odd, near)]
            for place, (even, odd) in pairs.items()
        }
        for place, (even, _) in pairs.items():
            moved[place].append(lane_take(even, (near + 1) & (LANES - 1)))
        for place, (_, odd) in pairs.items():
            moved[place].append(lane_take(odd, (near - 1) & (LANES - 1)))
        for (comp, at), (even_here, odd_here, even_next, odd_last) in moved.items():
            rows = slice(at, at + SUB)
            whole_rows[3 * comp, rows, :] = jnp.where(odd_lane, odd_here, even_here)
            whole_rows[3 * comp + 1, rows, :] = jnp.where(odd_lane, even_next, odd_here)
            whole_rows[3 * comp + 2, rows, :] = jnp.where(odd_lane, even_here, odd_last)
        if level > 0:
            first, tiles = -1, -(-count // SUB)
        else:
            first, tiles = 0, (count - 2) // SUB
        copies = []
        for tile in range(tiles):
            coarse_row = first + SUB * tile
            at = origin + coarse_row
            for comp in range(2):
                here, right, left = [tile_at(whole_rows, 3 * comp + k, at) for k in range(3)]
                for parity in range(2):
                    across = tile_at(whole_rows, 3 * comp, at + (1 if parity else -1))
                    found = swept_rows(
                        state, level, coarse_row, parity, here, (left, right), across, comp
                    )
                    if level > 0:
                        rows = pl.ds(GUARD + RIM[level] + 2 * coarse_row + parity, SUB, stride=2)
                        for p in range(2):
                            corrs[level][2 * comp + p, rows, :] = found[p]
                    else:
                        rows = pl.ds(2 * coarse_row + parity, SUB, stride=2)
                        finished[comp, rows, :] = jnp.where(
                            odd_lane,
                            lane_take(found[1], lane >> 1),
                            lane_take(found[0], lane >> 1),
                        )
            if level == 0 and tile + 1 in PIECES:
                piece = len(copies)
                begin = 2 * SUB * PIECES[piece - 1] if piece else 0
                rows = pl.ds(begin, 2 * SUB * (tile + 1) - begin)
                copy = pltpu.make_async_copy(
                    finished.at[:, rows, :], out.at[:, rows, :], sems.at[piece]
                )
                copy.start()
                copies.append(copy)
        for copy in copies:
            copy.wait()


def params():
    return pltpu.CompilerParams(vmem_limit_bytes=VMEM_LIMIT)


VMEM_SPEC = pl.BlockSpec(memory_space=pltpu.VMEM)
SMEM_SPEC = pl.BlockSpec(memory_space=pltpu.SMEM)
HBM_SPEC = pl.BlockSpec(memory_space=pltpu.HBM)


def swap_routes(size_x, size_y):
    def index(i, j):
        return i * size_y + j

    routes = []
    for axis in range(2):
        size = (size_x, size_y)[axis]
        for offset in range(2):
            route = []
            for i in range(size_x):
                for j in range(size_y):
                    here = (i, j)[axis]
                    other = here + 1 if here % 2 == offset else here - 1
                    if 0 <= other < size:
                        peer = (other, j) if axis == 0 else (i, other)
                    else:
                        peer = (i, j ^ 1) if axis == 0 else (i ^ 1, j)
                    route.append((index(i, j), index(*peer)))
            routes.append(route)
    return routes


def per_device(size_x, size_y, right_side, shift_coef, viscosity, wet_tiles):
    axes = ("gx", "gy")
    devices = size_x * size_y
    routes = swap_routes(size_x, size_y)
    band = pltpu.VMEM((4, HALO, LANES), F32)
    own = (right_side, shift_coef, viscosity)
    blank = pl.pallas_call(
        first_kernel,
        out_shape=pltpu.VMEM((SUB, LANES), F32),
        out_specs=VMEM_SPEC,
        cost_estimate=pl.CostEstimate(flops=FIRST_COST, bytes_accessed=FIRST_COST // 16, transcendentals=0),
        compiler_params=params(),
        name="first",
    )()
    wet_tiles, blank = lax.optimization_barrier((wet_tiles, blank))
    first, second = pl.pallas_call(
        bands_kernel,
        out_shape=(band, band),
        in_specs=[SMEM_SPEC] + [VMEM_SPEC] * 4,
        out_specs=(VMEM_SPEC,) * 2,
        compiler_params=params(),
        name="bands",
    )(wet_tiles, blank, *own)
    second = lax.ppermute(second, axes, routes[1])
    first = lax.ppermute(first, axes, routes[0])
    strip = jax.ShapeDtypeStruct((MESSAGE, LANES), F32)
    got = (second, first)
    meantime = pl.CostEstimate(flops=1 << 20, bytes_accessed=1 << 21, transcendentals=0)
    edges = pl.pallas_call(
        edges_kernel,
        out_shape=(pltpu.VMEM((MESSAGE, LANES), F32),) * 2,
        in_specs=[SMEM_SPEC] + [VMEM_SPEC] * 3,
        out_specs=(VMEM_SPEC,) * 2,
        cost_estimate=meantime,
        compiler_params=params(),
        name="edges",
    )(wet_tiles, *own)
    first, second = pl.pallas_call(
        functools.partial(strips_kernel, size_x),
        out_shape=(strip, strip),
        in_specs=[VMEM_SPEC] * 4,
        out_specs=(VMEM_SPEC,) * 2,
        compiler_params=params(),
        name="strips",
    )(*got, *edges)
    fields = pl.pallas_call(
        functools.partial(halves_kernel, size_x),
        out_shape=pltpu.VMEM((8, HELD[0], LANES), F32),
        in_specs=[SMEM_SPEC] + [VMEM_SPEC] * 5,
        out_specs=VMEM_SPEC,
        cost_estimate=meantime,
        compiler_params=params(),
        name="halves",
    )(wet_tiles, *got, *own)
    second = lax.ppermute(second, axes, routes[3])
    first = lax.ppermute(first, axes, routes[2])

    def buffers(counts):
        return [pltpu.VMEM((n, HELD[level], LANES), F32) for level, n in enumerate(counts)]

    chunks, *states = pl.pallas_call(
        functools.partial(down_kernel, size_y, devices),
        out_shape=(jax.ShapeDtypeStruct((CHUNK * devices, LANES), F32),)
        + tuple(buffers([STATE, STATE, STATE, STATE + 6])),
        in_specs=[VMEM_SPEC] * 3,
        out_specs=(VMEM_SPEC,) * (1 + LOCAL),
        scratch_shapes=buffers([2, 4, 4, 4])
        + buffers([2] * 4)
        + buffers([4, 8, 8, 8])
        + buffers([2, 4, 4, 4])
        + buffers([4] * 4)
        + buffers([4] * 4)
        + [pltpu.VMEM((2, HELD[0], LANES), F32), pltpu.VMEM((4, HELD[3], LANES), F32)],
        compiler_params=params(),
        name="down",
    )(second, first, fields)
    gathered = lax.all_to_all(chunks, axes, 0, 0, tiled=True)
    rows_total = CELLS * size_x
    width = 2 * CELLS * size_y
    return pl.pallas_call(
        functools.partial(up_kernel, size_x, size_y),
        out_shape=jax.ShapeDtypeStruct((2, LANES, LANES), F32),
        in_specs=[VMEM_SPEC] * (1 + LOCAL),
        out_specs=HBM_SPEC,
        scratch_shapes=[
            pltpu.VMEM((3, width // LANES, rows_total, LANES), F32),
            pltpu.VMEM((6, width // LANES, rows_total + 3 * SUB, LANES), F32),
            pltpu.VMEM((3, rows_total + 2 * SUB, width), F32),
            pltpu.VMEM((6, 5 * SUB, LANES), F32),
            pltpu.VMEM((4, HELD[3], LANES), F32),
        ]
        + [pltpu.VMEM((4, HELD[level], LANES), F32) for level in (1, 2, 3)]
        + [pltpu.VMEM((6, HELD[level + 1], LANES), F32) for level in (0, 1, 2)]
        + [pltpu.VMEM((2, LANES, LANES), F32), pltpu.SemaphoreType.DMA((len(PIECES),))],
        compiler_params=params(),
        name="up",
    )(gathered, *states)


def solution(mesh):
    sizes = dict(mesh.shape)
    placed = (P(None, "gx", "gy"), P("gx", "gy"), P("gx", "gy"), P("gx", "gy"))
    return jax.shard_map(
        functools.partial(per_device, sizes["gx"], sizes["gy"]),
        mesh=mesh,
        in_specs=placed,
        out_specs=P(None, "gx", "gy"),
        check_vma=False,
    )
```

```python
import functools

import jax
import jax.numpy as jnp
from jax import lax
from jax.experimental import pallas as pl
from jax.experimental.pallas import tpu as pltpu
from jax.sharding import PartitionSpec as P

LOCAL = 4
COARSE = 4
COARSE_SWEEPS = 8
OMEGA = 0.8
KEEP = 1.0 - OMEGA

LANES = 128
HALF = LANES // 2
SUB = 8
HALO = 16
GUARD = 8
CELLS = LANES >> LOCAL
ROWS = [(LANES + 2 * HALO) >> level for level in range(LOCAL)]
TILES = [-(-rows // SUB) for rows in ROWS]
HELD = [GUARD + SUB * tiles + 16 for tiles in TILES]
RIM = [HALO >> level for level in range(LOCAL)]
TOP = GUARD + HALO
LOW = TOP + LANES
HALF_TILES = TILES[0] // 2
MESSAGE = ROWS[0] // 2
CHUNK = 4
PIECES = (8,)
F32 = jnp.float32
FIRST_COST = 1 << 31
VMEM_LIMIT = 48 * 1024 * 1024

SWEPT, CENTRE, SIDE, ACROSS = 0, 4, 6, 8
STATE = 10
ITERATE, WEIGHT = 10, 14


def iota(dim, shape=(SUB, LANES)):
    return lax.broadcasted_iota(jnp.int32, shape, dim)


def lane_take(tile, index):
    return jnp.take_along_axis(tile, index, axis=1)


def lane_roll(tile, shift):
    return pltpu.roll(tile, shift % LANES, 1)


def tile_at(ref, slot, row):
    return ref[slot, row : row + SUB, :]


def first_kernel(blank):
    blank[...] = jnp.zeros((SUB, LANES), F32)


def bands_kernel(wet, blank, right_side, shift_coef, viscosity, first, second):
    odd = lax.axis_index("gx") % 2
    wetness = wet[0, 0].astype(F32)
    bottom = LANES - HALO
    for start, out in ((bottom - bottom * odd, first), (bottom * odd, second)):
        rows = pl.ds(pl.multiple_of(start, SUB), HALO)
        out[0] = right_side[0, rows, :] * wetness
        out[1] = right_side[1, rows, :] * wetness
        out[2] = shift_coef[rows, :]
        out[3] = viscosity[rows, :] * wetness


def own_rows(right_side, shift_coef, viscosity, field, tile):
    rows = slice(SUB * tile, SUB * tile + SUB)
    if field < 2:
        return right_side[field, rows, :]
    return shift_coef[rows, :] if field == 2 else viscosity[rows, :]


def rim_place(half, lane):
    to_left = ((lane >> 3) & 1) == half
    q = jnp.where(to_left, lane, (lane - (56 + 8 * half)) & (LANES - 1)) >> 4
    cell = 2 * (lane & 7) + (q & 1) + jnp.where(to_left, 0, LANES - HALO)
    return to_left, q >> 1, cell


def rim_value(pieces, place):
    _, owner, cell = place
    value = None
    for field in range(4):
        part = lane_take(pieces[field], cell)
        value = part if value is None else jnp.where(owner == field, part, value)
    return value


RIM_TILES = HALO // SUB


def edges_kernel(wet, right_side, shift_coef, viscosity, lefts, rights):
    wetness = wet[0, 0].astype(F32)
    lane = iota(1)
    places = [rim_place(half, lane) for half in range(2)]
    found = {}
    for half in range(2):
        mask = jnp.where(places[half][1] == 2, 1.0, wetness)
        for tile in range(HALF_TILES):
            at = tile + half * HALF_TILES - RIM_TILES
            if 0 <= at < LANES // SUB:
                pieces = [own_rows(right_side, shift_coef, viscosity, f, at) for f in range(4)]
                found[half, tile] = rim_value(pieces, places[half]) * mask
    blank = jnp.zeros((SUB, LANES), F32)
    for tile in range(HALF_TILES):
        upper, lower = (found.get((half, tile), blank) for half in range(2))
        rows = slice(SUB * tile, SUB * tile + SUB)
        lefts[rows, :] = jnp.where(places[0][0], upper, lower)
        rights[rows, :] = jnp.where(places[0][0], lower, upper)


def strips_kernel(size_x, got_second, got_first, lefts, rights, first, second):
    index_x = lax.axis_index("gx")
    odd_x = index_x % 2 == 1
    odd_y = lax.axis_index("gy") % 2 == 1
    above = (index_x > 0).astype(F32)
    below = (index_x < size_x - 1).astype(F32)
    lane = iota(1)
    places = [rim_place(half, lane) for half in range(2)]
    found = {}
    for half in range(2):
        mask = jnp.where(places[half][1] == 3, below if half else above, 1.0)
        for tile in range(RIM_TILES):
            row = SUB * tile
            pieces = []
            for field in range(4):
                one, two = tile_at(got_first, field, row), tile_at(got_second, field, row)
                pieces.append(jnp.where(odd_x, two, one) if half else jnp.where(odd_x, one, two))
            at = HALF_TILES - RIM_TILES + tile if half else tile
            found[at] = (half, rim_value(pieces, places[half]) * mask)
    for tile in range(HALF_TILES):
        rows = slice(SUB * tile, SUB * tile + SUB)
        left, right = lefts[rows, :], rights[rows, :]
        if tile in found:
            half, value = found[tile]
            left = jnp.where(places[half][0], value, left)
            right = jnp.where(places[half][0], right, value)
        first[rows, :] = jnp.where(odd_y, left, right)
        second[rows, :] = jnp.where(odd_y, right, left)


def halves_kernel(
    size_x, wet, got_second, got_first, right_side, shift_coef, viscosity, fields
):
    index_x = lax.axis_index("gx")
    odd_x = index_x % 2 == 1
    wetness = wet[0, 0].astype(F32)
    above = (index_x > 0).astype(F32)
    below = (index_x < size_x - 1).astype(F32)
    lane = iota(1)
    rim_tiles = HALO // SUB
    for tile in range(TILES[0]):
        row = GUARD + SUB * tile
        for field in range(4):
            if rim_tiles <= tile < TILES[0] - rim_tiles:
                value = own_rows(right_side, shift_coef, viscosity, field, tile - rim_tiles)
                if field != 2:
                    value = value * wetness
            else:
                top = tile < rim_tiles
                at = SUB * (tile if top else tile - (TILES[0] - rim_tiles))
                one, two = tile_at(got_first, field, at), tile_at(got_second, field, at)
                value = jnp.where(odd_x, one, two) if top else jnp.where(odd_x, two, one)
                if field == 3:
                    value = value * (above if top else below)
            for parity in range(2):
                fields[2 * field + parity, row : row + SUB, :] = lane_take(
                    value, (2 * lane + parity) & (LANES - 1)
                )


def down_kernel(size_y, devices, got_second, got_first, held, chunks, *refs):
    states, refs = refs[:LOCAL], refs[LOCAL:]
    viscous, refs = refs[:LOCAL], refs[LOCAL:]
    reactions, refs = refs[:LOCAL], refs[LOCAL:]
    sources, refs = refs[:LOCAL], refs[LOCAL:]
    weights, refs = refs[:LOCAL], refs[LOCAL:]
    iterates, refs = refs[:LOCAL], refs[LOCAL:]
    sums, (outers, ring) = refs[:LOCAL], refs[LOCAL:]
    index_y = lax.axis_index("gy")
    odd_y = index_y % 2 == 1
    lane, sub = iota(1), iota(0)
    side_ok = jnp.where(
        lane < 96, (index_y < size_y - 1).astype(F32), (index_y > 0).astype(F32)
    )
    odd_row = (sub & 1) == 1
    inner = lane < HALF
    even_block = ((lane >> 3) & 1) == 0

    def tiles(level):
        return [GUARD + SUB * tile for tile in range(TILES[level])]

    def put(ref, slot, row, value):
        ref[slot, row : row + SUB, :] = value

    def rims(row, slots):
        half, at = divmod((row - GUARD) // SUB, HALF_TILES)
        one, two = (r[SUB * at : SUB * at + SUB, :] for r in (got_first, got_second))
        after, before = jnp.where(odd_y, two, one), jnp.where(odd_y, one, two)
        if half == 0:
            both = jnp.where(even_block, after, before)
        else:
            both = jnp.where(even_block, before, after)
        values = []
        for slot in slots:
            shift = HALF - 16 * slot - 8 * half
            rim = lane_roll(both, shift) if shift else both
            if slot >= 4:
                rim = jnp.where(side_ok > 0, rim, 1.0 if slot < 6 else 0.0)
            values.append(jnp.where(inner, tile_at(held, slot, row), rim))
        return values

    def paired(ref, slot, start):
        return (
            ref[slot, pl.ds(start, SUB, stride=2), :] + ref[slot, pl.ds(start + 1, SUB, stride=2), :]
        )

    takes = [(2 * lane + offset) & (LANES - 1) for offset in (0, 1, -1, 2)]

    def coefficients(level):
        if level == 0:
            for row in tiles(level):
                values = rims(row, (4, 5, 6, 7))
                for slot, value in enumerate(values[:2]):
                    put(reactions[level], slot, row, value)
                for slot, value in enumerate(values[2:]):
                    put(viscous[level], slot, row, value)
                put(sums[level], 2, row, values[0] + values[1])
                put(sums[level], 3, row, values[2] + values[3])
            return
        ref = sums[level - 1]
        loaded = {
            row: [
                scale * paired(ref, slot, GUARD + 2 * (row - GUARD))
                for slot, scale in ((2, 0.25), (3, 0.0625))
            ]
            for row in tiles(level)
        }
        found = {row: ([], []) for row in loaded}
        for kind, index in enumerate(takes):
            for row, (reaction, viscosity) in loaded.items():
                value = lane_take(viscosity, index)
                put(viscous[level], kind, row, value)
                found[row][1].append(value)
                if kind < 2:
                    value = lane_take(reaction, index)
                    put(reactions[level], kind, row, value)
                    found[row][0].append(value)
        for row, (reaction, viscosity) in found.items():
            put(sums[level], 2, row, reaction[0] + reaction[1])
            put(sums[level], 3, row, viscosity[0] + viscosity[1])

    def faces(level, row):
        here = [tile_at(viscous[level], p, row) for p in range(2)]
        north = [jnp.minimum(here[p], tile_at(viscous[level], p, row - 1)) for p in range(2)]
        south = [jnp.minimum(here[p], tile_at(viscous[level], p, row + 1)) for p in range(2)]
        return here, jnp.minimum(here[0], here[1]), north, south

    def outside(level, row, here):
        if level == 0:
            beyond = [lane_roll(here[1], 1), lane_roll(here[0], -1)]
        else:
            beyond = [tile_at(viscous[level], 2 + p, row) for p in range(2)]
        return [jnp.minimum(h, b) for h, b in zip(here, beyond)]

    def weigh(level):
        for row in tiles(level):
            here, middle, north, south = faces(level, row)
            outer = outside(level, row, here)
            found = []
            for p in range(2):
                diagonal = tile_at(reactions[level], p, row) + (
                    (middle + outer[p]) + (north[p] + south[p])
                )
                found.append(OMEGA / diagonal)
                if level == 0:
                    put(outers, p, row, outer[p])
            if level > 0:
                found += [lane_roll(found[1], 1), lane_roll(found[0], -1)]
            for slot, value in enumerate(found):
                put(weights[level], slot, row, value)

    def take_sources(level):
        if level == 0:
            for row in tiles(level):
                for slot, value in enumerate(rims(row, (0, 1, 2, 3))):
                    put(sources[level], slot, row, value)
            return
        loaded = {
            row: [
                0.25 * paired(sums[level - 1], comp, GUARD + 2 * (row - GUARD))
                for comp in range(2)
            ]
            for row in tiles(level)
        }
        for kind, index in enumerate(takes):
            for row, values in loaded.items():
                for comp in range(2):
                    put(sources[level], 4 * comp + kind, row, lane_take(values[comp], index))

    def kinds(level):
        return 2 if level == 0 else 4

    def first_sweep(level):
        for row in tiles(level):
            for comp in range(2):
                for p in range(2):
                    put(
                        iterates[level],
                        2 * comp + p,
                        row,
                        tile_at(weights[level], p, row)
                        * tile_at(sources[level], kinds(level) * comp + p, row),
                    )

    def residual(level):
        state, iterate, weight, source = (
            states[level],
            iterates[level],
            weights[level],
            sources[level],
        )
        for row in tiles(level):
            _, middle, north, south = faces(level, row)
            if level == 0:
                outer = [tile_at(outers, p, row) for p in range(2)]
            else:
                outer = outside(level, row, [tile_at(viscous[level], p, row) for p in range(2)])
            scale = [tile_at(weight, p, row) for p in range(2)]
            kept = level > 0 or TOP <= row < LOW
            for comp in range(2):
                here = [tile_at(iterate, 2 * comp + p, row) for p in range(2)]
                if level == 0:
                    beyond = [lane_roll(here[1], 1), lane_roll(here[0], -1)]
                else:
                    beyond = [
                        tile_at(weight, 2 + p, row) * tile_at(source, 4 * comp + 2 + p, row)
                        for p in range(2)
                    ]
                total = None
                for p in range(2):
                    slot = 2 * comp + p
                    around = middle * here[1 - p] + outer[p] * beyond[p]
                    around = around + (
                        south[p] * tile_at(iterate, slot, row + 1)
                        + north[p] * tile_at(iterate, slot, row - 1)
                    )
                    left = KEEP * tile_at(source, kinds(level) * comp + p, row) + around
                    if kept:
                        put(state, SWEPT + slot, row, here[p] + scale[p] * left)
                    if level == LOCAL - 1:
                        put(ring, slot, row, left)
                        put(state, ITERATE + slot, row, here[p])
                    total = left if total is None else total + left
                put(sums[level], comp, row, total)
            if kept:
                for p in range(2):
                    within = jnp.where(odd_row, north[p], south[p])
                    across = jnp.where(odd_row, south[p], north[p])
                    put(state, CENTRE + p, row, KEEP + scale[p] * (middle + within))
                    put(state, SIDE + p, row, scale[p] * outer[p])
                    put(state, ACROSS + p, row, scale[p] * across)
                    if level == LOCAL - 1:
                        put(state, WEIGHT + p, row, scale[p])

    coefficients(0)
    take_sources(0)
    weigh(0)
    coefficients(1)
    first_sweep(0)
    residual(0)
    weigh(1)
    coefficients(2)
    take_sources(1)
    weigh(2)
    coefficients(3)
    first_sweep(1)
    residual(1)
    take_sources(2)
    weigh(3)
    first_sweep(2)
    residual(2)
    take_sources(3)
    first_sweep(3)
    residual(3)

    start = GUARD + RIM[LOCAL - 1]
    column = lane & (SUB - 1)
    own = [
        lane_take(scale * paired(sums[LOCAL - 1], slot, start), column)
        for slot, scale in enumerate((0.25, 0.25, 0.25, 0.0625))
    ]
    turned = ((lane >> 3) - index_y) & 15
    chosen = (turned & (SUB - 1)) == sub

    def packed(value):
        return jnp.sum(value, axis=0, keepdims=True)

    def joined(a, b):
        return packed(jnp.where(chosen, jnp.where(turned < SUB, a, b), 0.0))

    edge = (lane >> 4) & 3
    place = lane & 15

    rims = jnp.zeros((SUB, LANES), F32)
    for p in range(2):
        index = jnp.where(edge < 2, column, 0 if p == 0 else SUB - 1)
        for part in range(2):
            along = (edge == part) & ((place >> 3) == p) & (sub == (0 if part == 0 else SUB - 1))
            up = (edge == 2 + p) & (place == sub + SUB * part)
            row = start + SUB * part
            value = jnp.where(
                inner,
                lane_take(tile_at(ring, p, row), index),
                lane_take(tile_at(ring, 2 + p, row), index),
            )
            rims = jnp.where(along | up, value, rims)
    kind = sub % CHUNK
    parts = [joined(own[0], own[1]), joined(own[2], own[2]), packed(rims), joined(own[3], own[3])]
    tile = jnp.where(
        kind < 2,
        jnp.where(kind == 0, parts[0], parts[1]),
        jnp.where(kind == 2, parts[2], parts[3]),
    )
    for block in range(CHUNK * devices // SUB):
        chunks[SUB * block : SUB * block + SUB, :] = tile


def write(buffer, slot, rows, value):
    for column in range(buffer.shape[1]):
        buffer[slot, column, rows, :] = value[:, LANES * column : LANES * column + LANES]


def read(buffer, slot, rows):
    parts = [buffer[slot, column, rows, :] for column in range(buffer.shape[1])]
    return parts[0] if len(parts) == 1 else jnp.concatenate(parts, 1)


class Coarse:
    def __init__(self, step, row_step, rows, cols_total, width):
        self.step, self.row_step = step, row_step
        self.shape = (rows, width)
        lane, row = iota(1, self.shape), iota(0, self.shape)
        column = lane & (cols_total - 1)
        self.odd_lane, self.odd_row = (lane & step) != 0, (row & row_step) != 0
        self.leftmost = column < 2 * step
        self.rightmost = column >= cols_total - 2 * step
        self.top, self.bottom = row < row_step, row >= rows - row_step

    def along(self, value, amount):
        return pltpu.roll(value, amount % self.shape[1], 1)

    def down(self, value, amount):
        return pltpu.roll(value, amount % self.shape[0], 0)

    def paired(self, value):
        return (
            jnp.where(self.odd_lane, self.along(value, self.step), value),
            jnp.where(self.odd_lane, value, self.along(value, -self.step)),
        )

    def outside(self, value):
        return (
            jnp.where(
                self.odd_lane, self.along(value, 2 * self.step), self.along(value, self.step)
            ),
            jnp.where(
                self.odd_lane, self.along(value, -self.step), self.along(value, -2 * self.step)
            ),
        )

    def farther(self, value):
        return (
            jnp.where(
                self.odd_lane, self.along(value, 3 * self.step), self.along(value, 2 * self.step)
            ),
            jnp.where(
                self.odd_lane, self.along(value, -2 * self.step), self.along(value, -3 * self.step)
            ),
        )

    def rows_beside(self, here):
        above = jnp.where(self.top, 0.0, self.down(here, self.row_step))
        below = jnp.where(self.bottom, 0.0, self.down(here, -self.row_step))
        return jnp.minimum(here, above), jnp.minimum(here, below)

    def coefficients(self, viscous, reaction):
        here, beyond, far = self.paired(viscous), self.outside(viscous), self.farther(viscous)
        reactions, reactions_beyond = self.paired(reaction), self.outside(reaction)
        edges = (self.leftmost, self.rightmost)
        self.middle = jnp.minimum(here[0], here[1])
        self.outer, self.north, self.south = [], [], []
        self.weights, self.weights_beyond = [], []
        for p in range(2):
            outer = jnp.minimum(here[p], jnp.where(edges[p], 0.0, beyond[p]))
            north, south = self.rows_beside(here[p])
            diagonal = reactions[p] + ((self.middle + outer) + (north + south))
            self.weights.append(OMEGA / diagonal)
            self.outer.append(outer)
            self.north.append(north)
            self.south.append(south)
            next_outer = jnp.minimum(beyond[p], far[p])
            north, south = self.rows_beside(beyond[p])
            diagonal = reactions_beyond[p] + ((outer + next_outer) + (north + south))
            self.weights_beyond.append(OMEGA / diagonal)
        return here[0] + here[1], reactions[0] + reactions[1]

    def take(self, source):
        self.values, self.values_beyond = self.paired(source), self.outside(source)

    def residual(self):
        x = [w * s for w, s in zip(self.weights, self.values)]
        x_beyond = [w * s for w, s in zip(self.weights_beyond, self.values_beyond)]
        total, self.swept = None, []
        for p in range(2):
            around = self.middle * x[1 - p] + self.outer[p] * x_beyond[p]
            around = around + (
                self.south[p] * self.down(x[p], -self.row_step)
                + self.north[p] * self.down(x[p], self.row_step)
            )
            left = KEEP * self.values[p] + around
            self.swept.append(x[p] + self.weights[p] * left)
            total = left if total is None else total + left
        return total

    def prepare(self):
        parts = []
        for p in range(2):
            within = jnp.where(self.odd_row, self.north[p], self.south[p])
            out = jnp.where(self.odd_row, self.south[p], self.north[p])
            weight = self.weights[p]
            centre = KEEP + weight * (self.middle + within)
            parts.append((self.swept[p], centre, weight * self.outer[p], weight * out))
        self.parts = parts
        self.left_parts = [self.along(value, 2 * self.step) for value in parts[1]]
        self.right_parts = [self.along(value, -2 * self.step) for value in parts[0]]

    def corrected(self, here, left, right):
        def swept(part, own, side):
            return (part[0] + part[1] * own[0]) + (part[2] * side[0] + part[3] * own[1])

        even, odd = swept(self.parts[0], here, left), swept(self.parts[1], here, right)
        before, after = swept(self.left_parts, left, here), swept(self.right_parts, right, here)
        return (
            jnp.where(self.odd_lane, odd, even),
            jnp.where(self.odd_lane, even, before),
            jnp.where(self.odd_lane, after, odd),
        )


def coarse_solve(grid, buffer, rows_total, cols_total, width, meanwhile):
    columns = width // LANES

    def whole(slot):
        return jnp.concatenate([grid[slot, c] for c in range(columns)], 1) if columns > 1 else grid[slot, 0]

    levels, rows, row_step = [], rows_total, 1
    for index in range(COARSE + 1):
        levels.append(Coarse(1 << index, row_step, rows, cols_total, width))
        if rows > SUB:
            rows //= 2
        else:
            row_step *= 2

    def folded(index, value, slot, scale):
        level = levels[index]
        rows = level.shape[0]
        if levels[index + 1].shape[0] == rows:
            other = jnp.where(
                level.odd_row, level.down(value, level.row_step), level.down(value, -level.row_step)
            )
            return scale * (value + other)
        write(buffer, slot, slice(0, rows), value)
        first, second = [pl.ds(begin, rows // 2, stride=2) for begin in range(2)]
        return scale * (read(buffer, slot, first) + read(buffer, slot, second))

    def opened(index, value, slot):
        level = levels[index]
        rows = level.shape[0]
        if value.shape[0] == rows:
            return value, jnp.where(
                level.odd_row, level.down(value, -level.row_step), level.down(value, level.row_step)
            )
        half = rows // 2
        blank = jnp.zeros((SUB, width), F32)
        for begin in range(2):
            write(buffer, slot, pl.ds(begin, half, stride=2), value)
        write(buffer, slot + 1, slice(SUB, 2 * SUB), blank)
        write(buffer, slot + 1, slice(rows, rows + SUB), blank)
        for begin in (SUB + 2, SUB - 1):
            write(buffer, slot + 1, pl.ds(begin, half, stride=2), value)
        return read(buffer, slot, slice(0, rows)), read(buffer, slot + 1, slice(SUB, SUB + rows))

    viscous, reaction, source = [None] * 5, [None] * 5, [None] * 5
    viscous[0], reaction[0], source[0] = whole(2), whole(1), whole(0)

    def coefficients(index):
        pair, reactions = levels[index].coefficients(viscous[index], reaction[index])
        viscous[index + 1] = folded(index, pair, 0, 0.0625)
        reaction[index + 1] = folded(index, reactions, 1, 0.25)

    def residual(index):
        source[index + 1] = folded(index, levels[index].residual(), 2, 0.25)

    last = levels[COARSE]
    block = 1 << COARSE
    cols_left = cols_total // block
    rows_left = last.shape[0]
    lane = iota(1, (rows_left, LANES))
    groups = 1 if cols_total < LANES else 2
    per_group = columns // groups

    def spread(*arrays):
        found = [[] for _ in arrays]
        for group in range(groups):
            for j in range(cols_left):
                column, place = divmod(block * j, LANES)
                column += group * per_group
                if groups == 1:
                    place = place + (lane & (LANES - cols_total))
                else:
                    place = jnp.full((rows_left, LANES), place, jnp.int32)
                for value, columns_found in zip(arrays, found):
                    tile = value[:, LANES * column : LANES * column + LANES]
                    columns_found.append(lane_take(tile, place))
        return found

    def flat(values, group, j):
        return values[group * cols_left + j]

    levels[0].take(source[0])
    coefficients(0)
    coefficients(1)
    residual(0)
    levels[1].take(source[1])
    coefficients(2)
    residual(1)
    levels[2].take(source[2])
    coefficients(3)
    residual(2)
    levels[3].take(source[3])
    viscous_columns, reaction_columns = spread(viscous[4], reaction[4])

    top, bottom = last.top[:, :LANES], last.bottom[:, :LANES]
    pulls, weights = [], []
    for group in range(groups):
        for j in range(cols_left):
            here = flat(viscous_columns, group, j)
            above = jnp.where(top, 0.0, last.down(here, last.row_step))
            below = jnp.where(bottom, 0.0, last.down(here, -last.row_step))
            links = [jnp.minimum(here, above), jnp.minimum(here, below)]
            links += [
                jnp.minimum(here, flat(viscous_columns, group, other))
                for other in (j - 1, j + 1)
                if 0 <= other < cols_left
            ]
            weight = OMEGA / (flat(reaction_columns, group, j) + sum(links))
            weights.append(weight)
            pulls.append([weight * link for link in links])
    residual(3)
    pushed = [w * s for w, s in zip(weights, spread(source[4])[0])]
    meanwhile()
    for index in range(COARSE - 1, -1, -1):
        levels[index].prepare()
    values = pushed
    for _ in range(COARSE_SWEEPS - 1):
        following = []
        for group in range(groups):
            for j in range(cols_left):
                at = group * cols_left + j
                here, pull = values[at], pulls[at]
                total = (KEEP * here + pushed[at]) + (
                    pull[0] * last.down(here, last.row_step)
                    + pull[1] * last.down(here, -last.row_step)
                )
                sides = [other for other in (j - 1, j + 1) if 0 <= other < cols_left]
                for link, other in zip(pull[2:], sides):
                    total = total + link * flat(values, group, other)
                following.append(total)
        values = following

    def laid(shift):
        found = []
        for column in range(columns):
            group = column // per_group
            place = ((lane & (cols_total - 1)) if groups == 1 else lane) // block
            place = place + (column % per_group) * (LANES // block)
            value = jnp.zeros((rows_left, LANES), F32)
            for j in range(cols_left):
                value = jnp.where(place == j + shift, flat(values, group, j), value)
            found.append(value)
        return found[0] if columns == 1 else jnp.concatenate(found, 1)

    corrections = [laid(shift) for shift in (0, 1, -1)]
    for index in range(COARSE - 1, -1, -1):
        corrections = levels[index].corrected(
            *[opened(index, value, 2 * at) for at, value in enumerate(corrections)]
        )
    return corrections


def up_kernel(size_x, size_y, gathered, state0, state1, state2, state3, out, *refs):
    grid, buffer, whole, window, swept3, corr1, corr2, corr3, merged0, merged1, merged2 = refs[:11]
    finished, sems = refs[11:]
    index_x, index_y = lax.axis_index("gx"), lax.axis_index("gy")
    rows_total, cols_total = CELLS * size_x, CELLS * size_y
    width = 2 * cols_total
    columns = width // LANES
    per_column = LANES // CELLS
    lane, sub = iota(1), iota(0)

    tall = iota(1, (size_x, LANES)) // CELLS
    modulus = min(size_y, per_column)
    for column in range(columns):
        comp = column // (columns // 2) if columns > 1 else 0
        first = (column % (columns // 2)) * per_column if columns > 1 else 0
        for slot, kind in ((2, 3), (1, 1), (0, 0)):
            chunks = [
                gathered[pl.ds(CHUNK * (first + j) + kind, size_x, stride=CHUNK * size_y), :]
                for j in range(modulus)
            ]
            for r in range(CELLS):
                turn = r + CELLS * comp
                value = chunks[0]
                for j in range(1, modulus):
                    value = jnp.where(((tall - turn) & (modulus - 1)) == j, chunks[j], value)
                grid[slot, column, pl.ds(r, size_x, stride=CELLS), :] = lane_roll(
                    value, -CELLS * turn
                )

    def ring_row(dx, dy):
        i = jnp.clip(index_x + dx, 0, size_x - 1)
        j = jnp.clip(index_y + dy, 0, size_y - 1)
        return jnp.broadcast_to(
            gathered[pl.ds(CHUNK * (i * size_y + j) + 2, 1), :], (SUB, LANES)
        )

    start = GUARD + RIM[3]

    def complete_ring():
        beside = {
            (dx, dy): ring_row(dx, dy) for dx in (-1, 0, 1) for dy in (-1, 0, 1) if dx or dy
        }
        for comp in range(2):
            base = comp * HALF
            for p in range(2):
                slot = 2 * comp + p
                end = 7 if p else 0
                corner_lane = LANES - 1 if p else SUB
                dy = -1 if p else 1
                for tile in range(2):
                    at = start + SUB * tile
                    index = base + (48 if p else 32) + SUB * tile + sub
                    ringed = lane_take(beside[0, dy], index)
                    swept = jnp.where(
                        lane == corner_lane,
                        tile_at(state3, ITERATE + slot, at)
                        + tile_at(state3, WEIGHT + p, at) * ringed,
                        tile_at(state3, SWEPT + slot, at),
                    )
                    swept3[slot, at : at + SUB, :] = swept
                for dx, at, edge in ((-1, start - 1, 16), (1, start + 2 * SUB, 0)):
                    index = base + edge + 8 * p
                    ringed = jnp.where(
                        lane == corner_lane,
                        lane_take(beside[dx, dy], jnp.full((SUB, LANES), index + end, jnp.int32)),
                        lane_take(beside[dx, 0], index + (lane & 7)),
                    )
                    rows = slice(at, at + 1)
                    swept3[slot, rows, :] = (
                        state3[ITERATE + slot, rows, :] + state3[WEIGHT + p, rows, :] * ringed[0:1]
                    )

    corrections = coarse_solve(grid, buffer, rows_total, cols_total, width, complete_ring)

    blank = jnp.zeros((SUB, width), F32)
    for kind, correction in enumerate(corrections):
        whole[kind, GUARD : GUARD + rows_total, :] = correction
        whole[kind, 0:GUARD, :] = blank
        whole[kind, GUARD + rows_total : GUARD + rows_total + SUB, :] = blank
    near_rows = pl.ds(pl.multiple_of(CELLS * index_x, SUB), 3 * SUB)
    for comp in range(2):
        shift = (2 * width - cols_total * comp - CELLS * index_y) % width
        for kind in range(3):
            turned = pltpu.roll(whole[kind, near_rows, :], shift, 1)
            if columns > 1:
                tall_lane = iota(1, (3 * SUB, LANES))
                turned = jnp.where(
                    tall_lane < HALF, turned[:, :LANES], turned[:, width - LANES :]
                )
            window[3 * comp + kind, 0 : 3 * SUB, :] = turned

    def swept_rows(ref, level, coarse_row, parity, here, beyond, across, comp):
        at = pl.ds(GUARD + RIM[level] + 2 * coarse_row + parity, SUB, stride=2)
        state = (state0, state1, state2, state3)[level]
        return [
            (ref[SWEPT + 2 * comp + p, at, :] + state[CENTRE + p, at, :] * here)
            + (state[SIDE + p, at, :] * beyond[p] + state[ACROSS + p, at, :] * across)
            for p in range(2)
        ]

    for comp in range(2):
        for tile in range(2):
            first = SUB * tile - 1
            at = GUARD + first
            here, left, right = [tile_at(window, 3 * comp + kind, at) for kind in range(3)]
            for parity in range(2):
                across = tile_at(window, 3 * comp, at + (1 if parity else -1))
                found = swept_rows(swept3, 3, first, parity, here, (left, right), across, comp)
                rows = pl.ds(GUARD + RIM[3] + 2 * first + parity, SUB, stride=2)
                for p in range(2):
                    corr3[2 * comp + p, rows, :] = found[p]

    corrs = [None, corr1, corr2, corr3]
    merged = [merged0, merged1, merged2]
    near = ((((lane + 32) & (LANES - 1)) - 32) >> 1) & (LANES - 1)
    odd_lane = (lane & 1) == 1
    for level in (2, 1, 0):
        coarse = level + 1
        corr, state, whole_rows = corrs[coarse], (state0, state1, state2)[level], merged[level]
        count = (LANES >> coarse) + 2
        origin = GUARD + RIM[coarse]
        places = [
            (comp, origin - 1 + SUB * tile)
            for tile in range(-(-count // SUB))
            for comp in range(2)
        ]
        pairs = {
            (comp, at): (tile_at(corr, 2 * comp, at), tile_at(corr, 2 * comp + 1, at))
            for comp, at in places
        }
        moved = {
            place: [lane_take(even, near), lane_take(odd, near)]
            for place, (even, odd) in pairs.items()
        }
        for place, (even, _) in pairs.items():
            moved[place].append(lane_take(even, (near + 1) & (LANES - 1)))
        for place, (_, odd) in pairs.items():
            moved[place].append(lane_take(odd, (near - 1) & (LANES - 1)))
        for (comp, at), (even_here, odd_here, even_next, odd_last) in moved.items():
            rows = slice(at, at + SUB)
            whole_rows[3 * comp, rows, :] = jnp.where(odd_lane, odd_here, even_here)
            whole_rows[3 * comp + 1, rows, :] = jnp.where(odd_lane, even_next, odd_here)
            whole_rows[3 * comp + 2, rows, :] = jnp.where(odd_lane, even_here, odd_last)
        if level > 0:
            first, tiles = -1, -(-count // SUB)
        else:
            first, tiles = 0, (count - 2) // SUB
        copies = []
        for tile in range(tiles):
            coarse_row = first + SUB * tile
            at = origin + coarse_row
            for comp in range(2):
                here, right, left = [tile_at(whole_rows, 3 * comp + k, at) for k in range(3)]
                for parity in range(2):
                    across = tile_at(whole_rows, 3 * comp, at + (1 if parity else -1))
                    found = swept_rows(
                        state, level, coarse_row, parity, here, (left, right), across, comp
                    )
                    if level > 0:
                        rows = pl.ds(GUARD + RIM[level] + 2 * coarse_row + parity, SUB, stride=2)
                        for p in range(2):
                            corrs[level][2 * comp + p, rows, :] = found[p]
                    else:
                        rows = pl.ds(2 * coarse_row + parity, SUB, stride=2)
                        finished[comp, rows, :] = jnp.where(
                            odd_lane,
                            lane_take(found[1], lane >> 1),
                            lane_take(found[0], lane >> 1),
                        )
            if level == 0 and tile + 1 in PIECES:
                piece = len(copies)
                begin = 2 * SUB * PIECES[piece - 1] if piece else 0
                rows = pl.ds(begin, 2 * SUB * (tile + 1) - begin)
                copy = pltpu.make_async_copy(
                    finished.at[:, rows, :], out.at[:, rows, :], sems.at[piece]
                )
                copy.start()
                copies.append(copy)
        for copy in copies:
            copy.wait()


def params():
    return pltpu.CompilerParams(vmem_limit_bytes=VMEM_LIMIT)


VMEM_SPEC = pl.BlockSpec(memory_space=pltpu.VMEM)
SMEM_SPEC = pl.BlockSpec(memory_space=pltpu.SMEM)
HBM_SPEC = pl.BlockSpec(memory_space=pltpu.HBM)


def swap_routes(size_x, size_y):
    def index(i, j):
        return i * size_y + j

    routes = []
    for axis in range(2):
        size = (size_x, size_y)[axis]
        for offset in range(2):
            route = []
            for i in range(size_x):
                for j in range(size_y):
                    here = (i, j)[axis]
                    other = here + 1 if here % 2 == offset else here - 1
                    if 0 <= other < size:
                        peer = (other, j) if axis == 0 else (i, other)
                    else:
                        peer = (i, j ^ 1) if axis == 0 else (i ^ 1, j)
                    route.append((index(i, j), index(*peer)))
            routes.append(route)
    return routes


def per_device(size_x, size_y, right_side, shift_coef, viscosity, wet_tiles):
    axes = ("gx", "gy")
    devices = size_x * size_y
    routes = swap_routes(size_x, size_y)
    band = pltpu.VMEM((4, HALO, LANES), F32)
    own = (right_side, shift_coef, viscosity)
    blank = pl.pallas_call(
        first_kernel,
        out_shape=pltpu.VMEM((SUB, LANES), F32),
        out_specs=VMEM_SPEC,
        cost_estimate=pl.CostEstimate(flops=FIRST_COST, bytes_accessed=FIRST_COST // 16, transcendentals=0),
        compiler_params=params(),
        name="first",
    )()
    wet_tiles, blank = lax.optimization_barrier((wet_tiles, blank))
    first, second = pl.pallas_call(
        bands_kernel,
        out_shape=(band, band),
        in_specs=[SMEM_SPEC] + [VMEM_SPEC] * 4,
        out_specs=(VMEM_SPEC,) * 2,
        compiler_params=params(),
        name="bands",
    )(wet_tiles, blank, *own)
    second = lax.ppermute(second, axes, routes[1])
    first = lax.ppermute(first, axes, routes[0])
    strip = jax.ShapeDtypeStruct((MESSAGE, LANES), F32)
    got = (second, first)
    meantime = pl.CostEstimate(flops=1 << 20, bytes_accessed=1 << 21, transcendentals=0)
    edges = pl.pallas_call(
        edges_kernel,
        out_shape=(pltpu.VMEM((MESSAGE, LANES), F32),) * 2,
        in_specs=[SMEM_SPEC] + [VMEM_SPEC] * 3,
        out_specs=(VMEM_SPEC,) * 2,
        cost_estimate=meantime,
        compiler_params=params(),
        name="edges",
    )(wet_tiles, *own)
    first, second = pl.pallas_call(
        functools.partial(strips_kernel, size_x),
        out_shape=(strip, strip),
        in_specs=[VMEM_SPEC] * 4,
        out_specs=(VMEM_SPEC,) * 2,
        compiler_params=params(),
        name="strips",
    )(*got, *edges)
    fields = pl.pallas_call(
        functools.partial(halves_kernel, size_x),
        out_shape=pltpu.VMEM((8, HELD[0], LANES), F32),
        in_specs=[SMEM_SPEC] + [VMEM_SPEC] * 5,
        out_specs=VMEM_SPEC,
        cost_estimate=meantime,
        compiler_params=params(),
        name="halves",
    )(wet_tiles, *got, *own)
    second = lax.ppermute(second, axes, routes[3])
    first = lax.ppermute(first, axes, routes[2])

    def buffers(counts):
        return [pltpu.VMEM((n, HELD[level], LANES), F32) for level, n in enumerate(counts)]

    chunks, *states = pl.pallas_call(
        functools.partial(down_kernel, size_y, devices),
        out_shape=(jax.ShapeDtypeStruct((CHUNK * devices, LANES), F32),)
        + tuple(buffers([STATE, STATE, STATE, STATE + 6])),
        in_specs=[VMEM_SPEC] * 3,
        out_specs=(VMEM_SPEC,) * (1 + LOCAL),
        scratch_shapes=buffers([2, 4, 4, 4])
        + buffers([2] * 4)
        + buffers([4, 8, 8, 8])
        + buffers([2, 4, 4, 4])
        + buffers([4] * 4)
        + buffers([4] * 4)
        + [pltpu.VMEM((2, HELD[0], LANES), F32), pltpu.VMEM((4, HELD[3], LANES), F32)],
        compiler_params=params(),
        name="down",
    )(second, first, fields)
    gathered = lax.all_to_all(chunks, axes, 0, 0, tiled=True)
    rows_total = CELLS * size_x
    width = 2 * CELLS * size_y
    return pl.pallas_call(
        functools.partial(up_kernel, size_x, size_y),
        out_shape=jax.ShapeDtypeStruct((2, LANES, LANES), F32),
        in_specs=[VMEM_SPEC] * (1 + LOCAL),
        out_specs=HBM_SPEC,
        scratch_shapes=[
            pltpu.VMEM((3, width // LANES, rows_total, LANES), F32),
            pltpu.VMEM((6, width // LANES, rows_total + 3 * SUB, LANES), F32),
            pltpu.VMEM((3, rows_total + 2 * SUB, width), F32),
            pltpu.VMEM((6, 5 * SUB, LANES), F32),
            pltpu.VMEM((4, HELD[3], LANES), F32),
        ]
        + [pltpu.VMEM((4, HELD[level], LANES), F32) for level in (1, 2, 3)]
        + [pltpu.VMEM((6, HELD[level + 1], LANES), F32) for level in (0, 1, 2)]
        + [pltpu.VMEM((2, LANES, LANES), F32), pltpu.SemaphoreType.DMA((len(PIECES),))],
        compiler_params=params(),
        name="up",
    )(gathered, *states)


def solution(mesh):
    sizes = dict(mesh.shape)
    placed = (P(None, "gx", "gy"), P("gx", "gy"), P("gx", "gy"), P("gx", "gy"))
    return jax.shard_map(
        functools.partial(per_device, sizes["gx"], sizes["gy"]),
        mesh=mesh,
        in_specs=placed,
        out_specs=P(None, "gx", "gy"),
        check_vma=False,
    )
```
